256 devices in a mesh: stream: 16 (over z, core), vert: 4 (over x), span: 4 (over y).
Axes of the slice: x: 4, y: 4, z: 8, core: 2. Of those that a mesh axis runs over, the one named last changes fastest.
Arguments:
- adjoint_source: float32 [3, 128, 48, 1024], P(None, 'stream', 'span', 'vert'), may hold values from -48 to 48
- velocity: float32 [3, 128, 48, 1024], P(None, 'stream', 'span', 'vert'), may hold values from -4 to 4
- penalty: float32 [128, 48, 1024], P('stream', 'span', 'vert'), may hold values from 0.05 to 2
- adjoint_start: float32 [3, 128, 48, 1024], P(None, 'stream', 'span', 'vert'), may hold values from -1800 to 1800
- cell_band: int32 [128, 48, 1024], P('stream', 'span', 'vert'), may hold values from 0 to 255
- tri_band: int32 [32768], P(('stream', 'vert', 'span')), may hold values from 0 to 255
- tri_weight: float32 [32768], P(('stream', 'vert', 'span')), may hold values from 0.5 to 2
Outputs:
- adjoint: float32 [3, 128, 48, 1024], P(None, 'stream', 'span', 'vert')
- tri_grad: float32 [32768], P(('stream', 'vert', 'span'))
The draws below stay inside these ranges and needn't reach their ends.
All inputs are finite; a program needn't handle non-finite values.
Results may differ from the reference program's by a relative error of at most 0.0003.
Values sent between devices are 32-bit elements; how exact they have to be, the bound alone decides.
A program may use at most 64 MiB of HBM per device.

```python
import math
import jax
import jax.numpy as jnp
from jax import lax

SWEEPS = 2
NBANDS = 256
NX = 128
NY = 1024
NZ = 48
NTRI = 32768


def set_ends(values, rng, low, high):
    longest = values.shape.index(max(values.shape))
    spots = []
    for shift in (0, 1):
        where = [jax.random.randint(jax.random.fold_in(rng, axis), (), 0, length) for axis, length in enumerate(values.shape)]
        where[longest] = (where[longest] + shift) % values.shape[longest]
        spots.append(tuple(where))
    return values.at[spots[0]].set(low).at[spots[1]].set(high)


def block_levels(own_key, dims, split, smallest, top_value):
    factor_of = 1.0
    for axis_at, parts in split:
        heights = jax.random.uniform(jax.random.fold_in(jax.random.fold_in(own_key, 6), axis_at), (parts,), jnp.float32, smallest / len(split), top_value / len(split))
        factor_of = factor_of * jnp.repeat(jnp.exp(heights), dims[axis_at] // parts).reshape((-1,) + (1,) * (len(dims) - 1 - axis_at))
    return factor_of


def bell_draw(stream_key, dims, scale, bound, shards=(), held_as=jnp.bfloat16):
    loudness = block_levels(stream_key, dims, shards, -0.22, 0.18) if shards else 1.0
    values = jax.random.normal(stream_key, dims, jnp.float32) * scale * loudness
    return jnp.minimum(jnp.maximum(values, -bound), bound).astype(held_as)


def setup_inputs(seed: int = 0) -> dict:
    keys = jax.random.split(jax.random.key(seed), 8)
    return {
        "adjoint_source": bell_draw(keys[0], (3, NX, NZ, NY), 8.0, 48.0, ((1, 16), (2, 4), (3, 4)), jnp.float32),
        "velocity": bell_draw(keys[1], (3, NX, NZ, NY), 1.0, 4.0, ((1, 16), (2, 4), (3, 4)), jnp.float32),
        "penalty": jnp.clip(jnp.exp(math.log(2.0) - 3.6888794 * jax.random.uniform(keys[2], (NX, NZ, NY), jnp.float32) ** block_levels(keys[2], (NX, NZ, NY), ((0, 16), (1, 4), (2, 4)), -0.2, 0.2)), 0.05, 2.0),
        "adjoint_start": bell_draw(keys[3], (3, NX, NZ, NY), 300.0, 1800.0, ((1, 16), (2, 4), (3, 4)), jnp.float32),
        "cell_band": set_ends(jax.random.randint(keys[4], (NX, NZ, NY), 0, NBANDS), jax.random.fold_in(keys[4], 1), 0, NBANDS - 1).astype(jnp.int32),
        "tri_band": set_ends(jax.random.randint(keys[5], (NTRI,), 0, NBANDS), jax.random.fold_in(keys[5], 1), 0, NBANDS - 1).astype(jnp.int32),
        "tri_weight": jnp.clip(jnp.exp(math.log(2.0) - 1.3862944 * jax.random.uniform(keys[6], (NTRI,), jnp.float32) ** block_levels(keys[6], (NTRI,), ((0, 256),), -0.2, 0.2)), 0.5, 2.0),
    }


stream_coef = 1000.0
stream_conv = 200.0
cross_coef = 0.25
cross_conv = 0.25
shift_coef = 0.5


def coefficients(velocity, penalty):
    along = velocity[0]
    vertical = velocity[1]
    spanwise = velocity[2]
    west_coef = stream_coef + stream_conv * jnp.maximum(-along, 0.0)
    east_coef = stream_coef + stream_conv * jnp.maximum(along, 0.0)
    south_coef = cross_coef + cross_conv * jnp.maximum(-vertical, 0.0)
    north_coef = cross_coef + cross_conv * jnp.maximum(vertical, 0.0)
    below_coef = cross_coef + cross_conv * jnp.maximum(-spanwise, 0.0)
    above_coef = cross_coef + cross_conv * jnp.maximum(spanwise, 0.0)
    diagonal_coef = west_coef + east_coef + south_coef + north_coef + below_coef + above_coef + penalty + shift_coef
    return west_coef, east_coef, (south_coef, north_coef, below_coef, above_coef), diagonal_coef


def explicit_side(adjoint_source, padded, adjoint, cross):
    south_coef, north_coef, below_coef, above_coef = cross
    result = adjoint_source + shift_coef * adjoint
    result = result + south_coef * padded[:, :, 1:-1, :-2] + north_coef * padded[:, :, 1:-1, 2:]
    result = result + below_coef * padded[:, :, :-2, 1:-1] + above_coef * padded[:, :, 2:, 1:-1]
    return result


def forward(carried, row_data):
    factor, offset = carried
    lower_coef, upper_coef, pivot_base, right_row = row_data
    pivot_value = pivot_base - lower_coef * factor
    factor_next = upper_coef / pivot_value
    offset_next = (right_row + lower_coef * offset) / pivot_value
    return (factor_next, offset_next), (factor_next, offset_next)


def line_solve(west_coef, east_coef, diagonal_coef, right_side):
    rows_first = jnp.moveaxis(right_side, 1, 0)
    zeros_line = jnp.zeros(rows_first.shape[1:], jnp.float32)
    ending, (factors, offsets) = lax.scan(forward, (zeros_line, zeros_line), (west_coef, east_coef, diagonal_coef, rows_first))

    def backward(following, row_data):
        factor, offset = row_data
        solved = offset + factor * following
        return solved, solved

    final, solved_rows = lax.scan(backward, zeros_line, (factors, offsets), reverse=True)
    return jnp.moveaxis(solved_rows, 0, 1)


def reference(adjoint_source, velocity, penalty, adjoint_start, cell_band, tri_band, tri_weight):
    west_coef, east_coef, cross, diagonal_coef = coefficients(velocity, penalty)
    adjoint = adjoint_start
    for sweep_index in range(SWEEPS):
        padded = jnp.pad(adjoint, ((0, 0), (0, 0), (1, 1), (1, 1)))
        right_side = explicit_side(adjoint_source, padded, adjoint, cross)
        adjoint = line_solve(west_coef, east_coef, diagonal_coef, right_side)
    sensitivity = penalty * jnp.sum(velocity * adjoint, axis=0)
    band_scale = (NBANDS / (NX * NY * NZ)) ** 0.5
    band_sums = jax.ops.segment_sum(sensitivity.reshape(-1), cell_band.reshape(-1), num_segments=NBANDS) * band_scale
    tri_grad = tri_weight * band_sums[tri_band]
    return adjoint, tri_grad
```

```python
import functools

import jax
import jax.numpy as jnp
from jax import lax
from jax.experimental import pallas as pl
from jax.experimental.pallas import tpu as pltpu
from jax.sharding import PartitionSpec as P

SWEEPS = 2
NBANDS = 256

STREAM = 16
VERT = 4
SPAN = 4
NC = 3
NXL = 8
NZL = 12
NYL = 256
ZP = 16
LANES = 128

stream_coef = 1000.0
stream_conv = 200.0
cross_coef = 0.25
cross_conv = 0.25
shift_coef = 0.5

MESH = pl.DeviceIdType.MESH
F32 = jnp.float32


OWNERS = 9


def owner_of(o):
    return jnp.where(o == OWNERS - 1, 9, 2 * o)


def kernel(
    src_h,
    vel_h,
    pen_h,
    start_h,
    band_h,
    tb_ref,
    tw_ref,
    out_h,
    tri_ref,
    SRC_IN,
    VEL,
    PEN,
    BAND,
    START,
    SRC,
    A1,
    A2,
    A3,
    PO,
    CR,
    IP,
    MM,
    FF,
    LL,
    RC,
    YS,
    YR,
    ZS,
    ZR,
    MS,
    MR,
    PS,
    PR,
    RS,
    RR,
    CO,
    OC,
    SH,
    SL,
    OHB,
    B1S,
    B1R,
    B2S,
    B2R,
    in_sem,
    out_sem,
    halo_send,
    halo_recv,
    m_send,
    m_recv,
    p_send,
    p_recv,
    r_send,
    r_recv,
    b_send,
    b_recv,
):
    me = lax.axis_index("stream")
    mv = lax.axis_index("vert")
    mp = lax.axis_index("span")

    def local_in(k, src, dst):
        return pltpu.make_async_copy(src, dst, in_sem.at[k])

    in_start = local_in(0, start_h, START)
    in_vel = local_in(1, vel_h, VEL)
    in_pen = local_in(2, pen_h, PEN)
    in_src = local_in(3, src_h, SRC_IN)
    in_band = local_in(4, band_h, BAND)
    for c in (in_start, in_vel, in_pen, in_src, in_band):
        c.start()

    YR[...] = jnp.zeros(YR.shape, F32)
    ZR[...] = jnp.zeros(ZR.shape, F32)

    barrier = pltpu.get_barrier_semaphore()

    def greet(j, carry):
        pl.semaphore_signal(
            barrier, inc=1, device_id=(lax.rem(me + j, STREAM), mv, mp), device_id_type=MESH
        )
        pl.semaphore_signal(
            barrier,
            inc=1,
            device_id=(me, lax.rem(mv + j // SPAN, VERT), lax.rem(mp + j % SPAN, SPAN)),
            device_id_type=MESH,
        )
        return carry

    lax.fori_loop(1, STREAM, greet, 0)

    lane = lax.broadcasted_iota(jnp.int32, (ZP, LANES), 1)

    def half(ref, c, x, t):
        return ref[c, x, :, t * LANES : (t + 1) * LANES]

    def pack_edges(k, a0, a1, low, high):
        low = jnp.where(lane == k, pltpu.roll(a0, k, 1), low)
        high = jnp.where(lane == k, pltpu.roll(a1, k + 1, 1), high)
        return low, high

    def halo_copies(s):
        def remote(i, src, dst, v, p):
            return pltpu.make_async_remote_copy(
                src_ref=src,
                dst_ref=dst,
                send_sem=halo_send.at[s, i],
                recv_sem=halo_recv.at[s, i],
                device_id=(me, v, p),
                device_id_type=MESH,
            )

        up = remote(0, ZS.at[s, 1], ZR.at[s, 0], mv, lax.rem(mp + 1, SPAN))
        down = remote(1, ZS.at[s, 0], ZR.at[s, 1], mv, lax.rem(mp + SPAN - 1, SPAN))
        north = remote(2, YS.at[s, 1], YR.at[s, 0], lax.rem(mv + 1, VERT), mp)
        south = remote(3, YS.at[s, 0], YR.at[s, 1], lax.rem(mv + VERT - 1, VERT), mp)
        return (
            (up, mp < SPAN - 1, mp > 0),
            (down, mp > 0, mp < SPAN - 1),
            (north, mv < VERT - 1, mv > 0),
            (south, mv > 0, mv < VERT - 1),
        )

    def each(copies, which, act):
        for item in copies:
            pl.when(item[which])(functools.partial(act, item[0]))

    def to_owners(src_of, dst, send_sem, recv_sem):
        def send(o, carry):
            owner = owner_of(o)

            @pl.when(owner != me)
            def _():
                pltpu.make_async_remote_copy(
                    src_ref=src_of(o),
                    dst_ref=dst,
                    send_sem=send_sem,
                    recv_sem=recv_sem,
                    device_id=(owner, mv, mp),
                    device_id_type=MESH,
                ).start()

            @pl.when(owner == me)
            def _():
                pltpu.make_async_copy(src_of(o), dst, recv_sem).start()

            return carry

        lax.fori_loop(0, OWNERS, send, 0)

    def drain(count, ref, sem):
        def one(j, carry):
            pltpu.make_async_copy(ref, ref, sem).wait()
            return carry

        lax.fori_loop(0, count, one, 0)

    is_owner = jnp.logical_or(lax.rem(me, 2) == 0, me == 9)
    my_o = jnp.where(me == 9, OWNERS - 1, me // 2)
    owner_sends = jnp.where(is_owner, OWNERS - 1, OWNERS)

    in_start.wait()
    zero_tile = jnp.zeros((ZP, LANES), F32)

    def pack_start(x, carry):
        low, high = carry
        for c in range(NC):
            k = c * NXL + x
            A1[c, x, 0:NZL, :] = START[c, x]
            ZS[0, 0, k] = START[c, x, 0:1, :]
            ZS[0, 1, k] = START[c, x, NZL - 1 : NZL, :]
            low, high = pack_edges(k, half(A1, c, x, 0), half(A1, c, x, 1), low, high)
        return low, high

    low, high = lax.fori_loop(0, NXL, pack_start, (zero_tile, zero_tile))
    YS[0, 0] = low
    YS[0, 1] = high

    pl.semaphore_wait(barrier, 2 * (STREAM - 1))
    halo1 = halo_copies(0)
    each(halo1, 1, lambda c: c.start())

    in_vel.wait()
    in_pen.wait()

    ones = jnp.ones((NZL, NYL), F32)

    def factor(x, carry):
        delta, lam = carry
        u = VEL[0, x]
        v = VEL[1, x]
        w = VEL[2, x]
        west = stream_coef + stream_conv * jnp.maximum(-u, 0.0)
        east = stream_coef + stream_conv * jnp.maximum(u, 0.0)
        CR[0, x, 0:NZL, :] = cross_coef + cross_conv * jnp.maximum(-v, 0.0)
        CR[1, x, 0:NZL, :] = cross_coef + cross_conv * jnp.maximum(v, 0.0)
        CR[2, x, 0:NZL, :] = cross_coef + cross_conv * jnp.maximum(-w, 0.0)
        CR[3, x, 0:NZL, :] = cross_coef + cross_conv * jnp.maximum(w, 0.0)
        excess = (
            (4.0 * cross_coef + shift_coef) + cross_conv * (jnp.abs(v) + jnp.abs(w)) + PEN[x]
        )
        ip = 1.0 / (east + (excess + west * delta))
        m = west * ip
        IP[x, 0:NZL, :] = ip
        MM[x, 0:NZL, :] = m
        FF[x, 0:NZL, :] = east * ip
        lam = m * lam
        LL[x, 0:NZL, :] = lam
        return (excess + west * delta) * ip, lam

    delta, lam = lax.fori_loop(0, NXL, factor, (ones, ones))
    l_last = LL[NXL - 1]
    r_last = FF[NXL - 1]
    RC[NXL - 1] = r_last

    def fold(i, carry):
        l, r = carry
        x = NXL - 2 - i
        f = FF[x]
        l = LL[x] + f * l
        r = f * r
        LL[x] = l
        RC[x] = r
        return l, r

    l_first, r_first = lax.fori_loop(0, NXL - 1, fold, (l_last, r_last))
    for k, value in enumerate((l_first, l_last, r_first, r_last)):
        for t in range(2):
            cut = slice(t * LANES, (t + 1) * LANES)
            MS[t, 8 * k : 8 * k + 8, :] = value[0:8, cut]
            MS[2, 8 * k + 4 * t : 8 * k + 4 * t + 4, :] = value[8:NZL, cut]
    to_owners(lambda o: MS.at[o // NC], MR.at[me], m_send, m_recv)

    in_band.wait()
    iota_l = lax.broadcasted_iota(jnp.int32, (16, NYL), 0)

    def onehot(x, carry):
        for z in range(NZL):
            low_part = lax.rem(BAND[x, z : z + 1, :], 16)
            OHB[x, :, z * NYL : (z + 1) * NYL] = jnp.where(
                jnp.broadcast_to(low_part, (16, NYL)) == iota_l, 1.0, 0.0
            ).astype(jnp.bfloat16)
        return carry

    lax.fori_loop(0, NXL, onehot, 0)

    drain(owner_sends, MS.at[0], m_send)

    @pl.when(is_owner)
    def _():
        pltpu.make_async_copy(MR, MR, m_recv).wait()

        def reduced(d, F):
            lf, lg, rf, rg = (MR[d, 8 * k : 8 * k + 8, :] for k in range(4))
            inv = 1.0 / (1.0 - lf * F)
            b = lg * inv
            g = b * F
            CO[d, 0] = g
            CO[d, 1] = b
            CO[d, 2] = inv
            CO[d, 3] = lf * inv
            CO[d, 4] = rf * inv
            CO[d, 5] = F
            return rg + g * rf

        lax.fori_loop(0, STREAM, reduced, jnp.zeros((8, LANES), F32))

    in_src.wait()

    def pad_source(x, carry):
        for c in range(NC):
            SRC[c, x, 0:NZL, :] = SRC_IN[c, x]
        return carry

    lax.fori_loop(0, NXL, pad_source, 0)
    first = lane == 0
    last = lane == LANES - 1
    depth = lax.broadcasted_iota(jnp.int32, (ZP, LANES), 0)
    floor = depth == 0
    top = depth == NZL - 1

    def sweep(s, A, halo, store):
        each(halo, 2, lambda c: c.wait_recv())
        hl = YR[s, 0]
        hh = YR[s, 1]

        def row(x, offsets):
            south, north, below, above = (CR[i, x] for i in range(4))
            ip = IP[x]
            m = MM[x]
            new = []
            for c in range(NC):
                k = c * NXL + x
                a0 = half(A, c, x, 0)
                a1 = half(A, c, x, 1)
                r0 = pltpu.roll(a0, 1, 1)
                r1 = pltpu.roll(a1, 1, 1)
                q0 = pltpu.roll(a0, LANES - 1, 1)
                q1 = pltpu.roll(a1, LANES - 1, 1)
                lo = pltpu.roll(hl, lax.rem(LANES - k, LANES), 1)
                hi = pltpu.roll(hh, LANES - 1 - k, 1)
                y_lo = (jnp.where(first, lo, r0), jnp.where(first, r0, r1))
                y_hi = (jnp.where(last, q1, q0), jnp.where(last, hi, q1))
                for t, a in enumerate((a0, a1)):
                    cut = slice(t * LANES, (t + 1) * LANES)
                    rhs = half(SRC, c, x, t) + shift_coef * a
                    rhs = rhs + south[:, cut] * y_lo[t] + north[:, cut] * y_hi[t]
                    z_lo = jnp.where(floor, ZR[s, 0, k, :, cut], pltpu.roll(a, 1, 0))
                    z_hi = jnp.where(top, ZR[s, 1, k, :, cut], pltpu.roll(a, ZP - 1, 0))
                    rhs = rhs + below[:, cut] * z_lo + above[:, cut] * z_hi
                    o = rhs * ip[:, cut] + m[:, cut] * offsets[2 * c + t]
                    PO[c, x, :, cut] = o
                    new.append(o)
            return tuple(new)

        o_last = lax.fori_loop(0, NXL, row, (zero_tile,) * 6)

        def back(i, p):
            x = NXL - 2 - i
            f = FF[x]
            new = []
            for c in range(NC):
                for t in range(2):
                    cut = slice(t * LANES, (t + 1) * LANES)
                    value = PO[c, x, :, cut] + f[:, cut] * p[2 * c + t]
                    PO[c, x, :, cut] = value
                    new.append(value)
            return tuple(new)

        p_first = lax.fori_loop(0, NXL - 1, back, o_last)
        for c in range(NC):
            for t in range(2):
                for place, value in ((0, p_first[2 * c + t]), (8, o_last[2 * c + t])):
                    PS[s, NC * t + c, place : place + 8, :] = value[0:8]
                    PS[s, 2 * NC + c, place + 4 * t : place + 4 * t + 4, :] = value[8:NZL]
        to_owners(lambda o: PS.at[s, o], PR.at[s, me], p_send.at[s], p_recv.at[s])

        @pl.when(is_owner)
        def _():
            everything = PR.at[s]
            pltpu.make_async_copy(everything, everything, p_recv.at[s]).wait()
            O = jnp.zeros((8, LANES), F32)
            for d in range(STREAM):
                OC[d] = O
                O = PR[s, d, 8:16, :] + CO[d, 0] * PR[s, d, 0:8, :] + CO[d, 1] * O
            f_next = jnp.zeros((8, LANES), F32)
            for d in reversed(range(STREAM)):
                RS[s, d, 8:16, :] = f_next
                O = OC[d]
                f_next = CO[d, 2] * PR[s, d, 0:8, :] + CO[d, 3] * O + CO[d, 4] * f_next
                RS[s, d, 0:8, :] = CO[d, 5] * f_next + O

            def reply(j, carry):
                d = lax.rem(me + j, STREAM)

                pltpu.make_async_remote_copy(
                    src_ref=RS.at[s, d],
                    dst_ref=RR.at[s, my_o, pl.ds(0, ZP), :],
                    send_sem=r_send.at[s],
                    recv_sem=r_recv.at[s],
                    device_id=(d, mv, mp),
                    device_id_type=MESH,
                ).start()
                return carry

            lax.fori_loop(1, STREAM, reply, 0)
            pltpu.make_async_copy(
                RS.at[s, me], RR.at[s, my_o, pl.ds(0, ZP), :], r_recv.at[s]
            ).start()

        drain(owner_sends, PS.at[s, 0], p_send.at[s])
        arrived = RR.at[s, :, pl.ds(0, ZP), :]
        pltpu.make_async_copy(arrived, arrived, r_recv.at[s]).wait()

        def interface(place):
            return [
                jnp.concatenate(
                    [
                        RR[s, NC * t + c, place : place + 8, :],
                        RR[s, 2 * NC + c, place + 4 * t : place + 4 * t + 8, :],
                    ],
                    axis=0,
                )
                for c in range(NC)
                for t in range(2)
            ]

        a_left = interface(0)
        a_right = interface(8)

        def solved(x, c, t):
            cut = slice(t * LANES, (t + 1) * LANES)
            return (
                PO[c, x, :, cut]
                + LL[x, :, cut] * a_left[2 * c + t]
                + RC[x, :, cut] * a_right[2 * c + t]
            )

        return store(solved)

    def store_first(solved):
        def line(x, carry):
            low, high = carry
            for c in range(NC):
                pair = [solved(x, c, t) for t in range(2)]
                for t in range(2):
                    A2[c, x, 0:NZL, t * LANES : (t + 1) * LANES] = pair[t][0:NZL]
                    ZS[1, 0, c * NXL + x, :, t * LANES : (t + 1) * LANES] = pair[t][0:1]
                    ZS[1, 1, c * NXL + x, :, t * LANES : (t + 1) * LANES] = pair[t][
                        NZL - 1 : NZL
                    ]
                low, high = pack_edges(c * NXL + x, pair[0], pair[1], low, high)
            return low, high

        low, high = lax.fori_loop(0, NXL, line, (zero_tile, zero_tile))
        YS[1, 0] = low
        YS[1, 1] = high

    sweep(0, A1, halo1, store_first)
    halo2 = halo_copies(1)
    each(halo2, 1, lambda c: c.start())

    def store_last(solved):
        def line(x, carry):
            for t in range(2):
                cut = slice(t * LANES, (t + 1) * LANES)
                total = None
                for c in range(NC):
                    a = solved(x, c, t)[0:NZL]
                    A3[c, x, :, cut] = a
                    term = half(VEL, c, x, t) * a
                    total = term if total is None else total + term
                total = total * PEN[x, :, cut]
                coarse = total.astype(jnp.bfloat16).astype(F32)
                SH[x, :, cut] = coarse
                SL[x, :, cut] = total - coarse
            return carry

        lax.fori_loop(0, NXL, line, 0)

    sweep(1, A2, halo2, store_last)
    out_copy = pltpu.make_async_copy(A3, out_h, out_sem)
    out_copy.start()

    def band_rows(x, acc):
        parts = []
        for z in range(NZL):
            high_part = jnp.broadcast_to(BAND[x, z : z + 1, :] // 16, (16, NYL)) == iota_l
            parts.append(
                jnp.concatenate(
                    [
                        jnp.where(high_part, jnp.broadcast_to(S[x, z : z + 1, :], (16, NYL)), 0.0)
                        for S in (SH, SL)
                    ],
                    axis=0,
                ).astype(jnp.bfloat16)
            )
        weights = jnp.concatenate(parts, axis=1)
        return acc + lax.dot_general(
            weights, OHB[x], (((1,), (1,)), ((), ())), preferred_element_type=F32
        )

    acc = lax.fori_loop(0, NXL, band_rows, jnp.zeros((32, 16), F32))
    sums = acc[0:16] + acc[16:32]
    wide = jnp.concatenate([sums] * 8, axis=1)
    keep = lax.broadcasted_iota(jnp.int32, (8, LANES), 1) // 16 == lax.broadcasted_iota(
        jnp.int32, (8, LANES), 0
    )
    for h in range(2):
        B1S[h : h + 1, :] = jnp.sum(
            jnp.where(keep, wide[8 * h : 8 * h + 8], 0.0), axis=0, keepdims=True
        )

    def band_round(r, own, slots, device_of):
        def send(j, carry):
            pltpu.make_async_remote_copy(
                src_ref=own,
                dst_ref=slots.at[j],
                send_sem=b_send.at[r],
                recv_sem=b_recv.at[r],
                device_id=device_of(j),
                device_id_type=MESH,
            ).start()
            return carry

        lax.fori_loop(1, STREAM, send, 0)
        got = slots.at[pl.ds(1, STREAM - 1)]
        pltpu.make_async_copy(got, got, b_recv.at[r]).wait()
        total = own[...]
        for j in range(1, STREAM):
            total = total + slots[j]
        return total

    B2S[...] = band_round(
        0, B1S, B1R, lambda j: (lax.rem(me + j, STREAM), mv, mp)
    )
    bands = band_round(
        1,
        B2S,
        B2R,
        lambda j: (me, lax.rem(mv + j // SPAN, VERT), lax.rem(mp + j % SPAN, SPAN)),
    )
    cells = STREAM * VERT * SPAN * NXL * NZL * NYL
    bands = bands * ((NBANDS / cells) ** 0.5)
    tb = tb_ref[...].reshape(1, LANES)
    spot = jnp.broadcast_to(lax.rem(tb, LANES), (8, LANES))
    low_half = jnp.take_along_axis(jnp.broadcast_to(bands[0:1], (8, LANES)), spot, axis=1)
    high_half = jnp.take_along_axis(jnp.broadcast_to(bands[1:2], (8, LANES)), spot, axis=1)
    picked = jnp.where(tb < LANES, low_half[0:1], high_half[0:1])
    tri_ref[...] = (tw_ref[...].reshape(1, LANES) * picked).reshape(LANES)

    out_copy.wait()
    each(halo1, 1, lambda c: c.wait_send())
    each(halo2, 1, lambda c: c.wait_send())

    @pl.when(is_owner)
    def _():
        for s in range(SWEEPS):
            drain(STREAM - 1, RS.at[s, 0], r_send.at[s])

    for r, own in enumerate((B1S, B2S)):
        drain(STREAM - 1, own, b_send.at[r])


def shards(adjoint_source, velocity, penalty, adjoint_start, cell_band, tri_band, tri_weight):
    anywhere = pl.BlockSpec(memory_space=pl.ANY)
    vmem = pl.BlockSpec(memory_space=pltpu.VMEM)
    scratch = [
        pltpu.VMEM((NC, NXL, NZL, NYL), F32),
        pltpu.VMEM((NC, NXL, NZL, NYL), F32),
        pltpu.VMEM((NXL, NZL, NYL), F32),
        pltpu.VMEM((NXL, NZL, NYL), jnp.int32),
        pltpu.VMEM((NC, NXL, NZL, NYL), F32),
        pltpu.VMEM((NC, NXL, ZP, NYL), F32),
        pltpu.VMEM((NC, NXL, ZP, NYL), F32),
        pltpu.VMEM((NC, NXL, ZP, NYL), F32),
        pltpu.VMEM((NC, NXL, NZL, NYL), F32),
        pltpu.VMEM((NC, NXL, ZP, NYL), F32),
        pltpu.VMEM((4, NXL, ZP, NYL), F32),
        pltpu.VMEM((NXL, ZP, NYL), F32),
        pltpu.VMEM((NXL, ZP, NYL), F32),
        pltpu.VMEM((NXL, ZP, NYL), F32),
        pltpu.VMEM((NXL, ZP, NYL), F32),
        pltpu.VMEM((NXL, ZP, NYL), F32),
        pltpu.VMEM((SWEEPS, 2, ZP, LANES), F32),
        pltpu.VMEM((SWEEPS, 2, ZP, LANES), F32),
        pltpu.VMEM((SWEEPS, 2, NC * NXL, 1, NYL), F32),
        pltpu.VMEM((SWEEPS, 2, NC * NXL, 1, NYL), F32),
        pltpu.VMEM((3, 32, LANES), F32),
        pltpu.VMEM((STREAM, 32, LANES), F32),
        pltpu.VMEM((SWEEPS, OWNERS, ZP, LANES), F32),
        pltpu.VMEM((SWEEPS, STREAM, ZP, LANES), F32),
        pltpu.VMEM((SWEEPS, STREAM, ZP, LANES), F32),
        pltpu.VMEM((SWEEPS, OWNERS, ZP + 8, LANES), F32),
        pltpu.VMEM((STREAM, 6, 8, LANES), F32),
        pltpu.VMEM((STREAM, 8, LANES), F32),
        pltpu.VMEM((NXL, NZL, NYL), F32),
        pltpu.VMEM((NXL, NZL, NYL), F32),
        pltpu.VMEM((NXL, 16, NZL * NYL), jnp.bfloat16),
        pltpu.VMEM((2, LANES), F32),
        pltpu.VMEM((STREAM, 2, LANES), F32),
        pltpu.VMEM((2, LANES), F32),
        pltpu.VMEM((STREAM, 2, LANES), F32),
        pltpu.SemaphoreType.DMA((5,)),
        pltpu.SemaphoreType.DMA,
        pltpu.SemaphoreType.DMA((SWEEPS, 4)),
        pltpu.SemaphoreType.DMA((SWEEPS, 4)),
        pltpu.SemaphoreType.DMA,
        pltpu.SemaphoreType.DMA,
        pltpu.SemaphoreType.DMA((SWEEPS,)),
        pltpu.SemaphoreType.DMA((SWEEPS,)),
        pltpu.SemaphoreType.DMA((SWEEPS,)),
        pltpu.SemaphoreType.DMA((SWEEPS,)),
        pltpu.SemaphoreType.DMA((2,)),
        pltpu.SemaphoreType.DMA((2,)),
    ]
    return pl.pallas_call(
        kernel,
        out_shape=(
            jax.ShapeDtypeStruct((NC, NXL, NZL, NYL), F32),
            jax.ShapeDtypeStruct((LANES,), F32),
        ),
        in_specs=[anywhere] * 5 + [vmem] * 2,
        out_specs=(anywhere, vmem),
        scratch_shapes=scratch,
        compiler_params=pltpu.CompilerParams(
            collective_id=0, has_side_effects=True, vmem_limit_bytes=32 * 1024 * 1024
        ),
    )(adjoint_source, velocity, penalty, adjoint_start, cell_band, tri_band, tri_weight)


def solution(mesh):
    return jax.shard_map(
        shards,
        mesh=mesh,
        in_specs=(
            P(None, "stream", "span", "vert"),
            P(None, "stream", "span", "vert"),
            P("stream", "span", "vert"),
            P(None, "stream", "span", "vert"),
            P("stream", "span", "vert"),
            P(("stream", "vert", "span")),
            P(("stream", "vert", "span")),
        ),
        out_specs=(P(None, "stream", "span", "vert"), P(("stream", "vert", "span"))),
        check_vma=False,
    )
```

```python
import functools

import jax
import jax.numpy as jnp
from jax import lax
from jax.experimental import pallas as pl
from jax.experimental.pallas import tpu as pltpu
from jax.sharding import PartitionSpec as P

SWEEPS = 2
NBANDS = 256

STREAM = 16
CHIPS = 8
VERT = 4
SPAN = 4
NC = 3
NXL = 8
NXC = 16
NZL = 12
NYL = 256
LANES = 128

stream_coef = 1000.0
stream_conv = 200.0
cross_coef = 0.25
cross_conv = 0.25
shift_coef = 0.5

MESH = pl.DeviceIdType.MESH
F32 = jnp.float32


def kernel(
    src_h,
    vel_h,
    pen_h,
    start_h,
    band_h,
    tb_h,
    tw_h,
    out_h,
    tri_h,
    SRC,
    VEL,
    PEN,
    BAND,
    A1,
    A2,
    A3,
    PP,
    IP,
    M1,
    M2,
    M4,
    MT,
    F1,
    F2,
    F4,
    FT,
    LL,
    RC,
    YS,
    YR,
    MS,
    MR,
    CB,
    CG,
    OWN,
    S1,
    R1,
    S2,
    R2,
    AL,
    AR,
    SH,
    SL,
    OHB,
    B1S,
    B1R,
    B2S,
    B2R,
    TB,
    TW,
    TRI,
    in_sem,
    side_send,
    side_recv,
    out_sem,
    tri_sem,
    halo_send,
    halo_recv,
    m_send,
    m_recv,
    p_send,
    p_recv,
    b_send,
    b_recv,
):
    me = lax.axis_index("stream")
    mv = lax.axis_index("vert")
    mp = lax.axis_index("span")
    chip = me // 2
    q = lax.rem(me, 2)
    partner = 2 * chip + (1 - q)

    def lanes_of(half):
        return pl.ds(pl.multiple_of(half * LANES, LANES), LANES)

    def pieces(ref, dst):
        rank = len(ref.shape)
        lead = (slice(None),) * (rank - 1)
        return lambda half: ref.at[lead + (lanes_of(half),)], dst

    inner = A1.at[:, pl.ds(1, NZL)]
    inputs = (
        (start_h, inner),
        (vel_h, VEL),
        (pen_h, PEN),
        (src_h, SRC),
        (band_h, BAND),
    )

    def slot(dst, half):
        if len(dst.shape) == 5:
            return dst.at[:, :, half]
        return dst.at[:, half]

    def part(src, half):
        if len(src.shape) == 4:
            return src.at[:, :, :, lanes_of(half)]
        return src.at[:, :, lanes_of(half)]

    own_copies = []
    side_copies = []
    for i, (src, dst) in enumerate(inputs):
        own_copies.append(pltpu.make_async_copy(part(src, q), slot(dst, q), in_sem.at[i]))
        side_copies.append(
            pltpu.make_async_remote_copy(
                src_ref=part(src, 1 - q),
                dst_ref=slot(dst, q),
                send_sem=side_send.at[i],
                recv_sem=side_recv.at[i],
                device_id=(partner, mv, mp),
                device_id_type=MESH,
            )
        )
    tb_copy = pltpu.make_async_copy(tb_h, TB, tri_sem.at[0])
    tw_copy = pltpu.make_async_copy(tw_h, TW, tri_sem.at[1])

    barrier = pltpu.get_barrier_semaphore()

    def greet(j, carry):
        pl.semaphore_signal(
            barrier, inc=1, device_id=(lax.rem(me + j, STREAM), mv, mp), device_id_type=MESH
        )
        pl.semaphore_signal(
            barrier,
            inc=1,
            device_id=(me, lax.rem(mv + j // SPAN, VERT), lax.rem(mp + j % SPAN, SPAN)),
            device_id_type=MESH,
        )
        return carry

    outer_v = mv - 1 + 2 * q
    has_outer = jnp.logical_and(outer_v >= 0, outer_v < VERT)
    outer_id = (partner, lax.rem(outer_v + VERT, VERT), mp)

    nothing = jnp.zeros((2, 8, LANES), F32)
    for A in (A1, A2):
        for c in range(NC):
            A[c, 0] = nothing
            A[c, NZL + 1] = nothing
    YR[...] = jnp.zeros(YR.shape, F32)

    lax.fori_loop(1, STREAM, greet, 0)

    @pl.when(has_outer)
    def _():
        pl.semaphore_signal(barrier, inc=1, device_id=outer_id, device_id_type=MESH)

    for copy in own_copies:
        copy.start()
    tb_copy.start()
    tw_copy.start()
    pl.semaphore_wait(barrier, 2 * (STREAM - 1) + jnp.where(has_outer, 1, 0))
    for copy in side_copies:
        copy.start()

    row = lax.broadcasted_iota(jnp.int32, (8, LANES), 0)
    lane = lax.broadcasted_iota(jnp.int32, (8, LANES), 1)

    def pack_edges(k, pair, packs):
        low, high = packs
        hit = lane == k
        low = tuple(jnp.where(hit, pltpu.roll(pair[h], k, 1), low[h]) for h in range(2))
        high = tuple(jnp.where(hit, pltpu.roll(pair[h], k + 1, 1), high[h]) for h in range(2))
        return low, high

    blank = jnp.zeros((8, LANES), F32)
    no_packs = ((blank, blank), (blank, blank))

    def send_halo(s, A, packs):
        for side in range(2):
            for h in range(2):
                YS[s, side, h] = packs[side][h]

        def remote(i, src, dst, device):
            return pltpu.make_async_remote_copy(
                src_ref=src,
                dst_ref=dst,
                send_sem=halo_send.at[s, i],
                recv_sem=halo_recv.at[s, i],
                device_id=device,
                device_id_type=MESH,
            )

        copies = (
            (
                remote(0, A.at[:, NZL], A.at[:, 0], (me, mv, lax.rem(mp + 1, SPAN))),
                mp < SPAN - 1,
                mp > 0,
            ),
            (
                remote(1, A.at[:, 1], A.at[:, NZL + 1], (me, mv, lax.rem(mp + SPAN - 1, SPAN))),
                mp > 0,
                mp < SPAN - 1,
            ),
            (remote(2, YS.at[s, q], YR.at[s, 1 - q], outer_id), has_outer, has_outer),
            (remote(3, YS.at[s, 1 - q], YR.at[s, q], (partner, mv, mp)), None, None),
        )
        each(copies, 1, lambda c: c.start())
        return copies

    def each(copies, which, act):
        for item in copies:
            if item[which] is None:
                act(item[0])
            else:
                pl.when(item[which])(functools.partial(act, item[0]))

    own_copies[0].wait()
    side_copies[0].wait_recv()

    def pack_start(z, packs):
        for c in range(NC):
            packs = pack_edges(c * NZL + z, (A1[c, z + 1, 0], A1[c, z + 1, 1]), packs)
        return packs

    halo1 = send_halo(0, A1, lax.fori_loop(0, NZL, pack_start, no_packs))

    for i in (1, 2):
        own_copies[i].wait()
        side_copies[i].wait_recv()

    def flat(ref):
        count = 1
        for size in ref.shape[:-1]:
            count *= size
        return ref.reshape(count, LANES)

    velocity2, penalty2 = flat(VEL), flat(PEN)
    ip2, m2, f2 = flat(IP), flat(M1), flat(F1)
    l2, r2, p2 = flat(LL), flat(RC), flat(PP)

    def level(ref2, x, c=0):
        return ref2[pl.ds(c * NZL * NXC + x, NZL, stride=NXC), :]

    delta = jnp.ones((NZL, LANES), F32)
    for x in range(NXC):
        u = level(velocity2, x, 0)
        west = stream_coef + stream_conv * jnp.maximum(-u, 0.0)
        east = stream_coef + stream_conv * jnp.maximum(u, 0.0)
        excess = (
            (4.0 * cross_coef + shift_coef)
            + cross_conv * (jnp.abs(level(velocity2, x, 1)) + jnp.abs(level(velocity2, x, 2)))
            + level(penalty2, x)
        )
        sink = excess + west * delta
        ip = 1.0 / (east + sink)
        delta = sink * ip
        place = pl.ds(x, NZL, stride=NXC)
        ip2[place, :] = ip
        m2[place, :] = west * ip
        f2[place, :] = east * ip

    def ahead(v, n, fill):
        return jnp.where(row >= n, pltpu.roll(v, n, 0), fill)

    def behind(v, n, fill):
        return jnp.where(row < 8 - n, pltpu.roll(v, 8 - n, 0), fill)

    def fold_up(values, f1, f2, f4, ft):
        new = []
        for h in range(2):
            v = values[h]
            v = v + f1[h] * pltpu.roll(v, 7, 0)
            v = v + f2[h] * pltpu.roll(v, 6, 0)
            v = v + f4[h] * pltpu.roll(v, 4, 0)
            new.append(v)
        new[0] = new[0] + ft * jnp.broadcast_to(new[1][0:1], (8, LANES))
        return new

    def factor(z, carry):
        chains = []
        tails = []
        f1s, f2s, f4s, fts = [], [], [], []
        for h in range(2):
            m = M1[z, h]
            f = F1[z, h]
            m1 = jnp.where(row >= 1, m, 0.0)
            mm = m1 * ahead(m, 1, 0.0)
            m4 = jnp.where(row >= 4, jnp.where(row >= 2, mm, 0.0) * pltpu.roll(mm, 2, 0), 0.0)
            mm = jnp.where(row >= 2, mm, 0.0)
            M1[z, h] = m1
            M2[z, h] = mm
            M4[z, h] = m4
            t = m * ahead(m, 1, 1.0)
            t = t * ahead(t, 2, 1.0)
            chains.append(t * ahead(t, 4, 1.0))
            f1 = jnp.where(row < 7, f, 0.0)
            ff = jnp.where(row < 6, f1 * behind(f, 1, 0.0), 0.0)
            f4 = jnp.where(row < 4, ff * pltpu.roll(ff, 6, 0), 0.0)
            F1[z, h] = f1
            F2[z, h] = ff
            F4[z, h] = f4
            f1s.append(f1)
            f2s.append(ff)
            f4s.append(f4)
            t = f * behind(f, 1, 1.0)
            t = t * behind(t, 2, 1.0)
            tails.append(t * behind(t, 4, 1.0))
        MT[z] = chains[1]
        FT[z] = tails[0]
        left = [chains[0], chains[1] * jnp.broadcast_to(chains[0][7:8], (8, LANES))]
        left = fold_up(left, f1s, f2s, f4s, tails[0])
        right = [tails[0] * jnp.broadcast_to(tails[1][0:1], (8, LANES)), tails[1]]
        for h in range(2):
            LL[z, h] = left[h]
            RC[z, h] = right[h]
        return carry

    lax.fori_loop(0, NZL, factor, 0)
    for k, ref2 in enumerate((l2, r2)):
        MS[2 * k] = level(ref2, 0)
        MS[2 * k + 1] = level(ref2, NXC - 1)

    def to_chips(src_of, dst, send_sem, recv_sem):
        def send(j, carry):
            target = lax.rem(chip + j, CHIPS)
            pltpu.make_async_remote_copy(
                src_ref=src_of(target),
                dst_ref=dst.at[chip],
                send_sem=send_sem,
                recv_sem=recv_sem,
                device_id=(2 * target + q, mv, mp),
                device_id_type=MESH,
            ).start()
            return carry

        lax.fori_loop(1, CHIPS, send, 0)

    def arrive(slots, sem):
        got = slots.at[pl.ds(1, CHIPS - 1)]
        pltpu.make_async_copy(got, got, sem).wait()

    to_chips(lambda target: MS, MR, m_send, m_recv)

    for i in (3,):
        own_copies[i].wait()
        side_copies[i].wait_recv()

    first = lane == 0
    last = lane == LANES - 1

    def eliminate(s, A, halo):
        each(halo, 2, lambda c: c.wait_recv())
        edges = [[YR[s, side, h] for h in range(2)] for side in range(2)]

        def plane(z, carry):
            cross = []
            for h in range(2):
                v = VEL[1, z, h]
                w = VEL[2, z, h]
                cross.append(
                    (
                        cross_coef + cross_conv * jnp.maximum(-v, 0.0),
                        cross_coef + cross_conv * jnp.maximum(v, 0.0),
                        cross_coef + cross_conv * jnp.maximum(-w, 0.0),
                        cross_coef + cross_conv * jnp.maximum(w, 0.0),
                    )
                )
            ip = [IP[z, h] for h in range(2)]
            m1 = [M1[z, h] for h in range(2)]
            m2 = [M2[z, h] for h in range(2)]
            m4 = [M4[z, h] for h in range(2)]
            f1 = [F1[z, h] for h in range(2)]
            f2 = [F2[z, h] for h in range(2)]
            f4 = [F4[z, h] for h in range(2)]
            mt = MT[z]
            ft = FT[z]
            for c in range(NC):
                k = c * NZL + z
                o = []
                for h in range(2):
                    south, north, below, above = cross[h]
                    a = A[c, z + 1, h]
                    lo = pltpu.roll(edges[0][h], lax.rem(LANES - k, LANES), 1)
                    hi = pltpu.roll(edges[1][h], LANES - 1 - k, 1)
                    y_lo = jnp.where(first, lo, pltpu.roll(a, 1, 1))
                    y_hi = jnp.where(last, hi, pltpu.roll(a, LANES - 1, 1))
                    rhs = SRC[c, z, h] + shift_coef * a
                    rhs = rhs + south * y_lo + north * y_hi
                    rhs = rhs + below * A[c, z, h] + above * A[c, z + 2, h]
                    v = rhs * ip[h]
                    v = v + m1[h] * pltpu.roll(v, 1, 0)
                    v = v + m2[h] * pltpu.roll(v, 2, 0)
                    v = v + m4[h] * pltpu.roll(v, 4, 0)
                    o.append(v)
                o[1] = o[1] + mt * jnp.broadcast_to(o[0][7:8], (8, LANES))
                p = fold_up(o, f1, f2, f4, ft)
                for h in range(2):
                    PP[c, z, h] = p[h]
            return carry

        lax.fori_loop(0, NZL, plane, 0)

    eliminate(0, A1, halo1)
    for c in range(NC):
        S1[0, c] = level(p2, 0, c)
        S1[1, c] = level(p2, NXC - 1, c)
    to_chips(lambda target: S1, R1, p_send.at[0], p_recv.at[0])

    own_copies[4].wait()
    side_copies[4].wait_recv()
    iota16 = lax.broadcasted_iota(jnp.int32, (16, LANES), 0)

    def onehot(z, carry):
        for h in range(2):
            low_part = lax.rem(BAND[z, h], 16)
            for i in range(8):
                at = (8 * h + i) * LANES
                OHB[z, :, at : at + LANES] = jnp.where(
                    jnp.broadcast_to(low_part[i : i + 1], (16, LANES)) == iota16, 1.0, 0.0
                ).astype(jnp.bfloat16)
        return carry

    lax.fori_loop(0, NZL, onehot, 0)

    arrive(MR, m_recv)

    def upstream(k, F):
        lf, lg, rf, rg = (MR[k, i] for i in range(4))
        b = lg / (1.0 - lf * F)
        g = b * F
        CB[k] = b
        CG[k] = g
        return rg + g * rf

    def downstream(i, H):
        k = CHIPS - 1 - i
        lf, lg, rf, rg = (MR[k, i] for i in range(4))
        b = rf / (1.0 - rg * H)
        g = b * H
        CB[k] = b
        CG[k] = g
        return lf + g * lg

    none = jnp.zeros((NZL, LANES), F32)
    F = lax.fori_loop(0, chip, upstream, none)
    H = lax.fori_loop(0, CHIPS - 1 - chip, downstream, none)
    lf, lg, rf, rg = (MS[i] for i in range(4))
    from_left = 1.0 - lf * F
    from_right = 1.0 - rg * H
    inv = 1.0 / (from_left * from_right - (F * rf) * (H * lg))
    for i, value in enumerate(
        (
            F,
            H,
            from_right * inv,
            F * rf * inv,
            H * lg * inv,
            from_left * inv,
            lg / from_left * F,
            rf / from_right * H,
        )
    ):
        OWN[i] = value

    def close(incoming):
        for c in range(NC):
            first_p = level(p2, 0, c)
            last_p = level(p2, NXC - 1, c)
            x = OWN[0] * first_p + incoming[0][c]
            y = OWN[1] * last_p + incoming[1][c]
            AL[c] = OWN[2] * x + OWN[3] * y
            AR[c] = OWN[4] * x + OWN[5] * y

    def solved(c, z, h):
        return (
            PP[c, z, h]
            + LL[z, h] * jnp.broadcast_to(AL[c, pl.ds(z, 1), :], (8, LANES))
            + RC[z, h] * jnp.broadcast_to(AR[c, pl.ds(z, 1), :], (8, LANES))
        )

    arrive(R1, p_recv.at[0])
    trio = (none,) * NC

    def up_first(k, O):
        return tuple(R1[k, 1, c] + CG[k] * R1[k, 0, c] + CB[k] * O[c] for c in range(NC))

    def down_first(i, Q):
        k = CHIPS - 1 - i
        return tuple(R1[k, 0, c] + CG[k] * R1[k, 1, c] + CB[k] * Q[c] for c in range(NC))

    close(
        (
            lax.fori_loop(0, chip, up_first, trio),
            lax.fori_loop(0, CHIPS - 1 - chip, down_first, trio),
        )
    )

    def line_first(z, packs):
        for c in range(NC):
            pair = tuple(solved(c, z, h) for h in range(2))
            for h in range(2):
                A2[c, z + 1, h] = pair[h]
            packs = pack_edges(c * NZL + z, pair, packs)
        return packs

    halo2 = send_halo(1, A2, lax.fori_loop(0, NZL, line_first, no_packs))

    eliminate(1, A2, halo2)
    for c in range(NC):
        first_p = level(p2, 0, c)
        last_p = level(p2, NXC - 1, c)
        S2[0, c] = last_p + OWN[6] * first_p
        S2[1, c] = first_p + OWN[7] * last_p
    to_chips(
        lambda target: S2.at[jnp.where(target > chip, 0, 1)], R2, p_send.at[1], p_recv.at[1]
    )
    arrive(R2, p_recv.at[1])

    def up_second(k, O):
        return tuple(R2[k, c] + CB[k] * O[c] for c in range(NC))

    def down_second(i, Q):
        k = CHIPS - 1 - i
        return tuple(R2[k, c] + CB[k] * Q[c] for c in range(NC))

    close(
        (
            lax.fori_loop(0, chip, up_second, trio),
            lax.fori_loop(0, CHIPS - 1 - chip, down_second, trio),
        )
    )

    def line_last(z, carry):
        for h in range(2):
            total = None
            for c in range(NC):
                a = solved(c, z, h)
                A3[c, z, h] = a
                term = VEL[c, z, h] * a
                total = term if total is None else total + term
            total = total * PEN[z, h]
            coarse = total.astype(jnp.bfloat16).astype(F32)
            SH[z, h] = coarse
            SL[z, h] = total - coarse
        return carry

    lax.fori_loop(0, NZL, line_last, 0)
    out_own = pltpu.make_async_copy(A3.at[:, :, q], out_h.at[:, :, :, lanes_of(q)], out_sem.at[0])
    out_side = pltpu.make_async_remote_copy(
        src_ref=A3.at[:, :, 1 - q],
        dst_ref=out_h.at[:, :, :, lanes_of(q)],
        send_sem=out_sem.at[1],
        recv_sem=out_sem.at[2],
        device_id=(partner, mv, mp),
        device_id_type=MESH,
    )
    out_own.start()
    out_side.start()

    def band_rows(z, acc):
        parts = []
        for h in range(2):
            high_part = BAND[z, h] // 16
            coarse = SH[z, h]
            fine = SL[z, h]
            for i in range(8):
                hit = jnp.broadcast_to(high_part[i : i + 1], (16, LANES)) == iota16
                parts.append(
                    jnp.concatenate(
                        [
                            jnp.where(hit, jnp.broadcast_to(v[i : i + 1], (16, LANES)), 0.0)
                            for v in (coarse, fine)
                        ],
                        axis=0,
                    ).astype(jnp.bfloat16)
                )
        weights = jnp.concatenate(parts, axis=1)
        return acc + lax.dot_general(
            weights, OHB[z], (((1,), (1,)), ((), ())), preferred_element_type=F32
        )

    acc = lax.fori_loop(0, NZL, band_rows, jnp.zeros((32, 16), F32))
    sums = acc[0:16] + acc[16:32]
    wide = jnp.concatenate([sums] * 8, axis=1)
    keep = lane // 16 == row
    for h in range(2):
        B1S[h : h + 1, :] = jnp.sum(
            jnp.where(keep, wide[8 * h : 8 * h + 8], 0.0), axis=0, keepdims=True
        )

    def band_round(r, own, slots, device_of):
        def send(j, carry):
            pltpu.make_async_remote_copy(
                src_ref=own,
                dst_ref=slots.at[j],
                send_sem=b_send.at[r],
                recv_sem=b_recv.at[r],
                device_id=device_of(j),
                device_id_type=MESH,
            ).start()
            return carry

        lax.fori_loop(1, STREAM, send, 0)
        got = slots.at[pl.ds(1, STREAM - 1)]
        pltpu.make_async_copy(got, got, b_recv.at[r]).wait()
        total = own[...]
        for j in range(1, STREAM):
            total = total + slots[j]
        return total

    B2S[...] = band_round(0, B1S, B1R, lambda j: (lax.rem(me + j, STREAM), mv, mp))
    bands = band_round(
        1,
        B2S,
        B2R,
        lambda j: (me, lax.rem(mv + j // SPAN, VERT), lax.rem(mp + j % SPAN, SPAN)),
    )
    cells = STREAM * VERT * SPAN * NXL * NZL * NYL
    bands = bands * ((NBANDS / cells) ** 0.5)
    tb_copy.wait()
    tw_copy.wait()
    tb = TB[...].reshape(1, LANES)
    spot = jnp.broadcast_to(lax.rem(tb, LANES), (8, LANES))
    low_half = jnp.take_along_axis(jnp.broadcast_to(bands[0:1], (8, LANES)), spot, axis=1)
    high_half = jnp.take_along_axis(jnp.broadcast_to(bands[1:2], (8, LANES)), spot, axis=1)
    picked = jnp.where(tb < LANES, low_half[0:1], high_half[0:1])
    TRI[...] = (TW[...].reshape(1, LANES) * picked).reshape(LANES)
    tri_copy = pltpu.make_async_copy(TRI, tri_h, tri_sem.at[2])
    tri_copy.start()

    def drain(count, ref, sem):
        def one(j, carry):
            pltpu.make_async_copy(ref, ref, sem).wait()
            return carry

        lax.fori_loop(0, count, one, 0)

    for copy in side_copies:
        copy.wait_send()
    each(halo1, 1, lambda c: c.wait_send())
    each(halo2, 1, lambda c: c.wait_send())
    drain(CHIPS - 1, MS, m_send)
    drain(CHIPS - 1, S1, p_send.at[0])
    drain(CHIPS - 1, S2.at[0], p_send.at[1])
    for r, own in enumerate((B1S, B2S)):
        drain(STREAM - 1, own, b_send.at[r])
    out_own.wait()
    out_side.wait()
    tri_copy.wait()


def shards(adjoint_source, velocity, penalty, adjoint_start, cell_band, tri_band, tri_weight):
    anywhere = pl.BlockSpec(memory_space=pl.ANY)

    def field():
        return pltpu.VMEM((NZL, 2, 8, LANES), F32)

    scratch = [
        pltpu.VMEM((NC, NZL, 2, 8, LANES), F32),
        pltpu.VMEM((NC, NZL, 2, 8, LANES), F32),
        field(),
        pltpu.VMEM((NZL, 2, 8, LANES), jnp.int32),
        pltpu.VMEM((NC, NZL + 2, 2, 8, LANES), F32),
        pltpu.VMEM((NC, NZL + 2, 2, 8, LANES), F32),
        pltpu.VMEM((NC, NZL, 2, 8, LANES), F32),
        pltpu.VMEM((NC, NZL, 2, 8, LANES), F32),
        field(),
        field(),
        field(),
        field(),
        pltpu.VMEM((NZL, 8, LANES), F32),
        field(),
        field(),
        field(),
        pltpu.VMEM((NZL, 8, LANES), F32),
        field(),
        field(),
        pltpu.VMEM((SWEEPS, 2, 2, 8, LANES), F32),
        pltpu.VMEM((SWEEPS, 2, 2, 8, LANES), F32),
        pltpu.VMEM((4, NZL, LANES), F32),
        pltpu.VMEM((CHIPS, 4, NZL, LANES), F32),
        pltpu.VMEM((CHIPS, NZL, LANES), F32),
        pltpu.VMEM((CHIPS, NZL, LANES), F32),
        pltpu.VMEM((8, NZL, LANES), F32),
        pltpu.VMEM((2, NC, NZL, LANES), F32),
        pltpu.VMEM((CHIPS, 2, NC, NZL, LANES), F32),
        pltpu.VMEM((2, NC, NZL, LANES), F32),
        pltpu.VMEM((CHIPS, NC, NZL, LANES), F32),
        pltpu.VMEM((NC, NZL, LANES), F32),
        pltpu.VMEM((NC, NZL, LANES), F32),
        field(),
        field(),
        pltpu.VMEM((NZL, 16, NXC * LANES), jnp.bfloat16),
        pltpu.VMEM((2, LANES), F32),
        pltpu.VMEM((STREAM, 2, LANES), F32),
        pltpu.VMEM((2, LANES), F32),
        pltpu.VMEM((STREAM, 2, LANES), F32),
        pltpu.VMEM((LANES,), jnp.int32),
        pltpu.VMEM((LANES,), F32),
        pltpu.VMEM((LANES,), F32),
        pltpu.SemaphoreType.DMA((5,)),
        pltpu.SemaphoreType.DMA((5,)),
        pltpu.SemaphoreType.DMA((5,)),
        pltpu.SemaphoreType.DMA((3,)),
        pltpu.SemaphoreType.DMA((3,)),
        pltpu.SemaphoreType.DMA((SWEEPS, 4)),
        pltpu.SemaphoreType.DMA((SWEEPS, 4)),
        pltpu.SemaphoreType.DMA,
        pltpu.SemaphoreType.DMA,
        pltpu.SemaphoreType.DMA((SWEEPS,)),
        pltpu.SemaphoreType.DMA((SWEEPS,)),
        pltpu.SemaphoreType.DMA((2,)),
        pltpu.SemaphoreType.DMA((2,)),
    ]

    def planes(x):
        return jnp.swapaxes(x, -3, -2)

    adjoint, tri_grad = pl.pallas_call(
        kernel,
        out_shape=(
            jax.ShapeDtypeStruct((NC, NZL, NXL, NYL), F32),
            jax.ShapeDtypeStruct((LANES,), F32),
        ),
        in_specs=[anywhere] * 7,
        out_specs=(anywhere, anywhere),
        scratch_shapes=scratch,
        compiler_params=pltpu.CompilerParams(
            collective_id=0, has_side_effects=True, vmem_limit_bytes=56 * 1024 * 1024
        ),
    )(
        planes(adjoint_source),
        planes(velocity),
        planes(penalty),
        planes(adjoint_start),
        planes(cell_band),
        tri_band,
        tri_weight,
    )
    return planes(adjoint), tri_grad


def solution(mesh):
    return jax.shard_map(
        shards,
        mesh=mesh,
        in_specs=(
            P(None, "stream", "span", "vert"),
            P(None, "stream", "span", "vert"),
            P("stream", "span", "vert"),
            P(None, "stream", "span", "vert"),
            P("stream", "span", "vert"),
            P(("stream", "vert", "span")),
            P(("stream", "vert", "span")),
        ),
        out_specs=(P(None, "stream", "span", "vert"), P(("stream", "vert", "span"))),
        check_vma=False,
    )
```

```python
import functools

import jax
import jax.numpy as jnp
from jax import lax
from jax.experimental import pallas as pl
from jax.experimental.pallas import tpu as pltpu
from jax.sharding import PartitionSpec as P

SWEEPS = 2
NBANDS = 256

STREAM = 16
CHIPS = 8
VERT = 4
SPAN = 4
NC = 3
NXL = 8
NXC = 16
NZL = 12
NYL = 256
LANES = 128
OWNERS = 6

stream_coef = 1000.0
stream_conv = 200.0
cross_coef = 0.25
cross_conv = 0.25
shift_coef = 0.5

MESH = pl.DeviceIdType.MESH
F32 = jnp.float32


def kernel(
    src_h,
    vel_h,
    pen_h,
    start_h,
    band_h,
    tb_h,
    tw_h,
    out_h,
    tri_h,
    SRC,
    VEL,
    PEN,
    BAND,
    A1,
    A2,
    A3,
    PP,
    IP,
    M1,
    M2,
    M4,
    MT,
    F1,
    F2,
    F4,
    FT,
    LL,
    RC,
    STG,
    YF,
    YS,
    YR,
    MS,
    MR,
    CB,
    CG,
    OWN,
    QS,
    QR,
    CO,
    OC,
    S1,
    G1,
    D1,
    R1,
    S2,
    R2,
    AL,
    AR,
    SH,
    SL,
    OHB,
    B1S,
    B1R,
    B2S,
    B2R,
    TB,
    TW,
    TRI,
    in_sem,
    side_send,
    side_recv,
    out_sem,
    tri_sem,
    LT,
    LP,
    fz_send,
    fz_recv,
    fv_send,
    fv_recv,
    halo_send,
    halo_recv,
    m_send,
    m_recv,
    q_send,
    q_recv,
    d_send,
    d_recv,
    p_send,
    p_recv,
    b_send,
    b_recv,
):
    me = lax.axis_index("stream")
    mv = lax.axis_index("vert")
    mp = lax.axis_index("span")
    chip = me // 2
    q = lax.rem(me, 2)
    partner = 2 * chip + (1 - q)

    def lanes_of(half):
        return pl.ds(pl.multiple_of(half * LANES, LANES), LANES)

    def pieces(ref, dst):
        rank = len(ref.shape)
        lead = (slice(None),) * (rank - 1)
        return lambda half: ref.at[lead + (lanes_of(half),)], dst

    inner = A1.at[:, pl.ds(1, NZL)]
    inputs = (
        (start_h, inner),
        (vel_h, VEL),
        (pen_h, PEN),
        (src_h, SRC),
        (band_h, BAND),
    )

    def slot(dst, half):
        if len(dst.shape) == 5:
            return dst.at[:, :, half]
        return dst.at[:, half]

    def part(src, half):
        if len(src.shape) == 4:
            return src.at[:, :, :, lanes_of(half)]
        return src.at[:, :, lanes_of(half)]

    own_copies = []
    side_copies = []
    for i, (src, dst) in enumerate(inputs):
        own_copies.append(pltpu.make_async_copy(part(src, q), slot(dst, q), in_sem.at[i]))
        side_copies.append(
            pltpu.make_async_remote_copy(
                src_ref=part(src, 1 - q),
                dst_ref=slot(dst, q),
                send_sem=side_send.at[i],
                recv_sem=side_recv.at[i],
                device_id=(partner, mv, mp),
                device_id_type=MESH,
            )
        )
    tb_copy = pltpu.make_async_copy(tb_h, TB, tri_sem.at[0])
    tw_copy = pltpu.make_async_copy(tw_h, TW, tri_sem.at[1])

    barrier = pltpu.get_barrier_semaphore()

    def either(condition):
        return jnp.where(condition, 1, 0)

    has_v = (mv > 0, mv < VERT - 1)
    has_p = (mp > 0, mp < SPAN - 1)
    v_near = either(has_v[0]) + either(has_v[1])
    p_near = either(has_p[0]) + either(has_p[1])

    def call(sem, device):
        pl.semaphore_signal(sem, inc=1, device_id=device, device_id_type=MESH)

    def stream_at(step):
        return (lax.rem(me + 2 * step + STREAM, STREAM), mv, mp)

    def call_line(sem, along_v):
        for i, step in enumerate((-1, 1)):
            if along_v:
                pl.when(has_v[i])(lambda: call(sem, (me, mv + step, mp)))
            else:
                pl.when(has_p[i])(lambda: call(sem, (me, mv, mp + step)))

    outer_v = mv - 1 + 2 * q
    has_outer = jnp.logical_and(outer_v >= 0, outer_v < VERT)
    outer_id = (partner, lax.rem(outer_v + VERT, VERT), mp)

    nothing = jnp.zeros((2, 8, LANES), F32)
    for A in (A1, A2):
        for c in range(NC):
            A[c, 0] = nothing
            A[c, NZL + 1] = nothing
    YR[...] = jnp.zeros(YR.shape, F32)

    call(barrier, (partner, mv, mp))
    call(barrier, stream_at(-1))
    call(barrier, stream_at(1))
    for i, step in enumerate((-1, 1)):
        for core in range(2):
            other = 2 * chip + core
            pl.when(has_v[i])(lambda: call(barrier, (other, mv + step, mp)))
            pl.when(has_p[i])(lambda: call(barrier, (other, mv, mp + step)))

    stage = pltpu.make_async_copy(start_h, STG, in_sem.at[5])
    stage.start()
    for i in (1, 2, 0, 3, 4):
        own_copies[i].start()
    tb_copy.start()
    tw_copy.start()
    pl.semaphore_wait(barrier, 3 + 2 * v_near + 2 * p_near)
    for i in range(3):
        side_copies[i].start()
    call(LT.at[0], stream_at(-1))
    call(LT.at[0], stream_at(1))
    call_line(LP.at[0], True)

    row = lax.broadcasted_iota(jnp.int32, (8, LANES), 0)
    lane = lax.broadcasted_iota(jnp.int32, (8, LANES), 1)

    def pack_edges(k, pair, packs):
        low, high = packs
        hit = lane == k
        low = tuple(jnp.where(hit, pltpu.roll(pair[h], k, 1), low[h]) for h in range(2))
        high = tuple(jnp.where(hit, pltpu.roll(pair[h], k + 1, 1), high[h]) for h in range(2))
        return low, high

    blank = jnp.zeros((8, LANES), F32)
    no_packs = ((blank, blank), (blank, blank))

    def send_halo(s, A, packs):
        for side in range(2):
            for h in range(2):
                YS[s, side, h] = packs[side][h]

        def remote(i, src, dst, device):
            return pltpu.make_async_remote_copy(
                src_ref=src,
                dst_ref=dst,
                send_sem=halo_send.at[s, i],
                recv_sem=halo_recv.at[s, i],
                device_id=device,
                device_id_type=MESH,
            )

        copies = (
            (
                remote(0, A.at[:, NZL], A.at[:, 0], (me, mv, lax.rem(mp + 1, SPAN))),
                mp < SPAN - 1,
                mp > 0,
            ),
            (
                remote(1, A.at[:, 1], A.at[:, NZL + 1], (me, mv, lax.rem(mp + SPAN - 1, SPAN))),
                mp > 0,
                mp < SPAN - 1,
            ),
            (remote(2, YS.at[s, q], YR.at[s, 1 - q], outer_id), has_outer, has_outer),
            (remote(3, YS.at[s, 1 - q], YR.at[s, q], (partner, mv, mp)), None, None),
        )
        each(copies, 1, lambda c: c.start())
        return copies

    def each(copies, which, act):
        for item in copies:
            if item[which] is None:
                act(item[0])
            else:
                pl.when(item[which])(functools.partial(act, item[0]))

    first_halo = []
    for i, step in enumerate((-1, 1)):
        for core in range(2):
            first_halo.append(
                (
                    pltpu.make_async_remote_copy(
                        src_ref=start_h.at[:, (0, NZL - 1)[i], :, pl.ds(core * LANES, LANES)],
                        dst_ref=A1.at[:, (NZL + 1, 0)[i], q],
                        send_sem=fz_send.at[i, core],
                        recv_sem=fz_recv.at[i, q],
                        device_id=(2 * chip + core, mv, mp + step),
                        device_id_type=MESH,
                    ),
                    has_p[i],
                )
            )
    for copy, there in first_halo:
        pl.when(there)(copy.start)

    stage.wait()

    def pack_start(z, packs):
        low, high = packs
        for c in range(NC):
            pair = (STG[c, z, :, 0:LANES], STG[c, z, :, LANES:NYL])
            low, high = pack_edges(c * NZL + z, pair, (low, high))
        return low, high

    low, high = lax.fori_loop(0, NZL, pack_start, no_packs)
    for i, value in enumerate((low[0], high[1], high[0], low[1])):
        YF[i] = value
    for i, step in enumerate((-1, 1)):
        copy = pltpu.make_async_remote_copy(
            src_ref=YF.at[i],
            dst_ref=YR.at[0, 1 - i, q],
            send_sem=fv_send.at[i],
            recv_sem=fv_recv.at[q],
            device_id=(2 * chip + 1 - i, mv + step, mp),
            device_id_type=MESH,
        )
        first_halo.append((copy, has_v[i]))
        pl.when(has_v[i])(copy.start)
    middle = pltpu.make_async_remote_copy(
        src_ref=YF.at[2 + q],
        dst_ref=YR.at[0, q, q],
        send_sem=fv_send.at[2],
        recv_sem=fv_recv.at[2],
        device_id=(partner, mv, mp),
        device_id_type=MESH,
    )
    middle.start()
    YR[0, 1 - q, q] = YF[3 - q]

    def first_arrivals():
        for i in range(2):
            for sender in range(2):
                slab = A1.at[:, (0, NZL + 1)[i], sender]
                pl.when(has_p[i])(
                    lambda: pltpu.make_async_copy(slab, slab, fz_recv.at[1 - i, sender]).wait()
                )
        for sender in range(2):
            pl.when(has_outer)(
                lambda: pltpu.make_async_copy(YF.at[0], YF.at[0], fv_recv.at[sender]).wait()
            )
        middle.wait_recv()

    for i in range(3, 5):
        side_copies[i].start()

    for i in (1, 2):
        own_copies[i].wait()
        side_copies[i].wait_recv()

    def flat(ref):
        count = 1
        for size in ref.shape[:-1]:
            count *= size
        return ref.reshape(count, LANES)

    velocity2, penalty2 = flat(VEL), flat(PEN)
    ip2, m2, f2 = flat(IP), flat(M1), flat(F1)
    l2, r2, p2 = flat(LL), flat(RC), flat(PP)

    def level(ref2, x, c=0):
        return ref2[pl.ds(c * NZL * NXC + x, NZL, stride=NXC), :]

    delta = jnp.ones((NZL, LANES), F32)
    for x in range(NXC):
        u = level(velocity2, x, 0)
        west = stream_coef + stream_conv * jnp.maximum(-u, 0.0)
        east = stream_coef + stream_conv * jnp.maximum(u, 0.0)
        excess = (
            (4.0 * cross_coef + shift_coef)
            + cross_conv * (jnp.abs(level(velocity2, x, 1)) + jnp.abs(level(velocity2, x, 2)))
            + level(penalty2, x)
        )
        sink = excess + west * delta
        ip = 1.0 / (east + sink)
        delta = sink * ip
        place = pl.ds(x, NZL, stride=NXC)
        ip2[place, :] = ip
        m2[place, :] = west * ip
        f2[place, :] = east * ip

    def ahead(v, n, fill):
        return jnp.where(row >= n, pltpu.roll(v, n, 0), fill)

    def behind(v, n, fill):
        return jnp.where(row < 8 - n, pltpu.roll(v, 8 - n, 0), fill)

    def fold_up(values, f1, f2, f4, ft):
        new = []
        for h in range(2):
            v = values[h]
            v = v + f1[h] * pltpu.roll(v, 7, 0)
            v = v + f2[h] * pltpu.roll(v, 6, 0)
            v = v + f4[h] * pltpu.roll(v, 4, 0)
            new.append(v)
        new[0] = new[0] + ft * jnp.broadcast_to(new[1][0:1], (8, LANES))
        return new

    def factor(z, carry):
        chains = []
        tails = []
        f1s, f2s, f4s, fts = [], [], [], []
        for h in range(2):
            m = M1[z, h]
            f = F1[z, h]
            m1 = jnp.where(row >= 1, m, 0.0)
            mm = m1 * ahead(m, 1, 0.0)
            m4 = jnp.where(row >= 4, jnp.where(row >= 2, mm, 0.0) * pltpu.roll(mm, 2, 0), 0.0)
            mm = jnp.where(row >= 2, mm, 0.0)
            M1[z, h] = m1
            M2[z, h] = mm
            M4[z, h] = m4
            t = m * ahead(m, 1, 1.0)
            t = t * ahead(t, 2, 1.0)
            chains.append(t * ahead(t, 4, 1.0))
            f1 = jnp.where(row < 7, f, 0.0)
            ff = jnp.where(row < 6, f1 * behind(f, 1, 0.0), 0.0)
            f4 = jnp.where(row < 4, ff * pltpu.roll(ff, 6, 0), 0.0)
            F1[z, h] = f1
            F2[z, h] = ff
            F4[z, h] = f4
            f1s.append(f1)
            f2s.append(ff)
            f4s.append(f4)
            t = f * behind(f, 1, 1.0)
            t = t * behind(t, 2, 1.0)
            tails.append(t * behind(t, 4, 1.0))
        MT[z] = chains[1]
        FT[z] = tails[0]
        left = [chains[0], chains[1] * jnp.broadcast_to(chains[0][7:8], (8, LANES))]
        left = fold_up(left, f1s, f2s, f4s, tails[0])
        right = [tails[0] * jnp.broadcast_to(tails[1][0:1], (8, LANES)), tails[1]]
        for h in range(2):
            LL[z, h] = left[h]
            RC[z, h] = right[h]
        return carry

    lax.fori_loop(0, NZL, factor, 0)
    for k, ref2 in enumerate((l2, r2)):
        MS[2 * k] = level(ref2, 0)
        MS[2 * k + 1] = level(ref2, NXC - 1)

    def to_chips(src_of, dst, send_sem, recv_sem):
        def send(j, carry):
            target = lax.rem(chip + j, CHIPS)
            pltpu.make_async_remote_copy(
                src_ref=src_of(target),
                dst_ref=dst.at[chip],
                send_sem=send_sem,
                recv_sem=recv_sem,
                device_id=(2 * target + q, mv, mp),
                device_id_type=MESH,
            ).start()
            return carry

        lax.fori_loop(1, CHIPS, send, 0)

    def arrive(slots, sem):
        got = slots.at[pl.ds(1, CHIPS - 1)]
        pltpu.make_async_copy(got, got, sem).wait()

    pl.semaphore_wait(LT.at[0], 2)
    call(LT.at[1], stream_at(-2))
    call(LT.at[1], stream_at(2))
    pl.semaphore_wait(LT.at[1], 2)
    call(LT.at[2], (partner, mv, mp))

    is_owner = lax.rem(chip, 4) < 3
    my_o = (chip // 4) * 3 + lax.rem(chip, 4)
    owner_sends = jnp.where(is_owner, OWNERS - 1, OWNERS)

    def to_owners(src_of, dst, send_sem, recv_sem):
        def send(o, carry):
            target = o + o // 3

            @pl.when(target != chip)
            def _():
                pltpu.make_async_remote_copy(
                    src_ref=src_of(o),
                    dst_ref=dst,
                    send_sem=send_sem,
                    recv_sem=recv_sem,
                    device_id=(2 * target + q, mv, mp),
                    device_id_type=MESH,
                ).start()

            @pl.when(target == chip)
            def _():
                pltpu.make_async_copy(src_of(o), dst, recv_sem).start()

            return carry

        lax.fori_loop(0, OWNERS, send, 0)

    for k in range(4):
        value = MS[k]
        for o in range(OWNERS):
            QS[k, o] = value[2 * o : 2 * o + 2]
    to_owners(lambda o: QS.at[:, o], QR.at[chip], q_send, q_recv)

    for i in (3,):
        own_copies[i].wait()
        side_copies[i].wait_recv()

    first = lane == 0
    last = lane == LANES - 1

    def eliminate(s, A):
        edges = [[YR[s, side, h] for h in range(2)] for side in range(2)]

        def plane(z, carry):
            cross = []
            for h in range(2):
                v = VEL[1, z, h]
                w = VEL[2, z, h]
                cross.append(
                    (
                        cross_coef + cross_conv * jnp.maximum(-v, 0.0),
                        cross_coef + cross_conv * jnp.maximum(v, 0.0),
                        cross_coef + cross_conv * jnp.maximum(-w, 0.0),
                        cross_coef + cross_conv * jnp.maximum(w, 0.0),
                    )
                )
            ip = [IP[z, h] for h in range(2)]
            m1 = [M1[z, h] for h in range(2)]
            m2 = [M2[z, h] for h in range(2)]
            m4 = [M4[z, h] for h in range(2)]
            f1 = [F1[z, h] for h in range(2)]
            f2 = [F2[z, h] for h in range(2)]
            f4 = [F4[z, h] for h in range(2)]
            mt = MT[z]
            ft = FT[z]
            for c in range(NC):
                k = c * NZL + z
                o = []
                for h in range(2):
                    south, north, below, above = cross[h]
                    a = A[c, z + 1, h]
                    lo = pltpu.roll(edges[0][h], lax.rem(LANES - k, LANES), 1)
                    hi = pltpu.roll(edges[1][h], LANES - 1 - k, 1)
                    y_lo = jnp.where(first, lo, pltpu.roll(a, 1, 1))
                    y_hi = jnp.where(last, hi, pltpu.roll(a, LANES - 1, 1))
                    rhs = SRC[c, z, h] + shift_coef * a
                    rhs = rhs + south * y_lo + north * y_hi
                    rhs = rhs + below * A[c, z, h] + above * A[c, z + 2, h]
                    v = rhs * ip[h]
                    v = v + m1[h] * pltpu.roll(v, 1, 0)
                    v = v + m2[h] * pltpu.roll(v, 2, 0)
                    v = v + m4[h] * pltpu.roll(v, 4, 0)
                    o.append(v)
                o[1] = o[1] + mt * jnp.broadcast_to(o[0][7:8], (8, LANES))
                p = fold_up(o, f1, f2, f4, ft)
                for h in range(2):
                    PP[c, z, h] = p[h]
            return carry

        lax.fori_loop(0, NZL, plane, 0)

    own_copies[0].wait()
    side_copies[0].wait_recv()
    first_arrivals()
    pl.semaphore_wait(LP.at[0], v_near)
    call_line(LP.at[1], True)
    eliminate(0, A1)
    for c in range(NC):
        for i, x in enumerate((0, NXC - 1)):
            value = level(p2, x, c)
            for o in range(OWNERS):
                S1[i, c, o] = value[2 * o : 2 * o + 2]
    to_owners(lambda o: S1.at[:, :, o], G1.at[chip], p_send.at[0], p_recv.at[0])
    pl.semaphore_wait(LP.at[1], v_near)
    call_line(LP.at[2], False)
    to_chips(lambda target: MS, MR, m_send, m_recv)

    own_copies[4].wait()
    side_copies[4].wait_recv()
    iota16 = lax.broadcasted_iota(jnp.int32, (16, LANES), 0)

    def onehot(z, carry):
        for h in range(2):
            low_part = lax.rem(BAND[z, h], 16)
            for i in range(8):
                at = (8 * h + i) * LANES
                OHB[z, :, at : at + LANES] = jnp.where(
                    jnp.broadcast_to(low_part[i : i + 1], (16, LANES)) == iota16, 1.0, 0.0
                ).astype(jnp.bfloat16)
        return carry

    lax.fori_loop(0, NZL, onehot, 0)

    @pl.when(is_owner)
    def _():
        pltpu.make_async_copy(QR, QR, q_recv).wait()
        ahead_f = jnp.zeros((2, LANES), F32)
        for k in range(CHIPS):
            lf, lg, rf, rg = (QR[k, i] for i in range(4))
            inv = 1.0 / (1.0 - lf * ahead_f)
            b = lg * inv
            g = b * ahead_f
            for i, value in enumerate((g, b, inv, lf * inv, rf * inv, ahead_f)):
                CO[k, i] = value
            ahead_f = rg + g * rf

        pltpu.make_async_copy(G1, G1, p_recv.at[0]).wait()
        nil = jnp.zeros((2, LANES), F32)
        O = [nil] * NC
        for k in range(CHIPS):
            for c in range(NC):
                OC[k, c] = O[c]
                O[c] = G1[k, 1, c] + CO[k, 0] * G1[k, 0, c] + CO[k, 1] * O[c]
        after = [nil] * NC
        for k in reversed(range(CHIPS)):
            for c in range(NC):
                D1[k, 1, c] = after[c]
                before = OC[k, c]
                after[c] = CO[k, 2] * G1[k, 0, c] + CO[k, 3] * before + CO[k, 4] * after[c]
                D1[k, 0, c] = CO[k, 5] * after[c] + before

        def reply(j, carry):
            target = lax.rem(chip + j, CHIPS)
            pltpu.make_async_remote_copy(
                src_ref=D1.at[target],
                dst_ref=R1.at[:, :, my_o],
                send_sem=d_send,
                recv_sem=d_recv,
                device_id=(2 * target + q, mv, mp),
                device_id_type=MESH,
            ).start()
            return carry

        lax.fori_loop(1, CHIPS, reply, 0)
        pltpu.make_async_copy(D1.at[chip], R1.at[:, :, my_o], d_recv).start()

    arrive(MR, m_recv)

    def upstream(k, F):
        lf, lg, rf, rg = (MR[k, i] for i in range(4))
        b = lg / (1.0 - lf * F)
        g = b * F
        CB[k] = b
        CG[k] = g
        return rg + g * rf

    def downstream(i, H):
        k = CHIPS - 1 - i
        lf, lg, rf, rg = (MR[k, i] for i in range(4))
        b = rf / (1.0 - rg * H)
        g = b * H
        CB[k] = b
        CG[k] = g
        return lf + g * lg

    none = jnp.zeros((NZL, LANES), F32)
    F = lax.fori_loop(0, chip, upstream, none)
    H = lax.fori_loop(0, CHIPS - 1 - chip, downstream, none)
    lf, lg, rf, rg = (MS[i] for i in range(4))
    from_left = 1.0 - lf * F
    from_right = 1.0 - rg * H
    inv = 1.0 / (from_left * from_right - (F * rf) * (H * lg))
    for i, value in enumerate(
        (
            F,
            H,
            from_right * inv,
            F * rf * inv,
            H * lg * inv,
            from_left * inv,
            lg / from_left * F,
            rf / from_right * H,
        )
    ):
        OWN[i] = value

    def close(incoming):
        for c in range(NC):
            first_p = level(p2, 0, c)
            last_p = level(p2, NXC - 1, c)
            x = OWN[0] * first_p + incoming[0][c]
            y = OWN[1] * last_p + incoming[1][c]
            AL[c] = OWN[2] * x + OWN[3] * y
            AR[c] = OWN[4] * x + OWN[5] * y

    def solved(c, z, h):
        return (
            PP[c, z, h]
            + LL[z, h] * jnp.broadcast_to(AL[c, pl.ds(z, 1), :], (8, LANES))
            + RC[z, h] * jnp.broadcast_to(AR[c, pl.ds(z, 1), :], (8, LANES))
        )

    pltpu.make_async_copy(R1, R1, d_recv).wait()
    pl.semaphore_wait(LP.at[2], p_near)
    call_line(LP.at[3], False)
    trio = (none,) * NC
    for c in range(NC):
        for o in range(OWNERS):
            AL[c, 2 * o : 2 * o + 2, :] = R1[0, c, o]
            AR[c, 2 * o : 2 * o + 2, :] = R1[1, c, o]

    def line_first(z, packs):
        for c in range(NC):
            pair = tuple(solved(c, z, h) for h in range(2))
            for h in range(2):
                A2[c, z + 1, h] = pair[h]
            packs = pack_edges(c * NZL + z, pair, packs)
        return packs

    halo2 = send_halo(1, A2, lax.fori_loop(0, NZL, line_first, no_packs))

    each(halo2, 2, lambda c: c.wait_recv())
    pl.semaphore_wait(LP.at[3], p_near)
    call_line(LP.at[4], False)
    eliminate(1, A2)
    for c in range(NC):
        first_p = level(p2, 0, c)
        last_p = level(p2, NXC - 1, c)
        S2[0, c] = last_p + OWN[6] * first_p
        S2[1, c] = first_p + OWN[7] * last_p
    to_chips(
        lambda target: S2.at[jnp.where(target > chip, 0, 1)], R2, p_send.at[1], p_recv.at[1]
    )
    arrive(R2, p_recv.at[1])

    def up_second(k, O):
        return tuple(R2[k, c] + CB[k] * O[c] for c in range(NC))

    def down_second(i, Q):
        k = CHIPS - 1 - i
        return tuple(R2[k, c] + CB[k] * Q[c] for c in range(NC))

    close(
        (
            lax.fori_loop(0, chip, up_second, trio),
            lax.fori_loop(0, CHIPS - 1 - chip, down_second, trio),
        )
    )

    def line_last(z, carry):
        for h in range(2):
            total = None
            for c in range(NC):
                a = solved(c, z, h)
                A3[c, z, h] = a
                term = VEL[c, z, h] * a
                total = term if total is None else total + term
            total = total * PEN[z, h]
            coarse = total.astype(jnp.bfloat16).astype(F32)
            SH[z, h] = coarse
            SL[z, h] = total - coarse
        return carry

    lax.fori_loop(0, NZL, line_last, 0)
    def band_rows(z, acc):
        parts = []
        for h in range(2):
            high_part = BAND[z, h] // 16
            coarse = SH[z, h]
            fine = SL[z, h]
            for i in range(8):
                hit = jnp.broadcast_to(high_part[i : i + 1], (16, LANES)) == iota16
                parts.append(
                    jnp.concatenate(
                        [
                            jnp.where(hit, jnp.broadcast_to(v[i : i + 1], (16, LANES)), 0.0)
                            for v in (coarse, fine)
                        ],
                        axis=0,
                    ).astype(jnp.bfloat16)
                )
        weights = jnp.concatenate(parts, axis=1)
        return acc + lax.dot_general(
            weights, OHB[z], (((1,), (1,)), ((), ())), preferred_element_type=F32
        )

    pl.semaphore_wait(LT.at[2], 1)
    pl.semaphore_wait(LP.at[4], p_near)
    acc = lax.fori_loop(0, NZL, band_rows, jnp.zeros((32, 16), F32))
    sums = acc[0:16] + acc[16:32]
    wide = jnp.concatenate([sums] * 8, axis=1)
    keep = lane // 16 == row
    for h in range(2):
        B1S[h : h + 1, :] = jnp.sum(
            jnp.where(keep, wide[8 * h : 8 * h + 8], 0.0), axis=0, keepdims=True
        )

    def band_round(r, own, slots, device_of, beside):
        def send(j, carry):
            pltpu.make_async_remote_copy(
                src_ref=own,
                dst_ref=slots.at[j],
                send_sem=b_send.at[r],
                recv_sem=b_recv.at[r],
                device_id=device_of(j),
                device_id_type=MESH,
            ).start()
            return carry

        lax.fori_loop(1, STREAM, send, 0)
        beside()
        got = slots.at[pl.ds(1, STREAM - 1)]
        pltpu.make_async_copy(got, got, b_recv.at[r]).wait()
        total = own[...]
        for j in range(1, STREAM):
            total = total + slots[j]
        return total

    out_own = pltpu.make_async_copy(A3.at[:, :, q], out_h.at[:, :, :, lanes_of(q)], out_sem.at[0])
    out_side = pltpu.make_async_remote_copy(
        src_ref=A3.at[:, :, 1 - q],
        dst_ref=out_h.at[:, :, :, lanes_of(q)],
        send_sem=out_sem.at[1],
        recv_sem=out_sem.at[2],
        device_id=(partner, mv, mp),
        device_id_type=MESH,
    )

    def send_out():
        out_own.start()
        out_side.start()

    B2S[...] = band_round(0, B1S, B1R, lambda j: (lax.rem(me + j, STREAM), mv, mp), send_out)
    bands = band_round(
        1,
        B2S,
        B2R,
        lambda j: (me, lax.rem(mv + j // SPAN, VERT), lax.rem(mp + j % SPAN, SPAN)),
        lambda: None,
    )
    cells = STREAM * VERT * SPAN * NXL * NZL * NYL
    bands = bands * ((NBANDS / cells) ** 0.5)
    tb_copy.wait()
    tw_copy.wait()
    tb = TB[...].reshape(1, LANES)
    spot = jnp.broadcast_to(lax.rem(tb, LANES), (8, LANES))
    low_half = jnp.take_along_axis(jnp.broadcast_to(bands[0:1], (8, LANES)), spot, axis=1)
    high_half = jnp.take_along_axis(jnp.broadcast_to(bands[1:2], (8, LANES)), spot, axis=1)
    picked = jnp.where(tb < LANES, low_half[0:1], high_half[0:1])
    TRI[...] = (TW[...].reshape(1, LANES) * picked).reshape(LANES)
    tri_copy = pltpu.make_async_copy(TRI, tri_h, tri_sem.at[2])
    tri_copy.start()

    def drain(count, ref, sem):
        def one(j, carry):
            pltpu.make_async_copy(ref, ref, sem).wait()
            return carry

        lax.fori_loop(0, count, one, 0)

    for copy in side_copies:
        copy.wait_send()
    for copy, there in first_halo:
        pl.when(there)(copy.wait_send)
    middle.wait_send()
    each(halo2, 1, lambda c: c.wait_send())
    drain(CHIPS - 1, MS, m_send)
    drain(owner_sends, QS.at[:, 0], q_send)
    drain(owner_sends, S1.at[:, :, 0], p_send.at[0])

    @pl.when(is_owner)
    def _():
        drain(CHIPS - 1, D1.at[0], d_send)

    drain(CHIPS - 1, S2.at[0], p_send.at[1])
    for r, own in enumerate((B1S, B2S)):
        drain(STREAM - 1, own, b_send.at[r])
    out_own.wait()
    out_side.wait()
    tri_copy.wait()


def shards(adjoint_source, velocity, penalty, adjoint_start, cell_band, tri_band, tri_weight):
    anywhere = pl.BlockSpec(memory_space=pl.ANY)

    def field():
        return pltpu.VMEM((NZL, 2, 8, LANES), F32)

    scratch = [
        pltpu.VMEM((NC, NZL, 2, 8, LANES), F32),
        pltpu.VMEM((NC, NZL, 2, 8, LANES), F32),
        field(),
        pltpu.VMEM((NZL, 2, 8, LANES), jnp.int32),
        pltpu.VMEM((NC, NZL + 2, 2, 8, LANES), F32),
        pltpu.VMEM((NC, NZL + 2, 2, 8, LANES), F32),
        pltpu.VMEM((NC, NZL, 2, 8, LANES), F32),
        pltpu.VMEM((NC, NZL, 2, 8, LANES), F32),
        field(),
        field(),
        field(),
        field(),
        pltpu.VMEM((NZL, 8, LANES), F32),
        field(),
        field(),
        field(),
        pltpu.VMEM((NZL, 8, LANES), F32),
        field(),
        field(),
        pltpu.VMEM((NC, NZL, NXL, NYL), F32),
        pltpu.VMEM((4, 8, LANES), F32),
        pltpu.VMEM((SWEEPS, 2, 2, 8, LANES), F32),
        pltpu.VMEM((SWEEPS, 2, 2, 8, LANES), F32),
        pltpu.VMEM((4, NZL, LANES), F32),
        pltpu.VMEM((CHIPS, 4, NZL, LANES), F32),
        pltpu.VMEM((CHIPS, NZL, LANES), F32),
        pltpu.VMEM((CHIPS, NZL, LANES), F32),
        pltpu.VMEM((8, NZL, LANES), F32),
        pltpu.VMEM((4, OWNERS, 2, LANES), F32),
        pltpu.VMEM((CHIPS, 4, 2, LANES), F32),
        pltpu.VMEM((CHIPS, 6, 2, LANES), F32),
        pltpu.VMEM((CHIPS, NC, 2, LANES), F32),
        pltpu.VMEM((2, NC, OWNERS, 2, LANES), F32),
        pltpu.VMEM((CHIPS, 2, NC, 2, LANES), F32),
        pltpu.VMEM((CHIPS, 2, NC, 2, LANES), F32),
        pltpu.VMEM((2, NC, OWNERS, 2, LANES), F32),
        pltpu.VMEM((2, NC, NZL, LANES), F32),
        pltpu.VMEM((CHIPS, NC, NZL, LANES), F32),
        pltpu.VMEM((NC, NZL, LANES), F32),
        pltpu.VMEM((NC, NZL, LANES), F32),
        field(),
        field(),
        pltpu.VMEM((NZL, 16, NXC * LANES), jnp.bfloat16),
        pltpu.VMEM((2, LANES), F32),
        pltpu.VMEM((STREAM, 2, LANES), F32),
        pltpu.VMEM((2, LANES), F32),
        pltpu.VMEM((STREAM, 2, LANES), F32),
        pltpu.VMEM((LANES,), jnp.int32),
        pltpu.VMEM((LANES,), F32),
        pltpu.VMEM((LANES,), F32),
        pltpu.SemaphoreType.DMA((6,)),
        pltpu.SemaphoreType.DMA((5,)),
        pltpu.SemaphoreType.DMA((5,)),
        pltpu.SemaphoreType.DMA((3,)),
        pltpu.SemaphoreType.DMA((3,)),
        pltpu.SemaphoreType.REGULAR((3,)),
        pltpu.SemaphoreType.REGULAR((5,)),
        pltpu.SemaphoreType.DMA((2, 2)),
        pltpu.SemaphoreType.DMA((2, 2)),
        pltpu.SemaphoreType.DMA((3,)),
        pltpu.SemaphoreType.DMA((3,)),
        pltpu.SemaphoreType.DMA((SWEEPS, 4)),
        pltpu.SemaphoreType.DMA((SWEEPS, 4)),
        pltpu.SemaphoreType.DMA,
        pltpu.SemaphoreType.DMA,
        pltpu.SemaphoreType.DMA,
        pltpu.SemaphoreType.DMA,
        pltpu.SemaphoreType.DMA,
        pltpu.SemaphoreType.DMA,
        pltpu.SemaphoreType.DMA((SWEEPS,)),
        pltpu.SemaphoreType.DMA((SWEEPS,)),
        pltpu.SemaphoreType.DMA((2,)),
        pltpu.SemaphoreType.DMA((2,)),
    ]

    def planes(x):
        return jnp.swapaxes(x, -3, -2)

    adjoint, tri_grad = pl.pallas_call(
        kernel,
        out_shape=(
            jax.ShapeDtypeStruct((NC, NZL, NXL, NYL), F32),
            jax.ShapeDtypeStruct((LANES,), F32),
        ),
        in_specs=[pl.BlockSpec(memory_space=pltpu.HBM)] * 7,
        out_specs=(anywhere, anywhere),
        scratch_shapes=scratch,
        compiler_params=pltpu.CompilerParams(
            collective_id=0, has_side_effects=True, vmem_limit_bytes=56 * 1024 * 1024
        ),
    )(
        planes(adjoint_source),
        planes(velocity),
        planes(penalty),
        planes(adjoint_start),
        planes(cell_band),
        tri_band,
        tri_weight,
    )
    return planes(adjoint), tri_grad


def solution(mesh):
    return jax.shard_map(
        shards,
        mesh=mesh,
        in_specs=(
            P(None, "stream", "span", "vert"),
            P(None, "stream", "span", "vert"),
            P("stream", "span", "vert"),
            P(None, "stream", "span", "vert"),
            P("stream", "span", "vert"),
            P(("stream", "vert", "span")),
            P(("stream", "vert", "span")),
        ),
        out_specs=(P(None, "stream", "span", "vert"), P(("stream", "vert", "span"))),
        check_vma=False,
    )
```

```python
import functools

import jax
import jax.numpy as jnp
from jax import lax
from jax.experimental import pallas as pl
from jax.experimental.pallas import tpu as pltpu
from jax.sharding import PartitionSpec as P

SWEEPS = 2
NBANDS = 256

STREAM = 16
CHIPS = 8
VERT = 4
SPAN = 4
NC = 3
NXL = 8
NXC = 16
NZL = 12
NYL = 256
LANES = 128
OWNERS = 6

stream_coef = 1000.0
stream_conv = 200.0
cross_coef = 0.25
cross_conv = 0.25
shift_coef = 0.5

MESH = pl.DeviceIdType.MESH
F32 = jnp.float32


def kernel(
    src_h,
    vel_h,
    pen_h,
    start_h,
    band_h,
    tb_h,
    tw_h,
    out_h,
    tri_h,
    SRC,
    VEL,
    PEN,
    BAND,
    A1,
    A2,
    A3,
    PP,
    IP,
    M1,
    M2,
    M4,
    MT,
    F1,
    F2,
    F4,
    FT,
    LL,
    RC,
    STG,
    YF,
    YS,
    YR,
    MS,
    MR,
    CB,
    CE,
    OWN,
    QS,
    QR,
    CO,
    OC,
    S1,
    G1,
    D1,
    R1,
    S2,
    R2,
    E2,
    RE,
    AL,
    AR,
    OHH,
    OHL,
    B1S,
    B1R,
    B2S,
    B2R,
    TB,
    TW,
    TRI,
    in_sem,
    side_send,
    side_recv,
    out_sem,
    tri_sem,
    LT,
    LP,
    fz_send,
    fz_recv,
    fv_send,
    fv_recv,
    halo_send,
    halo_recv,
    m_send,
    m_recv,
    q_send,
    q_recv,
    d_send,
    d_recv,
    p_send,
    p_recv,
    e_send,
    e_recv,
    b_send,
    b_recv,
):
    me = lax.axis_index("stream")
    mv = lax.axis_index("vert")
    mp = lax.axis_index("span")
    chip = me // 2
    q = lax.rem(me, 2)
    partner = 2 * chip + (1 - q)

    def lanes_of(half):
        return pl.ds(pl.multiple_of(half * LANES, LANES), LANES)

    def pieces(ref, dst):
        rank = len(ref.shape)
        lead = (slice(None),) * (rank - 1)
        return lambda half: ref.at[lead + (lanes_of(half),)], dst

    inner = A1.at[:, pl.ds(1, NZL)]
    inputs = (
        (start_h, inner),
        (vel_h, VEL),
        (pen_h, PEN),
        (src_h, SRC),
        (band_h, BAND),
    )

    def slot(dst, half):
        if len(dst.shape) == 5:
            return dst.at[:, :, half]
        return dst.at[:, half]

    def part(src, half):
        if len(src.shape) == 4:
            return src.at[:, :, :, lanes_of(half)]
        return src.at[:, :, lanes_of(half)]

    own_copies = []
    side_copies = []
    for i, (src, dst) in enumerate(inputs):
        own_copies.append(pltpu.make_async_copy(part(src, q), slot(dst, q), in_sem.at[i]))
        side_copies.append(
            pltpu.make_async_remote_copy(
                src_ref=part(src, 1 - q),
                dst_ref=slot(dst, q),
                send_sem=side_send.at[i],
                recv_sem=side_recv.at[i],
                device_id=(partner, mv, mp),
                device_id_type=MESH,
            )
        )
    tb_copy = pltpu.make_async_copy(tb_h, TB, tri_sem.at[0])
    tw_copy = pltpu.make_async_copy(tw_h, TW, tri_sem.at[1])

    barrier = pltpu.get_barrier_semaphore()

    def either(condition):
        return jnp.where(condition, 1, 0)

    has_v = (mv > 0, mv < VERT - 1)
    has_p = (mp > 0, mp < SPAN - 1)
    v_near = either(has_v[0]) + either(has_v[1])
    p_near = either(has_p[0]) + either(has_p[1])

    def call(sem, device):
        pl.semaphore_signal(sem, inc=1, device_id=device, device_id_type=MESH)

    def stream_at(step):
        return (lax.rem(me + 2 * step + STREAM, STREAM), mv, mp)

    def call_line(sem, along_v):
        for i, step in enumerate((-1, 1)):
            if along_v:
                pl.when(has_v[i])(lambda: call(sem, (me, mv + step, mp)))
            else:
                pl.when(has_p[i])(lambda: call(sem, (me, mv, mp + step)))

    outer_v = mv - 1 + 2 * q
    has_outer = jnp.logical_and(outer_v >= 0, outer_v < VERT)
    outer_id = (partner, lax.rem(outer_v + VERT, VERT), mp)

    nothing = jnp.zeros((2, 8, LANES), F32)
    for A in (A1, A2):
        for c in range(NC):
            A[c, 0] = nothing
            A[c, NZL + 1] = nothing
    YR[...] = jnp.zeros(YR.shape, F32)

    call(barrier, (partner, mv, mp))
    call(barrier, stream_at(-1))
    call(barrier, stream_at(1))
    for i, step in enumerate((-1, 1)):
        for core in range(2):
            other = 2 * chip + core
            pl.when(has_v[i])(lambda: call(barrier, (other, mv + step, mp)))
            pl.when(has_p[i])(lambda: call(barrier, (other, mv, mp + step)))

    stage = pltpu.make_async_copy(start_h, STG, in_sem.at[5])
    stage.start()
    for i in (1, 2, 0, 3, 4):
        own_copies[i].start()
    tb_copy.start()
    tw_copy.start()
    pl.semaphore_wait(barrier, 3 + 2 * v_near + 2 * p_near)
    for i in range(3):
        side_copies[i].start()
    call(LT.at[0], stream_at(-1))
    call(LT.at[0], stream_at(1))
    call_line(LP.at[0], True)

    row = lax.broadcasted_iota(jnp.int32, (8, LANES), 0)
    lane = lax.broadcasted_iota(jnp.int32, (8, LANES), 1)

    def pack_edges(k, pair, packs):
        low, high = packs
        hit = lane == k
        low = tuple(jnp.where(hit, pltpu.roll(pair[h], k, 1), low[h]) for h in range(2))
        high = tuple(jnp.where(hit, pltpu.roll(pair[h], k + 1, 1), high[h]) for h in range(2))
        return low, high

    blank = jnp.zeros((8, LANES), F32)
    no_packs = ((blank, blank), (blank, blank))

    def send_halo(s, A, packs):
        for side in range(2):
            for h in range(2):
                YS[s, side, h] = packs[side][h]

        def remote(i, src, dst, device):
            return pltpu.make_async_remote_copy(
                src_ref=src,
                dst_ref=dst,
                send_sem=halo_send.at[s, i],
                recv_sem=halo_recv.at[s, i],
                device_id=device,
                device_id_type=MESH,
            )

        copies = (
            (
                remote(0, A.at[:, NZL], A.at[:, 0], (me, mv, lax.rem(mp + 1, SPAN))),
                mp < SPAN - 1,
                mp > 0,
            ),
            (
                remote(1, A.at[:, 1], A.at[:, NZL + 1], (me, mv, lax.rem(mp + SPAN - 1, SPAN))),
                mp > 0,
                mp < SPAN - 1,
            ),
            (remote(2, YS.at[s, q], YR.at[s, 1 - q], outer_id), has_outer, has_outer),
            (remote(3, YS.at[s, 1 - q], YR.at[s, q], (partner, mv, mp)), None, None),
        )
        each(copies, 1, lambda c: c.start())
        return copies

    def each(copies, which, act):
        for item in copies:
            if item[which] is None:
                act(item[0])
            else:
                pl.when(item[which])(functools.partial(act, item[0]))

    first_halo = []
    for i, step in enumerate((-1, 1)):
        for core in range(2):
            first_halo.append(
                (
                    pltpu.make_async_remote_copy(
                        src_ref=start_h.at[:, (0, NZL - 1)[i], :, pl.ds(core * LANES, LANES)],
                        dst_ref=A1.at[:, (NZL + 1, 0)[i], q],
                        send_sem=fz_send.at[i, core],
                        recv_sem=fz_recv.at[i, q],
                        device_id=(2 * chip + core, mv, mp + step),
                        device_id_type=MESH,
                    ),
                    has_p[i],
                )
            )
    for copy, there in first_halo:
        pl.when(there)(copy.start)

    stage.wait()

    def pack_start(z, packs):
        low, high = packs
        for c in range(NC):
            pair = (STG[c, z, :, 0:LANES], STG[c, z, :, LANES:NYL])
            low, high = pack_edges(c * NZL + z, pair, (low, high))
        return low, high

    low, high = lax.fori_loop(0, NZL, pack_start, no_packs)
    for i, value in enumerate((low[0], high[1], high[0], low[1])):
        YF[i] = value
    for i, step in enumerate((-1, 1)):
        copy = pltpu.make_async_remote_copy(
            src_ref=YF.at[i],
            dst_ref=YR.at[0, 1 - i, q],
            send_sem=fv_send.at[i],
            recv_sem=fv_recv.at[q],
            device_id=(2 * chip + 1 - i, mv + step, mp),
            device_id_type=MESH,
        )
        first_halo.append((copy, has_v[i]))
        pl.when(has_v[i])(copy.start)
    middle = pltpu.make_async_remote_copy(
        src_ref=YF.at[2 + q],
        dst_ref=YR.at[0, q, q],
        send_sem=fv_send.at[2],
        recv_sem=fv_recv.at[2],
        device_id=(partner, mv, mp),
        device_id_type=MESH,
    )
    middle.start()
    YR[0, 1 - q, q] = YF[3 - q]

    def first_arrivals():
        for i in range(2):
            for sender in range(2):
                slab = A1.at[:, (0, NZL + 1)[i], sender]
                pl.when(has_p[i])(
                    lambda: pltpu.make_async_copy(slab, slab, fz_recv.at[1 - i, sender]).wait()
                )
        for sender in range(2):
            pl.when(has_outer)(
                lambda: pltpu.make_async_copy(YF.at[0], YF.at[0], fv_recv.at[sender]).wait()
            )
        middle.wait_recv()

    for i in range(3, 5):
        side_copies[i].start()

    for i in (1, 2):
        own_copies[i].wait()
        side_copies[i].wait_recv()

    def flat(ref):
        count = 1
        for size in ref.shape[:-1]:
            count *= size
        return ref.reshape(count, LANES)

    velocity2, penalty2 = flat(VEL), flat(PEN)
    ip2, m2, f2 = flat(IP), flat(M1), flat(F1)
    l2, r2, p2 = flat(LL), flat(RC), flat(PP)

    def level(ref2, x, c=0):
        return ref2[pl.ds(c * NZL * NXC + x, NZL, stride=NXC), :]

    delta = jnp.ones((NZL, LANES), F32)
    for x in range(NXC):
        u = level(velocity2, x, 0)
        west = stream_coef + stream_conv * jnp.maximum(-u, 0.0)
        east = stream_coef + stream_conv * jnp.maximum(u, 0.0)
        excess = (
            (4.0 * cross_coef + shift_coef)
            + cross_conv * (jnp.abs(level(velocity2, x, 1)) + jnp.abs(level(velocity2, x, 2)))
            + level(penalty2, x)
        )
        sink = excess + west * delta
        ip = 1.0 / (east + sink)
        delta = sink * ip
        place = pl.ds(x, NZL, stride=NXC)
        ip2[place, :] = ip
        m2[place, :] = west * ip
        f2[place, :] = east * ip

    def ahead(v, n, fill):
        return jnp.where(row >= n, pltpu.roll(v, n, 0), fill)

    def behind(v, n, fill):
        return jnp.where(row < 8 - n, pltpu.roll(v, 8 - n, 0), fill)

    def fold_up(values, f1, f2, f4, ft):
        new = []
        for h in range(2):
            v = values[h]
            v = v + f1[h] * pltpu.roll(v, 7, 0)
            v = v + f2[h] * pltpu.roll(v, 6, 0)
            v = v + f4[h] * pltpu.roll(v, 4, 0)
            new.append(v)
        new[0] = new[0] + ft * jnp.broadcast_to(new[1][0:1], (8, LANES))
        return new

    def factor(z, carry):
        chains = []
        tails = []
        f1s, f2s, f4s, fts = [], [], [], []
        for h in range(2):
            m = M1[z, h]
            f = F1[z, h]
            m1 = jnp.where(row >= 1, m, 0.0)
            mm = m1 * ahead(m, 1, 0.0)
            m4 = jnp.where(row >= 4, jnp.where(row >= 2, mm, 0.0) * pltpu.roll(mm, 2, 0), 0.0)
            mm = jnp.where(row >= 2, mm, 0.0)
            M1[z, h] = m1
            M2[z, h] = mm
            M4[z, h] = m4
            t = m * ahead(m, 1, 1.0)
            t = t * ahead(t, 2, 1.0)
            chains.append(t * ahead(t, 4, 1.0))
            f1 = jnp.where(row < 7, f, 0.0)
            ff = jnp.where(row < 6, f1 * behind(f, 1, 0.0), 0.0)
            f4 = jnp.where(row < 4, ff * pltpu.roll(ff, 6, 0), 0.0)
            F1[z, h] = f1
            F2[z, h] = ff
            F4[z, h] = f4
            f1s.append(f1)
            f2s.append(ff)
            f4s.append(f4)
            t = f * behind(f, 1, 1.0)
            t = t * behind(t, 2, 1.0)
            tails.append(t * behind(t, 4, 1.0))
        MT[z] = chains[1]
        FT[z] = tails[0]
        left = [chains[0], chains[1] * jnp.broadcast_to(chains[0][7:8], (8, LANES))]
        left = fold_up(left, f1s, f2s, f4s, tails[0])
        right = [tails[0] * jnp.broadcast_to(tails[1][0:1], (8, LANES)), tails[1]]
        for h in range(2):
            LL[z, h] = left[h]
            RC[z, h] = right[h]
        return carry

    lax.fori_loop(0, NZL, factor, 0)
    for k, ref2 in enumerate((l2, r2)):
        MS[2 * k] = level(ref2, 0)
        MS[2 * k + 1] = level(ref2, NXC - 1)

    def to_chips(src_of, dst, send_sem, recv_sem):
        def send(j, carry):
            target = lax.rem(chip + j, CHIPS)
            pltpu.make_async_remote_copy(
                src_ref=src_of(target),
                dst_ref=dst.at[chip],
                send_sem=send_sem,
                recv_sem=recv_sem,
                device_id=(2 * target + q, mv, mp),
                device_id_type=MESH,
            ).start()
            return carry

        lax.fori_loop(1, CHIPS, send, 0)

    def arrive(slots, sem):
        got = slots.at[pl.ds(1, CHIPS - 1)]
        pltpu.make_async_copy(got, got, sem).wait()

    pl.semaphore_wait(LT.at[0], 2)
    call(LT.at[1], stream_at(-2))
    call(LT.at[1], stream_at(2))
    pl.semaphore_wait(LT.at[1], 2)
    call(LT.at[2], (partner, mv, mp))

    is_owner = lax.rem(chip, 4) < 3
    my_o = (chip // 4) * 3 + lax.rem(chip, 4)
    owner_sends = jnp.where(is_owner, OWNERS - 1, OWNERS)

    def to_owners(src_of, dst, send_sem, recv_sem):
        def send(o, carry):
            target = o + o // 3

            @pl.when(target != chip)
            def _():
                pltpu.make_async_remote_copy(
                    src_ref=src_of(o),
                    dst_ref=dst,
                    send_sem=send_sem,
                    recv_sem=recv_sem,
                    device_id=(2 * target + q, mv, mp),
                    device_id_type=MESH,
                ).start()

            @pl.when(target == chip)
            def _():
                pltpu.make_async_copy(src_of(o), dst, recv_sem).start()

            return carry

        lax.fori_loop(0, OWNERS, send, 0)

    for k in range(4):
        value = MS[k]
        for o in range(OWNERS):
            QS[k, o] = value[2 * o : 2 * o + 2]
    to_owners(lambda o: QS.at[:, o], QR.at[chip], q_send, q_recv)

    for i in (3,):
        own_copies[i].wait()
        side_copies[i].wait_recv()

    first = lane == 0
    last = lane == LANES - 1

    def eliminate(s, A, low, count, unroll):
        if s is not None:
            edges = [[YR[s, side, h] for h in range(2)] for side in range(2)]

        def plane(z, carry):
            cross = []
            for h in range(2):
                v = VEL[1, z, h]
                w = VEL[2, z, h]
                cross.append(
                    (
                        cross_coef + cross_conv * jnp.maximum(-v, 0.0),
                        cross_coef + cross_conv * jnp.maximum(v, 0.0),
                        cross_coef + cross_conv * jnp.maximum(-w, 0.0),
                        cross_coef + cross_conv * jnp.maximum(w, 0.0),
                    )
                )
            ip = [IP[z, h] for h in range(2)]
            m1 = [M1[z, h] for h in range(2)]
            m2 = [M2[z, h] for h in range(2)]
            m4 = [M4[z, h] for h in range(2)]
            f1 = [F1[z, h] for h in range(2)]
            f2 = [F2[z, h] for h in range(2)]
            f4 = [F4[z, h] for h in range(2)]
            mt = MT[z]
            ft = FT[z]
            for c in range(NC):
                k = c * NZL + z
                o = []
                for h in range(2):
                    south, north, below, above = cross[h]
                    a = A[c, z + 1, h]
                    lo = hi = blank
                    if s is not None:
                        lo = pltpu.roll(edges[0][h], lax.rem(LANES - k, LANES), 1)
                        hi = pltpu.roll(edges[1][h], LANES - 1 - k, 1)
                    y_lo = jnp.where(first, lo, pltpu.roll(a, 1, 1))
                    y_hi = jnp.where(last, hi, pltpu.roll(a, LANES - 1, 1))
                    rhs = SRC[c, z, h] + shift_coef * a
                    rhs = rhs + south * y_lo + north * y_hi
                    rhs = rhs + below * A[c, z, h] + above * A[c, z + 2, h]
                    v = rhs * ip[h]
                    v = v + m1[h] * pltpu.roll(v, 1, 0)
                    v = v + m2[h] * pltpu.roll(v, 2, 0)
                    v = v + m4[h] * pltpu.roll(v, 4, 0)
                    o.append(v)
                o[1] = o[1] + mt * jnp.broadcast_to(o[0][7:8], (8, LANES))
                p = fold_up(o, f1, f2, f4, ft)
                for h in range(2):
                    PP[c, z, h] = p[h]
            return carry

        lax.fori_loop(low, low + count, plane, 0, unroll=unroll)

    own_copies[0].wait()
    side_copies[0].wait_recv()
    first_arrivals()
    pl.semaphore_wait(LP.at[0], v_near)
    call_line(LP.at[1], True)
    eliminate(0, A1, 0, NZL, 12)
    for c in range(NC):
        for i, x in enumerate((0, NXC - 1)):
            value = level(p2, x, c)
            for o in range(OWNERS):
                S1[i, c, o] = value[2 * o : 2 * o + 2]
    to_owners(lambda o: S1.at[:, :, o], G1.at[chip], p_send.at[0], p_recv.at[0])
    pl.semaphore_wait(LP.at[1], v_near)
    call_line(LP.at[2], False)
    to_chips(lambda target: MS, MR, m_send, m_recv)

    own_copies[4].wait()
    side_copies[4].wait_recv()

    def indicator(digit):
        return jnp.concatenate(
            [jnp.where(digit == i, 1.0, 0.0) for i in range(16)], axis=0
        ).astype(jnp.bfloat16)

    def onehot(z, carry):
        for h in range(2):
            cut = slice(h * LANES, (h + 1) * LANES)
            OHL[z, :, cut] = indicator(lax.rem(BAND[z, h], 16))
            OHH[z, :, cut] = indicator(BAND[z, h] // 16)
        return carry

    lax.fori_loop(0, NZL, onehot, 0)

    @pl.when(is_owner)
    def _():
        pltpu.make_async_copy(QR, QR, q_recv).wait()
        ahead_f = jnp.zeros((2, LANES), F32)
        for k in range(CHIPS):
            lf, lg, rf, rg = (QR[k, i] for i in range(4))
            inv = 1.0 / (1.0 - lf * ahead_f)
            b = lg * inv
            g = b * ahead_f
            for i, value in enumerate((g, b, inv, lf * inv, rf * inv, ahead_f)):
                CO[k, i] = value
            ahead_f = rg + g * rf

        pltpu.make_async_copy(G1, G1, p_recv.at[0]).wait()
        nil = jnp.zeros((2, LANES), F32)
        O = [nil] * NC
        for k in range(CHIPS):
            for c in range(NC):
                OC[k, c] = O[c]
                O[c] = G1[k, 1, c] + CO[k, 0] * G1[k, 0, c] + CO[k, 1] * O[c]
        after = [nil] * NC
        for k in reversed(range(CHIPS)):
            for c in range(NC):
                D1[k, 1, c] = after[c]
                before = OC[k, c]
                after[c] = CO[k, 2] * G1[k, 0, c] + CO[k, 3] * before + CO[k, 4] * after[c]
                D1[k, 0, c] = CO[k, 5] * after[c] + before

        def reply(j, carry):
            target = lax.rem(chip + j, CHIPS)
            pltpu.make_async_remote_copy(
                src_ref=D1.at[target],
                dst_ref=R1.at[:, :, my_o],
                send_sem=d_send,
                recv_sem=d_recv,
                device_id=(2 * target + q, mv, mp),
                device_id_type=MESH,
            ).start()
            return carry

        lax.fori_loop(1, CHIPS, reply, 0)
        pltpu.make_async_copy(D1.at[chip], R1.at[:, :, my_o], d_recv).start()

    arrive(MR, m_recv)

    row_z = lax.broadcasted_iota(jnp.int32, (NZL, LANES), 0)
    lane_z = lax.broadcasted_iota(jnp.int32, (NZL, LANES), 1)

    def write_edges(ref, values):
        packed = jnp.zeros((NZL, LANES), F32)
        for c in range(NC):
            v = values[c]
            for side in range(2):
                ref[2 * c + side : 2 * c + side + 1, :] = v[
                    side * (NZL - 1) : side * (NZL - 1) + 1
                ]
                column = v[:, side * (LANES - 1) : side * (LANES - 1) + 1]
                packed = jnp.where(
                    lane_z == NZL * (2 * c + side) + row_z,
                    jnp.broadcast_to(column, (NZL, LANES)),
                    packed,
                )
        ref[6:7, :] = jnp.sum(packed, axis=0, keepdims=True)
        ref[7:8, :] = jnp.zeros((1, LANES), F32)

    def upstream(k, F):
        lf, lg, rf, rg = (MR[k, i] for i in range(4))
        b = lg / (1.0 - lf * F)
        g = b * F
        CB[k] = b
        write_edges(CE.at[k], (b, b, b))
        return rg + g * rf

    def downstream(i, H):
        k = CHIPS - 1 - i
        lf, lg, rf, rg = (MR[k, i] for i in range(4))
        b = rf / (1.0 - rg * H)
        g = b * H
        CB[k] = b
        write_edges(CE.at[k], (b, b, b))
        return lf + g * lg

    none = jnp.zeros((NZL, LANES), F32)
    F = lax.fori_loop(0, chip, upstream, none)
    H = lax.fori_loop(0, CHIPS - 1 - chip, downstream, none)
    lf, lg, rf, rg = (MS[i] for i in range(4))
    from_left = 1.0 - lf * F
    from_right = 1.0 - rg * H
    inv = 1.0 / (from_left * from_right - (F * rf) * (H * lg))
    for i, value in enumerate(
        (
            F,
            H,
            from_right * inv,
            F * rf * inv,
            H * lg * inv,
            from_left * inv,
            lg / from_left * F,
            rf / from_right * H,
        )
    ):
        OWN[i] = value

    def close(incoming):
        for c in range(NC):
            first_p = level(p2, 0, c)
            last_p = level(p2, NXC - 1, c)
            x = OWN[0] * first_p + incoming[0][c]
            y = OWN[1] * last_p + incoming[1][c]
            AL[c] = OWN[2] * x + OWN[3] * y
            AR[c] = OWN[4] * x + OWN[5] * y

    def solved(c, z, h):
        return (
            PP[c, z, h]
            + LL[z, h] * jnp.broadcast_to(AL[c, pl.ds(z, 1), :], (8, LANES))
            + RC[z, h] * jnp.broadcast_to(AR[c, pl.ds(z, 1), :], (8, LANES))
        )

    pltpu.make_async_copy(R1, R1, d_recv).wait()
    pl.semaphore_wait(LP.at[2], p_near)
    call_line(LP.at[3], False)
    trio = (none,) * NC
    for c in range(NC):
        for o in range(OWNERS):
            AL[c, 2 * o : 2 * o + 2, :] = R1[0, c, o]
            AR[c, 2 * o : 2 * o + 2, :] = R1[1, c, o]

    def line_first(z, packs):
        for c in range(NC):
            pair = tuple(solved(c, z, h) for h in range(2))
            for h in range(2):
                A2[c, z + 1, h] = pair[h]
            packs = pack_edges(c * NZL + z, pair, packs)
        return packs

    halo2 = send_halo(1, A2, lax.fori_loop(0, NZL, line_first, no_packs, unroll=4))

    def ends(write):
        for c in range(NC):
            first_p = level(p2, 0, c)
            last_p = level(p2, NXC - 1, c)
            write(c, last_p + OWN[6] * first_p, first_p + OWN[7] * last_p)

    def write_rows(c, up, down):
        S2[0, c] = up
        S2[1, c] = down

    def side_of(target):
        return jnp.where(target > chip, 0, 1)

    eliminate(None, A2, 1, NZL - 2, 5)
    ends(write_rows)
    to_chips(lambda target: S2.at[side_of(target)], R2, p_send.at[1], p_recv.at[1])

    each(halo2, 2, lambda c: c.wait_recv())
    pl.semaphore_wait(LP.at[3], p_near)
    call_line(LP.at[4], False)
    eliminate(1, A2, 0, NZL, 12)
    final = ([], [])

    def keep_ends(c, up, down):
        final[0].append(up)
        final[1].append(down)

    ends(keep_ends)
    for i in range(2):
        write_edges(E2.at[i], final[i])
    to_chips(lambda target: E2.at[side_of(target)], RE, e_send, e_recv)
    arrive(R2, p_recv.at[1])
    arrive(RE, e_recv)

    def bring(k, carry):
        O, edge = carry
        return (
            tuple(R2[k, c] + CB[k] * O[c] for c in range(NC)),
            RE[k] + CE[k] * edge,
        )

    def brought(steps, chip_of):
        O, edge = lax.fori_loop(0, steps, lambda i, v: bring(chip_of(i), v), (trio, blank))
        packed = jnp.broadcast_to(edge[6:7], (NZL, LANES))
        whole = []
        for c in range(NC):
            value = O[c]
            for side in range(2):
                at = lane_z == NZL * (2 * c + side) + row_z
                column = jnp.sum(jnp.where(at, packed, 0.0), axis=1, keepdims=True)
                value = jnp.where(
                    lane_z == side * (LANES - 1), jnp.broadcast_to(column, (NZL, LANES)), value
                )
            for side in range(2):
                value = jnp.where(
                    row_z == side * (NZL - 1),
                    jnp.broadcast_to(edge[2 * c + side : 2 * c + side + 1], (NZL, LANES)),
                    value,
                )
            whole.append(value)
        return whole

    close(
        (
            brought(chip, lambda i: i),
            brought(CHIPS - 1 - chip, lambda i: CHIPS - 1 - i),
        )
    )

    pl.semaphore_wait(LT.at[2], 1)
    pl.semaphore_wait(LP.at[4], p_near)

    def line_last(z, acc):
        parts = ([], [])
        for h in range(2):
            total = None
            for c in range(NC):
                a = solved(c, z, h)
                A3[c, z, h] = a
                term = VEL[c, z, h] * a
                total = term if total is None else total + term
            total = total * PEN[z, h]
            coarse = total.astype(jnp.bfloat16).astype(F32)
            for part, value in zip(parts, (coarse, total - coarse)):
                part.append(jnp.concatenate([value, value], axis=0).astype(jnp.bfloat16))
        weights = jnp.concatenate(
            [
                jnp.concatenate([jnp.concatenate(part, axis=1)] * 8, axis=0) * OHH[z]
                for part in parts
            ],
            axis=0,
        )
        return acc + lax.dot_general(
            weights, OHL[z], (((1,), (1,)), ((), ())), preferred_element_type=F32
        )

    acc = lax.fori_loop(0, NZL, line_last, jnp.zeros((2 * LANES, LANES), F32), unroll=3)
    acc = acc[0:LANES] + acc[LANES : 2 * LANES]
    keep = lax.rem(lane, 8) == row
    for r in range(2):
        tall = blank
        for j in range(8):
            at = 8 * (8 * r + j)
            line = jnp.sum(jnp.where(keep, acc[at : at + 8], 0.0), axis=0, keepdims=True)
            tall = jnp.where(row == j, jnp.broadcast_to(line, (8, LANES)), tall)
        for d in (1, 2, 4):
            tall = tall + jnp.where(
                lax.rem(lane // d, 2) == 0, pltpu.roll(tall, LANES - d, 1), pltpu.roll(tall, d, 1)
            )
        B1S[r : r + 1, :] = jnp.sum(jnp.where(keep, tall, 0.0), axis=0, keepdims=True)

    def band_round(r, own, slots, device_of, beside):
        def send(j, carry):
            pltpu.make_async_remote_copy(
                src_ref=own,
                dst_ref=slots.at[j],
                send_sem=b_send.at[r],
                recv_sem=b_recv.at[r],
                device_id=device_of(j),
                device_id_type=MESH,
            ).start()
            return carry

        lax.fori_loop(1, STREAM, send, 0)
        beside()
        got = slots.at[pl.ds(1, STREAM - 1)]
        pltpu.make_async_copy(got, got, b_recv.at[r]).wait()
        total = own[...]
        for j in range(1, STREAM):
            total = total + slots[j]
        return total

    out_own = pltpu.make_async_copy(A3.at[:, :, q], out_h.at[:, :, :, lanes_of(q)], out_sem.at[0])
    out_side = pltpu.make_async_remote_copy(
        src_ref=A3.at[:, :, 1 - q],
        dst_ref=out_h.at[:, :, :, lanes_of(q)],
        send_sem=out_sem.at[1],
        recv_sem=out_sem.at[2],
        device_id=(partner, mv, mp),
        device_id_type=MESH,
    )

    def send_out():
        out_own.start()
        out_side.start()

    B2S[...] = band_round(0, B1S, B1R, lambda j: (lax.rem(me + j, STREAM), mv, mp), send_out)
    bands = band_round(
        1,
        B2S,
        B2R,
        lambda j: (me, lax.rem(mv + j // SPAN, VERT), lax.rem(mp + j % SPAN, SPAN)),
        lambda: None,
    )
    cells = STREAM * VERT * SPAN * NXL * NZL * NYL
    bands = bands * ((NBANDS / cells) ** 0.5)
    tb_copy.wait()
    tw_copy.wait()
    tb = TB[...].reshape(1, LANES)
    spot = lax.rem(tb, 16) * 8 + lax.rem(tb // 16, 8)
    spot = jnp.broadcast_to(spot, (8, LANES))
    low_half = jnp.take_along_axis(jnp.broadcast_to(bands[0:1], (8, LANES)), spot, axis=1)
    high_half = jnp.take_along_axis(jnp.broadcast_to(bands[1:2], (8, LANES)), spot, axis=1)
    picked = jnp.where(tb < LANES, low_half[0:1], high_half[0:1])
    TRI[...] = (TW[...].reshape(1, LANES) * picked).reshape(LANES)
    tri_copy = pltpu.make_async_copy(TRI, tri_h, tri_sem.at[2])
    tri_copy.start()

    def drain(count, ref, sem):
        def one(j, carry):
            pltpu.make_async_copy(ref, ref, sem).wait()
            return carry

        lax.fori_loop(0, count, one, 0)

    for copy in side_copies:
        copy.wait_send()
    for copy, there in first_halo:
        pl.when(there)(copy.wait_send)
    middle.wait_send()
    each(halo2, 1, lambda c: c.wait_send())
    drain(CHIPS - 1, MS, m_send)
    drain(owner_sends, QS.at[:, 0], q_send)
    drain(owner_sends, S1.at[:, :, 0], p_send.at[0])

    @pl.when(is_owner)
    def _():
        drain(CHIPS - 1, D1.at[0], d_send)

    drain(CHIPS - 1, S2.at[0], p_send.at[1])
    drain(CHIPS - 1, E2.at[0], e_send)
    for r, own in enumerate((B1S, B2S)):
        drain(STREAM - 1, own, b_send.at[r])
    out_own.wait()
    out_side.wait()
    tri_copy.wait()


def shards(adjoint_source, velocity, penalty, adjoint_start, cell_band, tri_band, tri_weight):
    anywhere = pl.BlockSpec(memory_space=pl.ANY)

    def field():
        return pltpu.VMEM((NZL, 2, 8, LANES), F32)

    scratch = [
        pltpu.VMEM((NC, NZL, 2, 8, LANES), F32),
        pltpu.VMEM((NC, NZL, 2, 8, LANES), F32),
        field(),
        pltpu.VMEM((NZL, 2, 8, LANES), jnp.int32),
        pltpu.VMEM((NC, NZL + 2, 2, 8, LANES), F32),
        pltpu.VMEM((NC, NZL + 2, 2, 8, LANES), F32),
        pltpu.VMEM((NC, NZL, 2, 8, LANES), F32),
        pltpu.VMEM((NC, NZL, 2, 8, LANES), F32),
        field(),
        field(),
        field(),
        field(),
        pltpu.VMEM((NZL, 8, LANES), F32),
        field(),
        field(),
        field(),
        pltpu.VMEM((NZL, 8, LANES), F32),
        field(),
        field(),
        pltpu.VMEM((NC, NZL, NXL, NYL), F32),
        pltpu.VMEM((4, 8, LANES), F32),
        pltpu.VMEM((SWEEPS, 2, 2, 8, LANES), F32),
        pltpu.VMEM((SWEEPS, 2, 2, 8, LANES), F32),
        pltpu.VMEM((4, NZL, LANES), F32),
        pltpu.VMEM((CHIPS, 4, NZL, LANES), F32),
        pltpu.VMEM((CHIPS, NZL, LANES), F32),
        pltpu.VMEM((CHIPS, 8, LANES), F32),
        pltpu.VMEM((8, NZL, LANES), F32),
        pltpu.VMEM((4, OWNERS, 2, LANES), F32),
        pltpu.VMEM((CHIPS, 4, 2, LANES), F32),
        pltpu.VMEM((CHIPS, 6, 2, LANES), F32),
        pltpu.VMEM((CHIPS, NC, 2, LANES), F32),
        pltpu.VMEM((2, NC, OWNERS, 2, LANES), F32),
        pltpu.VMEM((CHIPS, 2, NC, 2, LANES), F32),
        pltpu.VMEM((CHIPS, 2, NC, 2, LANES), F32),
        pltpu.VMEM((2, NC, OWNERS, 2, LANES), F32),
        pltpu.VMEM((2, NC, NZL, LANES), F32),
        pltpu.VMEM((CHIPS, NC, NZL, LANES), F32),
        pltpu.VMEM((2, 8, LANES), F32),
        pltpu.VMEM((CHIPS, 8, LANES), F32),
        pltpu.VMEM((NC, NZL, LANES), F32),
        pltpu.VMEM((NC, NZL, LANES), F32),
        pltpu.VMEM((NZL, LANES, 2 * LANES), jnp.bfloat16),
        pltpu.VMEM((NZL, LANES, 2 * LANES), jnp.bfloat16),
        pltpu.VMEM((2, LANES), F32),
        pltpu.VMEM((STREAM, 2, LANES), F32),
        pltpu.VMEM((2, LANES), F32),
        pltpu.VMEM((STREAM, 2, LANES), F32),
        pltpu.VMEM((LANES,), jnp.int32),
        pltpu.VMEM((LANES,), F32),
        pltpu.VMEM((LANES,), F32),
        pltpu.SemaphoreType.DMA((6,)),
        pltpu.SemaphoreType.DMA((5,)),
        pltpu.SemaphoreType.DMA((5,)),
        pltpu.SemaphoreType.DMA((3,)),
        pltpu.SemaphoreType.DMA((3,)),
        pltpu.SemaphoreType.REGULAR((3,)),
        pltpu.SemaphoreType.REGULAR((5,)),
        pltpu.SemaphoreType.DMA((2, 2)),
        pltpu.SemaphoreType.DMA((2, 2)),
        pltpu.SemaphoreType.DMA((3,)),
        pltpu.SemaphoreType.DMA((3,)),
        pltpu.SemaphoreType.DMA((SWEEPS, 4)),
        pltpu.SemaphoreType.DMA((SWEEPS, 4)),
        pltpu.SemaphoreType.DMA,
        pltpu.SemaphoreType.DMA,
        pltpu.SemaphoreType.DMA,
        pltpu.SemaphoreType.DMA,
        pltpu.SemaphoreType.DMA,
        pltpu.SemaphoreType.DMA,
        pltpu.SemaphoreType.DMA((SWEEPS,)),
        pltpu.SemaphoreType.DMA((SWEEPS,)),
        pltpu.SemaphoreType.DMA,
        pltpu.SemaphoreType.DMA,
        pltpu.SemaphoreType.DMA((2,)),
        pltpu.SemaphoreType.DMA((2,)),
    ]

    def planes(x):
        return jnp.swapaxes(x, -3, -2)

    adjoint, tri_grad = pl.pallas_call(
        kernel,
        out_shape=(
            jax.ShapeDtypeStruct((NC, NZL, NXL, NYL), F32),
            jax.ShapeDtypeStruct((LANES,), F32),
        ),
        in_specs=[pl.BlockSpec(memory_space=pltpu.HBM)] * 7,
        out_specs=(anywhere, anywhere),
        scratch_shapes=scratch,
        compiler_params=pltpu.CompilerParams(
            collective_id=0, has_side_effects=True, vmem_limit_bytes=56 * 1024 * 1024
        ),
    )(
        planes(adjoint_source),
        planes(velocity),
        planes(penalty),
        planes(adjoint_start),
        planes(cell_band),
        tri_band,
        tri_weight,
    )
    return planes(adjoint), tri_grad


def solution(mesh):
    return jax.shard_map(
        shards,
        mesh=mesh,
        in_specs=(
            P(None, "stream", "span", "vert"),
            P(None, "stream", "span", "vert"),
            P("stream", "span", "vert"),
            P(None, "stream", "span", "vert"),
            P("stream", "span", "vert"),
            P(("stream", "vert", "span")),
            P(("stream", "vert", "span")),
        ),
        out_specs=(P(None, "stream", "span", "vert"), P(("stream", "vert", "span"))),
        check_vma=False,
    )
```

```python
import functools

import jax
import jax.numpy as jnp
from jax import lax
from jax.experimental import pallas as pl
from jax.experimental.pallas import tpu as pltpu
from jax.sharding import PartitionSpec as P

SWEEPS = 2
NBANDS = 256

STREAM = 16
CHIPS = 8
VERT = 4
SPAN = 4
NC = 3
NXL = 8
NXC = 16
NZL = 12
NYL = 256
LANES = 128
OWNERS = 6

stream_coef = 1000.0
stream_conv = 200.0
cross_coef = 0.25
cross_conv = 0.25
shift_coef = 0.5

MESH = pl.DeviceIdType.MESH
F32 = jnp.float32


def kernel(
    src_h,
    vel_h,
    pen_h,
    start_h,
    band_h,
    tb_h,
    tw_h,
    out_h,
    tri_h,
    SRC,
    VEL,
    PEN,
    BAND,
    A1,
    A2,
    A3,
    PP,
    IP,
    M1,
    M2,
    M4,
    MT,
    F1,
    F2,
    F4,
    FT,
    LL,
    RC,
    STG,
    YF,
    YS,
    YR,
    MS,
    MR,
    CB,
    CE,
    OWN,
    QS,
    QR,
    CO,
    OC,
    S1,
    G1,
    D1,
    R1,
    S2,
    R2,
    E2,
    RE,
    AL,
    AR,
    OHH,
    OHL,
    B1S,
    B1R,
    B2S,
    B2R,
    TB,
    TW,
    TRI,
    in_sem,
    side_send,
    side_recv,
    out_sem,
    tri_sem,
    LT,
    LP,
    fz_send,
    fz_recv,
    fv_send,
    fv_recv,
    halo_send,
    halo_recv,
    m_send,
    m_recv,
    q_send,
    q_recv,
    d_send,
    d_recv,
    p_send,
    p_recv,
    e_send,
    e_recv,
    b_send,
    b_recv,
):
    me = lax.axis_index("stream")
    mv = lax.axis_index("vert")
    mp = lax.axis_index("span")
    chip = me // 2
    q = lax.rem(me, 2)
    partner = 2 * chip + (1 - q)

    def lanes_of(half):
        return pl.ds(pl.multiple_of(half * LANES, LANES), LANES)

    def pieces(ref, dst):
        rank = len(ref.shape)
        lead = (slice(None),) * (rank - 1)
        return lambda half: ref.at[lead + (lanes_of(half),)], dst

    inner = A1.at[:, pl.ds(1, NZL)]
    inputs = (
        (start_h, inner),
        (vel_h, VEL),
        (pen_h, PEN),
        (src_h, SRC),
        (band_h, BAND),
    )

    def slot(dst, half):
        if len(dst.shape) == 5:
            return dst.at[:, :, half]
        return dst.at[:, half]

    def part(src, half):
        if len(src.shape) == 4:
            return src.at[:, :, :, lanes_of(half)]
        return src.at[:, :, lanes_of(half)]

    own_copies = []
    side_copies = []
    for i, (src, dst) in enumerate(inputs):
        own_copies.append(pltpu.make_async_copy(part(src, q), slot(dst, q), in_sem.at[i]))
        side_copies.append(
            pltpu.make_async_remote_copy(
                src_ref=part(src, 1 - q),
                dst_ref=slot(dst, q),
                send_sem=side_send.at[i],
                recv_sem=side_recv.at[i],
                device_id=(partner, mv, mp),
                device_id_type=MESH,
            )
        )
    tb_copy = pltpu.make_async_copy(tb_h, TB, tri_sem.at[0])
    tw_copy = pltpu.make_async_copy(tw_h, TW, tri_sem.at[1])

    barrier = pltpu.get_barrier_semaphore()

    def either(condition):
        return jnp.where(condition, 1, 0)

    has_v = (mv > 0, mv < VERT - 1)
    has_p = (mp > 0, mp < SPAN - 1)
    v_near = either(has_v[0]) + either(has_v[1])
    p_near = either(has_p[0]) + either(has_p[1])

    def call(sem, device):
        pl.semaphore_signal(sem, inc=1, device_id=device, device_id_type=MESH)

    def stream_at(step):
        return (lax.rem(me + 2 * step + STREAM, STREAM), mv, mp)

    def call_line(sem, along_v):
        for i, step in enumerate((-1, 1)):
            if along_v:
                pl.when(has_v[i])(lambda: call(sem, (me, mv + step, mp)))
            else:
                pl.when(has_p[i])(lambda: call(sem, (me, mv, mp + step)))

    outer_v = mv - 1 + 2 * q
    has_outer = jnp.logical_and(outer_v >= 0, outer_v < VERT)
    outer_id = (partner, lax.rem(outer_v + VERT, VERT), mp)

    nothing = jnp.zeros((2, 8, LANES), F32)
    for A in (A1, A2):
        for c in range(NC):
            A[c, 0] = nothing
            A[c, NZL + 1] = nothing
    YR[...] = jnp.zeros(YR.shape, F32)

    call(barrier, (partner, mv, mp))
    call(barrier, stream_at(-1))
    call(barrier, stream_at(1))
    for i, step in enumerate((-1, 1)):
        for core in range(2):
            other = 2 * chip + core
            pl.when(has_v[i])(lambda: call(barrier, (other, mv + step, mp)))
            pl.when(has_p[i])(lambda: call(barrier, (other, mv, mp + step)))

    stage = pltpu.make_async_copy(start_h, STG, in_sem.at[5])
    stage.start()
    for i in (1, 2, 0, 3, 4):
        own_copies[i].start()
    tb_copy.start()
    tw_copy.start()
    pl.semaphore_wait(barrier, 3 + 2 * v_near + 2 * p_near)
    for i in range(3):
        side_copies[i].start()
    call(LT.at[0], stream_at(-1))
    call(LT.at[0], stream_at(1))
    call_line(LP.at[0], True)

    row = lax.broadcasted_iota(jnp.int32, (8, LANES), 0)
    lane = lax.broadcasted_iota(jnp.int32, (8, LANES), 1)

    def pack_edges(k, pair, packs):
        low, high = packs
        hit = lane == k
        low = tuple(jnp.where(hit, pltpu.roll(pair[h], k, 1), low[h]) for h in range(2))
        high = tuple(jnp.where(hit, pltpu.roll(pair[h], k + 1, 1), high[h]) for h in range(2))
        return low, high

    blank = jnp.zeros((8, LANES), F32)
    no_packs = ((blank, blank), (blank, blank))

    def send_halo(s, A, packs):
        for side in range(2):
            for h in range(2):
                YS[s, side, h] = packs[side][h]

        def remote(i, src, dst, device):
            return pltpu.make_async_remote_copy(
                src_ref=src,
                dst_ref=dst,
                send_sem=halo_send.at[s, i],
                recv_sem=halo_recv.at[s, i],
                device_id=device,
                device_id_type=MESH,
            )

        copies = (
            (
                remote(0, A.at[:, NZL], A.at[:, 0], (me, mv, lax.rem(mp + 1, SPAN))),
                mp < SPAN - 1,
                mp > 0,
            ),
            (
                remote(1, A.at[:, 1], A.at[:, NZL + 1], (me, mv, lax.rem(mp + SPAN - 1, SPAN))),
                mp > 0,
                mp < SPAN - 1,
            ),
            (remote(2, YS.at[s, q], YR.at[s, 1 - q], outer_id), has_outer, has_outer),
            (remote(3, YS.at[s, 1 - q], YR.at[s, q], (partner, mv, mp)), None, None),
        )
        each(copies, 1, lambda c: c.start())
        return copies

    def each(copies, which, act):
        for item in copies:
            if item[which] is None:
                act(item[0])
            else:
                pl.when(item[which])(functools.partial(act, item[0]))

    first_halo = []
    for i, step in enumerate((-1, 1)):
        for core in range(2):
            first_halo.append(
                (
                    pltpu.make_async_remote_copy(
                        src_ref=start_h.at[:, (0, NZL - 1)[i], :, pl.ds(core * LANES, LANES)],
                        dst_ref=A1.at[:, (NZL + 1, 0)[i], q],
                        send_sem=fz_send.at[i, core],
                        recv_sem=fz_recv.at[i, q],
                        device_id=(2 * chip + core, mv, mp + step),
                        device_id_type=MESH,
                    ),
                    has_p[i],
                )
            )
    for copy, there in first_halo:
        pl.when(there)(copy.start)

    stage.wait()

    def pack_start(z, packs):
        low, high = packs
        for c in range(NC):
            pair = (STG[c, z, :, 0:LANES], STG[c, z, :, LANES:NYL])
            low, high = pack_edges(c * NZL + z, pair, (low, high))
        return low, high

    low, high = lax.fori_loop(0, NZL, pack_start, no_packs)
    for i, value in enumerate((low[0], high[1], high[0], low[1])):
        YF[i] = value
    for i, step in enumerate((-1, 1)):
        copy = pltpu.make_async_remote_copy(
            src_ref=YF.at[i],
            dst_ref=YR.at[0, 1 - i, q],
            send_sem=fv_send.at[i],
            recv_sem=fv_recv.at[q],
            device_id=(2 * chip + 1 - i, mv + step, mp),
            device_id_type=MESH,
        )
        first_halo.append((copy, has_v[i]))
        pl.when(has_v[i])(copy.start)
    middle = pltpu.make_async_remote_copy(
        src_ref=YF.at[2 + q],
        dst_ref=YR.at[0, q, q],
        send_sem=fv_send.at[2],
        recv_sem=fv_recv.at[2],
        device_id=(partner, mv, mp),
        device_id_type=MESH,
    )
    middle.start()
    YR[0, 1 - q, q] = YF[3 - q]

    def first_arrivals():
        for i in range(2):
            for sender in range(2):
                slab = A1.at[:, (0, NZL + 1)[i], sender]
                pl.when(has_p[i])(
                    lambda: pltpu.make_async_copy(slab, slab, fz_recv.at[1 - i, sender]).wait()
                )
        for sender in range(2):
            pl.when(has_outer)(
                lambda: pltpu.make_async_copy(YF.at[0], YF.at[0], fv_recv.at[sender]).wait()
            )
        middle.wait_recv()

    for i in range(3, 5):
        side_copies[i].start()

    for i in (1, 2):
        own_copies[i].wait()
        side_copies[i].wait_recv()

    def flat(ref):
        count = 1
        for size in ref.shape[:-1]:
            count *= size
        return ref.reshape(count, LANES)

    velocity2, penalty2 = flat(VEL), flat(PEN)
    ip2, m2, f2 = flat(IP), flat(M1), flat(F1)
    l2, r2, p2 = flat(LL), flat(RC), flat(PP)

    def level(ref2, x, c=0):
        return ref2[pl.ds(c * NZL * NXC + x, NZL, stride=NXC), :]

    delta = jnp.ones((NZL, LANES), F32)
    for x in range(NXC):
        u = level(velocity2, x, 0)
        west = stream_coef + stream_conv * jnp.maximum(-u, 0.0)
        east = stream_coef + stream_conv * jnp.maximum(u, 0.0)
        excess = (
            (4.0 * cross_coef + shift_coef)
            + cross_conv * (jnp.abs(level(velocity2, x, 1)) + jnp.abs(level(velocity2, x, 2)))
            + level(penalty2, x)
        )
        sink = excess + west * delta
        ip = 1.0 / (east + sink)
        delta = sink * ip
        place = pl.ds(x, NZL, stride=NXC)
        ip2[place, :] = ip
        m2[place, :] = west * ip
        f2[place, :] = east * ip

    def ahead(v, n, fill):
        return jnp.where(row >= n, pltpu.roll(v, n, 0), fill)

    def behind(v, n, fill):
        return jnp.where(row < 8 - n, pltpu.roll(v, 8 - n, 0), fill)

    def fold_up(values, f1, f2, f4, ft):
        new = []
        for h in range(2):
            v = values[h]
            v = v + f1[h] * pltpu.roll(v, 7, 0)
            v = v + f2[h] * pltpu.roll(v, 6, 0)
            v = v + f4[h] * pltpu.roll(v, 4, 0)
            new.append(v)
        new[0] = new[0] + ft * jnp.broadcast_to(new[1][0:1], (8, LANES))
        return new

    def factor(z, carry):
        chains = []
        tails = []
        f1s, f2s, f4s, fts = [], [], [], []
        for h in range(2):
            m = M1[z, h]
            f = F1[z, h]
            m1 = jnp.where(row >= 1, m, 0.0)
            mm = m1 * ahead(m, 1, 0.0)
            m4 = jnp.where(row >= 4, jnp.where(row >= 2, mm, 0.0) * pltpu.roll(mm, 2, 0), 0.0)
            mm = jnp.where(row >= 2, mm, 0.0)
            M1[z, h] = m1
            M2[z, h] = mm
            M4[z, h] = m4
            t = m * ahead(m, 1, 1.0)
            t = t * ahead(t, 2, 1.0)
            chains.append(t * ahead(t, 4, 1.0))
            f1 = jnp.where(row < 7, f, 0.0)
            ff = jnp.where(row < 6, f1 * behind(f, 1, 0.0), 0.0)
            f4 = jnp.where(row < 4, ff * pltpu.roll(ff, 6, 0), 0.0)
            F1[z, h] = f1
            F2[z, h] = ff
            F4[z, h] = f4
            f1s.append(f1)
            f2s.append(ff)
            f4s.append(f4)
            t = f * behind(f, 1, 1.0)
            t = t * behind(t, 2, 1.0)
            tails.append(t * behind(t, 4, 1.0))
        MT[z] = chains[1]
        FT[z] = tails[0]
        left = [chains[0], chains[1] * jnp.broadcast_to(chains[0][7:8], (8, LANES))]
        left = fold_up(left, f1s, f2s, f4s, tails[0])
        right = [tails[0] * jnp.broadcast_to(tails[1][0:1], (8, LANES)), tails[1]]
        for h in range(2):
            LL[z, h] = left[h]
            RC[z, h] = right[h]
        return carry

    lax.fori_loop(0, NZL, factor, 0)
    for k, ref2 in enumerate((l2, r2)):
        MS[2 * k] = level(ref2, 0)
        MS[2 * k + 1] = level(ref2, NXC - 1)

    def to_chips(src_of, dst, send_sem, recv_sem):
        def send(j, carry):
            target = lax.rem(chip + j, CHIPS)
            pltpu.make_async_remote_copy(
                src_ref=src_of(target),
                dst_ref=dst.at[chip],
                send_sem=send_sem,
                recv_sem=recv_sem,
                device_id=(2 * target + q, mv, mp),
                device_id_type=MESH,
            ).start()
            return carry

        lax.fori_loop(1, CHIPS, send, 0)

    def arrive(slots, sem):
        got = slots.at[pl.ds(1, CHIPS - 1)]
        pltpu.make_async_copy(got, got, sem).wait()

    pl.semaphore_wait(LT.at[0], 2)
    call(LT.at[1], stream_at(-2))
    call(LT.at[1], stream_at(2))
    pl.semaphore_wait(LT.at[1], 2)
    call(LT.at[2], (partner, mv, mp))

    is_owner = lax.rem(chip, 4) < 3
    my_o = (chip // 4) * 3 + lax.rem(chip, 4)
    owner_sends = jnp.where(is_owner, OWNERS - 1, OWNERS)

    def to_owners(src_of, dst, send_sem, recv_sem):
        def send(o, carry):
            target = o + o // 3

            @pl.when(target != chip)
            def _():
                pltpu.make_async_remote_copy(
                    src_ref=src_of(o),
                    dst_ref=dst,
                    send_sem=send_sem,
                    recv_sem=recv_sem,
                    device_id=(2 * target + q, mv, mp),
                    device_id_type=MESH,
                ).start()

            @pl.when(target == chip)
            def _():
                pltpu.make_async_copy(src_of(o), dst, recv_sem).start()

            return carry

        lax.fori_loop(0, OWNERS, send, 0)

    for k in range(4):
        value = MS[k]
        for o in range(OWNERS):
            QS[k, o] = value[2 * o : 2 * o + 2]
    to_owners(lambda o: QS.at[:, o], QR.at[chip], q_send, q_recv)

    for i in (3,):
        own_copies[i].wait()
        side_copies[i].wait_recv()

    first = lane == 0
    last = lane == LANES - 1

    def eliminate(s, A, low, count, unroll):
        if s is not None:
            edges = [[YR[s, side, h] for h in range(2)] for side in range(2)]

        def plane(z, carry):
            cross = []
            for h in range(2):
                v = VEL[1, z, h]
                w = VEL[2, z, h]
                cross.append(
                    (
                        cross_coef + cross_conv * jnp.maximum(-v, 0.0),
                        cross_coef + cross_conv * jnp.maximum(v, 0.0),
                        cross_coef + cross_conv * jnp.maximum(-w, 0.0),
                        cross_coef + cross_conv * jnp.maximum(w, 0.0),
                    )
                )
            ip = [IP[z, h] for h in range(2)]
            m1 = [M1[z, h] for h in range(2)]
            m2 = [M2[z, h] for h in range(2)]
            m4 = [M4[z, h] for h in range(2)]
            f1 = [F1[z, h] for h in range(2)]
            f2 = [F2[z, h] for h in range(2)]
            f4 = [F4[z, h] for h in range(2)]
            mt = MT[z]
            ft = FT[z]
            for c in range(NC):
                k = c * NZL + z
                o = []
                for h in range(2):
                    south, north, below, above = cross[h]
                    a = A[c, z + 1, h]
                    lo = hi = blank
                    if s is not None:
                        lo = pltpu.roll(edges[0][h], lax.rem(LANES - k, LANES), 1)
                        hi = pltpu.roll(edges[1][h], LANES - 1 - k, 1)
                    y_lo = jnp.where(first, lo, pltpu.roll(a, 1, 1))
                    y_hi = jnp.where(last, hi, pltpu.roll(a, LANES - 1, 1))
                    rhs = SRC[c, z, h] + shift_coef * a
                    rhs = rhs + south * y_lo + north * y_hi
                    rhs = rhs + below * A[c, z, h] + above * A[c, z + 2, h]
                    v = rhs * ip[h]
                    v = v + m1[h] * pltpu.roll(v, 1, 0)
                    v = v + m2[h] * pltpu.roll(v, 2, 0)
                    v = v + m4[h] * pltpu.roll(v, 4, 0)
                    o.append(v)
                o[1] = o[1] + mt * jnp.broadcast_to(o[0][7:8], (8, LANES))
                p = fold_up(o, f1, f2, f4, ft)
                for h in range(2):
                    PP[c, z, h] = p[h]
            return carry

        lax.fori_loop(low, low + count, plane, 0, unroll=unroll)

    own_copies[0].wait()
    side_copies[0].wait_recv()
    first_arrivals()
    pl.semaphore_wait(LP.at[0], v_near)
    call_line(LP.at[1], True)
    eliminate(0, A1, 0, NZL, 12)
    for c in range(NC):
        for i, x in enumerate((0, NXC - 1)):
            value = level(p2, x, c)
            for o in range(OWNERS):
                S1[i, c, o] = value[2 * o : 2 * o + 2]
    to_owners(lambda o: S1.at[:, :, o], G1.at[chip], p_send.at[0], p_recv.at[0])
    pl.semaphore_wait(LP.at[1], v_near)
    call_line(LP.at[2], False)
    to_chips(lambda target: MS, MR, m_send, m_recv)

    own_copies[4].wait()
    side_copies[4].wait_recv()

    def indicator(digit):
        return jnp.concatenate(
            [jnp.where(digit == i, 1.0, 0.0) for i in range(16)], axis=0
        ).astype(jnp.bfloat16)

    def onehot(z, carry):
        for h in range(2):
            cut = slice(h * LANES, (h + 1) * LANES)
            OHL[z, :, cut] = indicator(lax.rem(BAND[z, h], 16))
            OHH[z, :, cut] = indicator(BAND[z, h] // 16)
        return carry

    lax.fori_loop(0, NZL, onehot, 0)

    @pl.when(is_owner)
    def _():
        pltpu.make_async_copy(QR, QR, q_recv).wait()
        ahead_f = jnp.zeros((2, LANES), F32)
        for k in range(CHIPS):
            lf, lg, rf, rg = (QR[k, i] for i in range(4))
            inv = 1.0 / (1.0 - lf * ahead_f)
            b = lg * inv
            g = b * ahead_f
            for i, value in enumerate((g, b, inv, lf * inv, rf * inv, ahead_f)):
                CO[k, i] = value
            ahead_f = rg + g * rf

        pltpu.make_async_copy(G1, G1, p_recv.at[0]).wait()
        nil = jnp.zeros((2, LANES), F32)
        O = [nil] * NC
        for k in range(CHIPS):
            for c in range(NC):
                OC[k, c] = O[c]
                O[c] = G1[k, 1, c] + CO[k, 0] * G1[k, 0, c] + CO[k, 1] * O[c]
        after = [nil] * NC
        for k in reversed(range(CHIPS)):
            for c in range(NC):
                D1[k, 1, c] = after[c]
                before = OC[k, c]
                after[c] = CO[k, 2] * G1[k, 0, c] + CO[k, 3] * before + CO[k, 4] * after[c]
                D1[k, 0, c] = CO[k, 5] * after[c] + before

        def reply(j, carry):
            target = lax.rem(chip + j, CHIPS)
            pltpu.make_async_remote_copy(
                src_ref=D1.at[target],
                dst_ref=R1.at[:, :, my_o],
                send_sem=d_send,
                recv_sem=d_recv,
                device_id=(2 * target + q, mv, mp),
                device_id_type=MESH,
            ).start()
            return carry

        lax.fori_loop(1, CHIPS, reply, 0)
        pltpu.make_async_copy(D1.at[chip], R1.at[:, :, my_o], d_recv).start()

    arrive(MR, m_recv)

    row_z = lax.broadcasted_iota(jnp.int32, (NZL, LANES), 0)
    lane_z = lax.broadcasted_iota(jnp.int32, (NZL, LANES), 1)

    def write_edges(ref, values):
        packed = jnp.zeros((NZL, LANES), F32)
        for c in range(NC):
            v = values[c]
            for side in range(2):
                ref[2 * c + side : 2 * c + side + 1, :] = v[
                    side * (NZL - 1) : side * (NZL - 1) + 1
                ]
                column = v[:, side * (LANES - 1) : side * (LANES - 1) + 1]
                packed = jnp.where(
                    lane_z == NZL * (2 * c + side) + row_z,
                    jnp.broadcast_to(column, (NZL, LANES)),
                    packed,
                )
        ref[6:7, :] = jnp.sum(packed, axis=0, keepdims=True)
        ref[7:8, :] = jnp.zeros((1, LANES), F32)

    def upstream(k, F):
        lf, lg, rf, rg = (MR[k, i] for i in range(4))
        b = lg / (1.0 - lf * F)
        g = b * F
        CB[k] = b
        write_edges(CE.at[k], (b, b, b))
        return rg + g * rf

    def downstream(i, H):
        k = CHIPS - 1 - i
        lf, lg, rf, rg = (MR[k, i] for i in range(4))
        b = rf / (1.0 - rg * H)
        g = b * H
        CB[k] = b
        write_edges(CE.at[k], (b, b, b))
        return lf + g * lg

    none = jnp.zeros((NZL, LANES), F32)
    F = lax.fori_loop(0, chip, upstream, none)
    H = lax.fori_loop(0, CHIPS - 1 - chip, downstream, none)
    lf, lg, rf, rg = (MS[i] for i in range(4))
    from_left = 1.0 - lf * F
    from_right = 1.0 - rg * H
    inv = 1.0 / (from_left * from_right - (F * rf) * (H * lg))
    for i, value in enumerate(
        (
            F,
            H,
            from_right * inv,
            F * rf * inv,
            H * lg * inv,
            from_left * inv,
            lg / from_left * F,
            rf / from_right * H,
        )
    ):
        OWN[i] = value

    def close(incoming):
        for c in range(NC):
            first_p = level(p2, 0, c)
            last_p = level(p2, NXC - 1, c)
            x = OWN[0] * first_p + incoming[0][c]
            y = OWN[1] * last_p + incoming[1][c]
            AL[c] = OWN[2] * x + OWN[3] * y
            AR[c] = OWN[4] * x + OWN[5] * y

    def solved(c, z, h):
        return (
            PP[c, z, h]
            + LL[z, h] * jnp.broadcast_to(AL[c, pl.ds(z, 1), :], (8, LANES))
            + RC[z, h] * jnp.broadcast_to(AR[c, pl.ds(z, 1), :], (8, LANES))
        )

    pltpu.make_async_copy(R1, R1, d_recv).wait()
    pl.semaphore_wait(LP.at[2], p_near)
    call_line(LP.at[3], False)
    trio = (none,) * NC
    for c in range(NC):
        for o in range(OWNERS):
            AL[c, 2 * o : 2 * o + 2, :] = R1[0, c, o]
            AR[c, 2 * o : 2 * o + 2, :] = R1[1, c, o]

    def line_first(z, packs):
        for c in range(NC):
            pair = tuple(solved(c, z, h) for h in range(2))
            for h in range(2):
                A2[c, z + 1, h] = pair[h]
            packs = pack_edges(c * NZL + z, pair, packs)
        return packs

    halo2 = send_halo(1, A2, lax.fori_loop(0, NZL, line_first, no_packs, unroll=4))

    def ends(write):
        for c in range(NC):
            first_p = level(p2, 0, c)
            last_p = level(p2, NXC - 1, c)
            write(c, last_p + OWN[6] * first_p, first_p + OWN[7] * last_p)

    def write_rows(c, up, down):
        S2[0, c] = up
        S2[1, c] = down

    def side_of(target):
        return jnp.where(target > chip, 0, 1)

    eliminate(None, A2, 1, NZL - 2, 5)
    ends(write_rows)
    to_chips(lambda target: S2.at[side_of(target)], R2, p_send.at[1], p_recv.at[1])

    each(halo2, 2, lambda c: c.wait_recv())
    pl.semaphore_wait(LP.at[3], p_near)
    call_line(LP.at[4], False)
    eliminate(1, A2, 0, NZL, 12)
    final = ([], [])

    def keep_ends(c, up, down):
        final[0].append(up)
        final[1].append(down)

    ends(keep_ends)
    for i in range(2):
        write_edges(E2.at[i], final[i])
    to_chips(lambda target: E2.at[side_of(target)], RE, e_send, e_recv)
    arrive(R2, p_recv.at[1])
    arrive(RE, e_recv)

    def bring(k, carry):
        O, edge = carry
        return (
            tuple(R2[k, c] + CB[k] * O[c] for c in range(NC)),
            RE[k] + CE[k] * edge,
        )

    def brought(steps, chip_of):
        O, edge = lax.fori_loop(0, steps, lambda i, v: bring(chip_of(i), v), (trio, blank))
        packed = jnp.broadcast_to(edge[6:7], (NZL, LANES))
        whole = []
        for c in range(NC):
            value = O[c]
            for side in range(2):
                at = lane_z == NZL * (2 * c + side) + row_z
                column = jnp.sum(jnp.where(at, packed, 0.0), axis=1, keepdims=True)
                value = jnp.where(
                    lane_z == side * (LANES - 1), jnp.broadcast_to(column, (NZL, LANES)), value
                )
            for side in range(2):
                value = jnp.where(
                    row_z == side * (NZL - 1),
                    jnp.broadcast_to(edge[2 * c + side : 2 * c + side + 1], (NZL, LANES)),
                    value,
                )
            whole.append(value)
        return whole

    close(
        (
            brought(chip, lambda i: i),
            brought(CHIPS - 1 - chip, lambda i: CHIPS - 1 - i),
        )
    )

    pl.semaphore_wait(LT.at[2], 1)
    pl.semaphore_wait(LP.at[4], p_near)

    def line_last(z, acc):
        parts = ([], [])
        for h in range(2):
            total = None
            for c in range(NC):
                a = solved(c, z, h)
                A3[c, z, h] = a
                term = VEL[c, z, h] * a
                total = term if total is None else total + term
            total = total * PEN[z, h]
            coarse = total.astype(jnp.bfloat16).astype(F32)
            for part, value in zip(parts, (coarse, total - coarse)):
                part.append(jnp.concatenate([value, value], axis=0).astype(jnp.bfloat16))
        weights = jnp.concatenate(
            [
                jnp.concatenate([jnp.concatenate(part, axis=1)] * 8, axis=0) * OHH[z]
                for part in parts
            ],
            axis=0,
        )
        return acc + lax.dot_general(
            weights, OHL[z], (((1,), (1,)), ((), ())), preferred_element_type=F32
        )

    acc = lax.fori_loop(0, NZL, line_last, jnp.zeros((2 * LANES, LANES), F32), unroll=3)
    acc = acc[0:LANES] + acc[LANES : 2 * LANES]
    keep = lax.rem(lane, 8) == row
    for r in range(2):
        tall = blank
        for j in range(8):
            at = 8 * (8 * r + j)
            line = jnp.sum(jnp.where(keep, acc[at : at + 8], 0.0), axis=0, keepdims=True)
            tall = jnp.where(row == j, jnp.broadcast_to(line, (8, LANES)), tall)
        for d in (1, 2, 4):
            tall = tall + jnp.where(
                lax.rem(lane // d, 2) == 0, pltpu.roll(tall, LANES - d, 1), pltpu.roll(tall, d, 1)
            )
        B1S[r : r + 1, :] = jnp.sum(jnp.where(keep, tall, 0.0), axis=0, keepdims=True)

    def band_round(r, own, slots, device_of, beside):
        def send(j, carry):
            pltpu.make_async_remote_copy(
                src_ref=own,
                dst_ref=slots.at[j],
                send_sem=b_send.at[r],
                recv_sem=b_recv.at[r],
                device_id=device_of(j),
                device_id_type=MESH,
            ).start()
            return carry

        lax.fori_loop(1, STREAM, send, 0)
        beside()
        got = slots.at[pl.ds(1, STREAM - 1)]
        pltpu.make_async_copy(got, got, b_recv.at[r]).wait()
        total = own[...]
        for j in range(1, STREAM):
            total = total + slots[j]
        return total

    out_own = pltpu.make_async_copy(A3.at[:, :, q], out_h.at[:, :, :, lanes_of(q)], out_sem.at[0])
    out_side = pltpu.make_async_remote_copy(
        src_ref=A3.at[:, :, 1 - q],
        dst_ref=out_h.at[:, :, :, lanes_of(q)],
        send_sem=out_sem.at[1],
        recv_sem=out_sem.at[2],
        device_id=(partner, mv, mp),
        device_id_type=MESH,
    )

    def send_out():
        out_own.start()
        out_side.start()

    B2S[...] = band_round(0, B1S, B1R, lambda j: (lax.rem(me + j, STREAM), mv, mp), send_out)
    bands = band_round(
        1,
        B2S,
        B2R,
        lambda j: (me, lax.rem(mv + j // SPAN, VERT), lax.rem(mp + j % SPAN, SPAN)),
        lambda: None,
    )
    cells = STREAM * VERT * SPAN * NXL * NZL * NYL
    bands = bands * ((NBANDS / cells) ** 0.5)
    tb_copy.wait()
    tw_copy.wait()
    tb = TB[...].reshape(1, LANES)
    spot = lax.rem(tb, 16) * 8 + lax.rem(tb // 16, 8)
    spot = jnp.broadcast_to(spot, (8, LANES))
    low_half = jnp.take_along_axis(jnp.broadcast_to(bands[0:1], (8, LANES)), spot, axis=1)
    high_half = jnp.take_along_axis(jnp.broadcast_to(bands[1:2], (8, LANES)), spot, axis=1)
    picked = jnp.where(tb < LANES, low_half[0:1], high_half[0:1])
    TRI[...] = (TW[...].reshape(1, LANES) * picked).reshape(LANES)
    tri_copy = pltpu.make_async_copy(TRI, tri_h, tri_sem.at[2])
    tri_copy.start()

    def drain(count, ref, sem):
        def one(j, carry):
            pltpu.make_async_copy(ref, ref, sem).wait()
            return carry

        lax.fori_loop(0, count, one, 0)

    for copy in side_copies:
        copy.wait_send()
    for copy, there in first_halo:
        pl.when(there)(copy.wait_send)
    middle.wait_send()
    each(halo2, 1, lambda c: c.wait_send())
    drain(CHIPS - 1, MS, m_send)
    drain(owner_sends, QS.at[:, 0], q_send)
    drain(owner_sends, S1.at[:, :, 0], p_send.at[0])

    @pl.when(is_owner)
    def _():
        drain(CHIPS - 1, D1.at[0], d_send)

    drain(CHIPS - 1, S2.at[0], p_send.at[1])
    drain(CHIPS - 1, E2.at[0], e_send)
    for r, own in enumerate((B1S, B2S)):
        drain(STREAM - 1, own, b_send.at[r])
    out_own.wait()
    out_side.wait()
    tri_copy.wait()


def shards(adjoint_source, velocity, penalty, adjoint_start, cell_band, tri_band, tri_weight):
    anywhere = pl.BlockSpec(memory_space=pl.ANY)

    def field():
        return pltpu.VMEM((NZL, 2, 8, LANES), F32)

    scratch = [
        pltpu.VMEM((NC, NZL, 2, 8, LANES), F32),
        pltpu.VMEM((NC, NZL, 2, 8, LANES), F32),
        field(),
        pltpu.VMEM((NZL, 2, 8, LANES), jnp.int32),
        pltpu.VMEM((NC, NZL + 2, 2, 8, LANES), F32),
        pltpu.VMEM((NC, NZL + 2, 2, 8, LANES), F32),
        pltpu.VMEM((NC, NZL, 2, 8, LANES), F32),
        pltpu.VMEM((NC, NZL, 2, 8, LANES), F32),
        field(),
        field(),
        field(),
        field(),
        pltpu.VMEM((NZL, 8, LANES), F32),
        field(),
        field(),
        field(),
        pltpu.VMEM((NZL, 8, LANES), F32),
        field(),
        field(),
        pltpu.VMEM((NC, NZL, NXL, NYL), F32),
        pltpu.VMEM((4, 8, LANES), F32),
        pltpu.VMEM((SWEEPS, 2, 2, 8, LANES), F32),
        pltpu.VMEM((SWEEPS, 2, 2, 8, LANES), F32),
        pltpu.VMEM((4, NZL, LANES), F32),
        pltpu.VMEM((CHIPS, 4, NZL, LANES), F32),
        pltpu.VMEM((CHIPS, NZL, LANES), F32),
        pltpu.VMEM((CHIPS, 8, LANES), F32),
        pltpu.VMEM((8, NZL, LANES), F32),
        pltpu.VMEM((4, OWNERS, 2, LANES), F32),
        pltpu.VMEM((CHIPS, 4, 2, LANES), F32),
        pltpu.VMEM((CHIPS, 6, 2, LANES), F32),
        pltpu.VMEM((CHIPS, NC, 2, LANES), F32),
        pltpu.VMEM((2, NC, OWNERS, 2, LANES), F32),
        pltpu.VMEM((CHIPS, 2, NC, 2, LANES), F32),
        pltpu.VMEM((CHIPS, 2, NC, 2, LANES), F32),
        pltpu.VMEM((2, NC, OWNERS, 2, LANES), F32),
        pltpu.VMEM((2, NC, NZL, LANES), F32),
        pltpu.VMEM((CHIPS, NC, NZL, LANES), F32),
        pltpu.VMEM((2, 8, LANES), F32),
        pltpu.VMEM((CHIPS, 8, LANES), F32),
        pltpu.VMEM((NC, NZL, LANES), F32),
        pltpu.VMEM((NC, NZL, LANES), F32),
        pltpu.VMEM((NZL, LANES, 2 * LANES), jnp.bfloat16),
        pltpu.VMEM((NZL, LANES, 2 * LANES), jnp.bfloat16),
        pltpu.VMEM((2, LANES), F32),
        pltpu.VMEM((STREAM, 2, LANES), F32),
        pltpu.VMEM((2, LANES), F32),
        pltpu.VMEM((STREAM, 2, LANES), F32),
        pltpu.VMEM((LANES,), jnp.int32),
        pltpu.VMEM((LANES,), F32),
        pltpu.VMEM((LANES,), F32),
        pltpu.SemaphoreType.DMA((6,)),
        pltpu.SemaphoreType.DMA((5,)),
        pltpu.SemaphoreType.DMA((5,)),
        pltpu.SemaphoreType.DMA((3,)),
        pltpu.SemaphoreType.DMA((3,)),
        pltpu.SemaphoreType.REGULAR((3,)),
        pltpu.SemaphoreType.REGULAR((5,)),
        pltpu.SemaphoreType.DMA((2, 2)),
        pltpu.SemaphoreType.DMA((2, 2)),
        pltpu.SemaphoreType.DMA((3,)),
        pltpu.SemaphoreType.DMA((3,)),
        pltpu.SemaphoreType.DMA((SWEEPS, 4)),
        pltpu.SemaphoreType.DMA((SWEEPS, 4)),
        pltpu.SemaphoreType.DMA,
        pltpu.SemaphoreType.DMA,
        pltpu.SemaphoreType.DMA,
        pltpu.SemaphoreType.DMA,
        pltpu.SemaphoreType.DMA,
        pltpu.SemaphoreType.DMA,
        pltpu.SemaphoreType.DMA((SWEEPS,)),
        pltpu.SemaphoreType.DMA((SWEEPS,)),
        pltpu.SemaphoreType.DMA,
        pltpu.SemaphoreType.DMA,
        pltpu.SemaphoreType.DMA((2,)),
        pltpu.SemaphoreType.DMA((2,)),
    ]

    def planes(x):
        return jnp.swapaxes(x, -3, -2)

    adjoint, tri_grad = pl.pallas_call(
        kernel,
        out_shape=(
            jax.ShapeDtypeStruct((NC, NZL, NXL, NYL), F32),
            jax.ShapeDtypeStruct((LANES,), F32),
        ),
        in_specs=[pl.BlockSpec(memory_space=pltpu.HBM)] * 7,
        out_specs=(anywhere, anywhere),
        scratch_shapes=scratch,
        compiler_params=pltpu.CompilerParams(
            collective_id=0, has_side_effects=True, vmem_limit_bytes=32 * 1024 * 1024
        ),
    )(
        *(
            pltpu.with_memory_space_constraint(x, pltpu.HBM)
            for x in (
                planes(adjoint_source),
                planes(velocity),
                planes(penalty),
                planes(adjoint_start),
                planes(cell_band),
                tri_band,
                tri_weight,
            )
        )
    )
    return planes(adjoint), tri_grad


def solution(mesh):
    return jax.shard_map(
        shards,
        mesh=mesh,
        in_specs=(
            P(None, "stream", "span", "vert"),
            P(None, "stream", "span", "vert"),
            P("stream", "span", "vert"),
            P(None, "stream", "span", "vert"),
            P("stream", "span", "vert"),
            P(("stream", "vert", "span")),
            P(("stream", "vert", "span")),
        ),
        out_specs=(P(None, "stream", "span", "vert"), P(("stream", "vert", "span"))),
        check_vma=False,
    )
```

```python
import functools

import jax
import jax.numpy as jnp
from jax import lax
from jax.experimental import pallas as pl
from jax.experimental.pallas import tpu as pltpu
from jax.sharding import PartitionSpec as P

SWEEPS = 2
NBANDS = 256

STREAM = 16
CHIPS = 8
VERT = 4
SPAN = 4
NC = 3
NXL = 8
NXC = 16
NZL = 12
NYL = 256
LANES = 128
OWNERS = 6

stream_coef = 1000.0
stream_conv = 200.0
cross_coef = 0.25
cross_conv = 0.25
shift_coef = 0.5

MESH = pl.DeviceIdType.MESH
F32 = jnp.float32


def kernel(
    src_h,
    vel_h,
    pen_h,
    start_h,
    band_h,
    tb_h,
    tw_h,
    out_h,
    tri_h,
    SRC,
    VEL,
    PEN,
    BAND,
    A1,
    A2,
    A3,
    PP,
    IP,
    M1,
    M2,
    M4,
    MT,
    F1,
    F2,
    F4,
    FT,
    LL,
    RC,
    STG,
    YF,
    YS,
    YR,
    MS,
    MR,
    CB,
    CE,
    OWN,
    QS,
    QR,
    CO,
    OC,
    S1,
    G1,
    D1,
    R1,
    S2,
    R2,
    E2,
    RE,
    AL,
    AR,
    OHH,
    OHL,
    B1S,
    B1R,
    B2S,
    B2R,
    TB,
    TW,
    TRI,
    in_sem,
    side_send,
    side_recv,
    out_sem,
    tri_sem,
    LT,
    LP,
    fz_send,
    fz_recv,
    fv_send,
    fv_recv,
    halo_send,
    halo_recv,
    m_send,
    m_recv,
    q_send,
    q_recv,
    d_send,
    d_recv,
    p_send,
    p_recv,
    e_send,
    e_recv,
    b_send,
    b_recv,
):
    me = lax.axis_index("stream")
    mv = lax.axis_index("vert")
    mp = lax.axis_index("span")
    chip = me // 2
    q = lax.rem(me, 2)
    partner = 2 * chip + (1 - q)

    def lanes_of(half):
        return pl.ds(pl.multiple_of(half * LANES, LANES), LANES)

    def pieces(ref, dst):
        rank = len(ref.shape)
        lead = (slice(None),) * (rank - 1)
        return lambda half: ref.at[lead + (lanes_of(half),)], dst

    inner = A1.at[:, pl.ds(1, NZL)]
    inputs = (
        (start_h, inner),
        (vel_h, VEL),
        (pen_h, PEN),
        (src_h, SRC),
        (band_h, BAND),
    )

    def slot(dst, half):
        if len(dst.shape) == 5:
            return dst.at[:, :, half]
        return dst.at[:, half]

    def part(src, half):
        if len(src.shape) == 4:
            return src.at[:, :, :, lanes_of(half)]
        return src.at[:, :, lanes_of(half)]

    own_copies = []
    side_copies = []
    for i, (src, dst) in enumerate(inputs):
        own_copies.append(pltpu.make_async_copy(part(src, q), slot(dst, q), in_sem.at[i]))
        side_copies.append(
            pltpu.make_async_remote_copy(
                src_ref=part(src, 1 - q),
                dst_ref=slot(dst, q),
                send_sem=side_send.at[i],
                recv_sem=side_recv.at[i],
                device_id=(partner, mv, mp),
                device_id_type=MESH,
            )
        )
    tb_copy = pltpu.make_async_copy(tb_h, TB, tri_sem.at[0])
    tw_copy = pltpu.make_async_copy(tw_h, TW, tri_sem.at[1])

    barrier = pltpu.get_barrier_semaphore()

    def either(condition):
        return jnp.where(condition, 1, 0)

    has_v = (mv > 0, mv < VERT - 1)
    has_p = (mp > 0, mp < SPAN - 1)
    v_near = either(has_v[0]) + either(has_v[1])
    p_near = either(has_p[0]) + either(has_p[1])

    def call(sem, device):
        pl.semaphore_signal(sem, inc=1, device_id=device, device_id_type=MESH)

    def stream_at(step):
        return (lax.rem(me + 2 * step + STREAM, STREAM), mv, mp)

    def call_line(sem, along_v):
        for i, step in enumerate((-1, 1)):
            if along_v:
                pl.when(has_v[i])(lambda: call(sem, (me, mv + step, mp)))
            else:
                pl.when(has_p[i])(lambda: call(sem, (me, mv, mp + step)))

    outer_v = mv - 1 + 2 * q
    has_outer = jnp.logical_and(outer_v >= 0, outer_v < VERT)
    outer_id = (partner, lax.rem(outer_v + VERT, VERT), mp)

    nothing = jnp.zeros((2, 8, LANES), F32)
    for A in (A1, A2):
        for c in range(NC):
            A[c, 0] = nothing
            A[c, NZL + 1] = nothing
    YR[...] = jnp.zeros(YR.shape, F32)

    call(barrier, (partner, mv, mp))
    call(barrier, stream_at(-1))
    call(barrier, stream_at(1))
    for i, step in enumerate((-1, 1)):
        for core in range(2):
            other = 2 * chip + core
            pl.when(has_v[i])(lambda: call(barrier, (other, mv + step, mp)))
            pl.when(has_p[i])(lambda: call(barrier, (other, mv, mp + step)))

    stage = pltpu.make_async_copy(start_h, STG, in_sem.at[5])
    stage.start()
    for i in (1, 2, 0, 3, 4):
        own_copies[i].start()
    tb_copy.start()
    tw_copy.start()
    row = lax.broadcasted_iota(jnp.int32, (8, LANES), 0)
    lane = lax.broadcasted_iota(jnp.int32, (8, LANES), 1)

    def pack_edges(k, pair, packs):
        low, high = packs
        hit = lane == k
        low = tuple(jnp.where(hit, pltpu.roll(pair[h], k, 1), low[h]) for h in range(2))
        high = tuple(jnp.where(hit, pltpu.roll(pair[h], k + 1, 1), high[h]) for h in range(2))
        return low, high

    blank = jnp.zeros((8, LANES), F32)
    no_packs = ((blank, blank), (blank, blank))

    stage.wait()

    def pack_start(z, packs):
        low, high = packs
        for c in range(NC):
            pair = (STG[c, z, :, 0:LANES], STG[c, z, :, LANES:NYL])
            low, high = pack_edges(c * NZL + z, pair, (low, high))
        return low, high

    low, high = lax.fori_loop(0, NZL, pack_start, no_packs, unroll=4)
    for i, value in enumerate((low[0], high[1], high[0], low[1])):
        YF[i] = value
    pl.semaphore_wait(barrier, 3 + 2 * v_near + 2 * p_near)
    for i in range(3):
        side_copies[i].start()
    call(LT.at[0], stream_at(-1))
    call(LT.at[0], stream_at(1))
    call_line(LP.at[0], True)

    def send_halo(s, A, packs):
        for side in range(2):
            for h in range(2):
                YS[s, side, h] = packs[side][h]

        def remote(i, src, dst, device):
            return pltpu.make_async_remote_copy(
                src_ref=src,
                dst_ref=dst,
                send_sem=halo_send.at[s, i],
                recv_sem=halo_recv.at[s, i],
                device_id=device,
                device_id_type=MESH,
            )

        copies = (
            (
                remote(0, A.at[:, NZL], A.at[:, 0], (me, mv, lax.rem(mp + 1, SPAN))),
                mp < SPAN - 1,
                mp > 0,
            ),
            (
                remote(1, A.at[:, 1], A.at[:, NZL + 1], (me, mv, lax.rem(mp + SPAN - 1, SPAN))),
                mp > 0,
                mp < SPAN - 1,
            ),
            (remote(2, YS.at[s, q], YR.at[s, 1 - q], outer_id), has_outer, has_outer),
            (remote(3, YS.at[s, 1 - q], YR.at[s, q], (partner, mv, mp)), None, None),
        )
        each(copies, 1, lambda c: c.start())
        return copies

    def each(copies, which, act):
        for item in copies:
            if item[which] is None:
                act(item[0])
            else:
                pl.when(item[which])(functools.partial(act, item[0]))

    first_halo = []
    for i, step in enumerate((-1, 1)):
        for core in range(2):
            first_halo.append(
                (
                    pltpu.make_async_remote_copy(
                        src_ref=start_h.at[:, (0, NZL - 1)[i], :, pl.ds(core * LANES, LANES)],
                        dst_ref=A1.at[:, (NZL + 1, 0)[i], q],
                        send_sem=fz_send.at[i, core],
                        recv_sem=fz_recv.at[i, q],
                        device_id=(2 * chip + core, mv, mp + step),
                        device_id_type=MESH,
                    ),
                    has_p[i],
                )
            )
    for copy, there in first_halo:
        pl.when(there)(copy.start)

    for i, step in enumerate((-1, 1)):
        copy = pltpu.make_async_remote_copy(
            src_ref=YF.at[i],
            dst_ref=YR.at[0, 1 - i, q],
            send_sem=fv_send.at[i],
            recv_sem=fv_recv.at[q],
            device_id=(2 * chip + 1 - i, mv + step, mp),
            device_id_type=MESH,
        )
        first_halo.append((copy, has_v[i]))
        pl.when(has_v[i])(copy.start)
    middle = pltpu.make_async_remote_copy(
        src_ref=YF.at[2 + q],
        dst_ref=YR.at[0, q, q],
        send_sem=fv_send.at[2],
        recv_sem=fv_recv.at[2],
        device_id=(partner, mv, mp),
        device_id_type=MESH,
    )
    middle.start()
    YR[0, 1 - q, q] = YF[3 - q]

    def first_arrivals():
        for i in range(2):
            for sender in range(2):
                slab = A1.at[:, (0, NZL + 1)[i], sender]
                pl.when(has_p[i])(
                    lambda: pltpu.make_async_copy(slab, slab, fz_recv.at[1 - i, sender]).wait()
                )
        for sender in range(2):
            pl.when(has_outer)(
                lambda: pltpu.make_async_copy(YF.at[0], YF.at[0], fv_recv.at[sender]).wait()
            )
        middle.wait_recv()

    for i in range(3, 5):
        side_copies[i].start()

    for i in (1, 2):
        own_copies[i].wait()
        side_copies[i].wait_recv()

    pl.semaphore_wait(LT.at[0], 2)
    call(LT.at[1], stream_at(-2))
    call(LT.at[1], stream_at(2))

    def flat(ref):
        count = 1
        for size in ref.shape[:-1]:
            count *= size
        return ref.reshape(count, LANES)

    velocity2, penalty2 = flat(VEL), flat(PEN)
    ip2, m2, f2 = flat(IP), flat(M1), flat(F1)
    l2, r2, p2 = flat(LL), flat(RC), flat(PP)

    def level(ref2, x, c=0):
        return ref2[pl.ds(c * NZL * NXC + x, NZL, stride=NXC), :]

    delta = jnp.ones((NZL, LANES), F32)
    for x in range(NXC):
        u = level(velocity2, x, 0)
        west = stream_coef + stream_conv * jnp.maximum(-u, 0.0)
        east = stream_coef + stream_conv * jnp.maximum(u, 0.0)
        excess = (
            (4.0 * cross_coef + shift_coef)
            + cross_conv * (jnp.abs(level(velocity2, x, 1)) + jnp.abs(level(velocity2, x, 2)))
            + level(penalty2, x)
        )
        sink = excess + west * delta
        ip = 1.0 / (east + sink)
        delta = sink * ip
        place = pl.ds(x, NZL, stride=NXC)
        ip2[place, :] = ip
        m2[place, :] = west * ip
        f2[place, :] = east * ip

    def ahead(v, n, fill):
        return jnp.where(row >= n, pltpu.roll(v, n, 0), fill)

    def behind(v, n, fill):
        return jnp.where(row < 8 - n, pltpu.roll(v, 8 - n, 0), fill)

    def fold_up(values, f1, f2, f4, ft):
        new = []
        for h in range(2):
            v = values[h]
            v = v + f1[h] * pltpu.roll(v, 7, 0)
            v = v + f2[h] * pltpu.roll(v, 6, 0)
            v = v + f4[h] * pltpu.roll(v, 4, 0)
            new.append(v)
        new[0] = new[0] + ft * jnp.broadcast_to(new[1][0:1], (8, LANES))
        return new

    def factor(z, carry):
        chains = []
        tails = []
        f1s, f2s, f4s, fts = [], [], [], []
        for h in range(2):
            m = M1[z, h]
            f = F1[z, h]
            m1 = jnp.where(row >= 1, m, 0.0)
            mm = m1 * ahead(m, 1, 0.0)
            m4 = jnp.where(row >= 4, jnp.where(row >= 2, mm, 0.0) * pltpu.roll(mm, 2, 0), 0.0)
            mm = jnp.where(row >= 2, mm, 0.0)
            M1[z, h] = m1
            M2[z, h] = mm
            M4[z, h] = m4
            t = m * ahead(m, 1, 1.0)
            t = t * ahead(t, 2, 1.0)
            chains.append(t * ahead(t, 4, 1.0))
            f1 = jnp.where(row < 7, f, 0.0)
            ff = jnp.where(row < 6, f1 * behind(f, 1, 0.0), 0.0)
            f4 = jnp.where(row < 4, ff * pltpu.roll(ff, 6, 0), 0.0)
            F1[z, h] = f1
            F2[z, h] = ff
            F4[z, h] = f4
            f1s.append(f1)
            f2s.append(ff)
            f4s.append(f4)
            t = f * behind(f, 1, 1.0)
            t = t * behind(t, 2, 1.0)
            tails.append(t * behind(t, 4, 1.0))
        MT[z] = chains[1]
        FT[z] = tails[0]
        left = [chains[0], chains[1] * jnp.broadcast_to(chains[0][7:8], (8, LANES))]
        left = fold_up(left, f1s, f2s, f4s, tails[0])
        right = [tails[0] * jnp.broadcast_to(tails[1][0:1], (8, LANES)), tails[1]]
        for h in range(2):
            LL[z, h] = left[h]
            RC[z, h] = right[h]
        return carry

    lax.fori_loop(0, NZL, factor, 0)
    for k, ref2 in enumerate((l2, r2)):
        MS[2 * k] = level(ref2, 0)
        MS[2 * k + 1] = level(ref2, NXC - 1)

    def to_chips(src_of, dst, send_sem, recv_sem):
        def send(j, carry):
            target = lax.rem(chip + j, CHIPS)
            pltpu.make_async_remote_copy(
                src_ref=src_of(target),
                dst_ref=dst.at[chip],
                send_sem=send_sem,
                recv_sem=recv_sem,
                device_id=(2 * target + q, mv, mp),
                device_id_type=MESH,
            ).start()
            return carry

        lax.fori_loop(1, CHIPS, send, 0)

    def arrive(slots, sem):
        got = slots.at[pl.ds(1, CHIPS - 1)]
        pltpu.make_async_copy(got, got, sem).wait()

    pl.semaphore_wait(LT.at[1], 2)
    call(LT.at[2], (partner, mv, mp))

    is_owner = lax.rem(chip, 4) < 3
    my_o = (chip // 4) * 3 + lax.rem(chip, 4)
    owner_sends = jnp.where(is_owner, OWNERS - 1, OWNERS)

    def to_owners(src_of, dst, send_sem, recv_sem):
        def send(o, carry):
            target = o + o // 3

            @pl.when(target != chip)
            def _():
                pltpu.make_async_remote_copy(
                    src_ref=src_of(o),
                    dst_ref=dst,
                    send_sem=send_sem,
                    recv_sem=recv_sem,
                    device_id=(2 * target + q, mv, mp),
                    device_id_type=MESH,
                ).start()

            @pl.when(target == chip)
            def _():
                pltpu.make_async_copy(src_of(o), dst, recv_sem).start()

            return carry

        lax.fori_loop(0, OWNERS, send, 0)

    for k in range(4):
        value = MS[k]
        for o in range(OWNERS):
            QS[k, o] = value[2 * o : 2 * o + 2]
    to_owners(lambda o: QS.at[:, o], QR.at[chip], q_send, q_recv)

    for i in (3,):
        own_copies[i].wait()
        side_copies[i].wait_recv()

    first = lane == 0
    last = lane == LANES - 1

    def eliminate(s, A, low, count, unroll):
        if s is not None:
            edges = [[YR[s, side, h] for h in range(2)] for side in range(2)]

        def plane(z, carry):
            cross = []
            for h in range(2):
                v = VEL[1, z, h]
                w = VEL[2, z, h]
                cross.append(
                    (
                        cross_coef + cross_conv * jnp.maximum(-v, 0.0),
                        cross_coef + cross_conv * jnp.maximum(v, 0.0),
                        cross_coef + cross_conv * jnp.maximum(-w, 0.0),
                        cross_coef + cross_conv * jnp.maximum(w, 0.0),
                    )
                )
            ip = [IP[z, h] for h in range(2)]
            m1 = [M1[z, h] for h in range(2)]
            m2 = [M2[z, h] for h in range(2)]
            m4 = [M4[z, h] for h in range(2)]
            f1 = [F1[z, h] for h in range(2)]
            f2 = [F2[z, h] for h in range(2)]
            f4 = [F4[z, h] for h in range(2)]
            mt = MT[z]
            ft = FT[z]
            for c in range(NC):
                k = c * NZL + z
                o = []
                for h in range(2):
                    south, north, below, above = cross[h]
                    a = A[c, z + 1, h]
                    lo = hi = blank
                    if s is not None:
                        lo = pltpu.roll(edges[0][h], lax.rem(LANES - k, LANES), 1)
                        hi = pltpu.roll(edges[1][h], LANES - 1 - k, 1)
                    y_lo = jnp.where(first, lo, pltpu.roll(a, 1, 1))
                    y_hi = jnp.where(last, hi, pltpu.roll(a, LANES - 1, 1))
                    rhs = SRC[c, z, h] + shift_coef * a
                    rhs = rhs + south * y_lo + north * y_hi
                    rhs = rhs + below * A[c, z, h] + above * A[c, z + 2, h]
                    v = rhs * ip[h]
                    v = v + m1[h] * pltpu.roll(v, 1, 0)
                    v = v + m2[h] * pltpu.roll(v, 2, 0)
                    v = v + m4[h] * pltpu.roll(v, 4, 0)
                    o.append(v)
                o[1] = o[1] + mt * jnp.broadcast_to(o[0][7:8], (8, LANES))
                p = fold_up(o, f1, f2, f4, ft)
                for h in range(2):
                    PP[c, z, h] = p[h]
            return carry

        lax.fori_loop(low, low + count, plane, 0, unroll=unroll)

    own_copies[0].wait()
    side_copies[0].wait_recv()
    first_arrivals()
    pl.semaphore_wait(LP.at[0], v_near)
    call_line(LP.at[1], True)
    eliminate(0, A1, 0, NZL, 12)
    for c in range(NC):
        for i, x in enumerate((0, NXC - 1)):
            value = level(p2, x, c)
            for o in range(OWNERS):
                S1[i, c, o] = value[2 * o : 2 * o + 2]
    to_owners(lambda o: S1.at[:, :, o], G1.at[chip], p_send.at[0], p_recv.at[0])
    pl.semaphore_wait(LP.at[1], v_near)
    call_line(LP.at[2], False)
    to_chips(lambda target: MS, MR, m_send, m_recv)

    own_copies[4].wait()
    side_copies[4].wait_recv()

    def indicator(digit, count):
        return jnp.concatenate(
            [jnp.where(digit == i, 1.0, 0.0) for i in range(count)], axis=0
        ).astype(jnp.bfloat16)

    def onehot(z, carry):
        for h in range(2):
            cut = slice(h * LANES, (h + 1) * LANES)
            OHL[z, :, cut] = indicator(lax.rem(BAND[z, h], 32), 32)
            OHH[z, :, cut] = indicator(BAND[z, h] // 32, 8)
        return carry

    lax.fori_loop(0, NZL, onehot, 0)

    @pl.when(is_owner)
    def _():
        pltpu.make_async_copy(QR, QR, q_recv).wait()
        ahead_f = jnp.zeros((2, LANES), F32)
        for k in range(CHIPS):
            lf, lg, rf, rg = (QR[k, i] for i in range(4))
            inv = 1.0 / (1.0 - lf * ahead_f)
            b = lg * inv
            g = b * ahead_f
            for i, value in enumerate((g, b, inv, lf * inv, rf * inv, ahead_f)):
                CO[k, i] = value
            ahead_f = rg + g * rf

        pltpu.make_async_copy(G1, G1, p_recv.at[0]).wait()
        nil = jnp.zeros((2, LANES), F32)
        O = [nil] * NC
        for k in range(CHIPS):
            for c in range(NC):
                OC[k, c] = O[c]
                O[c] = G1[k, 1, c] + CO[k, 0] * G1[k, 0, c] + CO[k, 1] * O[c]
        after = [nil] * NC
        for k in reversed(range(CHIPS)):
            for c in range(NC):
                D1[k, 1, c] = after[c]
                before = OC[k, c]
                after[c] = CO[k, 2] * G1[k, 0, c] + CO[k, 3] * before + CO[k, 4] * after[c]
                D1[k, 0, c] = CO[k, 5] * after[c] + before

        def reply(j, carry):
            target = lax.rem(chip + j, CHIPS)
            pltpu.make_async_remote_copy(
                src_ref=D1.at[target],
                dst_ref=R1.at[:, :, my_o],
                send_sem=d_send,
                recv_sem=d_recv,
                device_id=(2 * target + q, mv, mp),
                device_id_type=MESH,
            ).start()
            return carry

        lax.fori_loop(1, CHIPS, reply, 0)
        pltpu.make_async_copy(D1.at[chip], R1.at[:, :, my_o], d_recv).start()

    arrive(MR, m_recv)

    row_z = lax.broadcasted_iota(jnp.int32, (NZL, LANES), 0)
    lane_z = lax.broadcasted_iota(jnp.int32, (NZL, LANES), 1)

    def write_edges(ref, values):
        packed = jnp.zeros((NZL, LANES), F32)
        for c in range(NC):
            v = values[c]
            for side in range(2):
                ref[2 * c + side : 2 * c + side + 1, :] = v[
                    side * (NZL - 1) : side * (NZL - 1) + 1
                ]
                column = v[:, side * (LANES - 1) : side * (LANES - 1) + 1]
                packed = jnp.where(
                    lane_z == NZL * (2 * c + side) + row_z,
                    jnp.broadcast_to(column, (NZL, LANES)),
                    packed,
                )
        ref[6:7, :] = jnp.sum(packed, axis=0, keepdims=True)
        ref[7:8, :] = jnp.zeros((1, LANES), F32)

    def upstream(k, F):
        lf, lg, rf, rg = (MR[k, i] for i in range(4))
        b = lg / (1.0 - lf * F)
        g = b * F
        CB[k] = b
        return rg + g * rf

    def downstream(i, H):
        k = CHIPS - 1 - i
        lf, lg, rf, rg = (MR[k, i] for i in range(4))
        b = rf / (1.0 - rg * H)
        g = b * H
        CB[k] = b
        return lf + g * lg

    none = jnp.zeros((NZL, LANES), F32)
    F = lax.fori_loop(0, chip, upstream, none)
    H = lax.fori_loop(0, CHIPS - 1 - chip, downstream, none)
    lf, lg, rf, rg = (MS[i] for i in range(4))
    from_left = 1.0 - lf * F
    from_right = 1.0 - rg * H
    inv = 1.0 / (from_left * from_right - (F * rf) * (H * lg))
    for i, value in enumerate(
        (
            F,
            H,
            from_right * inv,
            F * rf * inv,
            H * lg * inv,
            from_left * inv,
            lg / from_left * F,
            rf / from_right * H,
        )
    ):
        OWN[i] = value

    def close(incoming):
        for c in range(NC):
            first_p = level(p2, 0, c)
            last_p = level(p2, NXC - 1, c)
            x = OWN[0] * first_p + incoming[0][c]
            y = OWN[1] * last_p + incoming[1][c]
            AL[c] = OWN[2] * x + OWN[3] * y
            AR[c] = OWN[4] * x + OWN[5] * y

    def solved(c, z, h):
        return (
            PP[c, z, h]
            + LL[z, h] * jnp.broadcast_to(AL[c, pl.ds(z, 1), :], (8, LANES))
            + RC[z, h] * jnp.broadcast_to(AR[c, pl.ds(z, 1), :], (8, LANES))
        )

    pltpu.make_async_copy(R1, R1, d_recv).wait()
    pl.semaphore_wait(LP.at[2], p_near)
    call_line(LP.at[3], False)
    trio = (none,) * NC
    for c in range(NC):
        for o in range(OWNERS):
            AL[c, 2 * o : 2 * o + 2, :] = R1[0, c, o]
            AR[c, 2 * o : 2 * o + 2, :] = R1[1, c, o]

    def line_first(z, packs):
        for c in range(NC):
            pair = tuple(solved(c, z, h) for h in range(2))
            for h in range(2):
                A2[c, z + 1, h] = pair[h]
            packs = pack_edges(c * NZL + z, pair, packs)
        return packs

    halo2 = send_halo(1, A2, lax.fori_loop(0, NZL, line_first, no_packs, unroll=4))

    def ends(write):
        for c in range(NC):
            first_p = level(p2, 0, c)
            last_p = level(p2, NXC - 1, c)
            write(c, last_p + OWN[6] * first_p, first_p + OWN[7] * last_p)

    def write_rows(c, up, down):
        S2[0, c] = up
        S2[1, c] = down

    def side_of(target):
        return jnp.where(target > chip, 0, 1)

    eliminate(None, A2, 1, NZL - 2, 5)
    ends(write_rows)
    to_chips(lambda target: S2.at[side_of(target)], R2, p_send.at[1], p_recv.at[1])

    def edge_coefficients(k, carry):
        write_edges(CE.at[k], (CB[k],) * NC)
        return carry

    lax.fori_loop(0, chip, edge_coefficients, 0)
    lax.fori_loop(chip + 1, CHIPS, edge_coefficients, 0)

    each(halo2, 2, lambda c: c.wait_recv())
    pl.semaphore_wait(LP.at[3], p_near)
    call_line(LP.at[4], False)
    eliminate(1, A2, 0, NZL, 12)
    final = ([], [])

    def keep_ends(c, up, down):
        final[0].append(up)
        final[1].append(down)

    ends(keep_ends)
    for i in range(2):
        write_edges(E2.at[i], final[i])
    to_chips(lambda target: E2.at[side_of(target)], RE, e_send, e_recv)
    arrive(R2, p_recv.at[1])
    arrive(RE, e_recv)

    def bring(k, carry):
        O, edge = carry
        return (
            tuple(R2[k, c] + CB[k] * O[c] for c in range(NC)),
            RE[k] + CE[k] * edge,
        )

    def brought(steps, chip_of):
        O, edge = lax.fori_loop(0, steps, lambda i, v: bring(chip_of(i), v), (trio, blank))
        packed = jnp.broadcast_to(edge[6:7], (NZL, LANES))
        whole = []
        for c in range(NC):
            value = O[c]
            for side in range(2):
                at = lane_z == NZL * (2 * c + side) + row_z
                column = jnp.sum(jnp.where(at, packed, 0.0), axis=1, keepdims=True)
                value = jnp.where(
                    lane_z == side * (LANES - 1), jnp.broadcast_to(column, (NZL, LANES)), value
                )
            for side in range(2):
                value = jnp.where(
                    row_z == side * (NZL - 1),
                    jnp.broadcast_to(edge[2 * c + side : 2 * c + side + 1], (NZL, LANES)),
                    value,
                )
            whole.append(value)
        return whole

    close(
        (
            brought(chip, lambda i: i),
            brought(CHIPS - 1 - chip, lambda i: CHIPS - 1 - i),
        )
    )

    pl.semaphore_wait(LT.at[2], 1)
    pl.semaphore_wait(LP.at[4], p_near)

    def line_last(z, acc):
        parts = ([], [])
        for h in range(2):
            total = None
            for c in range(NC):
                a = solved(c, z, h)
                A3[c, z, h] = a
                term = VEL[c, z, h] * a
                total = term if total is None else total + term
            total = total * PEN[z, h]
            coarse = total.astype(jnp.bfloat16).astype(F32)
            for part, value in zip(parts, (coarse, total - coarse)):
                part.append(jnp.concatenate([value, value], axis=0).astype(jnp.bfloat16))
        weights = jnp.concatenate(
            [
                jnp.concatenate([jnp.concatenate(part, axis=1)] * 4, axis=0) * OHH[z]
                for part in parts
            ],
            axis=0,
        )
        return acc + lax.dot_general(
            weights, OHL[z], (((1,), (1,)), ((), ())), preferred_element_type=F32
        )

    acc = lax.fori_loop(0, NZL, line_last, jnp.zeros((LANES, 2 * LANES), F32), unroll=12)
    acc = acc[0:64] + acc[64:128]
    keep = lax.rem(lane, 8) == row
    for r in range(2):
        tall = blank
        for j in range(8):
            tile = acc[8 * j : 8 * j + 8, r * LANES : (r + 1) * LANES]
            line = jnp.sum(jnp.where(keep, tile, 0.0), axis=0, keepdims=True)
            tall = jnp.where(row == j, jnp.broadcast_to(line, (8, LANES)), tall)
        for d in (1, 2, 4):
            tall = tall + jnp.where(
                lax.rem(lane // d, 2) == 0, pltpu.roll(tall, LANES - d, 1), pltpu.roll(tall, d, 1)
            )
        B1S[r : r + 1, :] = jnp.sum(jnp.where(keep, tall, 0.0), axis=0, keepdims=True)

    def band_round(r, own, slots, device_of, beside):
        def send(j, carry):
            pltpu.make_async_remote_copy(
                src_ref=own,
                dst_ref=slots.at[j],
                send_sem=b_send.at[r],
                recv_sem=b_recv.at[r],
                device_id=device_of(j),
                device_id_type=MESH,
            ).start()
            return carry

        lax.fori_loop(1, STREAM, send, 0)
        beside()
        got = slots.at[pl.ds(1, STREAM - 1)]
        pltpu.make_async_copy(got, got, b_recv.at[r]).wait()
        total = own[...]
        for j in range(1, STREAM):
            total = total + slots[j]
        return total

    out_own = pltpu.make_async_copy(A3.at[:, :, q], out_h.at[:, :, :, lanes_of(q)], out_sem.at[0])
    out_side = pltpu.make_async_remote_copy(
        src_ref=A3.at[:, :, 1 - q],
        dst_ref=out_h.at[:, :, :, lanes_of(q)],
        send_sem=out_sem.at[1],
        recv_sem=out_sem.at[2],
        device_id=(partner, mv, mp),
        device_id_type=MESH,
    )

    def send_out():
        out_own.start()
        out_side.start()

    B2S[...] = band_round(0, B1S, B1R, lambda j: (lax.rem(me + j, STREAM), mv, mp), send_out)
    bands = band_round(
        1,
        B2S,
        B2R,
        lambda j: (me, lax.rem(mv + j // SPAN, VERT), lax.rem(mp + j % SPAN, SPAN)),
        lambda: None,
    )
    cells = STREAM * VERT * SPAN * NXL * NZL * NYL
    bands = bands * ((NBANDS / cells) ** 0.5)
    tb_copy.wait()
    tw_copy.wait()
    tb = TB[...].reshape(1, LANES)
    spot = lax.rem(tb, 16) * 8 + tb // 32
    spot = jnp.broadcast_to(spot, (8, LANES))
    low_half = jnp.take_along_axis(jnp.broadcast_to(bands[0:1], (8, LANES)), spot, axis=1)
    high_half = jnp.take_along_axis(jnp.broadcast_to(bands[1:2], (8, LANES)), spot, axis=1)
    picked = jnp.where(lax.rem(tb, 32) < 16, low_half[0:1], high_half[0:1])
    TRI[...] = (TW[...].reshape(1, LANES) * picked).reshape(LANES)
    tri_copy = pltpu.make_async_copy(TRI, tri_h, tri_sem.at[2])
    tri_copy.start()

    def drain(count, ref, sem):
        def one(j, carry):
            pltpu.make_async_copy(ref, ref, sem).wait()
            return carry

        lax.fori_loop(0, count, one, 0)

    for copy in side_copies:
        copy.wait_send()
    for copy, there in first_halo:
        pl.when(there)(copy.wait_send)
    middle.wait_send()
    each(halo2, 1, lambda c: c.wait_send())
    drain(CHIPS - 1, MS, m_send)
    drain(owner_sends, QS.at[:, 0], q_send)
    drain(owner_sends, S1.at[:, :, 0], p_send.at[0])

    @pl.when(is_owner)
    def _():
        drain(CHIPS - 1, D1.at[0], d_send)

    drain(CHIPS - 1, S2.at[0], p_send.at[1])
    drain(CHIPS - 1, E2.at[0], e_send)
    for r, own in enumerate((B1S, B2S)):
        drain(STREAM - 1, own, b_send.at[r])
    out_own.wait()
    out_side.wait()
    tri_copy.wait()


def shards(adjoint_source, velocity, penalty, adjoint_start, cell_band, tri_band, tri_weight):
    anywhere = pl.BlockSpec(memory_space=pl.ANY)

    def field():
        return pltpu.VMEM((NZL, 2, 8, LANES), F32)

    scratch = [
        pltpu.VMEM((NC, NZL, 2, 8, LANES), F32),
        pltpu.VMEM((NC, NZL, 2, 8, LANES), F32),
        field(),
        pltpu.VMEM((NZL, 2, 8, LANES), jnp.int32),
        pltpu.VMEM((NC, NZL + 2, 2, 8, LANES), F32),
        pltpu.VMEM((NC, NZL + 2, 2, 8, LANES), F32),
        pltpu.VMEM((NC, NZL, 2, 8, LANES), F32),
        pltpu.VMEM((NC, NZL, 2, 8, LANES), F32),
        field(),
        field(),
        field(),
        field(),
        pltpu.VMEM((NZL, 8, LANES), F32),
        field(),
        field(),
        field(),
        pltpu.VMEM((NZL, 8, LANES), F32),
        field(),
        field(),
        pltpu.VMEM((NC, NZL, NXL, NYL), F32),
        pltpu.VMEM((4, 8, LANES), F32),
        pltpu.VMEM((SWEEPS, 2, 2, 8, LANES), F32),
        pltpu.VMEM((SWEEPS, 2, 2, 8, LANES), F32),
        pltpu.VMEM((4, NZL, LANES), F32),
        pltpu.VMEM((CHIPS, 4, NZL, LANES), F32),
        pltpu.VMEM((CHIPS, NZL, LANES), F32),
        pltpu.VMEM((CHIPS, 8, LANES), F32),
        pltpu.VMEM((8, NZL, LANES), F32),
        pltpu.VMEM((4, OWNERS, 2, LANES), F32),
        pltpu.VMEM((CHIPS, 4, 2, LANES), F32),
        pltpu.VMEM((CHIPS, 6, 2, LANES), F32),
        pltpu.VMEM((CHIPS, NC, 2, LANES), F32),
        pltpu.VMEM((2, NC, OWNERS, 2, LANES), F32),
        pltpu.VMEM((CHIPS, 2, NC, 2, LANES), F32),
        pltpu.VMEM((CHIPS, 2, NC, 2, LANES), F32),
        pltpu.VMEM((2, NC, OWNERS, 2, LANES), F32),
        pltpu.VMEM((2, NC, NZL, LANES), F32),
        pltpu.VMEM((CHIPS, NC, NZL, LANES), F32),
        pltpu.VMEM((2, 8, LANES), F32),
        pltpu.VMEM((CHIPS, 8, LANES), F32),
        pltpu.VMEM((NC, NZL, LANES), F32),
        pltpu.VMEM((NC, NZL, LANES), F32),
        pltpu.VMEM((NZL, 64, 2 * LANES), jnp.bfloat16),
        pltpu.VMEM((NZL, 2 * LANES, 2 * LANES), jnp.bfloat16),
        pltpu.VMEM((2, LANES), F32),
        pltpu.VMEM((STREAM, 2, LANES), F32),
        pltpu.VMEM((2, LANES), F32),
        pltpu.VMEM((STREAM, 2, LANES), F32),
        pltpu.VMEM((LANES,), jnp.int32),
        pltpu.VMEM((LANES,), F32),
        pltpu.VMEM((LANES,), F32),
        pltpu.SemaphoreType.DMA((6,)),
        pltpu.SemaphoreType.DMA((5,)),
        pltpu.SemaphoreType.DMA((5,)),
        pltpu.SemaphoreType.DMA((3,)),
        pltpu.SemaphoreType.DMA((3,)),
        pltpu.SemaphoreType.REGULAR((3,)),
        pltpu.SemaphoreType.REGULAR((5,)),
        pltpu.SemaphoreType.DMA((2, 2)),
        pltpu.SemaphoreType.DMA((2, 2)),
        pltpu.SemaphoreType.DMA((3,)),
        pltpu.SemaphoreType.DMA((3,)),
        pltpu.SemaphoreType.DMA((SWEEPS, 4)),
        pltpu.SemaphoreType.DMA((SWEEPS, 4)),
        pltpu.SemaphoreType.DMA,
        pltpu.SemaphoreType.DMA,
        pltpu.SemaphoreType.DMA,
        pltpu.SemaphoreType.DMA,
        pltpu.SemaphoreType.DMA,
        pltpu.SemaphoreType.DMA,
        pltpu.SemaphoreType.DMA((SWEEPS,)),
        pltpu.SemaphoreType.DMA((SWEEPS,)),
        pltpu.SemaphoreType.DMA,
        pltpu.SemaphoreType.DMA,
        pltpu.SemaphoreType.DMA((2,)),
        pltpu.SemaphoreType.DMA((2,)),
    ]

    def planes(x):
        return jnp.swapaxes(x, -3, -2)

    adjoint, tri_grad = pl.pallas_call(
        kernel,
        out_shape=(
            jax.ShapeDtypeStruct((NC, NZL, NXL, NYL), F32),
            jax.ShapeDtypeStruct((LANES,), F32),
        ),
        in_specs=[pl.BlockSpec(memory_space=pltpu.HBM)] * 7,
        out_specs=(anywhere, anywhere),
        scratch_shapes=scratch,
        compiler_params=pltpu.CompilerParams(
            collective_id=0, has_side_effects=True, vmem_limit_bytes=32 * 1024 * 1024
        ),
    )(
        *(
            pltpu.with_memory_space_constraint(x, pltpu.HBM)
            for x in (
                planes(adjoint_source),
                planes(velocity),
                planes(penalty),
                planes(adjoint_start),
                planes(cell_band),
                tri_band,
                tri_weight,
            )
        )
    )
    return planes(adjoint), tri_grad


def solution(mesh):
    return jax.shard_map(
        shards,
        mesh=mesh,
        in_specs=(
            P(None, "stream", "span", "vert"),
            P(None, "stream", "span", "vert"),
            P("stream", "span", "vert"),
            P(None, "stream", "span", "vert"),
            P("stream", "span", "vert"),
            P(("stream", "vert", "span")),
            P(("stream", "vert", "span")),
        ),
        out_specs=(P(None, "stream", "span", "vert"), P(("stream", "vert", "span"))),
        check_vma=False,
    )
```

```python
import functools

import jax
import jax.numpy as jnp
from jax import lax
from jax.experimental import pallas as pl
from jax.experimental.pallas import tpu as pltpu
from jax.sharding import PartitionSpec as P

SWEEPS = 2
NBANDS = 256

STREAM = 16
CHIPS = 8
VERT = 4
SPAN = 4
NC = 3
NXL = 8
NXC = 16
NZL = 12
NYL = 256
LANES = 128
OWNERS = 6
FAR_FIRST = (4, 3, 5, 2, 6, 1, 7)

stream_coef = 1000.0
stream_conv = 200.0
cross_coef = 0.25
cross_conv = 0.25
shift_coef = 0.5

MESH = pl.DeviceIdType.MESH
F32 = jnp.float32


def kernel(
    src_h,
    vel_h,
    pen_h,
    start_h,
    band_h,
    tb_h,
    tw_h,
    out_h,
    tri_ref,
    SRC,
    VEL,
    PEN,
    BAND,
    A1,
    A2,
    A3,
    PP,
    IP,
    M1,
    M2,
    M4,
    MT,
    F1,
    F2,
    F4,
    FT,
    LL,
    RC,
    STG,
    YF,
    YS,
    YR,
    MS,
    MR,
    CB,
    CE,
    OWN,
    QS,
    QR,
    CO,
    OC,
    S1,
    G1,
    D1,
    R1,
    S2,
    R2,
    E2,
    RE,
    AL,
    AR,
    OHH,
    OHL,
    B1S,
    B1R,
    B2S,
    B2R,
    TB,
    TW,
    in_sem,
    side_send,
    side_recv,
    out_sem,
    tri_sem,
    LT,
    LP,
    fz_send,
    fz_recv,
    fv_send,
    fv_recv,
    halo_send,
    halo_recv,
    m_send,
    m_recv,
    q_send,
    q_recv,
    d_send,
    d_recv,
    p_send,
    p_recv,
    e_send,
    e_recv,
    b_send,
    b_recv,
):
    me = lax.axis_index("stream")
    mv = lax.axis_index("vert")
    mp = lax.axis_index("span")
    chip = me // 2
    q = lax.rem(me, 2)
    partner = 2 * chip + (1 - q)

    def lanes_of(half):
        return pl.ds(pl.multiple_of(half * LANES, LANES), LANES)

    def pieces(ref, dst):
        rank = len(ref.shape)
        lead = (slice(None),) * (rank - 1)
        return lambda half: ref.at[lead + (lanes_of(half),)], dst

    inner = A1.at[:, pl.ds(1, NZL)]
    inputs = (
        (start_h, inner),
        (vel_h, VEL),
        (pen_h, PEN),
        (src_h, SRC),
        (band_h, BAND),
    )

    def slot(dst, half):
        if len(dst.shape) == 5:
            return dst.at[:, :, half]
        return dst.at[:, half]

    def part(src, half):
        if len(src.shape) == 4:
            return src.at[:, :, :, lanes_of(half)]
        return src.at[:, :, lanes_of(half)]

    own_copies = []
    side_copies = []
    for i, (src, dst) in enumerate(inputs):
        own_copies.append(pltpu.make_async_copy(part(src, q), slot(dst, q), in_sem.at[i]))
        side_copies.append(
            pltpu.make_async_remote_copy(
                src_ref=part(src, 1 - q),
                dst_ref=slot(dst, q),
                send_sem=side_send.at[i],
                recv_sem=side_recv.at[i],
                device_id=(partner, mv, mp),
                device_id_type=MESH,
            )
        )
    tb_copy = pltpu.make_async_copy(tb_h, TB, tri_sem.at[0])
    tw_copy = pltpu.make_async_copy(tw_h, TW, tri_sem.at[1])

    barrier = pltpu.get_barrier_semaphore()

    def either(condition):
        return jnp.where(condition, 1, 0)

    has_v = (mv > 0, mv < VERT - 1)
    has_p = (mp > 0, mp < SPAN - 1)
    v_near = either(has_v[0]) + either(has_v[1])
    p_near = either(has_p[0]) + either(has_p[1])

    def call(sem, device):
        pl.semaphore_signal(sem, inc=1, device_id=device, device_id_type=MESH)

    def stream_at(step):
        return (lax.rem(me + 2 * step + STREAM, STREAM), mv, mp)

    def call_line(sem, along_v):
        for i, step in enumerate((-1, 1)):
            if along_v:
                pl.when(has_v[i])(lambda: call(sem, (me, mv + step, mp)))
            else:
                pl.when(has_p[i])(lambda: call(sem, (me, mv, mp + step)))

    outer_v = mv - 1 + 2 * q
    has_outer = jnp.logical_and(outer_v >= 0, outer_v < VERT)
    outer_id = (partner, lax.rem(outer_v + VERT, VERT), mp)

    nothing = jnp.zeros((2, 8, LANES), F32)
    for A in (A1, A2):
        for c in range(NC):
            A[c, 0] = nothing
            A[c, NZL + 1] = nothing
    YR[...] = jnp.zeros(YR.shape, F32)

    call(barrier, (partner, mv, mp))
    call(barrier, stream_at(-1))
    call(barrier, stream_at(1))
    for i, step in enumerate((-1, 1)):
        for core in range(2):
            other = 2 * chip + core
            pl.when(has_v[i])(lambda: call(barrier, (other, mv + step, mp)))
            pl.when(has_p[i])(lambda: call(barrier, (other, mv, mp + step)))

    stage = pltpu.make_async_copy(start_h, STG, in_sem.at[5])
    stage.start()
    for i in (1, 2, 0, 3, 4):
        own_copies[i].start()
    tb_copy.start()
    tw_copy.start()
    row = lax.broadcasted_iota(jnp.int32, (8, LANES), 0)
    lane = lax.broadcasted_iota(jnp.int32, (8, LANES), 1)

    def pack_edges(k, pair, packs):
        low, high = packs
        hit = lane == k
        low = tuple(jnp.where(hit, pltpu.roll(pair[h], k, 1), low[h]) for h in range(2))
        high = tuple(jnp.where(hit, pltpu.roll(pair[h], k + 1, 1), high[h]) for h in range(2))
        return low, high

    blank = jnp.zeros((8, LANES), F32)
    no_packs = ((blank, blank), (blank, blank))

    stage.wait()

    def pack_start(z, packs):
        low, high = packs
        for c in range(NC):
            pair = (STG[c, z, :, 0:LANES], STG[c, z, :, LANES:NYL])
            low, high = pack_edges(c * NZL + z, pair, (low, high))
        return low, high

    low, high = lax.fori_loop(0, NZL, pack_start, no_packs, unroll=4)
    for i, value in enumerate((low[0], high[1], high[0], low[1])):
        YF[i] = value
    pl.semaphore_wait(barrier, 3 + 2 * v_near + 2 * p_near)
    for i in range(3):
        side_copies[i].start()
    call(LT.at[0], stream_at(-1))
    call(LT.at[0], stream_at(1))
    call_line(LP.at[0], True)

    def send_halo(s, A, packs):
        for side in range(2):
            for h in range(2):
                YS[s, side, h] = packs[side][h]

        def remote(i, src, dst, device):
            return pltpu.make_async_remote_copy(
                src_ref=src,
                dst_ref=dst,
                send_sem=halo_send.at[s, i],
                recv_sem=halo_recv.at[s, i],
                device_id=device,
                device_id_type=MESH,
            )

        copies = (
            (
                remote(0, A.at[:, NZL], A.at[:, 0], (me, mv, lax.rem(mp + 1, SPAN))),
                mp < SPAN - 1,
                mp > 0,
            ),
            (
                remote(1, A.at[:, 1], A.at[:, NZL + 1], (me, mv, lax.rem(mp + SPAN - 1, SPAN))),
                mp > 0,
                mp < SPAN - 1,
            ),
            (remote(2, YS.at[s, q], YR.at[s, 1 - q], outer_id), has_outer, has_outer),
            (remote(3, YS.at[s, 1 - q], YR.at[s, q], (partner, mv, mp)), None, None),
        )
        each(copies, 1, lambda c: c.start())
        return copies

    def each(copies, which, act):
        for item in copies:
            if item[which] is None:
                act(item[0])
            else:
                pl.when(item[which])(functools.partial(act, item[0]))

    first_halo = []
    for i, step in enumerate((-1, 1)):
        for core in range(2):
            first_halo.append(
                (
                    pltpu.make_async_remote_copy(
                        src_ref=start_h.at[:, (0, NZL - 1)[i], :, pl.ds(core * LANES, LANES)],
                        dst_ref=A1.at[:, (NZL + 1, 0)[i], q],
                        send_sem=fz_send.at[i, core],
                        recv_sem=fz_recv.at[i, q],
                        device_id=(2 * chip + core, mv, mp + step),
                        device_id_type=MESH,
                    ),
                    has_p[i],
                )
            )
    for copy, there in first_halo:
        pl.when(there)(copy.start)

    for i, step in enumerate((-1, 1)):
        copy = pltpu.make_async_remote_copy(
            src_ref=YF.at[i],
            dst_ref=YR.at[0, 1 - i, q],
            send_sem=fv_send.at[i],
            recv_sem=fv_recv.at[q],
            device_id=(2 * chip + 1 - i, mv + step, mp),
            device_id_type=MESH,
        )
        first_halo.append((copy, has_v[i]))
        pl.when(has_v[i])(copy.start)
    middle = pltpu.make_async_remote_copy(
        src_ref=YF.at[2 + q],
        dst_ref=YR.at[0, q, q],
        send_sem=fv_send.at[2],
        recv_sem=fv_recv.at[2],
        device_id=(partner, mv, mp),
        device_id_type=MESH,
    )
    middle.start()
    YR[0, 1 - q, q] = YF[3 - q]

    def first_arrivals():
        for i in range(2):
            for sender in range(2):
                slab = A1.at[:, (0, NZL + 1)[i], sender]
                pl.when(has_p[i])(
                    lambda: pltpu.make_async_copy(slab, slab, fz_recv.at[1 - i, sender]).wait()
                )
        for sender in range(2):
            pl.when(has_outer)(
                lambda: pltpu.make_async_copy(YF.at[0], YF.at[0], fv_recv.at[sender]).wait()
            )
        middle.wait_recv()

    for i in range(3, 5):
        side_copies[i].start()

    for i in (1, 2):
        own_copies[i].wait()
        side_copies[i].wait_recv()

    pl.semaphore_wait(LT.at[0], 2)
    call(LT.at[1], stream_at(-2))
    call(LT.at[1], stream_at(2))

    def flat(ref):
        count = 1
        for size in ref.shape[:-1]:
            count *= size
        return ref.reshape(count, LANES)

    velocity2, penalty2 = flat(VEL), flat(PEN)
    ip2, m2, f2 = flat(IP), flat(M1), flat(F1)
    l2, r2, p2 = flat(LL), flat(RC), flat(PP)

    def level(ref2, x, c=0):
        return ref2[pl.ds(c * NZL * NXC + x, NZL, stride=NXC), :]

    delta = jnp.ones((NZL, LANES), F32)
    for x in range(NXC):
        u = level(velocity2, x, 0)
        west = stream_coef + stream_conv * jnp.maximum(-u, 0.0)
        east = stream_coef + stream_conv * jnp.maximum(u, 0.0)
        excess = (
            (4.0 * cross_coef + shift_coef)
            + cross_conv * (jnp.abs(level(velocity2, x, 1)) + jnp.abs(level(velocity2, x, 2)))
            + level(penalty2, x)
        )
        sink = excess + west * delta
        ip = 1.0 / (east + sink)
        delta = sink * ip
        place = pl.ds(x, NZL, stride=NXC)
        ip2[place, :] = ip
        m2[place, :] = west * ip
        f2[place, :] = east * ip

    def ahead(v, n, fill):
        return jnp.where(row >= n, pltpu.roll(v, n, 0), fill)

    def behind(v, n, fill):
        return jnp.where(row < 8 - n, pltpu.roll(v, 8 - n, 0), fill)

    def fold_up(values, f1, f2, f4, ft):
        new = []
        for h in range(2):
            v = values[h]
            v = v + f1[h] * pltpu.roll(v, 7, 0)
            v = v + f2[h] * pltpu.roll(v, 6, 0)
            v = v + f4[h] * pltpu.roll(v, 4, 0)
            new.append(v)
        new[0] = new[0] + ft * jnp.broadcast_to(new[1][0:1], (8, LANES))
        return new

    def factor(z, carry):
        chains = []
        tails = []
        f1s, f2s, f4s, fts = [], [], [], []
        for h in range(2):
            m = M1[z, h]
            f = F1[z, h]
            m1 = jnp.where(row >= 1, m, 0.0)
            mm = m1 * ahead(m, 1, 0.0)
            m4 = jnp.where(row >= 4, jnp.where(row >= 2, mm, 0.0) * pltpu.roll(mm, 2, 0), 0.0)
            mm = jnp.where(row >= 2, mm, 0.0)
            M1[z, h] = m1
            M2[z, h] = mm
            M4[z, h] = m4
            t = m * ahead(m, 1, 1.0)
            t = t * ahead(t, 2, 1.0)
            chains.append(t * ahead(t, 4, 1.0))
            f1 = jnp.where(row < 7, f, 0.0)
            ff = jnp.where(row < 6, f1 * behind(f, 1, 0.0), 0.0)
            f4 = jnp.where(row < 4, ff * pltpu.roll(ff, 6, 0), 0.0)
            F1[z, h] = f1
            F2[z, h] = ff
            F4[z, h] = f4
            f1s.append(f1)
            f2s.append(ff)
            f4s.append(f4)
            t = f * behind(f, 1, 1.0)
            t = t * behind(t, 2, 1.0)
            tails.append(t * behind(t, 4, 1.0))
        MT[z] = chains[1]
        FT[z] = tails[0]
        left = [chains[0], chains[1] * jnp.broadcast_to(chains[0][7:8], (8, LANES))]
        left = fold_up(left, f1s, f2s, f4s, tails[0])
        right = [tails[0] * jnp.broadcast_to(tails[1][0:1], (8, LANES)), tails[1]]
        for h in range(2):
            LL[z, h] = left[h]
            RC[z, h] = right[h]
        return carry

    lax.fori_loop(0, NZL, factor, 0)
    for k, ref2 in enumerate((l2, r2)):
        MS[2 * k] = level(ref2, 0)
        MS[2 * k + 1] = level(ref2, NXC - 1)

    def to_chips(src_of, dst, send_sem, recv_sem):
        for j in FAR_FIRST:
            target = lax.rem(chip + j, CHIPS)
            pltpu.make_async_remote_copy(
                src_ref=src_of(target),
                dst_ref=dst.at[chip],
                send_sem=send_sem,
                recv_sem=recv_sem,
                device_id=(2 * target + q, mv, mp),
                device_id_type=MESH,
            ).start()

    def arrive(slots, sem):
        got = slots.at[pl.ds(1, CHIPS - 1)]
        pltpu.make_async_copy(got, got, sem).wait()

    pl.semaphore_wait(LT.at[1], 2)
    call(LT.at[2], (partner, mv, mp))

    is_owner = lax.rem(chip, 4) < 3
    my_o = (chip // 4) * 3 + lax.rem(chip, 4)
    owner_sends = jnp.where(is_owner, OWNERS - 1, OWNERS)

    def to_owners(src_of, dst, send_sem, recv_sem):
        for j in FAR_FIRST:
            target = lax.rem(chip + j, CHIPS)
            o = (target // 4) * 3 + lax.rem(target, 4)

            @pl.when(lax.rem(target, 4) < 3)
            def _():
                pltpu.make_async_remote_copy(
                    src_ref=src_of(o),
                    dst_ref=dst,
                    send_sem=send_sem,
                    recv_sem=recv_sem,
                    device_id=(2 * target + q, mv, mp),
                    device_id_type=MESH,
                ).start()

        @pl.when(is_owner)
        def _():
            pltpu.make_async_copy(src_of(my_o), dst, recv_sem).start()

    for k in range(4):
        value = MS[k]
        for o in range(OWNERS):
            QS[k, o] = value[2 * o : 2 * o + 2]
    to_owners(lambda o: QS.at[:, o], QR.at[chip], q_send, q_recv)

    for i in (3,):
        own_copies[i].wait()
        side_copies[i].wait_recv()

    first = lane == 0
    last = lane == LANES - 1

    def eliminate(s, A, low, count, unroll):
        if s is not None:
            edges = [[YR[s, side, h] for h in range(2)] for side in range(2)]

        def plane(z, carry):
            cross = []
            for h in range(2):
                v = VEL[1, z, h]
                w = VEL[2, z, h]
                cross.append(
                    (
                        cross_coef + cross_conv * jnp.maximum(-v, 0.0),
                        cross_coef + cross_conv * jnp.maximum(v, 0.0),
                        cross_coef + cross_conv * jnp.maximum(-w, 0.0),
                        cross_coef + cross_conv * jnp.maximum(w, 0.0),
                    )
                )
            ip = [IP[z, h] for h in range(2)]
            m1 = [M1[z, h] for h in range(2)]
            m2 = [M2[z, h] for h in range(2)]
            m4 = [M4[z, h] for h in range(2)]
            f1 = [F1[z, h] for h in range(2)]
            f2 = [F2[z, h] for h in range(2)]
            f4 = [F4[z, h] for h in range(2)]
            mt = MT[z]
            ft = FT[z]
            for c in range(NC):
                k = c * NZL + z
                o = []
                for h in range(2):
                    south, north, below, above = cross[h]
                    a = A[c, z + 1, h]
                    lo = hi = blank
                    if s is not None:
                        lo = pltpu.roll(edges[0][h], lax.rem(LANES - k, LANES), 1)
                        hi = pltpu.roll(edges[1][h], LANES - 1 - k, 1)
                    y_lo = jnp.where(first, lo, pltpu.roll(a, 1, 1))
                    y_hi = jnp.where(last, hi, pltpu.roll(a, LANES - 1, 1))
                    rhs = SRC[c, z, h] + shift_coef * a
                    rhs = rhs + south * y_lo + north * y_hi
                    rhs = rhs + below * A[c, z, h] + above * A[c, z + 2, h]
                    v = rhs * ip[h]
                    v = v + m1[h] * pltpu.roll(v, 1, 0)
                    v = v + m2[h] * pltpu.roll(v, 2, 0)
                    v = v + m4[h] * pltpu.roll(v, 4, 0)
                    o.append(v)
                o[1] = o[1] + mt * jnp.broadcast_to(o[0][7:8], (8, LANES))
                p = fold_up(o, f1, f2, f4, ft)
                for h in range(2):
                    PP[c, z, h] = p[h]
            return carry

        lax.fori_loop(low, low + count, plane, 0, unroll=unroll)

    own_copies[0].wait()
    side_copies[0].wait_recv()
    first_arrivals()
    pl.semaphore_wait(LP.at[0], v_near)
    call_line(LP.at[1], True)
    eliminate(0, A1, 0, NZL, 12)
    for c in range(NC):
        for i, x in enumerate((0, NXC - 1)):
            value = level(p2, x, c)
            for o in range(OWNERS):
                S1[i, c, o] = value[2 * o : 2 * o + 2]
    to_owners(lambda o: S1.at[:, :, o], G1.at[chip], p_send.at[0], p_recv.at[0])
    pl.semaphore_wait(LP.at[1], v_near)
    call_line(LP.at[2], False)
    to_chips(lambda target: MS, MR, m_send, m_recv)

    own_copies[4].wait()
    side_copies[4].wait_recv()

    def indicator(digit, count):
        return jnp.concatenate(
            [jnp.where(digit == i, 1.0, 0.0) for i in range(count)], axis=0
        ).astype(jnp.bfloat16)

    def onehot(z, carry):
        for h in range(2):
            cut = slice(h * LANES, (h + 1) * LANES)
            OHL[z, :, cut] = indicator(lax.rem(BAND[z, h], 32), 32)
            OHH[z, :, cut] = indicator(BAND[z, h] // 32, 8)
        return carry

    lax.fori_loop(0, NZL, onehot, 0)

    @pl.when(is_owner)
    def _():
        pltpu.make_async_copy(QR, QR, q_recv).wait()
        ahead_f = jnp.zeros((2, LANES), F32)
        for k in range(CHIPS):
            lf, lg, rf, rg = (QR[k, i] for i in range(4))
            inv = 1.0 / (1.0 - lf * ahead_f)
            b = lg * inv
            g = b * ahead_f
            for i, value in enumerate((g, b, inv, lf * inv, rf * inv, ahead_f)):
                CO[k, i] = value
            ahead_f = rg + g * rf

        pltpu.make_async_copy(G1, G1, p_recv.at[0]).wait()
        nil = jnp.zeros((2, LANES), F32)
        O = [nil] * NC
        for k in range(CHIPS):
            for c in range(NC):
                OC[k, c] = O[c]
                O[c] = G1[k, 1, c] + CO[k, 0] * G1[k, 0, c] + CO[k, 1] * O[c]
        after = [nil] * NC
        for k in reversed(range(CHIPS)):
            for c in range(NC):
                D1[k, 1, c] = after[c]
                before = OC[k, c]
                after[c] = CO[k, 2] * G1[k, 0, c] + CO[k, 3] * before + CO[k, 4] * after[c]
                D1[k, 0, c] = CO[k, 5] * after[c] + before

        for j in FAR_FIRST:
            target = lax.rem(chip + j, CHIPS)
            pltpu.make_async_remote_copy(
                src_ref=D1.at[target],
                dst_ref=R1.at[:, :, my_o],
                send_sem=d_send,
                recv_sem=d_recv,
                device_id=(2 * target + q, mv, mp),
                device_id_type=MESH,
            ).start()

        pltpu.make_async_copy(D1.at[chip], R1.at[:, :, my_o], d_recv).start()

    arrive(MR, m_recv)

    row_z = lax.broadcasted_iota(jnp.int32, (NZL, LANES), 0)
    lane_z = lax.broadcasted_iota(jnp.int32, (NZL, LANES), 1)

    def write_edges(ref, values):
        packed = jnp.zeros((NZL, LANES), F32)
        for c in range(NC):
            v = values[c]
            for side in range(2):
                ref[2 * c + side : 2 * c + side + 1, :] = v[
                    side * (NZL - 1) : side * (NZL - 1) + 1
                ]
                column = v[:, side * (LANES - 1) : side * (LANES - 1) + 1]
                packed = jnp.where(
                    lane_z == NZL * (2 * c + side) + row_z,
                    jnp.broadcast_to(column, (NZL, LANES)),
                    packed,
                )
        ref[6:7, :] = jnp.sum(packed, axis=0, keepdims=True)
        ref[7:8, :] = jnp.zeros((1, LANES), F32)

    def upstream(k, F):
        lf, lg, rf, rg = (MR[k, i] for i in range(4))
        b = lg / (1.0 - lf * F)
        g = b * F
        CB[k] = b
        return rg + g * rf

    def downstream(i, H):
        k = CHIPS - 1 - i
        lf, lg, rf, rg = (MR[k, i] for i in range(4))
        b = rf / (1.0 - rg * H)
        g = b * H
        CB[k] = b
        return lf + g * lg

    none = jnp.zeros((NZL, LANES), F32)
    F = lax.fori_loop(0, chip, upstream, none)
    H = lax.fori_loop(0, CHIPS - 1 - chip, downstream, none)
    lf, lg, rf, rg = (MS[i] for i in range(4))
    from_left = 1.0 - lf * F
    from_right = 1.0 - rg * H
    inv = 1.0 / (from_left * from_right - (F * rf) * (H * lg))
    for i, value in enumerate(
        (
            F,
            H,
            from_right * inv,
            F * rf * inv,
            H * lg * inv,
            from_left * inv,
            lg / from_left * F,
            rf / from_right * H,
        )
    ):
        OWN[i] = value

    def close(incoming):
        for c in range(NC):
            first_p = level(p2, 0, c)
            last_p = level(p2, NXC - 1, c)
            x = OWN[0] * first_p + incoming[0][c]
            y = OWN[1] * last_p + incoming[1][c]
            AL[c] = OWN[2] * x + OWN[3] * y
            AR[c] = OWN[4] * x + OWN[5] * y

    def solved(c, z, h):
        return (
            PP[c, z, h]
            + LL[z, h] * jnp.broadcast_to(AL[c, pl.ds(z, 1), :], (8, LANES))
            + RC[z, h] * jnp.broadcast_to(AR[c, pl.ds(z, 1), :], (8, LANES))
        )

    pltpu.make_async_copy(R1, R1, d_recv).wait()
    pl.semaphore_wait(LP.at[2], p_near)
    call_line(LP.at[3], False)
    trio = (none,) * NC
    for c in range(NC):
        for o in range(OWNERS):
            AL[c, 2 * o : 2 * o + 2, :] = R1[0, c, o]
            AR[c, 2 * o : 2 * o + 2, :] = R1[1, c, o]

    def line_first(z, packs):
        for c in range(NC):
            pair = tuple(solved(c, z, h) for h in range(2))
            for h in range(2):
                A2[c, z + 1, h] = pair[h]
            packs = pack_edges(c * NZL + z, pair, packs)
        return packs

    halo2 = send_halo(1, A2, lax.fori_loop(0, NZL, line_first, no_packs, unroll=4))

    def ends(write):
        for c in range(NC):
            first_p = level(p2, 0, c)
            last_p = level(p2, NXC - 1, c)
            write(c, last_p + OWN[6] * first_p, first_p + OWN[7] * last_p)

    def write_rows(c, up, down):
        S2[0, c] = up
        S2[1, c] = down

    def side_of(target):
        return jnp.where(target > chip, 0, 1)

    eliminate(None, A2, 1, NZL - 2, 5)
    ends(write_rows)
    to_chips(lambda target: S2.at[side_of(target)], R2, p_send.at[1], p_recv.at[1])

    def edge_coefficients(k, carry):
        write_edges(CE.at[k], (CB[k],) * NC)
        return carry

    lax.fori_loop(0, chip, edge_coefficients, 0)
    lax.fori_loop(chip + 1, CHIPS, edge_coefficients, 0)

    each(halo2, 2, lambda c: c.wait_recv())
    pl.semaphore_wait(LP.at[3], p_near)
    call_line(LP.at[4], False)
    eliminate(1, A2, 0, NZL, 12)
    final = ([], [])

    def keep_ends(c, up, down):
        final[0].append(up)
        final[1].append(down)

    ends(keep_ends)
    for i in range(2):
        write_edges(E2.at[i], final[i])
    to_chips(lambda target: E2.at[side_of(target)], RE, e_send, e_recv)
    arrive(R2, p_recv.at[1])
    arrive(RE, e_recv)

    def bring(k, carry):
        O, edge = carry
        return (
            tuple(R2[k, c] + CB[k] * O[c] for c in range(NC)),
            RE[k] + CE[k] * edge,
        )

    def brought(steps, chip_of):
        O, edge = lax.fori_loop(0, steps, lambda i, v: bring(chip_of(i), v), (trio, blank))
        packed = jnp.broadcast_to(edge[6:7], (NZL, LANES))
        whole = []
        for c in range(NC):
            value = O[c]
            for side in range(2):
                at = lane_z == NZL * (2 * c + side) + row_z
                column = jnp.sum(jnp.where(at, packed, 0.0), axis=1, keepdims=True)
                value = jnp.where(
                    lane_z == side * (LANES - 1), jnp.broadcast_to(column, (NZL, LANES)), value
                )
            for side in range(2):
                value = jnp.where(
                    row_z == side * (NZL - 1),
                    jnp.broadcast_to(edge[2 * c + side : 2 * c + side + 1], (NZL, LANES)),
                    value,
                )
            whole.append(value)
        return whole

    close(
        (
            brought(chip, lambda i: i),
            brought(CHIPS - 1 - chip, lambda i: CHIPS - 1 - i),
        )
    )

    pl.semaphore_wait(LT.at[2], 1)
    pl.semaphore_wait(LP.at[4], p_near)

    def line_last(z, acc):
        parts = ([], [])
        for h in range(2):
            total = None
            for c in range(NC):
                a = solved(c, z, h)
                A3[c, z, h] = a
                term = VEL[c, z, h] * a
                total = term if total is None else total + term
            total = total * PEN[z, h]
            coarse = total.astype(jnp.bfloat16).astype(F32)
            for part, value in zip(parts, (coarse, total - coarse)):
                part.append(jnp.concatenate([value, value], axis=0).astype(jnp.bfloat16))
        weights = jnp.concatenate(
            [
                jnp.concatenate([jnp.concatenate(part, axis=1)] * 4, axis=0) * OHH[z]
                for part in parts
            ],
            axis=0,
        )
        return acc + lax.dot_general(
            weights, OHL[z], (((1,), (1,)), ((), ())), preferred_element_type=F32
        )

    acc = lax.fori_loop(0, NZL, line_last, jnp.zeros((LANES, 2 * LANES), F32), unroll=12)
    acc = acc[0:64] + acc[64:128]
    keep = lax.rem(lane, 8) == row
    for r in range(2):
        tall = blank
        for j in range(8):
            tile = acc[8 * j : 8 * j + 8, r * LANES : (r + 1) * LANES]
            line = jnp.sum(jnp.where(keep, tile, 0.0), axis=0, keepdims=True)
            tall = jnp.where(row == j, jnp.broadcast_to(line, (8, LANES)), tall)
        for d in (1, 2, 4):
            tall = tall + jnp.where(
                lax.rem(lane // d, 2) == 0, pltpu.roll(tall, LANES - d, 1), pltpu.roll(tall, d, 1)
            )
        B1S[r : r + 1, :] = jnp.sum(jnp.where(keep, tall, 0.0), axis=0, keepdims=True)

    def band_round(r, own, slots, order, device_of, beside):
        for j in order:
            pltpu.make_async_remote_copy(
                src_ref=own,
                dst_ref=slots.at[j],
                send_sem=b_send.at[r],
                recv_sem=b_recv.at[r],
                device_id=device_of(j),
                device_id_type=MESH,
            ).start()
        beside()
        got = slots.at[pl.ds(1, STREAM - 1)]
        pltpu.make_async_copy(got, got, b_recv.at[r]).wait()
        total = own[...]
        for j in range(1, STREAM):
            total = total + slots[j]
        return total

    def drain(count, ref, sem):
        def one(j, carry):
            pltpu.make_async_copy(ref, ref, sem).wait()
            return carry

        lax.fori_loop(0, count, one, 0)

    def sent(bytes_like, sem):
        pltpu.make_async_copy(bytes_like, bytes_like, sem).wait()

    out_own = pltpu.make_async_copy(A3.at[:, :, q], out_h.at[:, :, :, lanes_of(q)], out_sem.at[0])
    out_side = pltpu.make_async_remote_copy(
        src_ref=A3.at[:, :, 1 - q],
        dst_ref=out_h.at[:, :, :, lanes_of(q)],
        send_sem=out_sem.at[1],
        recv_sem=out_sem.at[2],
        device_id=(partner, mv, mp),
        device_id_type=MESH,
    )

    def beside_first():
        out_own.start()
        out_side.start()
        for copy in side_copies:
            copy.wait_send()
        for copy, there in first_halo:
            pl.when(there)(copy.wait_send)
        middle.wait_send()
        each(halo2, 1, lambda c: c.wait_send())
        others = pl.ds(1, CHIPS - 1)
        sent(MR.at[others], m_send)
        sent(R2.at[others], p_send.at[1])
        sent(RE.at[others], e_send)
        drain(owner_sends, QS.at[:, 0], q_send)
        drain(owner_sends, S1.at[:, :, 0], p_send.at[0])

        @pl.when(is_owner)
        def _():
            sent(D1.at[others], d_send)

        tb_copy.wait()
        tw_copy.wait()

    def beside_second():
        sent(B1R.at[pl.ds(1, STREAM - 1)], b_send.at[0])
        out_own.wait()
        out_side.wait()

    line_order = (8, 7, 9, 6, 10, 5, 11, 4, 12, 3, 13, 2, 14, 1, 15)
    plane_order = (10, 6, 9, 11, 14, 2, 8, 5, 7, 13, 15, 1, 3, 4, 12)
    B2S[...] = band_round(
        0, B1S, B1R, line_order, lambda j: (lax.rem(me + j, STREAM), mv, mp), beside_first
    )
    bands = band_round(
        1,
        B2S,
        B2R,
        plane_order,
        lambda j: (me, lax.rem(mv + j // SPAN, VERT), lax.rem(mp + j % SPAN, SPAN)),
        beside_second,
    )
    cells = STREAM * VERT * SPAN * NXL * NZL * NYL
    bands = bands * ((NBANDS / cells) ** 0.5)
    tb = TB[...].reshape(1, LANES)
    spot = lax.rem(tb, 16) * 8 + tb // 32
    spot = jnp.broadcast_to(spot, (8, LANES))
    low_half = jnp.take_along_axis(jnp.broadcast_to(bands[0:1], (8, LANES)), spot, axis=1)
    high_half = jnp.take_along_axis(jnp.broadcast_to(bands[1:2], (8, LANES)), spot, axis=1)
    picked = jnp.where(lax.rem(tb, 32) < 16, low_half[0:1], high_half[0:1])
    tri_ref[...] = (TW[...].reshape(1, LANES) * picked).reshape(LANES)
    sent(B2R.at[pl.ds(1, STREAM - 1)], b_send.at[1])


def shards(adjoint_source, velocity, penalty, adjoint_start, cell_band, tri_band, tri_weight):
    anywhere = pl.BlockSpec(memory_space=pl.ANY)

    def field():
        return pltpu.VMEM((NZL, 2, 8, LANES), F32)

    scratch = [
        pltpu.VMEM((NC, NZL, 2, 8, LANES), F32),
        pltpu.VMEM((NC, NZL, 2, 8, LANES), F32),
        field(),
        pltpu.VMEM((NZL, 2, 8, LANES), jnp.int32),
        pltpu.VMEM((NC, NZL + 2, 2, 8, LANES), F32),
        pltpu.VMEM((NC, NZL + 2, 2, 8, LANES), F32),
        pltpu.VMEM((NC, NZL, 2, 8, LANES), F32),
        pltpu.VMEM((NC, NZL, 2, 8, LANES), F32),
        field(),
        field(),
        field(),
        field(),
        pltpu.VMEM((NZL, 8, LANES), F32),
        field(),
        field(),
        field(),
        pltpu.VMEM((NZL, 8, LANES), F32),
        field(),
        field(),
        pltpu.VMEM((NC, NZL, NXL, NYL), F32),
        pltpu.VMEM((4, 8, LANES), F32),
        pltpu.VMEM((SWEEPS, 2, 2, 8, LANES), F32),
        pltpu.VMEM((SWEEPS, 2, 2, 8, LANES), F32),
        pltpu.VMEM((4, NZL, LANES), F32),
        pltpu.VMEM((CHIPS, 4, NZL, LANES), F32),
        pltpu.VMEM((CHIPS, NZL, LANES), F32),
        pltpu.VMEM((CHIPS, 8, LANES), F32),
        pltpu.VMEM((8, NZL, LANES), F32),
        pltpu.VMEM((4, OWNERS, 2, LANES), F32),
        pltpu.VMEM((CHIPS, 4, 2, LANES), F32),
        pltpu.VMEM((CHIPS, 6, 2, LANES), F32),
        pltpu.VMEM((CHIPS, NC, 2, LANES), F32),
        pltpu.VMEM((2, NC, OWNERS, 2, LANES), F32),
        pltpu.VMEM((CHIPS, 2, NC, 2, LANES), F32),
        pltpu.VMEM((CHIPS, 2, NC, 2, LANES), F32),
        pltpu.VMEM((2, NC, OWNERS, 2, LANES), F32),
        pltpu.VMEM((2, NC, NZL, LANES), F32),
        pltpu.VMEM((CHIPS, NC, NZL, LANES), F32),
        pltpu.VMEM((2, 8, LANES), F32),
        pltpu.VMEM((CHIPS, 8, LANES), F32),
        pltpu.VMEM((NC, NZL, LANES), F32),
        pltpu.VMEM((NC, NZL, LANES), F32),
        pltpu.VMEM((NZL, 64, 2 * LANES), jnp.bfloat16),
        pltpu.VMEM((NZL, 2 * LANES, 2 * LANES), jnp.bfloat16),
        pltpu.VMEM((2, LANES), F32),
        pltpu.VMEM((STREAM, 2, LANES), F32),
        pltpu.VMEM((2, LANES), F32),
        pltpu.VMEM((STREAM, 2, LANES), F32),
        pltpu.VMEM((LANES,), jnp.int32),
        pltpu.VMEM((LANES,), F32),
        pltpu.SemaphoreType.DMA((6,)),
        pltpu.SemaphoreType.DMA((5,)),
        pltpu.SemaphoreType.DMA((5,)),
        pltpu.SemaphoreType.DMA((3,)),
        pltpu.SemaphoreType.DMA((2,)),
        pltpu.SemaphoreType.REGULAR((3,)),
        pltpu.SemaphoreType.REGULAR((5,)),
        pltpu.SemaphoreType.DMA((2, 2)),
        pltpu.SemaphoreType.DMA((2, 2)),
        pltpu.SemaphoreType.DMA((3,)),
        pltpu.SemaphoreType.DMA((3,)),
        pltpu.SemaphoreType.DMA((SWEEPS, 4)),
        pltpu.SemaphoreType.DMA((SWEEPS, 4)),
        pltpu.SemaphoreType.DMA,
        pltpu.SemaphoreType.DMA,
        pltpu.SemaphoreType.DMA,
        pltpu.SemaphoreType.DMA,
        pltpu.SemaphoreType.DMA,
        pltpu.SemaphoreType.DMA,
        pltpu.SemaphoreType.DMA((SWEEPS,)),
        pltpu.SemaphoreType.DMA((SWEEPS,)),
        pltpu.SemaphoreType.DMA,
        pltpu.SemaphoreType.DMA,
        pltpu.SemaphoreType.DMA((2,)),
        pltpu.SemaphoreType.DMA((2,)),
    ]

    def planes(x):
        return jnp.swapaxes(x, -3, -2)

    adjoint, tri_grad = pl.pallas_call(
        kernel,
        out_shape=(
            jax.ShapeDtypeStruct((NC, NZL, NXL, NYL), F32),
            jax.ShapeDtypeStruct((LANES,), F32),
        ),
        in_specs=[pl.BlockSpec(memory_space=pltpu.HBM)] * 7,
        out_specs=(anywhere, pl.BlockSpec(memory_space=pltpu.VMEM)),
        scratch_shapes=scratch,
        compiler_params=pltpu.CompilerParams(
            collective_id=0, has_side_effects=True, vmem_limit_bytes=32 * 1024 * 1024
        ),
    )(
        *(
            pltpu.with_memory_space_constraint(x, pltpu.HBM)
            for x in (
                planes(adjoint_source),
                planes(velocity),
                planes(penalty),
                planes(adjoint_start),
                planes(cell_band),
                tri_band,
                tri_weight,
            )
        )
    )
    return planes(adjoint), tri_grad


def solution(mesh):
    return jax.shard_map(
        shards,
        mesh=mesh,
        in_specs=(
            P(None, "stream", "span", "vert"),
            P(None, "stream", "span", "vert"),
            P("stream", "span", "vert"),
            P(None, "stream", "span", "vert"),
            P("stream", "span", "vert"),
            P(("stream", "vert", "span")),
            P(("stream", "vert", "span")),
        ),
        out_specs=(P(None, "stream", "span", "vert"), P(("stream", "vert", "span"))),
        check_vma=False,
    )
```

```python
import functools

import jax
import jax.numpy as jnp
from jax import lax
from jax.experimental import pallas as pl
from jax.experimental.pallas import tpu as pltpu
from jax.sharding import PartitionSpec as P

SWEEPS = 2
NBANDS = 256

STREAM = 16
CHIPS = 8
VERT = 4
SPAN = 4
NC = 3
NXL = 8
NXC = 16
NZL = 12
NYL = 256
LANES = 128
OWNERS = 6
ROWS = NZL // OWNERS
FIRST = 2
FAR_FIRST = (4, 3, 5, 2, 6, 1, 7)

stream_coef = 1000.0
stream_conv = 200.0
cross_coef = 0.25
cross_conv = 0.25
shift_coef = 0.5

MESH = pl.DeviceIdType.MESH
F32 = jnp.float32


def kernel(
    src_h,
    vel_h,
    pen_h,
    start_h,
    band_h,
    tb_h,
    tw_h,
    out_h,
    tri_ref,
    SRC,
    VEL,
    PEN,
    BAND,
    A1,
    A2,
    A3,
    PP,
    IP,
    M1,
    M2,
    M4,
    MT,
    F1,
    F2,
    F4,
    FT,
    LL,
    RC,
    STG,
    YF,
    YS,
    YR,
    MS,
    MR,
    CB,
    CE,
    OWN,
    QS,
    QR,
    CO,
    OC,
    S1,
    G1,
    D1,
    R1,
    S2,
    R2,
    E2,
    RE,
    AL,
    AR,
    OHH,
    OHL,
    B1S,
    B1R,
    B2S,
    B2R,
    TB,
    TW,
    in_sem,
    side_send,
    side_recv,
    out_sem,
    tri_sem,
    LT,
    LP,
    fz_send,
    fz_recv,
    fv_send,
    fv_recv,
    halo_send,
    halo_recv,
    m_send,
    m_recv,
    q_send,
    q_recv,
    d_send,
    d_recv,
    p_send,
    p_recv,
    e_send,
    e_recv,
    b_send,
    b_recv,
):
    me = lax.axis_index("stream")
    mv = lax.axis_index("vert")
    mp = lax.axis_index("span")
    chip = me // 2
    q = lax.rem(me, 2)
    partner = 2 * chip + (1 - q)

    def lanes_of(half):
        return pl.ds(pl.multiple_of(half * LANES, LANES), LANES)

    def pieces(ref, dst):
        rank = len(ref.shape)
        lead = (slice(None),) * (rank - 1)
        return lambda half: ref.at[lead + (lanes_of(half),)], dst

    inner = A1.at[:, pl.ds(1, NZL)]
    inputs = (
        (start_h, inner),
        (vel_h, VEL),
        (pen_h, PEN),
        (src_h, SRC),
        (band_h, BAND),
    )

    def slot(dst, half):
        if len(dst.shape) == 5:
            return dst.at[:, :, half]
        return dst.at[:, half]

    def part(src, half):
        if len(src.shape) == 4:
            return src.at[:, :, :, lanes_of(half)]
        return src.at[:, :, lanes_of(half)]

    own_copies = []
    side_copies = []
    for i, (src, dst) in enumerate(inputs):
        own_copies.append(pltpu.make_async_copy(part(src, q), slot(dst, q), in_sem.at[i]))
        side_copies.append(
            pltpu.make_async_remote_copy(
                src_ref=part(src, 1 - q),
                dst_ref=slot(dst, q),
                send_sem=side_send.at[i],
                recv_sem=side_recv.at[i],
                device_id=(partner, mv, mp),
                device_id_type=MESH,
            )
        )
    tb_copy = pltpu.make_async_copy(tb_h, TB, tri_sem.at[0])
    tw_copy = pltpu.make_async_copy(tw_h, TW, tri_sem.at[1])

    barrier = pltpu.get_barrier_semaphore()

    def either(condition):
        return jnp.where(condition, 1, 0)

    has_v = (mv > 0, mv < VERT - 1)
    has_p = (mp > 0, mp < SPAN - 1)
    v_near = either(has_v[0]) + either(has_v[1])
    p_near = either(has_p[0]) + either(has_p[1])

    def call(sem, device):
        pl.semaphore_signal(sem, inc=1, device_id=device, device_id_type=MESH)

    def stream_at(step):
        return (lax.rem(me + 2 * step + STREAM, STREAM), mv, mp)

    def call_line(sem, along_v):
        for i, step in enumerate((-1, 1)):
            if along_v:
                pl.when(has_v[i])(lambda: call(sem, (me, mv + step, mp)))
            else:
                pl.when(has_p[i])(lambda: call(sem, (me, mv, mp + step)))

    outer_v = mv - 1 + 2 * q
    has_outer = jnp.logical_and(outer_v >= 0, outer_v < VERT)
    outer_id = (partner, lax.rem(outer_v + VERT, VERT), mp)

    nothing = jnp.zeros((2, 8, LANES), F32)
    for A in (A1, A2):
        for c in range(NC):
            A[c, 0] = nothing
            A[c, NZL + 1] = nothing
    YR[...] = jnp.zeros(YR.shape, F32)

    call(barrier, (partner, mv, mp))
    call(barrier, stream_at(-1))
    call(barrier, stream_at(1))
    for i, step in enumerate((-1, 1)):
        for core in range(2):
            other = 2 * chip + core
            pl.when(has_v[i])(lambda: call(barrier, (other, mv + step, mp)))
            pl.when(has_p[i])(lambda: call(barrier, (other, mv, mp + step)))

    stage = pltpu.make_async_copy(start_h, STG, in_sem.at[5])
    stage.start()
    for i in (1, 2, 0, 3, 4):
        own_copies[i].start()
    tb_copy.start()
    tw_copy.start()
    row = lax.broadcasted_iota(jnp.int32, (8, LANES), 0)
    lane = lax.broadcasted_iota(jnp.int32, (8, LANES), 1)

    def pack_edges(k, pair, packs):
        low, high = packs
        hit = lane == k
        low = tuple(jnp.where(hit, pltpu.roll(pair[h], k, 1), low[h]) for h in range(2))
        high = tuple(jnp.where(hit, pltpu.roll(pair[h], k + 1, 1), high[h]) for h in range(2))
        return low, high

    blank = jnp.zeros((8, LANES), F32)
    no_packs = ((blank, blank), (blank, blank))

    stage.wait()

    def pack_start(z, packs):
        low, high = packs
        for c in range(NC):
            pair = (STG[c, z, :, 0:LANES], STG[c, z, :, LANES:NYL])
            low, high = pack_edges(c * NZL + z, pair, (low, high))
        return low, high

    low, high = lax.fori_loop(0, NZL, pack_start, no_packs, unroll=4)
    for i, value in enumerate((low[0], high[1], high[0], low[1])):
        YF[i] = value
    pl.semaphore_wait(barrier, 3 + 2 * v_near + 2 * p_near)
    for i in range(3):
        side_copies[i].start()
    call(LT.at[0], stream_at(-1))
    call(LT.at[0], stream_at(1))
    call_line(LP.at[0], True)

    def send_halo(s, A, packs):
        for side in range(2):
            for h in range(2):
                YS[s, side, h] = packs[side][h]

        def remote(i, src, dst, device):
            return pltpu.make_async_remote_copy(
                src_ref=src,
                dst_ref=dst,
                send_sem=halo_send.at[s, i],
                recv_sem=halo_recv.at[s, i],
                device_id=device,
                device_id_type=MESH,
            )

        copies = (
            (
                remote(0, A.at[:, NZL], A.at[:, 0], (me, mv, lax.rem(mp + 1, SPAN))),
                mp < SPAN - 1,
                mp > 0,
            ),
            (
                remote(1, A.at[:, 1], A.at[:, NZL + 1], (me, mv, lax.rem(mp + SPAN - 1, SPAN))),
                mp > 0,
                mp < SPAN - 1,
            ),
            (remote(2, YS.at[s, q], YR.at[s, 1 - q], outer_id), has_outer, has_outer),
            (remote(3, YS.at[s, 1 - q], YR.at[s, q], (partner, mv, mp)), None, None),
        )
        each(copies, 1, lambda c: c.start())
        return copies

    def each(copies, which, act):
        for item in copies:
            if item[which] is None:
                act(item[0])
            else:
                pl.when(item[which])(functools.partial(act, item[0]))

    first_halo = []
    for i, step in enumerate((-1, 1)):
        for core in range(2):
            first_halo.append(
                (
                    pltpu.make_async_remote_copy(
                        src_ref=start_h.at[:, (0, NZL - 1)[i], :, pl.ds(core * LANES, LANES)],
                        dst_ref=A1.at[:, (NZL + 1, 0)[i], q],
                        send_sem=fz_send.at[i, core],
                        recv_sem=fz_recv.at[i, q],
                        device_id=(2 * chip + core, mv, mp + step),
                        device_id_type=MESH,
                    ),
                    has_p[i],
                )
            )
    for copy, there in first_halo:
        pl.when(there)(copy.start)

    for i, step in enumerate((-1, 1)):
        copy = pltpu.make_async_remote_copy(
            src_ref=YF.at[i],
            dst_ref=YR.at[0, 1 - i, q],
            send_sem=fv_send.at[i],
            recv_sem=fv_recv.at[q],
            device_id=(2 * chip + 1 - i, mv + step, mp),
            device_id_type=MESH,
        )
        first_halo.append((copy, has_v[i]))
        pl.when(has_v[i])(copy.start)
    middle = pltpu.make_async_remote_copy(
        src_ref=YF.at[2 + q],
        dst_ref=YR.at[0, q, q],
        send_sem=fv_send.at[2],
        recv_sem=fv_recv.at[2],
        device_id=(partner, mv, mp),
        device_id_type=MESH,
    )
    middle.start()
    YR[0, 1 - q, q] = YF[3 - q]

    def first_arrivals():
        for i in range(2):
            for sender in range(2):
                slab = A1.at[:, (0, NZL + 1)[i], sender]
                pl.when(has_p[i])(
                    lambda: pltpu.make_async_copy(slab, slab, fz_recv.at[1 - i, sender]).wait()
                )
        for sender in range(2):
            pl.when(has_outer)(
                lambda: pltpu.make_async_copy(YF.at[0], YF.at[0], fv_recv.at[sender]).wait()
            )
        middle.wait_recv()

    for i in range(3, 5):
        side_copies[i].start()

    for i in (1, 2):
        own_copies[i].wait()
        side_copies[i].wait_recv()

    pl.semaphore_wait(LT.at[0], 2)
    call(LT.at[1], stream_at(-2))
    call(LT.at[1], stream_at(2))

    def flat(ref):
        count = 1
        for size in ref.shape[:-1]:
            count *= size
        return ref.reshape(count, LANES)

    velocity2, penalty2 = flat(VEL), flat(PEN)
    ip2, m2, f2 = flat(IP), flat(M1), flat(F1)
    l2, r2, p2 = flat(LL), flat(RC), flat(PP)

    def level(ref2, x, c=0):
        return ref2[pl.ds(c * NZL * NXC + x, NZL, stride=NXC), :]

    delta = jnp.ones((NZL, LANES), F32)
    for x in range(NXC):
        u = level(velocity2, x, 0)
        west = stream_coef + stream_conv * jnp.maximum(-u, 0.0)
        east = stream_coef + stream_conv * jnp.maximum(u, 0.0)
        excess = (
            (4.0 * cross_coef + shift_coef)
            + cross_conv * (jnp.abs(level(velocity2, x, 1)) + jnp.abs(level(velocity2, x, 2)))
            + level(penalty2, x)
        )
        sink = excess + west * delta
        ip = 1.0 / (east + sink)
        delta = sink * ip
        place = pl.ds(x, NZL, stride=NXC)
        ip2[place, :] = ip
        m2[place, :] = west * ip
        f2[place, :] = east * ip

    def ahead(v, n, fill):
        return jnp.where(row >= n, pltpu.roll(v, n, 0), fill)

    def behind(v, n, fill):
        return jnp.where(row < 8 - n, pltpu.roll(v, 8 - n, 0), fill)

    def fold_up(values, f1, f2, f4, ft):
        new = []
        for h in range(2):
            v = values[h]
            v = v + f1[h] * pltpu.roll(v, 7, 0)
            v = v + f2[h] * pltpu.roll(v, 6, 0)
            v = v + f4[h] * pltpu.roll(v, 4, 0)
            new.append(v)
        new[0] = new[0] + ft * jnp.broadcast_to(new[1][0:1], (8, LANES))
        return new

    def factor(z, carry):
        chains = []
        tails = []
        f1s, f2s, f4s, fts = [], [], [], []
        for h in range(2):
            m = M1[z, h]
            f = F1[z, h]
            m1 = jnp.where(row >= 1, m, 0.0)
            mm = m1 * ahead(m, 1, 0.0)
            m4 = jnp.where(row >= 4, jnp.where(row >= 2, mm, 0.0) * pltpu.roll(mm, 2, 0), 0.0)
            mm = jnp.where(row >= 2, mm, 0.0)
            M1[z, h] = m1
            M2[z, h] = mm
            M4[z, h] = m4
            t = m * ahead(m, 1, 1.0)
            t = t * ahead(t, 2, 1.0)
            chains.append(t * ahead(t, 4, 1.0))
            f1 = jnp.where(row < 7, f, 0.0)
            ff = jnp.where(row < 6, f1 * behind(f, 1, 0.0), 0.0)
            f4 = jnp.where(row < 4, ff * pltpu.roll(ff, 6, 0), 0.0)
            F1[z, h] = f1
            F2[z, h] = ff
            F4[z, h] = f4
            f1s.append(f1)
            f2s.append(ff)
            f4s.append(f4)
            t = f * behind(f, 1, 1.0)
            t = t * behind(t, 2, 1.0)
            tails.append(t * behind(t, 4, 1.0))
        MT[z] = chains[1]
        FT[z] = tails[0]
        left = [chains[0], chains[1] * jnp.broadcast_to(chains[0][7:8], (8, LANES))]
        left = fold_up(left, f1s, f2s, f4s, tails[0])
        right = [tails[0] * jnp.broadcast_to(tails[1][0:1], (8, LANES)), tails[1]]
        for h in range(2):
            LL[z, h] = left[h]
            RC[z, h] = right[h]
        return carry

    lax.fori_loop(0, NZL, factor, 0)
    for k, ref2 in enumerate((l2, r2)):
        MS[2 * k] = level(ref2, 0)
        MS[2 * k + 1] = level(ref2, NXC - 1)

    def to_chips(src_of, dst, send_sem, recv_sem):
        for j in FAR_FIRST:
            target = lax.rem(chip + j, CHIPS)
            pltpu.make_async_remote_copy(
                src_ref=src_of(target),
                dst_ref=dst.at[chip],
                send_sem=send_sem,
                recv_sem=recv_sem,
                device_id=(2 * target + q, mv, mp),
                device_id_type=MESH,
            ).start()

    def arrive(slots, sem):
        got = slots.at[pl.ds(1, CHIPS - 1)]
        pltpu.make_async_copy(got, got, sem).wait()

    pl.semaphore_wait(LT.at[1], 2)
    call(LT.at[2], (partner, mv, mp))

    my_o = lax.rem(chip + FIRST, CHIPS)
    is_owner = my_o < OWNERS
    owner_sends = jnp.where(is_owner, OWNERS - 1, OWNERS)

    def to_owners(src_of, dst, send_sem, recv_sem):
        for j in FAR_FIRST:
            target = lax.rem(chip + j, CHIPS)
            o = lax.rem(target + FIRST, CHIPS)

            @pl.when(o < OWNERS)
            def _():
                pltpu.make_async_remote_copy(
                    src_ref=src_of(o),
                    dst_ref=dst,
                    send_sem=send_sem,
                    recv_sem=recv_sem,
                    device_id=(2 * target + q, mv, mp),
                    device_id_type=MESH,
                ).start()

        @pl.when(is_owner)
        def _():
            pltpu.make_async_copy(src_of(my_o), dst, recv_sem).start()

    for k in range(4):
        value = MS[k]
        for o in range(OWNERS):
            QS[k, o] = value[ROWS * o : ROWS * o + ROWS]
    to_owners(lambda o: QS.at[:, o], QR.at[chip], q_send, q_recv)

    for i in (3,):
        own_copies[i].wait()
        side_copies[i].wait_recv()

    first = lane == 0
    last = lane == LANES - 1

    def eliminate(s, A, low, count, unroll):
        if s is not None:
            edges = [[YR[s, side, h] for h in range(2)] for side in range(2)]

        def plane(z, carry):
            cross = []
            for h in range(2):
                v = VEL[1, z, h]
                w = VEL[2, z, h]
                cross.append(
                    (
                        cross_coef + cross_conv * jnp.maximum(-v, 0.0),
                        cross_coef + cross_conv * jnp.maximum(v, 0.0),
                        cross_coef + cross_conv * jnp.maximum(-w, 0.0),
                        cross_coef + cross_conv * jnp.maximum(w, 0.0),
                    )
                )
            ip = [IP[z, h] for h in range(2)]
            m1 = [M1[z, h] for h in range(2)]
            m2 = [M2[z, h] for h in range(2)]
            m4 = [M4[z, h] for h in range(2)]
            f1 = [F1[z, h] for h in range(2)]
            f2 = [F2[z, h] for h in range(2)]
            f4 = [F4[z, h] for h in range(2)]
            mt = MT[z]
            ft = FT[z]
            for c in range(NC):
                k = c * NZL + z
                o = []
                for h in range(2):
                    south, north, below, above = cross[h]
                    a = A[c, z + 1, h]
                    lo = hi = blank
                    if s is not None:
                        lo = pltpu.roll(edges[0][h], lax.rem(LANES - k, LANES), 1)
                        hi = pltpu.roll(edges[1][h], LANES - 1 - k, 1)
                    y_lo = jnp.where(first, lo, pltpu.roll(a, 1, 1))
                    y_hi = jnp.where(last, hi, pltpu.roll(a, LANES - 1, 1))
                    rhs = SRC[c, z, h] + shift_coef * a
                    rhs = rhs + south * y_lo + north * y_hi
                    rhs = rhs + below * A[c, z, h] + above * A[c, z + 2, h]
                    v = rhs * ip[h]
                    v = v + m1[h] * pltpu.roll(v, 1, 0)
                    v = v + m2[h] * pltpu.roll(v, 2, 0)
                    v = v + m4[h] * pltpu.roll(v, 4, 0)
                    o.append(v)
                o[1] = o[1] + mt * jnp.broadcast_to(o[0][7:8], (8, LANES))
                p = fold_up(o, f1, f2, f4, ft)
                for h in range(2):
                    PP[c, z, h] = p[h]
            return carry

        lax.fori_loop(low, low + count, plane, 0, unroll=unroll)

    own_copies[0].wait()
    side_copies[0].wait_recv()
    first_arrivals()
    pl.semaphore_wait(LP.at[0], v_near)
    call_line(LP.at[1], True)
    eliminate(0, A1, 0, NZL, 12)
    for c in range(NC):
        for i, x in enumerate((0, NXC - 1)):
            value = level(p2, x, c)
            for o in range(OWNERS):
                S1[i, c, o] = value[ROWS * o : ROWS * o + ROWS]
    to_owners(lambda o: S1.at[:, :, o], G1.at[chip], p_send.at[0], p_recv.at[0])
    pl.semaphore_wait(LP.at[1], v_near)
    call_line(LP.at[2], False)
    to_chips(lambda target: MS, MR, m_send, m_recv)

    own_copies[4].wait()
    side_copies[4].wait_recv()

    def indicator(digit, count):
        return jnp.concatenate(
            [jnp.where(digit == i, 1.0, 0.0) for i in range(count)], axis=0
        ).astype(jnp.bfloat16)

    def onehot(z, carry):
        for h in range(2):
            cut = slice(h * LANES, (h + 1) * LANES)
            OHL[z, :, cut] = indicator(lax.rem(BAND[z, h], 32), 32)
            OHH[z, :, cut] = indicator(BAND[z, h] // 32, 8)
        return carry

    lax.fori_loop(0, NZL, onehot, 0)

    @pl.when(is_owner)
    def _():
        pltpu.make_async_copy(QR, QR, q_recv).wait()
        ahead_f = jnp.zeros((ROWS, LANES), F32)
        for k in range(CHIPS):
            lf, lg, rf, rg = (QR[k, i] for i in range(4))
            inv = 1.0 / (1.0 - lf * ahead_f)
            b = lg * inv
            g = b * ahead_f
            for i, value in enumerate((g, b, inv, lf * inv, rf * inv, ahead_f)):
                CO[k, i] = value
            ahead_f = rg + g * rf

        pltpu.make_async_copy(G1, G1, p_recv.at[0]).wait()
        nil = jnp.zeros((ROWS, LANES), F32)
        O = [nil] * NC
        for k in range(CHIPS):
            for c in range(NC):
                OC[k, c] = O[c]
                O[c] = G1[k, 1, c] + CO[k, 0] * G1[k, 0, c] + CO[k, 1] * O[c]
        after = [nil] * NC
        for k in reversed(range(CHIPS)):
            for c in range(NC):
                D1[k, 1, c] = after[c]
                before = OC[k, c]
                after[c] = CO[k, 2] * G1[k, 0, c] + CO[k, 3] * before + CO[k, 4] * after[c]
                D1[k, 0, c] = CO[k, 5] * after[c] + before

        for j in FAR_FIRST:
            target = lax.rem(chip + j, CHIPS)
            pltpu.make_async_remote_copy(
                src_ref=D1.at[target],
                dst_ref=R1.at[:, :, my_o],
                send_sem=d_send,
                recv_sem=d_recv,
                device_id=(2 * target + q, mv, mp),
                device_id_type=MESH,
            ).start()

        pltpu.make_async_copy(D1.at[chip], R1.at[:, :, my_o], d_recv).start()

    arrive(MR, m_recv)

    row_z = lax.broadcasted_iota(jnp.int32, (NZL, LANES), 0)
    lane_z = lax.broadcasted_iota(jnp.int32, (NZL, LANES), 1)

    def write_edges(ref, values):
        packed = jnp.zeros((NZL, LANES), F32)
        for c in range(NC):
            v = values[c]
            for side in range(2):
                ref[2 * c + side : 2 * c + side + 1, :] = v[
                    side * (NZL - 1) : side * (NZL - 1) + 1
                ]
                column = v[:, side * (LANES - 1) : side * (LANES - 1) + 1]
                packed = jnp.where(
                    lane_z == NZL * (2 * c + side) + row_z,
                    jnp.broadcast_to(column, (NZL, LANES)),
                    packed,
                )
        ref[6:7, :] = jnp.sum(packed, axis=0, keepdims=True)
        ref[7:8, :] = jnp.zeros((1, LANES), F32)

    def upstream(k, F):
        lf, lg, rf, rg = (MR[k, i] for i in range(4))
        b = lg / (1.0 - lf * F)
        g = b * F
        CB[k] = b
        return rg + g * rf

    def downstream(i, H):
        k = CHIPS - 1 - i
        lf, lg, rf, rg = (MR[k, i] for i in range(4))
        b = rf / (1.0 - rg * H)
        g = b * H
        CB[k] = b
        return lf + g * lg

    none = jnp.zeros((NZL, LANES), F32)
    F = lax.fori_loop(0, chip, upstream, none)
    H = lax.fori_loop(0, CHIPS - 1 - chip, downstream, none)
    lf, lg, rf, rg = (MS[i] for i in range(4))
    from_left = 1.0 - lf * F
    from_right = 1.0 - rg * H
    inv = 1.0 / (from_left * from_right - (F * rf) * (H * lg))
    for i, value in enumerate(
        (
            F,
            H,
            from_right * inv,
            F * rf * inv,
            H * lg * inv,
            from_left * inv,
            lg / from_left * F,
            rf / from_right * H,
        )
    ):
        OWN[i] = value

    def close(incoming):
        for c in range(NC):
            first_p = level(p2, 0, c)
            last_p = level(p2, NXC - 1, c)
            x = OWN[0] * first_p + incoming[0][c]
            y = OWN[1] * last_p + incoming[1][c]
            AL[c] = OWN[2] * x + OWN[3] * y
            AR[c] = OWN[4] * x + OWN[5] * y

    def solved(c, z, h):
        return (
            PP[c, z, h]
            + LL[z, h] * jnp.broadcast_to(AL[c, pl.ds(z, 1), :], (8, LANES))
            + RC[z, h] * jnp.broadcast_to(AR[c, pl.ds(z, 1), :], (8, LANES))
        )

    pltpu.make_async_copy(R1, R1, d_recv).wait()
    pl.semaphore_wait(LP.at[2], p_near)
    call_line(LP.at[3], False)
    trio = (none,) * NC
    for c in range(NC):
        for o in range(OWNERS):
            AL[c, ROWS * o : ROWS * o + ROWS, :] = R1[0, c, o]
            AR[c, ROWS * o : ROWS * o + ROWS, :] = R1[1, c, o]

    def line_first(z, packs):
        for c in range(NC):
            pair = tuple(solved(c, z, h) for h in range(2))
            for h in range(2):
                A2[c, z + 1, h] = pair[h]
            packs = pack_edges(c * NZL + z, pair, packs)
        return packs

    halo2 = send_halo(1, A2, lax.fori_loop(0, NZL, line_first, no_packs, unroll=4))

    def ends(write):
        for c in range(NC):
            first_p = level(p2, 0, c)
            last_p = level(p2, NXC - 1, c)
            write(c, last_p + OWN[6] * first_p, first_p + OWN[7] * last_p)

    def write_rows(c, up, down):
        S2[0, c] = up
        S2[1, c] = down

    def side_of(target):
        return jnp.where(target > chip, 0, 1)

    eliminate(None, A2, 1, NZL - 2, 5)
    ends(write_rows)
    to_chips(lambda target: S2.at[side_of(target)], R2, p_send.at[1], p_recv.at[1])

    def edge_coefficients(k, carry):
        write_edges(CE.at[k], (CB[k],) * NC)
        return carry

    lax.fori_loop(0, chip, edge_coefficients, 0)
    lax.fori_loop(chip + 1, CHIPS, edge_coefficients, 0)

    each(halo2, 2, lambda c: c.wait_recv())
    pl.semaphore_wait(LP.at[3], p_near)
    call_line(LP.at[4], False)
    eliminate(1, A2, 0, NZL, 12)
    final = ([], [])

    def keep_ends(c, up, down):
        final[0].append(up)
        final[1].append(down)

    ends(keep_ends)
    for i in range(2):
        write_edges(E2.at[i], final[i])
    to_chips(lambda target: E2.at[side_of(target)], RE, e_send, e_recv)
    arrive(R2, p_recv.at[1])
    arrive(RE, e_recv)

    def bring(k, carry):
        O, edge = carry
        return (
            tuple(R2[k, c] + CB[k] * O[c] for c in range(NC)),
            RE[k] + CE[k] * edge,
        )

    def brought(steps, chip_of):
        O, edge = lax.fori_loop(0, steps, lambda i, v: bring(chip_of(i), v), (trio, blank))
        packed = jnp.broadcast_to(edge[6:7], (NZL, LANES))
        whole = []
        for c in range(NC):
            value = O[c]
            for side in range(2):
                at = lane_z == NZL * (2 * c + side) + row_z
                column = jnp.sum(jnp.where(at, packed, 0.0), axis=1, keepdims=True)
                value = jnp.where(
                    lane_z == side * (LANES - 1), jnp.broadcast_to(column, (NZL, LANES)), value
                )
            for side in range(2):
                value = jnp.where(
                    row_z == side * (NZL - 1),
                    jnp.broadcast_to(edge[2 * c + side : 2 * c + side + 1], (NZL, LANES)),
                    value,
                )
            whole.append(value)
        return whole

    close(
        (
            brought(chip, lambda i: i),
            brought(CHIPS - 1 - chip, lambda i: CHIPS - 1 - i),
        )
    )

    pl.semaphore_wait(LT.at[2], 1)
    pl.semaphore_wait(LP.at[4], p_near)

    def line_last(z, acc):
        parts = ([], [])
        for h in range(2):
            total = None
            for c in range(NC):
                a = solved(c, z, h)
                A3[c, z, h] = a
                term = VEL[c, z, h] * a
                total = term if total is None else total + term
            total = total * PEN[z, h]
            coarse = total.astype(jnp.bfloat16).astype(F32)
            for part, value in zip(parts, (coarse, total - coarse)):
                part.append(jnp.concatenate([value, value], axis=0).astype(jnp.bfloat16))
        weights = jnp.concatenate(
            [
                jnp.concatenate([jnp.concatenate(part, axis=1)] * 4, axis=0) * OHH[z]
                for part in parts
            ],
            axis=0,
        )
        return acc + lax.dot_general(
            weights, OHL[z], (((1,), (1,)), ((), ())), preferred_element_type=F32
        )

    acc = lax.fori_loop(0, NZL, line_last, jnp.zeros((LANES, 2 * LANES), F32), unroll=12)
    acc = acc[0:64] + acc[64:128]
    keep = lax.rem(lane, 8) == row
    for r in range(2):
        tall = blank
        for j in range(8):
            tile = acc[8 * j : 8 * j + 8, r * LANES : (r + 1) * LANES]
            line = jnp.sum(jnp.where(keep, tile, 0.0), axis=0, keepdims=True)
            tall = jnp.where(row == j, jnp.broadcast_to(line, (8, LANES)), tall)
        for d in (1, 2, 4):
            tall = tall + jnp.where(
                lax.rem(lane // d, 2) == 0, pltpu.roll(tall, LANES - d, 1), pltpu.roll(tall, d, 1)
            )
        B1S[r : r + 1, :] = jnp.sum(jnp.where(keep, tall, 0.0), axis=0, keepdims=True)

    def band_round(r, own, slots, order, device_of, beside):
        for j in order:
            pltpu.make_async_remote_copy(
                src_ref=own,
                dst_ref=slots.at[j],
                send_sem=b_send.at[r],
                recv_sem=b_recv.at[r],
                device_id=device_of(j),
                device_id_type=MESH,
            ).start()
        beside()
        got = slots.at[pl.ds(1, STREAM - 1)]
        pltpu.make_async_copy(got, got, b_recv.at[r]).wait()
        total = own[...]
        for j in range(1, STREAM):
            total = total + slots[j]
        return total

    def drain(count, ref, sem):
        def one(j, carry):
            pltpu.make_async_copy(ref, ref, sem).wait()
            return carry

        lax.fori_loop(0, count, one, 0)

    def sent(bytes_like, sem):
        pltpu.make_async_copy(bytes_like, bytes_like, sem).wait()

    out_own = pltpu.make_async_copy(A3.at[:, :, q], out_h.at[:, :, :, lanes_of(q)], out_sem.at[0])
    out_side = pltpu.make_async_remote_copy(
        src_ref=A3.at[:, :, 1 - q],
        dst_ref=out_h.at[:, :, :, lanes_of(q)],
        send_sem=out_sem.at[1],
        recv_sem=out_sem.at[2],
        device_id=(partner, mv, mp),
        device_id_type=MESH,
    )

    def beside_first():
        out_own.start()
        out_side.start()
        for copy in side_copies:
            copy.wait_send()
        for copy, there in first_halo:
            pl.when(there)(copy.wait_send)
        middle.wait_send()
        each(halo2, 1, lambda c: c.wait_send())
        others = pl.ds(1, CHIPS - 1)
        sent(MR.at[others], m_send)
        sent(R2.at[others], p_send.at[1])
        sent(RE.at[others], e_send)
        drain(owner_sends, QS.at[:, 0], q_send)
        drain(owner_sends, S1.at[:, :, 0], p_send.at[0])

        @pl.when(is_owner)
        def _():
            sent(D1.at[others], d_send)

        tb_copy.wait()
        tw_copy.wait()

    def beside_second():
        sent(B1R.at[pl.ds(1, STREAM - 1)], b_send.at[0])
        out_own.wait()
        out_side.wait()

    line_order = (8, 7, 9, 6, 10, 5, 11, 4, 12, 3, 13, 2, 14, 1, 15)
    plane_order = (10, 6, 9, 11, 14, 2, 8, 5, 7, 13, 15, 1, 3, 4, 12)
    B2S[...] = band_round(
        0, B1S, B1R, line_order, lambda j: (lax.rem(me + j, STREAM), mv, mp), beside_first
    )
    bands = band_round(
        1,
        B2S,
        B2R,
        plane_order,
        lambda j: (me, lax.rem(mv + j // SPAN, VERT), lax.rem(mp + j % SPAN, SPAN)),
        beside_second,
    )
    cells = STREAM * VERT * SPAN * NXL * NZL * NYL
    bands = bands * ((NBANDS / cells) ** 0.5)
    tb = TB[...].reshape(1, LANES)
    spot = lax.rem(tb, 16) * 8 + tb // 32
    spot = jnp.broadcast_to(spot, (8, LANES))
    low_half = jnp.take_along_axis(jnp.broadcast_to(bands[0:1], (8, LANES)), spot, axis=1)
    high_half = jnp.take_along_axis(jnp.broadcast_to(bands[1:2], (8, LANES)), spot, axis=1)
    picked = jnp.where(lax.rem(tb, 32) < 16, low_half[0:1], high_half[0:1])
    tri_ref[...] = (TW[...].reshape(1, LANES) * picked).reshape(LANES)
    sent(B2R.at[pl.ds(1, STREAM - 1)], b_send.at[1])


def shards(adjoint_source, velocity, penalty, adjoint_start, cell_band, tri_band, tri_weight):
    anywhere = pl.BlockSpec(memory_space=pl.ANY)

    def field():
        return pltpu.VMEM((NZL, 2, 8, LANES), F32)

    scratch = [
        pltpu.VMEM((NC, NZL, 2, 8, LANES), F32),
        pltpu.VMEM((NC, NZL, 2, 8, LANES), F32),
        field(),
        pltpu.VMEM((NZL, 2, 8, LANES), jnp.int32),
        pltpu.VMEM((NC, NZL + 2, 2, 8, LANES), F32),
        pltpu.VMEM((NC, NZL + 2, 2, 8, LANES), F32),
        pltpu.VMEM((NC, NZL, 2, 8, LANES), F32),
        pltpu.VMEM((NC, NZL, 2, 8, LANES), F32),
        field(),
        field(),
        field(),
        field(),
        pltpu.VMEM((NZL, 8, LANES), F32),
        field(),
        field(),
        field(),
        pltpu.VMEM((NZL, 8, LANES), F32),
        field(),
        field(),
        pltpu.VMEM((NC, NZL, NXL, NYL), F32),
        pltpu.VMEM((4, 8, LANES), F32),
        pltpu.VMEM((SWEEPS, 2, 2, 8, LANES), F32),
        pltpu.VMEM((SWEEPS, 2, 2, 8, LANES), F32),
        pltpu.VMEM((4, NZL, LANES), F32),
        pltpu.VMEM((CHIPS, 4, NZL, LANES), F32),
        pltpu.VMEM((CHIPS, NZL, LANES), F32),
        pltpu.VMEM((CHIPS, 8, LANES), F32),
        pltpu.VMEM((8, NZL, LANES), F32),
        pltpu.VMEM((4, OWNERS, ROWS, LANES), F32),
        pltpu.VMEM((CHIPS, 4, ROWS, LANES), F32),
        pltpu.VMEM((CHIPS, 6, ROWS, LANES), F32),
        pltpu.VMEM((CHIPS, NC, ROWS, LANES), F32),
        pltpu.VMEM((2, NC, OWNERS, ROWS, LANES), F32),
        pltpu.VMEM((CHIPS, 2, NC, ROWS, LANES), F32),
        pltpu.VMEM((CHIPS, 2, NC, ROWS, LANES), F32),
        pltpu.VMEM((2, NC, OWNERS, ROWS, LANES), F32),
        pltpu.VMEM((2, NC, NZL, LANES), F32),
        pltpu.VMEM((CHIPS, NC, NZL, LANES), F32),
        pltpu.VMEM((2, 8, LANES), F32),
        pltpu.VMEM((CHIPS, 8, LANES), F32),
        pltpu.VMEM((NC, NZL, LANES), F32),
        pltpu.VMEM((NC, NZL, LANES), F32),
        pltpu.VMEM((NZL, 64, 2 * LANES), jnp.bfloat16),
        pltpu.VMEM((NZL, 2 * LANES, 2 * LANES), jnp.bfloat16),
        pltpu.VMEM((2, LANES), F32),
        pltpu.VMEM((STREAM, 2, LANES), F32),
        pltpu.VMEM((2, LANES), F32),
        pltpu.VMEM((STREAM, 2, LANES), F32),
        pltpu.VMEM((LANES,), jnp.int32),
        pltpu.VMEM((LANES,), F32),
        pltpu.SemaphoreType.DMA((6,)),
        pltpu.SemaphoreType.DMA((5,)),
        pltpu.SemaphoreType.DMA((5,)),
        pltpu.SemaphoreType.DMA((3,)),
        pltpu.SemaphoreType.DMA((2,)),
        pltpu.SemaphoreType.REGULAR((3,)),
        pltpu.SemaphoreType.REGULAR((5,)),
        pltpu.SemaphoreType.DMA((2, 2)),
        pltpu.SemaphoreType.DMA((2, 2)),
        pltpu.SemaphoreType.DMA((3,)),
        pltpu.SemaphoreType.DMA((3,)),
        pltpu.SemaphoreType.DMA((SWEEPS, 4)),
        pltpu.SemaphoreType.DMA((SWEEPS, 4)),
        pltpu.SemaphoreType.DMA,
        pltpu.SemaphoreType.DMA,
        pltpu.SemaphoreType.DMA,
        pltpu.SemaphoreType.DMA,
        pltpu.SemaphoreType.DMA,
        pltpu.SemaphoreType.DMA,
        pltpu.SemaphoreType.DMA((SWEEPS,)),
        pltpu.SemaphoreType.DMA((SWEEPS,)),
        pltpu.SemaphoreType.DMA,
        pltpu.SemaphoreType.DMA,
        pltpu.SemaphoreType.DMA((2,)),
        pltpu.SemaphoreType.DMA((2,)),
    ]

    def planes(x):
        return jnp.swapaxes(x, -3, -2)

    adjoint, tri_grad = pl.pallas_call(
        kernel,
        out_shape=(
            jax.ShapeDtypeStruct((NC, NZL, NXL, NYL), F32),
            jax.ShapeDtypeStruct((LANES,), F32),
        ),
        in_specs=[pl.BlockSpec(memory_space=pltpu.HBM)] * 7,
        out_specs=(anywhere, pl.BlockSpec(memory_space=pltpu.VMEM)),
        scratch_shapes=scratch,
        compiler_params=pltpu.CompilerParams(
            collective_id=0, has_side_effects=True, vmem_limit_bytes=32 * 1024 * 1024
        ),
    )(
        *(
            pltpu.with_memory_space_constraint(x, pltpu.HBM)
            for x in (
                planes(adjoint_source),
                planes(velocity),
                planes(penalty),
                planes(adjoint_start),
                planes(cell_band),
                tri_band,
                tri_weight,
            )
        )
    )
    return planes(adjoint), tri_grad


def solution(mesh):
    return jax.shard_map(
        shards,
        mesh=mesh,
        in_specs=(
            P(None, "stream", "span", "vert"),
            P(None, "stream", "span", "vert"),
            P("stream", "span", "vert"),
            P(None, "stream", "span", "vert"),
            P("stream", "span", "vert"),
            P(("stream", "vert", "span")),
            P(("stream", "vert", "span")),
        ),
        out_specs=(P(None, "stream", "span", "vert"), P(("stream", "vert", "span"))),
        check_vma=False,
    )
```

```python
import functools

import jax
import jax.numpy as jnp
from jax import lax
from jax.experimental import pallas as pl
from jax.experimental.pallas import tpu as pltpu
from jax.sharding import PartitionSpec as P

SWEEPS = 2
NBANDS = 256

STREAM = 16
CHIPS = 8
VERT = 4
SPAN = 4
NC = 3
NXL = 8
NXC = 16
NZL = 12
NYL = 256
LANES = 128
OWNERS = 6
ROWS = NZL // OWNERS
FIRST = 2
FAR_FIRST = (4, 3, 5, 2, 6, 1, 7)

stream_coef = 1000.0
stream_conv = 200.0
cross_coef = 0.25
cross_conv = 0.25
shift_coef = 0.5

MESH = pl.DeviceIdType.MESH
F32 = jnp.float32


def kernel(
    src_h,
    vel_h,
    pen_h,
    start_h,
    band_h,
    tb_h,
    tw_h,
    out_h,
    tri_ref,
    SRC,
    VEL,
    PEN,
    BAND,
    A1,
    A2,
    A3,
    PP,
    IP,
    M1,
    M2,
    M4,
    MT,
    F1,
    F2,
    F4,
    FT,
    LL,
    RC,
    STG,
    YF,
    YS,
    YR,
    MS,
    MR,
    CB,
    CE,
    OWN,
    QS,
    QR,
    CO,
    OC,
    S1,
    G1,
    D1,
    R1,
    S2,
    R2,
    E2,
    RE,
    AL,
    AR,
    OHH,
    OHL,
    B1S,
    B1R,
    B2S,
    B2R,
    TB,
    TW,
    in_sem,
    side_send,
    side_recv,
    out_sem,
    tri_sem,
    LT,
    LD,
    LP,
    fz_send,
    fz_recv,
    fv_send,
    fv_recv,
    halo_send,
    halo_recv,
    m_send,
    m_recv,
    q_send,
    q_recv,
    d_send,
    d_recv,
    p_send,
    p_recv,
    e_send,
    e_recv,
    b_send,
    b_recv,
):
    me = lax.axis_index("stream")
    mv = lax.axis_index("vert")
    mp = lax.axis_index("span")
    chip = me // 2
    q = lax.rem(me, 2)
    partner = 2 * chip + (1 - q)

    def lanes_of(half):
        return pl.ds(pl.multiple_of(half * LANES, LANES), LANES)

    def pieces(ref, dst):
        rank = len(ref.shape)
        lead = (slice(None),) * (rank - 1)
        return lambda half: ref.at[lead + (lanes_of(half),)], dst

    inner = A1.at[:, pl.ds(1, NZL)]
    inputs = (
        (start_h, inner),
        (vel_h, VEL),
        (pen_h, PEN),
        (src_h, SRC),
        (band_h, BAND),
    )

    def slot(dst, half):
        if len(dst.shape) == 5:
            return dst.at[:, :, half]
        return dst.at[:, half]

    def part(src, half):
        if len(src.shape) == 4:
            return src.at[:, :, :, lanes_of(half)]
        return src.at[:, :, lanes_of(half)]

    own_copies = []
    side_copies = []
    for i, (src, dst) in enumerate(inputs):
        own_copies.append(pltpu.make_async_copy(part(src, q), slot(dst, q), in_sem.at[i]))
        side_copies.append(
            pltpu.make_async_remote_copy(
                src_ref=part(src, 1 - q),
                dst_ref=slot(dst, q),
                send_sem=side_send.at[i],
                recv_sem=side_recv.at[i],
                device_id=(partner, mv, mp),
                device_id_type=MESH,
            )
        )
    tb_copy = pltpu.make_async_copy(tb_h, TB, tri_sem.at[0])
    tw_copy = pltpu.make_async_copy(tw_h, TW, tri_sem.at[1])

    barrier = pltpu.get_barrier_semaphore()

    def either(condition):
        return jnp.where(condition, 1, 0)

    has_v = (mv > 0, mv < VERT - 1)
    has_p = (mp > 0, mp < SPAN - 1)
    v_near = either(has_v[0]) + either(has_v[1])
    p_near = either(has_p[0]) + either(has_p[1])

    def call(sem, device):
        pl.semaphore_signal(sem, inc=1, device_id=device, device_id_type=MESH)

    def stream_at(step):
        return (lax.rem(me + 2 * step + STREAM, STREAM), mv, mp)

    def call_line(sem, along_v):
        for i, step in enumerate((-1, 1)):
            if along_v:
                pl.when(has_v[i])(lambda: call(sem, (me, mv + step, mp)))
            else:
                pl.when(has_p[i])(lambda: call(sem, (me, mv, mp + step)))

    outer_v = mv - 1 + 2 * q
    has_outer = jnp.logical_and(outer_v >= 0, outer_v < VERT)
    outer_id = (partner, lax.rem(outer_v + VERT, VERT), mp)

    nothing = jnp.zeros((2, 8, LANES), F32)
    for A in (A1, A2):
        for c in range(NC):
            A[c, 0] = nothing
            A[c, NZL + 1] = nothing
    YR[...] = jnp.zeros(YR.shape, F32)

    upper = chip >= CHIPS // 2
    inside = (lax.rem(chip, 4) > 0, lax.rem(chip, 4) < 3)
    in_near = either(inside[0]) + either(inside[1])
    from_lower = either(upper) * (4 - either(jnp.logical_or(chip == 4, chip == 7)))

    def chip_at(target):
        return (2 * target + q, mv, mp)

    def call_inside(sem):
        for i, step in enumerate((-1, 1)):
            pl.when(inside[i])(lambda: call(sem, chip_at(chip + step)))

    for target in range(4, CHIPS):
        apart = jnp.logical_and(chip != target - 1, lax.rem(target + 1, CHIPS) != chip)
        pl.when(jnp.logical_and(jnp.logical_not(upper), apart))(
            lambda: call(barrier, chip_at(target))
        )
    call(barrier, (partner, mv, mp))
    call(barrier, stream_at(-1))
    call(barrier, stream_at(1))
    for i, step in enumerate((-1, 1)):
        for core in range(2):
            other = 2 * chip + core
            pl.when(has_v[i])(lambda: call(barrier, (other, mv + step, mp)))
            pl.when(has_p[i])(lambda: call(barrier, (other, mv, mp + step)))

    stage = pltpu.make_async_copy(start_h, STG, in_sem.at[5])
    stage.start()
    for i in (1, 2, 0, 3, 4):
        own_copies[i].start()
    tb_copy.start()
    tw_copy.start()
    row = lax.broadcasted_iota(jnp.int32, (8, LANES), 0)
    lane = lax.broadcasted_iota(jnp.int32, (8, LANES), 1)

    def pack_edges(k, pair, packs):
        low, high = packs
        hit = lane == k
        low = tuple(jnp.where(hit, pltpu.roll(pair[h], k, 1), low[h]) for h in range(2))
        high = tuple(jnp.where(hit, pltpu.roll(pair[h], k + 1, 1), high[h]) for h in range(2))
        return low, high

    blank = jnp.zeros((8, LANES), F32)
    no_packs = ((blank, blank), (blank, blank))

    stage.wait()

    def pack_start(z, packs):
        low, high = packs
        for c in range(NC):
            pair = (STG[c, z, :, 0:LANES], STG[c, z, :, LANES:NYL])
            low, high = pack_edges(c * NZL + z, pair, (low, high))
        return low, high

    low, high = lax.fori_loop(0, NZL, pack_start, no_packs, unroll=4)
    for i, value in enumerate((low[0], high[1], high[0], low[1])):
        YF[i] = value
    pl.semaphore_wait(barrier, 3 + 2 * v_near + 2 * p_near + from_lower)
    for i in range(3):
        side_copies[i].start()
    for target in range(4):
        pl.when(upper)(lambda: call(LD, chip_at(target)))
    call_inside(LT.at[0])
    call_line(LP.at[0], True)

    def send_halo(s, A, packs):
        for side in range(2):
            for h in range(2):
                YS[s, side, h] = packs[side][h]

        def remote(i, src, dst, device):
            return pltpu.make_async_remote_copy(
                src_ref=src,
                dst_ref=dst,
                send_sem=halo_send.at[s, i],
                recv_sem=halo_recv.at[s, i],
                device_id=device,
                device_id_type=MESH,
            )

        copies = (
            (
                remote(0, A.at[:, NZL], A.at[:, 0], (me, mv, lax.rem(mp + 1, SPAN))),
                mp < SPAN - 1,
                mp > 0,
            ),
            (
                remote(1, A.at[:, 1], A.at[:, NZL + 1], (me, mv, lax.rem(mp + SPAN - 1, SPAN))),
                mp > 0,
                mp < SPAN - 1,
            ),
            (remote(2, YS.at[s, q], YR.at[s, 1 - q], outer_id), has_outer, has_outer),
            (remote(3, YS.at[s, 1 - q], YR.at[s, q], (partner, mv, mp)), None, None),
        )
        each(copies, 1, lambda c: c.start())
        return copies

    def each(copies, which, act):
        for item in copies:
            if item[which] is None:
                act(item[0])
            else:
                pl.when(item[which])(functools.partial(act, item[0]))

    first_halo = []
    for i, step in enumerate((-1, 1)):
        for core in range(2):
            first_halo.append(
                (
                    pltpu.make_async_remote_copy(
                        src_ref=start_h.at[:, (0, NZL - 1)[i], :, pl.ds(core * LANES, LANES)],
                        dst_ref=A1.at[:, (NZL + 1, 0)[i], q],
                        send_sem=fz_send.at[i, core],
                        recv_sem=fz_recv.at[i, q],
                        device_id=(2 * chip + core, mv, mp + step),
                        device_id_type=MESH,
                    ),
                    has_p[i],
                )
            )
    for copy, there in first_halo:
        pl.when(there)(copy.start)

    for i, step in enumerate((-1, 1)):
        copy = pltpu.make_async_remote_copy(
            src_ref=YF.at[i],
            dst_ref=YR.at[0, 1 - i, q],
            send_sem=fv_send.at[i],
            recv_sem=fv_recv.at[q],
            device_id=(2 * chip + 1 - i, mv + step, mp),
            device_id_type=MESH,
        )
        first_halo.append((copy, has_v[i]))
        pl.when(has_v[i])(copy.start)
    middle = pltpu.make_async_remote_copy(
        src_ref=YF.at[2 + q],
        dst_ref=YR.at[0, q, q],
        send_sem=fv_send.at[2],
        recv_sem=fv_recv.at[2],
        device_id=(partner, mv, mp),
        device_id_type=MESH,
    )
    middle.start()
    YR[0, 1 - q, q] = YF[3 - q]

    def first_arrivals():
        for i in range(2):
            for sender in range(2):
                slab = A1.at[:, (0, NZL + 1)[i], sender]
                pl.when(has_p[i])(
                    lambda: pltpu.make_async_copy(slab, slab, fz_recv.at[1 - i, sender]).wait()
                )
        for sender in range(2):
            pl.when(has_outer)(
                lambda: pltpu.make_async_copy(YF.at[0], YF.at[0], fv_recv.at[sender]).wait()
            )
        middle.wait_recv()

    for i in range(3, 5):
        side_copies[i].start()

    for i in (1, 2):
        own_copies[i].wait()
        side_copies[i].wait_recv()

    pl.semaphore_wait(LT.at[0], in_near)
    call_inside(LT.at[1])

    def flat(ref):
        count = 1
        for size in ref.shape[:-1]:
            count *= size
        return ref.reshape(count, LANES)

    velocity2, penalty2 = flat(VEL), flat(PEN)
    ip2, m2, f2 = flat(IP), flat(M1), flat(F1)
    l2, r2, p2 = flat(LL), flat(RC), flat(PP)

    def level(ref2, x, c=0):
        return ref2[pl.ds(c * NZL * NXC + x, NZL, stride=NXC), :]

    delta = jnp.ones((NZL, LANES), F32)
    for x in range(NXC):
        u = level(velocity2, x, 0)
        west = stream_coef + stream_conv * jnp.maximum(-u, 0.0)
        east = stream_coef + stream_conv * jnp.maximum(u, 0.0)
        excess = (
            (4.0 * cross_coef + shift_coef)
            + cross_conv * (jnp.abs(level(velocity2, x, 1)) + jnp.abs(level(velocity2, x, 2)))
            + level(penalty2, x)
        )
        sink = excess + west * delta
        ip = 1.0 / (east + sink)
        delta = sink * ip
        place = pl.ds(x, NZL, stride=NXC)
        ip2[place, :] = ip
        m2[place, :] = west * ip
        f2[place, :] = east * ip

    def ahead(v, n, fill):
        return jnp.where(row >= n, pltpu.roll(v, n, 0), fill)

    def behind(v, n, fill):
        return jnp.where(row < 8 - n, pltpu.roll(v, 8 - n, 0), fill)

    def fold_up(values, f1, f2, f4, ft):
        new = []
        for h in range(2):
            v = values[h]
            v = v + f1[h] * pltpu.roll(v, 7, 0)
            v = v + f2[h] * pltpu.roll(v, 6, 0)
            v = v + f4[h] * pltpu.roll(v, 4, 0)
            new.append(v)
        new[0] = new[0] + ft * jnp.broadcast_to(new[1][0:1], (8, LANES))
        return new

    def factor(z, carry):
        chains = []
        tails = []
        f1s, f2s, f4s, fts = [], [], [], []
        for h in range(2):
            m = M1[z, h]
            f = F1[z, h]
            m1 = jnp.where(row >= 1, m, 0.0)
            mm = m1 * ahead(m, 1, 0.0)
            m4 = jnp.where(row >= 4, jnp.where(row >= 2, mm, 0.0) * pltpu.roll(mm, 2, 0), 0.0)
            mm = jnp.where(row >= 2, mm, 0.0)
            M1[z, h] = m1
            M2[z, h] = mm
            M4[z, h] = m4
            t = m * ahead(m, 1, 1.0)
            t = t * ahead(t, 2, 1.0)
            chains.append(t * ahead(t, 4, 1.0))
            f1 = jnp.where(row < 7, f, 0.0)
            ff = jnp.where(row < 6, f1 * behind(f, 1, 0.0), 0.0)
            f4 = jnp.where(row < 4, ff * pltpu.roll(ff, 6, 0), 0.0)
            F1[z, h] = f1
            F2[z, h] = ff
            F4[z, h] = f4
            f1s.append(f1)
            f2s.append(ff)
            f4s.append(f4)
            t = f * behind(f, 1, 1.0)
            t = t * behind(t, 2, 1.0)
            tails.append(t * behind(t, 4, 1.0))
        MT[z] = chains[1]
        FT[z] = tails[0]
        left = [chains[0], chains[1] * jnp.broadcast_to(chains[0][7:8], (8, LANES))]
        left = fold_up(left, f1s, f2s, f4s, tails[0])
        right = [tails[0] * jnp.broadcast_to(tails[1][0:1], (8, LANES)), tails[1]]
        for h in range(2):
            LL[z, h] = left[h]
            RC[z, h] = right[h]
        return carry

    lax.fori_loop(0, NZL, factor, 0)
    for k, ref2 in enumerate((l2, r2)):
        MS[2 * k] = level(ref2, 0)
        MS[2 * k + 1] = level(ref2, NXC - 1)

    def to_chips(src_of, dst, send_sem, recv_sem):
        for j in FAR_FIRST:
            target = lax.rem(chip + j, CHIPS)
            pltpu.make_async_remote_copy(
                src_ref=src_of(target),
                dst_ref=dst.at[chip],
                send_sem=send_sem,
                recv_sem=recv_sem,
                device_id=(2 * target + q, mv, mp),
                device_id_type=MESH,
            ).start()

    def arrive(slots, sem):
        got = slots.at[pl.ds(1, CHIPS - 1)]
        pltpu.make_async_copy(got, got, sem).wait()

    pl.semaphore_wait(LT.at[1], in_near)

    @pl.when(jnp.logical_not(upper))
    def _():
        pl.semaphore_wait(LD, 4)

    call(LT.at[2], (partner, mv, mp))

    my_o = lax.rem(chip + FIRST, CHIPS)
    is_owner = my_o < OWNERS
    owner_sends = jnp.where(is_owner, OWNERS - 1, OWNERS)

    def to_owners(src_of, dst, send_sem, recv_sem):
        for j in FAR_FIRST:
            target = lax.rem(chip + j, CHIPS)
            o = lax.rem(target + FIRST, CHIPS)

            @pl.when(o < OWNERS)
            def _():
                pltpu.make_async_remote_copy(
                    src_ref=src_of(o),
                    dst_ref=dst,
                    send_sem=send_sem,
                    recv_sem=recv_sem,
                    device_id=(2 * target + q, mv, mp),
                    device_id_type=MESH,
                ).start()

        @pl.when(is_owner)
        def _():
            pltpu.make_async_copy(src_of(my_o), dst, recv_sem).start()

    for k in range(4):
        value = MS[k]
        for o in range(OWNERS):
            QS[k, o] = value[ROWS * o : ROWS * o + ROWS]
    to_owners(lambda o: QS.at[:, o], QR.at[chip], q_send, q_recv)

    for i in (3,):
        own_copies[i].wait()
        side_copies[i].wait_recv()

    first = lane == 0
    last = lane == LANES - 1

    def eliminate(s, A, low, count, unroll):
        if s is not None:
            edges = [[YR[s, side, h] for h in range(2)] for side in range(2)]

        def plane(z, carry):
            cross = []
            for h in range(2):
                v = VEL[1, z, h]
                w = VEL[2, z, h]
                cross.append(
                    (
                        cross_coef + cross_conv * jnp.maximum(-v, 0.0),
                        cross_coef + cross_conv * jnp.maximum(v, 0.0),
                        cross_coef + cross_conv * jnp.maximum(-w, 0.0),
                        cross_coef + cross_conv * jnp.maximum(w, 0.0),
                    )
                )
            ip = [IP[z, h] for h in range(2)]
            m1 = [M1[z, h] for h in range(2)]
            m2 = [M2[z, h] for h in range(2)]
            m4 = [M4[z, h] for h in range(2)]
            f1 = [F1[z, h] for h in range(2)]
            f2 = [F2[z, h] for h in range(2)]
            f4 = [F4[z, h] for h in range(2)]
            mt = MT[z]
            ft = FT[z]
            for c in range(NC):
                k = c * NZL + z
                o = []
                for h in range(2):
                    south, north, below, above = cross[h]
                    a = A[c, z + 1, h]
                    lo = hi = blank
                    if s is not None:
                        lo = pltpu.roll(edges[0][h], lax.rem(LANES - k, LANES), 1)
                        hi = pltpu.roll(edges[1][h], LANES - 1 - k, 1)
                    y_lo = jnp.where(first, lo, pltpu.roll(a, 1, 1))
                    y_hi = jnp.where(last, hi, pltpu.roll(a, LANES - 1, 1))
                    rhs = SRC[c, z, h] + shift_coef * a
                    rhs = rhs + south * y_lo + north * y_hi
                    rhs = rhs + below * A[c, z, h] + above * A[c, z + 2, h]
                    v = rhs * ip[h]
                    v = v + m1[h] * pltpu.roll(v, 1, 0)
                    v = v + m2[h] * pltpu.roll(v, 2, 0)
                    v = v + m4[h] * pltpu.roll(v, 4, 0)
                    o.append(v)
                o[1] = o[1] + mt * jnp.broadcast_to(o[0][7:8], (8, LANES))
                p = fold_up(o, f1, f2, f4, ft)
                for h in range(2):
                    PP[c, z, h] = p[h]
            return carry

        lax.fori_loop(low, low + count, plane, 0, unroll=unroll)

    own_copies[0].wait()
    side_copies[0].wait_recv()
    first_arrivals()
    pl.semaphore_wait(LP.at[0], v_near)
    call_line(LP.at[1], True)
    eliminate(0, A1, 0, NZL, 12)
    for c in range(NC):
        for i, x in enumerate((0, NXC - 1)):
            value = level(p2, x, c)
            for o in range(OWNERS):
                S1[i, c, o] = value[ROWS * o : ROWS * o + ROWS]
    to_owners(lambda o: S1.at[:, :, o], G1.at[chip], p_send.at[0], p_recv.at[0])
    pl.semaphore_wait(LP.at[1], v_near)
    call_line(LP.at[2], False)
    to_chips(lambda target: MS, MR, m_send, m_recv)

    own_copies[4].wait()
    side_copies[4].wait_recv()

    def indicator(digit, count):
        return jnp.concatenate(
            [jnp.where(digit == i, 1.0, 0.0) for i in range(count)], axis=0
        ).astype(jnp.bfloat16)

    def onehot(z, carry):
        for h in range(2):
            cut = slice(h * LANES, (h + 1) * LANES)
            OHL[z, :, cut] = indicator(lax.rem(BAND[z, h], 32), 32)
            OHH[z, :, cut] = indicator(BAND[z, h] // 32, 8)
        return carry

    lax.fori_loop(0, NZL, onehot, 0)

    @pl.when(is_owner)
    def _():
        pltpu.make_async_copy(QR, QR, q_recv).wait()
        ahead_f = jnp.zeros((ROWS, LANES), F32)
        for k in range(CHIPS):
            lf, lg, rf, rg = (QR[k, i] for i in range(4))
            inv = 1.0 / (1.0 - lf * ahead_f)
            b = lg * inv
            g = b * ahead_f
            for i, value in enumerate((g, b, inv, lf * inv, rf * inv, ahead_f)):
                CO[k, i] = value
            ahead_f = rg + g * rf

        pltpu.make_async_copy(G1, G1, p_recv.at[0]).wait()
        nil = jnp.zeros((ROWS, LANES), F32)
        O = [nil] * NC
        for k in range(CHIPS):
            for c in range(NC):
                OC[k, c] = O[c]
                O[c] = G1[k, 1, c] + CO[k, 0] * G1[k, 0, c] + CO[k, 1] * O[c]
        after = [nil] * NC
        for k in reversed(range(CHIPS)):
            for c in range(NC):
                D1[k, 1, c] = after[c]
                before = OC[k, c]
                after[c] = CO[k, 2] * G1[k, 0, c] + CO[k, 3] * before + CO[k, 4] * after[c]
                D1[k, 0, c] = CO[k, 5] * after[c] + before

        for j in FAR_FIRST:
            target = lax.rem(chip + j, CHIPS)
            pltpu.make_async_remote_copy(
                src_ref=D1.at[target],
                dst_ref=R1.at[:, :, my_o],
                send_sem=d_send,
                recv_sem=d_recv,
                device_id=(2 * target + q, mv, mp),
                device_id_type=MESH,
            ).start()

        pltpu.make_async_copy(D1.at[chip], R1.at[:, :, my_o], d_recv).start()

    arrive(MR, m_recv)

    row_z = lax.broadcasted_iota(jnp.int32, (NZL, LANES), 0)
    lane_z = lax.broadcasted_iota(jnp.int32, (NZL, LANES), 1)

    def write_edges(ref, values):
        packed = jnp.zeros((NZL, LANES), F32)
        for c in range(NC):
            v = values[c]
            for side in range(2):
                ref[2 * c + side : 2 * c + side + 1, :] = v[
                    side * (NZL - 1) : side * (NZL - 1) + 1
                ]
                column = v[:, side * (LANES - 1) : side * (LANES - 1) + 1]
                packed = jnp.where(
                    lane_z == NZL * (2 * c + side) + row_z,
                    jnp.broadcast_to(column, (NZL, LANES)),
                    packed,
                )
        ref[6:7, :] = jnp.sum(packed, axis=0, keepdims=True)
        ref[7:8, :] = jnp.zeros((1, LANES), F32)

    def upstream(k, F):
        lf, lg, rf, rg = (MR[k, i] for i in range(4))
        b = lg / (1.0 - lf * F)
        g = b * F
        CB[k] = b
        return rg + g * rf

    def downstream(i, H):
        k = CHIPS - 1 - i
        lf, lg, rf, rg = (MR[k, i] for i in range(4))
        b = rf / (1.0 - rg * H)
        g = b * H
        CB[k] = b
        return lf + g * lg

    none = jnp.zeros((NZL, LANES), F32)
    F = lax.fori_loop(0, chip, upstream, none)
    H = lax.fori_loop(0, CHIPS - 1 - chip, downstream, none)
    lf, lg, rf, rg = (MS[i] for i in range(4))
    from_left = 1.0 - lf * F
    from_right = 1.0 - rg * H
    inv = 1.0 / (from_left * from_right - (F * rf) * (H * lg))
    for i, value in enumerate(
        (
            F,
            H,
            from_right * inv,
            F * rf * inv,
            H * lg * inv,
            from_left * inv,
            lg / from_left * F,
            rf / from_right * H,
        )
    ):
        OWN[i] = value

    def close(incoming):
        for c in range(NC):
            first_p = level(p2, 0, c)
            last_p = level(p2, NXC - 1, c)
            x = OWN[0] * first_p + incoming[0][c]
            y = OWN[1] * last_p + incoming[1][c]
            AL[c] = OWN[2] * x + OWN[3] * y
            AR[c] = OWN[4] * x + OWN[5] * y

    def solved(c, z, h):
        return (
            PP[c, z, h]
            + LL[z, h] * jnp.broadcast_to(AL[c, pl.ds(z, 1), :], (8, LANES))
            + RC[z, h] * jnp.broadcast_to(AR[c, pl.ds(z, 1), :], (8, LANES))
        )

    pltpu.make_async_copy(R1, R1, d_recv).wait()
    pl.semaphore_wait(LP.at[2], p_near)
    call_line(LP.at[3], False)
    trio = (none,) * NC
    for c in range(NC):
        for o in range(OWNERS):
            AL[c, ROWS * o : ROWS * o + ROWS, :] = R1[0, c, o]
            AR[c, ROWS * o : ROWS * o + ROWS, :] = R1[1, c, o]

    def line_first(z, packs):
        for c in range(NC):
            pair = tuple(solved(c, z, h) for h in range(2))
            for h in range(2):
                A2[c, z + 1, h] = pair[h]
            packs = pack_edges(c * NZL + z, pair, packs)
        return packs

    halo2 = send_halo(1, A2, lax.fori_loop(0, NZL, line_first, no_packs, unroll=4))

    def ends(write):
        for c in range(NC):
            first_p = level(p2, 0, c)
            last_p = level(p2, NXC - 1, c)
            write(c, last_p + OWN[6] * first_p, first_p + OWN[7] * last_p)

    def write_rows(c, up, down):
        S2[0, c] = up
        S2[1, c] = down

    def side_of(target):
        return jnp.where(target > chip, 0, 1)

    eliminate(None, A2, 1, NZL - 2, 5)
    ends(write_rows)
    to_chips(lambda target: S2.at[side_of(target)], R2, p_send.at[1], p_recv.at[1])

    def edge_coefficients(k, carry):
        write_edges(CE.at[k], (CB[k],) * NC)
        return carry

    lax.fori_loop(0, chip, edge_coefficients, 0)
    lax.fori_loop(chip + 1, CHIPS, edge_coefficients, 0)

    each(halo2, 2, lambda c: c.wait_recv())
    pl.semaphore_wait(LP.at[3], p_near)
    call_line(LP.at[4], False)
    eliminate(1, A2, 0, NZL, 12)
    final = ([], [])

    def keep_ends(c, up, down):
        final[0].append(up)
        final[1].append(down)

    ends(keep_ends)
    for i in range(2):
        write_edges(E2.at[i], final[i])
    to_chips(lambda target: E2.at[side_of(target)], RE, e_send, e_recv)
    arrive(R2, p_recv.at[1])
    arrive(RE, e_recv)

    def bring(k, carry):
        O, edge = carry
        return (
            tuple(R2[k, c] + CB[k] * O[c] for c in range(NC)),
            RE[k] + CE[k] * edge,
        )

    def brought(steps, chip_of):
        O, edge = lax.fori_loop(0, steps, lambda i, v: bring(chip_of(i), v), (trio, blank))
        packed = jnp.broadcast_to(edge[6:7], (NZL, LANES))
        whole = []
        for c in range(NC):
            value = O[c]
            for side in range(2):
                at = lane_z == NZL * (2 * c + side) + row_z
                column = jnp.sum(jnp.where(at, packed, 0.0), axis=1, keepdims=True)
                value = jnp.where(
                    lane_z == side * (LANES - 1), jnp.broadcast_to(column, (NZL, LANES)), value
                )
            for side in range(2):
                value = jnp.where(
                    row_z == side * (NZL - 1),
                    jnp.broadcast_to(edge[2 * c + side : 2 * c + side + 1], (NZL, LANES)),
                    value,
                )
            whole.append(value)
        return whole

    close(
        (
            brought(chip, lambda i: i),
            brought(CHIPS - 1 - chip, lambda i: CHIPS - 1 - i),
        )
    )

    pl.semaphore_wait(LT.at[2], 1)
    pl.semaphore_wait(LP.at[4], p_near)

    def line_last(z, acc):
        parts = ([], [])
        for h in range(2):
            total = None
            for c in range(NC):
                a = solved(c, z, h)
                A3[c, z, h] = a
                term = VEL[c, z, h] * a
                total = term if total is None else total + term
            total = total * PEN[z, h]
            coarse = total.astype(jnp.bfloat16).astype(F32)
            for part, value in zip(parts, (coarse, total - coarse)):
                part.append(jnp.concatenate([value, value], axis=0).astype(jnp.bfloat16))
        weights = jnp.concatenate(
            [
                jnp.concatenate([jnp.concatenate(part, axis=1)] * 4, axis=0) * OHH[z]
                for part in parts
            ],
            axis=0,
        )
        return acc + lax.dot_general(
            weights, OHL[z], (((1,), (1,)), ((), ())), preferred_element_type=F32
        )

    acc = lax.fori_loop(0, NZL, line_last, jnp.zeros((LANES, 2 * LANES), F32), unroll=12)
    acc = acc[0:64] + acc[64:128]
    keep = lax.rem(lane, 8) == row
    for r in range(2):
        tall = blank
        for j in range(8):
            tile = acc[8 * j : 8 * j + 8, r * LANES : (r + 1) * LANES]
            line = jnp.sum(jnp.where(keep, tile, 0.0), axis=0, keepdims=True)
            tall = jnp.where(row == j, jnp.broadcast_to(line, (8, LANES)), tall)
        for d in (1, 2, 4):
            tall = tall + jnp.where(
                lax.rem(lane // d, 2) == 0, pltpu.roll(tall, LANES - d, 1), pltpu.roll(tall, d, 1)
            )
        B1S[r : r + 1, :] = jnp.sum(jnp.where(keep, tall, 0.0), axis=0, keepdims=True)

    def band_round(r, own, slots, order, device_of, beside):
        for j in order:
            pltpu.make_async_remote_copy(
                src_ref=own,
                dst_ref=slots.at[j],
                send_sem=b_send.at[r],
                recv_sem=b_recv.at[r],
                device_id=device_of(j),
                device_id_type=MESH,
            ).start()
        beside()
        got = slots.at[pl.ds(1, STREAM - 1)]
        pltpu.make_async_copy(got, got, b_recv.at[r]).wait()
        total = own[...]
        for j in range(1, STREAM):
            total = total + slots[j]
        return total

    def drain(count, ref, sem):
        def one(j, carry):
            pltpu.make_async_copy(ref, ref, sem).wait()
            return carry

        lax.fori_loop(0, count, one, 0)

    def sent(bytes_like, sem):
        pltpu.make_async_copy(bytes_like, bytes_like, sem).wait()

    out_own = pltpu.make_async_copy(A3.at[:, :, q], out_h.at[:, :, :, lanes_of(q)], out_sem.at[0])
    out_side = pltpu.make_async_remote_copy(
        src_ref=A3.at[:, :, 1 - q],
        dst_ref=out_h.at[:, :, :, lanes_of(q)],
        send_sem=out_sem.at[1],
        recv_sem=out_sem.at[2],
        device_id=(partner, mv, mp),
        device_id_type=MESH,
    )

    def beside_first():
        out_own.start()
        out_side.start()
        for copy in side_copies:
            copy.wait_send()
        for copy, there in first_halo:
            pl.when(there)(copy.wait_send)
        middle.wait_send()
        each(halo2, 1, lambda c: c.wait_send())
        others = pl.ds(1, CHIPS - 1)
        sent(MR.at[others], m_send)
        sent(R2.at[others], p_send.at[1])
        sent(RE.at[others], e_send)
        drain(owner_sends, QS.at[:, 0], q_send)
        drain(owner_sends, S1.at[:, :, 0], p_send.at[0])

        @pl.when(is_owner)
        def _():
            sent(D1.at[others], d_send)

        tb_copy.wait()
        tw_copy.wait()

    def beside_second():
        sent(B1R.at[pl.ds(1, STREAM - 1)], b_send.at[0])
        out_own.wait()
        out_side.wait()

    line_order = (8, 7, 9, 6, 10, 5, 11, 4, 12, 3, 13, 2, 14, 1, 15)
    plane_order = (10, 6, 9, 11, 14, 2, 8, 5, 7, 13, 15, 1, 3, 4, 12)
    B2S[...] = band_round(
        0, B1S, B1R, line_order, lambda j: (lax.rem(me + j, STREAM), mv, mp), beside_first
    )
    bands = band_round(
        1,
        B2S,
        B2R,
        plane_order,
        lambda j: (me, lax.rem(mv + j // SPAN, VERT), lax.rem(mp + j % SPAN, SPAN)),
        beside_second,
    )
    cells = STREAM * VERT * SPAN * NXL * NZL * NYL
    bands = bands * ((NBANDS / cells) ** 0.5)
    tb = TB[...].reshape(1, LANES)
    spot = lax.rem(tb, 16) * 8 + tb // 32
    spot = jnp.broadcast_to(spot, (8, LANES))
    low_half = jnp.take_along_axis(jnp.broadcast_to(bands[0:1], (8, LANES)), spot, axis=1)
    high_half = jnp.take_along_axis(jnp.broadcast_to(bands[1:2], (8, LANES)), spot, axis=1)
    picked = jnp.where(lax.rem(tb, 32) < 16, low_half[0:1], high_half[0:1])
    tri_ref[...] = (TW[...].reshape(1, LANES) * picked).reshape(LANES)
    sent(B2R.at[pl.ds(1, STREAM - 1)], b_send.at[1])


def shards(adjoint_source, velocity, penalty, adjoint_start, cell_band, tri_band, tri_weight):
    anywhere = pl.BlockSpec(memory_space=pl.ANY)

    def field():
        return pltpu.VMEM((NZL, 2, 8, LANES), F32)

    scratch = [
        pltpu.VMEM((NC, NZL, 2, 8, LANES), F32),
        pltpu.VMEM((NC, NZL, 2, 8, LANES), F32),
        field(),
        pltpu.VMEM((NZL, 2, 8, LANES), jnp.int32),
        pltpu.VMEM((NC, NZL + 2, 2, 8, LANES), F32),
        pltpu.VMEM((NC, NZL + 2, 2, 8, LANES), F32),
        pltpu.VMEM((NC, NZL, 2, 8, LANES), F32),
        pltpu.VMEM((NC, NZL, 2, 8, LANES), F32),
        field(),
        field(),
        field(),
        field(),
        pltpu.VMEM((NZL, 8, LANES), F32),
        field(),
        field(),
        field(),
        pltpu.VMEM((NZL, 8, LANES), F32),
        field(),
        field(),
        pltpu.VMEM((NC, NZL, NXL, NYL), F32),
        pltpu.VMEM((4, 8, LANES), F32),
        pltpu.VMEM((SWEEPS, 2, 2, 8, LANES), F32),
        pltpu.VMEM((SWEEPS, 2, 2, 8, LANES), F32),
        pltpu.VMEM((4, NZL, LANES), F32),
        pltpu.VMEM((CHIPS, 4, NZL, LANES), F32),
        pltpu.VMEM((CHIPS, NZL, LANES), F32),
        pltpu.VMEM((CHIPS, 8, LANES), F32),
        pltpu.VMEM((8, NZL, LANES), F32),
        pltpu.VMEM((4, OWNERS, ROWS, LANES), F32),
        pltpu.VMEM((CHIPS, 4, ROWS, LANES), F32),
        pltpu.VMEM((CHIPS, 6, ROWS, LANES), F32),
        pltpu.VMEM((CHIPS, NC, ROWS, LANES), F32),
        pltpu.VMEM((2, NC, OWNERS, ROWS, LANES), F32),
        pltpu.VMEM((CHIPS, 2, NC, ROWS, LANES), F32),
        pltpu.VMEM((CHIPS, 2, NC, ROWS, LANES), F32),
        pltpu.VMEM((2, NC, OWNERS, ROWS, LANES), F32),
        pltpu.VMEM((2, NC, NZL, LANES), F32),
        pltpu.VMEM((CHIPS, NC, NZL, LANES), F32),
        pltpu.VMEM((2, 8, LANES), F32),
        pltpu.VMEM((CHIPS, 8, LANES), F32),
        pltpu.VMEM((NC, NZL, LANES), F32),
        pltpu.VMEM((NC, NZL, LANES), F32),
        pltpu.VMEM((NZL, 64, 2 * LANES), jnp.bfloat16),
        pltpu.VMEM((NZL, 2 * LANES, 2 * LANES), jnp.bfloat16),
        pltpu.VMEM((2, LANES), F32),
        pltpu.VMEM((STREAM, 2, LANES), F32),
        pltpu.VMEM((2, LANES), F32),
        pltpu.VMEM((STREAM, 2, LANES), F32),
        pltpu.VMEM((LANES,), jnp.int32),
        pltpu.VMEM((LANES,), F32),
        pltpu.SemaphoreType.DMA((6,)),
        pltpu.SemaphoreType.DMA((5,)),
        pltpu.SemaphoreType.DMA((5,)),
        pltpu.SemaphoreType.DMA((3,)),
        pltpu.SemaphoreType.DMA((2,)),
        pltpu.SemaphoreType.REGULAR((3,)),
        pltpu.SemaphoreType.REGULAR,
        pltpu.SemaphoreType.REGULAR((5,)),
        pltpu.SemaphoreType.DMA((2, 2)),
        pltpu.SemaphoreType.DMA((2, 2)),
        pltpu.SemaphoreType.DMA((3,)),
        pltpu.SemaphoreType.DMA((3,)),
        pltpu.SemaphoreType.DMA((SWEEPS, 4)),
        pltpu.SemaphoreType.DMA((SWEEPS, 4)),
        pltpu.SemaphoreType.DMA,
        pltpu.SemaphoreType.DMA,
        pltpu.SemaphoreType.DMA,
        pltpu.SemaphoreType.DMA,
        pltpu.SemaphoreType.DMA,
        pltpu.SemaphoreType.DMA,
        pltpu.SemaphoreType.DMA((SWEEPS,)),
        pltpu.SemaphoreType.DMA((SWEEPS,)),
        pltpu.SemaphoreType.DMA,
        pltpu.SemaphoreType.DMA,
        pltpu.SemaphoreType.DMA((2,)),
        pltpu.SemaphoreType.DMA((2,)),
    ]

    def planes(x):
        return jnp.swapaxes(x, -3, -2)

    adjoint, tri_grad = pl.pallas_call(
        kernel,
        out_shape=(
            jax.ShapeDtypeStruct((NC, NZL, NXL, NYL), F32),
            jax.ShapeDtypeStruct((LANES,), F32),
        ),
        in_specs=[pl.BlockSpec(memory_space=pltpu.HBM)] * 7,
        out_specs=(anywhere, pl.BlockSpec(memory_space=pltpu.VMEM)),
        scratch_shapes=scratch,
        compiler_params=pltpu.CompilerParams(
            collective_id=0, has_side_effects=True, vmem_limit_bytes=32 * 1024 * 1024
        ),
    )(
        *(
            pltpu.with_memory_space_constraint(x, pltpu.HBM)
            for x in (
                planes(adjoint_source),
                planes(velocity),
                planes(penalty),
                planes(adjoint_start),
                planes(cell_band),
                tri_band,
                tri_weight,
            )
        )
    )
    return planes(adjoint), tri_grad


def solution(mesh):
    return jax.shard_map(
        shards,
        mesh=mesh,
        in_specs=(
            P(None, "stream", "span", "vert"),
            P(None, "stream", "span", "vert"),
            P("stream", "span", "vert"),
            P(None, "stream", "span", "vert"),
            P("stream", "span", "vert"),
            P(("stream", "vert", "span")),
            P(("stream", "vert", "span")),
        ),
        out_specs=(P(None, "stream", "span", "vert"), P(("stream", "vert", "span"))),
        check_vma=False,
    )
```

```python
import functools

import jax
import jax.numpy as jnp
from jax import lax
from jax.experimental import pallas as pl
from jax.experimental.pallas import tpu as pltpu
from jax.sharding import PartitionSpec as P

SWEEPS = 2
NBANDS = 256

STREAM = 16
CHIPS = 8
VERT = 4
SPAN = 4
NC = 3
NXL = 8
NXC = 16
NZL = 12
NYL = 256
LANES = 128
OWNERS = 6
ROWS = NZL // OWNERS
FIRST = 2
FAR_FIRST = (4, 3, 5, 2, 6, 1, 7)

stream_coef = 1000.0
stream_conv = 200.0
cross_coef = 0.25
cross_conv = 0.25
shift_coef = 0.5

MESH = pl.DeviceIdType.MESH
F32 = jnp.float32


def kernel(
    src_h,
    vel_h,
    pen_h,
    start_h,
    band_h,
    tb_h,
    tw_h,
    out_h,
    tri_ref,
    SRC,
    VEL,
    PEN,
    BAND,
    A1,
    A2,
    A3,
    PP,
    IP,
    M1,
    M2,
    M4,
    MT,
    F1,
    F2,
    F4,
    FT,
    LL,
    RC,
    STG,
    YF,
    YS,
    YR,
    MS,
    MR,
    CB,
    CE,
    OWN,
    QS,
    QR,
    CO,
    OC,
    S1,
    G1,
    D1,
    R1,
    S2,
    R2,
    E2,
    RE,
    AL,
    AR,
    OHH,
    OHL,
    B1S,
    B1R,
    B2S,
    B2R,
    TB,
    TW,
    in_sem,
    side_send,
    side_recv,
    out_sem,
    tri_sem,
    LT,
    LD,
    LP,
    fz_send,
    fz_recv,
    fv_send,
    fv_recv,
    halo_send,
    halo_recv,
    m_send,
    m_recv,
    q_send,
    q_recv,
    d_send,
    d_recv,
    p_send,
    p_recv,
    e_send,
    e_recv,
    b_send,
    b_recv,
):
    me = lax.axis_index("stream")
    mv = lax.axis_index("vert")
    mp = lax.axis_index("span")
    chip = me // 2
    q = lax.rem(me, 2)
    partner = 2 * chip + (1 - q)

    def lanes_of(half):
        return pl.ds(pl.multiple_of(half * LANES, LANES), LANES)

    def pieces(ref, dst):
        rank = len(ref.shape)
        lead = (slice(None),) * (rank - 1)
        return lambda half: ref.at[lead + (lanes_of(half),)], dst

    inner = A1.at[:, pl.ds(1, NZL)]
    inputs = (
        (start_h, inner),
        (vel_h, VEL),
        (pen_h, PEN),
        (src_h, SRC),
        (band_h, BAND),
    )

    def slot(dst, half):
        if len(dst.shape) == 5:
            return dst.at[:, :, half]
        return dst.at[:, half]

    def part(src, half):
        if len(src.shape) == 4:
            return src.at[:, :, :, lanes_of(half)]
        return src.at[:, :, lanes_of(half)]

    own_copies = []
    side_copies = []
    for i, (src, dst) in enumerate(inputs):
        own_copies.append(pltpu.make_async_copy(part(src, q), slot(dst, q), in_sem.at[i]))
        side_copies.append(
            pltpu.make_async_remote_copy(
                src_ref=part(src, 1 - q),
                dst_ref=slot(dst, q),
                send_sem=side_send.at[i],
                recv_sem=side_recv.at[i],
                device_id=(partner, mv, mp),
                device_id_type=MESH,
            )
        )
    stage = pltpu.make_async_copy(start_h, STG, in_sem.at[5])
    stage.start()
    for i in (1, 2, 0, 3, 4):
        own_copies[i].start()
    tb_copy = pltpu.make_async_copy(tb_h, TB, tri_sem.at[0])
    tw_copy = pltpu.make_async_copy(tw_h, TW, tri_sem.at[1])

    barrier = pltpu.get_barrier_semaphore()

    def either(condition):
        return jnp.where(condition, 1, 0)

    has_v = (mv > 0, mv < VERT - 1)
    has_p = (mp > 0, mp < SPAN - 1)
    v_near = either(has_v[0]) + either(has_v[1])
    p_near = either(has_p[0]) + either(has_p[1])

    def call(sem, device):
        pl.semaphore_signal(sem, inc=1, device_id=device, device_id_type=MESH)

    def stream_at(step):
        return (lax.rem(me + 2 * step + STREAM, STREAM), mv, mp)

    def call_line(sem, along_v):
        for i, step in enumerate((-1, 1)):
            if along_v:
                pl.when(has_v[i])(lambda: call(sem, (me, mv + step, mp)))
            else:
                pl.when(has_p[i])(lambda: call(sem, (me, mv, mp + step)))

    outer_v = mv - 1 + 2 * q
    has_outer = jnp.logical_and(outer_v >= 0, outer_v < VERT)
    outer_id = (partner, lax.rem(outer_v + VERT, VERT), mp)

    nothing = jnp.zeros((2, 8, LANES), F32)
    for A in (A1, A2):
        for c in range(NC):
            A[c, 0] = nothing
            A[c, NZL + 1] = nothing
    YR[...] = jnp.zeros(YR.shape, F32)

    upper = chip >= CHIPS // 2
    inside = (lax.rem(chip, 4) > 0, lax.rem(chip, 4) < 3)
    in_near = either(inside[0]) + either(inside[1])
    from_lower = either(upper) * (4 - either(jnp.logical_or(chip == 4, chip == 7)))

    def chip_at(target):
        return (2 * target + q, mv, mp)

    def call_inside(sem):
        for i, step in enumerate((-1, 1)):
            pl.when(inside[i])(lambda: call(sem, chip_at(chip + step)))

    for target in range(4, CHIPS):
        apart = jnp.logical_and(chip != target - 1, lax.rem(target + 1, CHIPS) != chip)
        pl.when(jnp.logical_and(jnp.logical_not(upper), apart))(
            lambda: call(barrier, chip_at(target))
        )
    call(barrier, (partner, mv, mp))
    call(barrier, stream_at(-1))
    call(barrier, stream_at(1))
    for i, step in enumerate((-1, 1)):
        for core in range(2):
            other = 2 * chip + core
            pl.when(has_v[i])(lambda: call(barrier, (other, mv + step, mp)))
            pl.when(has_p[i])(lambda: call(barrier, (other, mv, mp + step)))

    tb_copy.start()
    tw_copy.start()
    row = lax.broadcasted_iota(jnp.int32, (8, LANES), 0)
    lane = lax.broadcasted_iota(jnp.int32, (8, LANES), 1)

    def pack_edges(k, pair, packs):
        low, high = packs
        hit = lane == k
        low = tuple(jnp.where(hit, pltpu.roll(pair[h], k, 1), low[h]) for h in range(2))
        high = tuple(jnp.where(hit, pltpu.roll(pair[h], k + 1, 1), high[h]) for h in range(2))
        return low, high

    blank = jnp.zeros((8, LANES), F32)
    no_packs = ((blank, blank), (blank, blank))

    stage.wait()

    def pack_start(z, packs):
        low, high = packs
        for c in range(NC):
            pair = (STG[c, z, :, 0:LANES], STG[c, z, :, LANES:NYL])
            low, high = pack_edges(c * NZL + z, pair, (low, high))
        return low, high

    low, high = lax.fori_loop(0, NZL, pack_start, no_packs, unroll=4)
    for i, value in enumerate((low[0], high[1], high[0], low[1])):
        YF[i] = value
    pl.semaphore_wait(barrier, 3 + 2 * v_near + 2 * p_near + from_lower)
    for i in range(3):
        side_copies[i].start()
    for target in range(4):
        pl.when(upper)(lambda: call(LD, chip_at(target)))
    call_inside(LT.at[0])
    call_line(LP.at[0], True)

    def send_halo(s, A, packs):
        for side in range(2):
            for h in range(2):
                YS[s, side, h] = packs[side][h]

        def remote(i, src, dst, device):
            return pltpu.make_async_remote_copy(
                src_ref=src,
                dst_ref=dst,
                send_sem=halo_send.at[s, i],
                recv_sem=halo_recv.at[s, i],
                device_id=device,
                device_id_type=MESH,
            )

        copies = (
            (
                remote(0, A.at[:, NZL], A.at[:, 0], (me, mv, lax.rem(mp + 1, SPAN))),
                mp < SPAN - 1,
                mp > 0,
            ),
            (
                remote(1, A.at[:, 1], A.at[:, NZL + 1], (me, mv, lax.rem(mp + SPAN - 1, SPAN))),
                mp > 0,
                mp < SPAN - 1,
            ),
            (remote(2, YS.at[s, q], YR.at[s, 1 - q], outer_id), has_outer, has_outer),
            (remote(3, YS.at[s, 1 - q], YR.at[s, q], (partner, mv, mp)), None, None),
        )
        each(copies, 1, lambda c: c.start())
        return copies

    def each(copies, which, act):
        for item in copies:
            if item[which] is None:
                act(item[0])
            else:
                pl.when(item[which])(functools.partial(act, item[0]))

    first_halo = []
    for i, step in enumerate((-1, 1)):
        for core in range(2):
            first_halo.append(
                (
                    pltpu.make_async_remote_copy(
                        src_ref=start_h.at[:, (0, NZL - 1)[i], :, pl.ds(core * LANES, LANES)],
                        dst_ref=A1.at[:, (NZL + 1, 0)[i], q],
                        send_sem=fz_send.at[i, core],
                        recv_sem=fz_recv.at[i, q],
                        device_id=(2 * chip + core, mv, mp + step),
                        device_id_type=MESH,
                    ),
                    has_p[i],
                )
            )
    for copy, there in first_halo:
        pl.when(there)(copy.start)

    for i, step in enumerate((-1, 1)):
        copy = pltpu.make_async_remote_copy(
            src_ref=YF.at[i],
            dst_ref=YR.at[0, 1 - i, q],
            send_sem=fv_send.at[i],
            recv_sem=fv_recv.at[q],
            device_id=(2 * chip + 1 - i, mv + step, mp),
            device_id_type=MESH,
        )
        first_halo.append((copy, has_v[i]))
        pl.when(has_v[i])(copy.start)
    middle = pltpu.make_async_remote_copy(
        src_ref=YF.at[2 + q],
        dst_ref=YR.at[0, q, q],
        send_sem=fv_send.at[2],
        recv_sem=fv_recv.at[2],
        device_id=(partner, mv, mp),
        device_id_type=MESH,
    )
    middle.start()
    YR[0, 1 - q, q] = YF[3 - q]

    def first_arrivals():
        for i in range(2):
            for sender in range(2):
                slab = A1.at[:, (0, NZL + 1)[i], sender]
                pl.when(has_p[i])(
                    lambda: pltpu.make_async_copy(slab, slab, fz_recv.at[1 - i, sender]).wait()
                )
        for sender in range(2):
            pl.when(has_outer)(
                lambda: pltpu.make_async_copy(YF.at[0], YF.at[0], fv_recv.at[sender]).wait()
            )
        middle.wait_recv()

    for i in range(3, 5):
        side_copies[i].start()

    for i in (1, 2):
        own_copies[i].wait()
        side_copies[i].wait_recv()

    pl.semaphore_wait(LT.at[0], in_near)
    call_inside(LT.at[1])

    def flat(ref):
        count = 1
        for size in ref.shape[:-1]:
            count *= size
        return ref.reshape(count, LANES)

    velocity2, penalty2 = flat(VEL), flat(PEN)
    ip2, m2, f2 = flat(IP), flat(M1), flat(F1)
    l2, r2, p2 = flat(LL), flat(RC), flat(PP)

    def level(ref2, x, c=0):
        return ref2[pl.ds(c * NZL * NXC + x, NZL, stride=NXC), :]

    delta = jnp.ones((NZL, LANES), F32)
    for x in range(NXC):
        u = level(velocity2, x, 0)
        west = stream_coef + stream_conv * jnp.maximum(-u, 0.0)
        east = stream_coef + stream_conv * jnp.maximum(u, 0.0)
        excess = (
            (4.0 * cross_coef + shift_coef)
            + cross_conv * (jnp.abs(level(velocity2, x, 1)) + jnp.abs(level(velocity2, x, 2)))
            + level(penalty2, x)
        )
        sink = excess + west * delta
        ip = 1.0 / (east + sink)
        delta = sink * ip
        place = pl.ds(x, NZL, stride=NXC)
        ip2[place, :] = ip
        m2[place, :] = west * ip
        f2[place, :] = east * ip

    def ahead(v, n, fill):
        return jnp.where(row >= n, pltpu.roll(v, n, 0), fill)

    def behind(v, n, fill):
        return jnp.where(row < 8 - n, pltpu.roll(v, 8 - n, 0), fill)

    def fold_up(values, f1, f2, f4, ft):
        new = []
        for h in range(2):
            v = values[h]
            v = v + f1[h] * pltpu.roll(v, 7, 0)
            v = v + f2[h] * pltpu.roll(v, 6, 0)
            v = v + f4[h] * pltpu.roll(v, 4, 0)
            new.append(v)
        new[0] = new[0] + ft * jnp.broadcast_to(new[1][0:1], (8, LANES))
        return new

    def factor(z, carry):
        chains = []
        tails = []
        f1s, f2s, f4s, fts = [], [], [], []
        for h in range(2):
            m = M1[z, h]
            f = F1[z, h]
            m1 = jnp.where(row >= 1, m, 0.0)
            mm = m1 * ahead(m, 1, 0.0)
            m4 = jnp.where(row >= 4, jnp.where(row >= 2, mm, 0.0) * pltpu.roll(mm, 2, 0), 0.0)
            mm = jnp.where(row >= 2, mm, 0.0)
            M1[z, h] = m1
            M2[z, h] = mm
            M4[z, h] = m4
            t = m * ahead(m, 1, 1.0)
            t = t * ahead(t, 2, 1.0)
            chains.append(t * ahead(t, 4, 1.0))
            f1 = jnp.where(row < 7, f, 0.0)
            ff = jnp.where(row < 6, f1 * behind(f, 1, 0.0), 0.0)
            f4 = jnp.where(row < 4, ff * pltpu.roll(ff, 6, 0), 0.0)
            F1[z, h] = f1
            F2[z, h] = ff
            F4[z, h] = f4
            f1s.append(f1)
            f2s.append(ff)
            f4s.append(f4)
            t = f * behind(f, 1, 1.0)
            t = t * behind(t, 2, 1.0)
            tails.append(t * behind(t, 4, 1.0))
        MT[z] = chains[1]
        FT[z] = tails[0]
        left = [chains[0], chains[1] * jnp.broadcast_to(chains[0][7:8], (8, LANES))]
        left = fold_up(left, f1s, f2s, f4s, tails[0])
        right = [tails[0] * jnp.broadcast_to(tails[1][0:1], (8, LANES)), tails[1]]
        for h in range(2):
            LL[z, h] = left[h]
            RC[z, h] = right[h]
        return carry

    lax.fori_loop(0, NZL, factor, 0)
    for k, ref2 in enumerate((l2, r2)):
        MS[2 * k] = level(ref2, 0)
        MS[2 * k + 1] = level(ref2, NXC - 1)

    def to_chips(src_of, dst, send_sem, recv_sem):
        for j in FAR_FIRST:
            target = lax.rem(chip + j, CHIPS)
            pltpu.make_async_remote_copy(
                src_ref=src_of(target),
                dst_ref=dst.at[chip],
                send_sem=send_sem,
                recv_sem=recv_sem,
                device_id=(2 * target + q, mv, mp),
                device_id_type=MESH,
            ).start()

    def arrive(slots, sem):
        got = slots.at[pl.ds(1, CHIPS - 1)]
        pltpu.make_async_copy(got, got, sem).wait()

    pl.semaphore_wait(LT.at[1], in_near)

    @pl.when(jnp.logical_not(upper))
    def _():
        pl.semaphore_wait(LD, 4)

    call(LT.at[2], (partner, mv, mp))

    my_o = lax.rem(chip + FIRST, CHIPS)
    is_owner = my_o < OWNERS
    owner_sends = jnp.where(is_owner, OWNERS - 1, OWNERS)

    def to_owners(src_of, dst, send_sem, recv_sem):
        for j in FAR_FIRST:
            target = lax.rem(chip + j, CHIPS)
            o = lax.rem(target + FIRST, CHIPS)

            @pl.when(o < OWNERS)
            def _():
                pltpu.make_async_remote_copy(
                    src_ref=src_of(o),
                    dst_ref=dst,
                    send_sem=send_sem,
                    recv_sem=recv_sem,
                    device_id=(2 * target + q, mv, mp),
                    device_id_type=MESH,
                ).start()

        @pl.when(is_owner)
        def _():
            pltpu.make_async_copy(src_of(my_o), dst, recv_sem).start()

    for k in range(4):
        value = MS[k]
        for o in range(OWNERS):
            QS[k, o] = value[ROWS * o : ROWS * o + ROWS]
    to_owners(lambda o: QS.at[:, o], QR.at[chip], q_send, q_recv)

    for i in (3,):
        own_copies[i].wait()
        side_copies[i].wait_recv()

    first = lane == 0
    last = lane == LANES - 1

    def eliminate(s, A, low, count, unroll):
        if s is not None:
            edges = [[YR[s, side, h] for h in range(2)] for side in range(2)]

        def plane(z, carry):
            cross = []
            for h in range(2):
                v = VEL[1, z, h]
                w = VEL[2, z, h]
                cross.append(
                    (
                        cross_coef + cross_conv * jnp.maximum(-v, 0.0),
                        cross_coef + cross_conv * jnp.maximum(v, 0.0),
                        cross_coef + cross_conv * jnp.maximum(-w, 0.0),
                        cross_coef + cross_conv * jnp.maximum(w, 0.0),
                    )
                )
            ip = [IP[z, h] for h in range(2)]
            m1 = [M1[z, h] for h in range(2)]
            m2 = [M2[z, h] for h in range(2)]
            m4 = [M4[z, h] for h in range(2)]
            f1 = [F1[z, h] for h in range(2)]
            f2 = [F2[z, h] for h in range(2)]
            f4 = [F4[z, h] for h in range(2)]
            mt = MT[z]
            ft = FT[z]
            for c in range(NC):
                k = c * NZL + z
                o = []
                for h in range(2):
                    south, north, below, above = cross[h]
                    a = A[c, z + 1, h]
                    lo = hi = blank
                    if s is not None:
                        lo = pltpu.roll(edges[0][h], lax.rem(LANES - k, LANES), 1)
                        hi = pltpu.roll(edges[1][h], LANES - 1 - k, 1)
                    y_lo = jnp.where(first, lo, pltpu.roll(a, 1, 1))
                    y_hi = jnp.where(last, hi, pltpu.roll(a, LANES - 1, 1))
                    rhs = SRC[c, z, h] + shift_coef * a
                    rhs = rhs + south * y_lo + north * y_hi
                    rhs = rhs + below * A[c, z, h] + above * A[c, z + 2, h]
                    v = rhs * ip[h]
                    v = v + m1[h] * pltpu.roll(v, 1, 0)
                    v = v + m2[h] * pltpu.roll(v, 2, 0)
                    v = v + m4[h] * pltpu.roll(v, 4, 0)
                    o.append(v)
                o[1] = o[1] + mt * jnp.broadcast_to(o[0][7:8], (8, LANES))
                p = fold_up(o, f1, f2, f4, ft)
                for h in range(2):
                    PP[c, z, h] = p[h]
            return carry

        lax.fori_loop(low, low + count, plane, 0, unroll=unroll)

    own_copies[0].wait()
    side_copies[0].wait_recv()
    first_arrivals()
    pl.semaphore_wait(LP.at[0], v_near)
    call_line(LP.at[1], True)
    eliminate(0, A1, 0, NZL, 12)
    for c in range(NC):
        for i, x in enumerate((0, NXC - 1)):
            value = level(p2, x, c)
            for o in range(OWNERS):
                S1[i, c, o] = value[ROWS * o : ROWS * o + ROWS]
    to_owners(lambda o: S1.at[:, :, o], G1.at[chip], p_send.at[0], p_recv.at[0])
    pl.semaphore_wait(LP.at[1], v_near)
    call_line(LP.at[2], False)
    to_chips(lambda target: MS, MR, m_send, m_recv)

    own_copies[4].wait()
    side_copies[4].wait_recv()

    def indicator(digit, count):
        return jnp.concatenate(
            [jnp.where(digit == i, 1.0, 0.0) for i in range(count)], axis=0
        ).astype(jnp.bfloat16)

    digit32 = lax.broadcasted_iota(jnp.int32, (32, LANES), 0)

    def onehot(z, carry):
        for h in range(2):
            cut = slice(h * LANES, (h + 1) * LANES)
            low = lax.rem(BAND[z, h], 32)
            OHL[z, :, cut] = jnp.concatenate(
                [
                    jnp.where(jnp.broadcast_to(low[x : x + 1], (32, LANES)) == digit32, 1.0, 0.0)
                    for x in range(8)
                ],
                axis=0,
            ).astype(jnp.bfloat16)
            OHH[z, :, cut] = indicator(BAND[z, h] // 32, 8)
        return carry

    lax.fori_loop(0, NZL, onehot, 0)

    @pl.when(is_owner)
    def _():
        pltpu.make_async_copy(QR, QR, q_recv).wait()
        ahead_f = jnp.zeros((ROWS, LANES), F32)
        for k in range(CHIPS):
            lf, lg, rf, rg = (QR[k, i] for i in range(4))
            inv = 1.0 / (1.0 - lf * ahead_f)
            b = lg * inv
            g = b * ahead_f
            for i, value in enumerate((g, b, inv, lf * inv, rf * inv, ahead_f)):
                CO[k, i] = value
            ahead_f = rg + g * rf

        pltpu.make_async_copy(G1, G1, p_recv.at[0]).wait()
        nil = jnp.zeros((ROWS, LANES), F32)
        O = [nil] * NC
        for k in range(CHIPS):
            for c in range(NC):
                OC[k, c] = O[c]
                O[c] = G1[k, 1, c] + CO[k, 0] * G1[k, 0, c] + CO[k, 1] * O[c]
        after = [nil] * NC
        for k in reversed(range(CHIPS)):
            for c in range(NC):
                D1[k, 1, c] = after[c]
                before = OC[k, c]
                after[c] = CO[k, 2] * G1[k, 0, c] + CO[k, 3] * before + CO[k, 4] * after[c]
                D1[k, 0, c] = CO[k, 5] * after[c] + before

        for j in FAR_FIRST:
            target = lax.rem(chip + j, CHIPS)
            pltpu.make_async_remote_copy(
                src_ref=D1.at[target],
                dst_ref=R1.at[:, :, my_o],
                send_sem=d_send,
                recv_sem=d_recv,
                device_id=(2 * target + q, mv, mp),
                device_id_type=MESH,
            ).start()

        pltpu.make_async_copy(D1.at[chip], R1.at[:, :, my_o], d_recv).start()

    arrive(MR, m_recv)

    row_z = lax.broadcasted_iota(jnp.int32, (NZL, LANES), 0)
    lane_z = lax.broadcasted_iota(jnp.int32, (NZL, LANES), 1)

    def write_edges(ref, values):
        packed = jnp.zeros((NZL, LANES), F32)
        for c in range(NC):
            v = values[c]
            for side in range(2):
                ref[2 * c + side : 2 * c + side + 1, :] = v[
                    side * (NZL - 1) : side * (NZL - 1) + 1
                ]
                column = v[:, side * (LANES - 1) : side * (LANES - 1) + 1]
                packed = jnp.where(
                    lane_z == NZL * (2 * c + side) + row_z,
                    jnp.broadcast_to(column, (NZL, LANES)),
                    packed,
                )
        ref[6:7, :] = jnp.sum(packed, axis=0, keepdims=True)
        ref[7:8, :] = jnp.zeros((1, LANES), F32)

    def upstream(k, F):
        lf, lg, rf, rg = (MR[k, i] for i in range(4))
        b = lg / (1.0 - lf * F)
        g = b * F
        CB[k] = b
        return rg + g * rf

    def downstream(i, H):
        k = CHIPS - 1 - i
        lf, lg, rf, rg = (MR[k, i] for i in range(4))
        b = rf / (1.0 - rg * H)
        g = b * H
        CB[k] = b
        return lf + g * lg

    none = jnp.zeros((NZL, LANES), F32)
    F = lax.fori_loop(0, chip, upstream, none)
    H = lax.fori_loop(0, CHIPS - 1 - chip, downstream, none)
    lf, lg, rf, rg = (MS[i] for i in range(4))
    from_left = 1.0 - lf * F
    from_right = 1.0 - rg * H
    inv = 1.0 / (from_left * from_right - (F * rf) * (H * lg))
    for i, value in enumerate(
        (
            F,
            H,
            from_right * inv,
            F * rf * inv,
            H * lg * inv,
            from_left * inv,
            lg / from_left * F,
            rf / from_right * H,
        )
    ):
        OWN[i] = value

    def close(incoming):
        for c in range(NC):
            first_p = level(p2, 0, c)
            last_p = level(p2, NXC - 1, c)
            x = OWN[0] * first_p + incoming[0][c]
            y = OWN[1] * last_p + incoming[1][c]
            AL[c] = OWN[2] * x + OWN[3] * y
            AR[c] = OWN[4] * x + OWN[5] * y

    def solved(c, z, h):
        return (
            PP[c, z, h]
            + LL[z, h] * jnp.broadcast_to(AL[c, pl.ds(z, 1), :], (8, LANES))
            + RC[z, h] * jnp.broadcast_to(AR[c, pl.ds(z, 1), :], (8, LANES))
        )

    pltpu.make_async_copy(R1, R1, d_recv).wait()
    pl.semaphore_wait(LP.at[2], p_near)
    call_line(LP.at[3], False)
    trio = (none,) * NC
    for c in range(NC):
        for o in range(OWNERS):
            AL[c, ROWS * o : ROWS * o + ROWS, :] = R1[0, c, o]
            AR[c, ROWS * o : ROWS * o + ROWS, :] = R1[1, c, o]

    def line_first(z, packs):
        for c in range(NC):
            pair = tuple(solved(c, z, h) for h in range(2))
            for h in range(2):
                A2[c, z + 1, h] = pair[h]
            packs = pack_edges(c * NZL + z, pair, packs)
        return packs

    halo2 = send_halo(1, A2, lax.fori_loop(0, NZL, line_first, no_packs, unroll=4))

    def ends(write):
        for c in range(NC):
            first_p = level(p2, 0, c)
            last_p = level(p2, NXC - 1, c)
            write(c, last_p + OWN[6] * first_p, first_p + OWN[7] * last_p)

    def write_rows(c, up, down):
        S2[0, c] = up
        S2[1, c] = down

    def side_of(target):
        return jnp.where(target > chip, 0, 1)

    eliminate(None, A2, 1, NZL - 2, 5)
    ends(write_rows)
    to_chips(lambda target: S2.at[side_of(target)], R2, p_send.at[1], p_recv.at[1])

    def edge_coefficients(k, carry):
        write_edges(CE.at[k], (CB[k],) * NC)
        return carry

    lax.fori_loop(0, chip, edge_coefficients, 0)
    lax.fori_loop(chip + 1, CHIPS, edge_coefficients, 0)

    each(halo2, 2, lambda c: c.wait_recv())
    pl.semaphore_wait(LP.at[3], p_near)
    call_line(LP.at[4], False)
    eliminate(1, A2, 0, NZL, 12)
    final = ([], [])

    def keep_ends(c, up, down):
        final[0].append(up)
        final[1].append(down)

    ends(keep_ends)
    for i in range(2):
        write_edges(E2.at[i], final[i])
    to_chips(lambda target: E2.at[side_of(target)], RE, e_send, e_recv)
    ways = ((chip, lambda i: i), (CHIPS - 1 - chip, lambda i: CHIPS - 1 - i))
    arrive(R2, p_recv.at[1])

    def bring(k, O):
        return tuple(R2[k, c] + CB[k] * O[c] for c in range(NC))

    rows_brought = [
        lax.fori_loop(0, steps, lambda i, v: bring(chip_of(i), v), trio) for steps, chip_of in ways
    ]
    arrive(RE, e_recv)

    def brought(O, way):
        steps, chip_of = way
        edge = lax.fori_loop(
            0, steps, lambda i, v: RE[chip_of(i)] + CE[chip_of(i)] * v, blank
        )
        packed = jnp.broadcast_to(edge[6:7], (NZL, LANES))
        whole = []
        for c in range(NC):
            value = O[c]
            for side in range(2):
                at = lane_z == NZL * (2 * c + side) + row_z
                column = jnp.sum(jnp.where(at, packed, 0.0), axis=1, keepdims=True)
                value = jnp.where(
                    lane_z == side * (LANES - 1), jnp.broadcast_to(column, (NZL, LANES)), value
                )
            for side in range(2):
                value = jnp.where(
                    row_z == side * (NZL - 1),
                    jnp.broadcast_to(edge[2 * c + side : 2 * c + side + 1], (NZL, LANES)),
                    value,
                )
            whole.append(value)
        return whole

    close(
        (
            brought(rows_brought[0], ways[0]),
            brought(rows_brought[1], ways[1]),
        )
    )

    pl.semaphore_wait(LT.at[2], 1)
    pl.semaphore_wait(LP.at[4], p_near)

    def line_last(z, acc):
        parts = ([], [])
        for h in range(2):
            total = None
            for c in range(NC):
                a = solved(c, z, h)
                A3[c, z, h] = a
                term = VEL[c, z, h] * a
                total = term if total is None else total + term
            total = total * PEN[z, h]
            coarse = total.astype(jnp.bfloat16).astype(F32)
            for part, value in zip(parts, (coarse, total - coarse)):
                part.append(jnp.concatenate([value, value], axis=0).astype(jnp.bfloat16))
        weights = jnp.concatenate(
            [
                jnp.concatenate([jnp.concatenate(part, axis=1)] * 4, axis=0) * OHH[z]
                for part in parts
            ],
            axis=0,
        )
        return acc + lax.dot_general(
            weights, OHL[z], (((1,), (1,)), ((), ())), preferred_element_type=F32
        )

    acc = lax.fori_loop(0, NZL, line_last, jnp.zeros((LANES, 2 * LANES), F32), unroll=12)
    acc = acc[0:64] + acc[64:128]
    keep = [lane // 32 + 4 * r == row for r in range(2)]
    tall = blank
    for j in range(8):
        tile = acc[8 * j : 8 * j + 8]
        own_x = jnp.where(keep[0], tile[:, 0:LANES], 0.0) + jnp.where(
            keep[1], tile[:, LANES : 2 * LANES], 0.0
        )
        line = jnp.sum(own_x, axis=0, keepdims=True)
        tall = jnp.where(row == j, jnp.broadcast_to(line, (8, LANES)), tall)
    tall = tall + pltpu.roll(tall, 64, 1)
    tall = tall + pltpu.roll(tall, 32, 1)
    for r in range(2):
        B1S[r : r + 1, :] = jnp.sum(jnp.where(keep[r], tall, 0.0), axis=0, keepdims=True)

    def band_round(r, own, slots, order, device_of, beside):
        for j in order:
            pltpu.make_async_remote_copy(
                src_ref=own,
                dst_ref=slots.at[j],
                send_sem=b_send.at[r],
                recv_sem=b_recv.at[r],
                device_id=device_of(j),
                device_id_type=MESH,
            ).start()
        beside()
        got = slots.at[pl.ds(1, STREAM - 1)]
        pltpu.make_async_copy(got, got, b_recv.at[r]).wait()
        terms = [own[...]] + [slots[j] for j in range(1, STREAM)]
        while len(terms) > 1:
            terms = [terms[i] + terms[i + 1] for i in range(0, len(terms), 2)]
        return terms[0]

    def drain(count, ref, sem):
        def one(j, carry):
            pltpu.make_async_copy(ref, ref, sem).wait()
            return carry

        lax.fori_loop(0, count, one, 0)

    def sent(bytes_like, sem):
        pltpu.make_async_copy(bytes_like, bytes_like, sem).wait()

    out_own = pltpu.make_async_copy(A3.at[:, :, q], out_h.at[:, :, :, lanes_of(q)], out_sem.at[0])
    out_side = pltpu.make_async_remote_copy(
        src_ref=A3.at[:, :, 1 - q],
        dst_ref=out_h.at[:, :, :, lanes_of(q)],
        send_sem=out_sem.at[1],
        recv_sem=out_sem.at[2],
        device_id=(partner, mv, mp),
        device_id_type=MESH,
    )

    def beside_first():
        out_own.start()
        out_side.start()
        for copy in side_copies:
            copy.wait_send()
        for copy, there in first_halo:
            pl.when(there)(copy.wait_send)
        middle.wait_send()
        each(halo2, 1, lambda c: c.wait_send())
        others = pl.ds(1, CHIPS - 1)
        sent(MR.at[others], m_send)
        sent(R2.at[others], p_send.at[1])
        sent(RE.at[others], e_send)
        drain(owner_sends, QS.at[:, 0], q_send)
        drain(owner_sends, S1.at[:, :, 0], p_send.at[0])

        @pl.when(is_owner)
        def _():
            sent(D1.at[others], d_send)

        tb_copy.wait()
        tw_copy.wait()

    def beside_second():
        sent(B1R.at[pl.ds(1, STREAM - 1)], b_send.at[0])
        out_own.wait()
        out_side.wait()

    line_order = (8, 7, 9, 6, 10, 5, 11, 4, 12, 3, 13, 2, 14, 1, 15)
    plane_order = (10, 6, 9, 11, 14, 2, 8, 5, 7, 13, 15, 1, 3, 4, 12)
    B2S[...] = band_round(
        0, B1S, B1R, line_order, lambda j: (lax.rem(me + j, STREAM), mv, mp), beside_first
    )
    bands = band_round(
        1,
        B2S,
        B2R,
        plane_order,
        lambda j: (me, lax.rem(mv + j // SPAN, VERT), lax.rem(mp + j % SPAN, SPAN)),
        beside_second,
    )
    cells = STREAM * VERT * SPAN * NXL * NZL * NYL
    bands = bands * ((NBANDS / cells) ** 0.5)
    tb = TB[...].reshape(1, LANES)
    spot = lax.rem(tb, LANES)
    spot = jnp.broadcast_to(spot, (8, LANES))
    low_half = jnp.take_along_axis(jnp.broadcast_to(bands[0:1], (8, LANES)), spot, axis=1)
    high_half = jnp.take_along_axis(jnp.broadcast_to(bands[1:2], (8, LANES)), spot, axis=1)
    picked = jnp.where(tb < LANES, low_half[0:1], high_half[0:1])
    tri_ref[...] = (TW[...].reshape(1, LANES) * picked).reshape(LANES)
    sent(B2R.at[pl.ds(1, STREAM - 1)], b_send.at[1])


def shards(adjoint_source, velocity, penalty, adjoint_start, cell_band, tri_band, tri_weight):
    anywhere = pl.BlockSpec(memory_space=pl.ANY)

    def field():
        return pltpu.VMEM((NZL, 2, 8, LANES), F32)

    scratch = [
        pltpu.VMEM((NC, NZL, 2, 8, LANES), F32),
        pltpu.VMEM((NC, NZL, 2, 8, LANES), F32),
        field(),
        pltpu.VMEM((NZL, 2, 8, LANES), jnp.int32),
        pltpu.VMEM((NC, NZL + 2, 2, 8, LANES), F32),
        pltpu.VMEM((NC, NZL + 2, 2, 8, LANES), F32),
        pltpu.VMEM((NC, NZL, 2, 8, LANES), F32),
        pltpu.VMEM((NC, NZL, 2, 8, LANES), F32),
        field(),
        field(),
        field(),
        field(),
        pltpu.VMEM((NZL, 8, LANES), F32),
        field(),
        field(),
        field(),
        pltpu.VMEM((NZL, 8, LANES), F32),
        field(),
        field(),
        pltpu.VMEM((NC, NZL, NXL, NYL), F32),
        pltpu.VMEM((4, 8, LANES), F32),
        pltpu.VMEM((SWEEPS, 2, 2, 8, LANES), F32),
        pltpu.VMEM((SWEEPS, 2, 2, 8, LANES), F32),
        pltpu.VMEM((4, NZL, LANES), F32),
        pltpu.VMEM((CHIPS, 4, NZL, LANES), F32),
        pltpu.VMEM((CHIPS, NZL, LANES), F32),
        pltpu.VMEM((CHIPS, 8, LANES), F32),
        pltpu.VMEM((8, NZL, LANES), F32),
        pltpu.VMEM((4, OWNERS, ROWS, LANES), F32),
        pltpu.VMEM((CHIPS, 4, ROWS, LANES), F32),
        pltpu.VMEM((CHIPS, 6, ROWS, LANES), F32),
        pltpu.VMEM((CHIPS, NC, ROWS, LANES), F32),
        pltpu.VMEM((2, NC, OWNERS, ROWS, LANES), F32),
        pltpu.VMEM((CHIPS, 2, NC, ROWS, LANES), F32),
        pltpu.VMEM((CHIPS, 2, NC, ROWS, LANES), F32),
        pltpu.VMEM((2, NC, OWNERS, ROWS, LANES), F32),
        pltpu.VMEM((2, NC, NZL, LANES), F32),
        pltpu.VMEM((CHIPS, NC, NZL, LANES), F32),
        pltpu.VMEM((2, 8, LANES), F32),
        pltpu.VMEM((CHIPS, 8, LANES), F32),
        pltpu.VMEM((NC, NZL, LANES), F32),
        pltpu.VMEM((NC, NZL, LANES), F32),
        pltpu.VMEM((NZL, 64, 2 * LANES), jnp.bfloat16),
        pltpu.VMEM((NZL, 2 * LANES, 2 * LANES), jnp.bfloat16),
        pltpu.VMEM((2, LANES), F32),
        pltpu.VMEM((STREAM, 2, LANES), F32),
        pltpu.VMEM((2, LANES), F32),
        pltpu.VMEM((STREAM, 2, LANES), F32),
        pltpu.VMEM((LANES,), jnp.int32),
        pltpu.VMEM((LANES,), F32),
        pltpu.SemaphoreType.DMA((6,)),
        pltpu.SemaphoreType.DMA((5,)),
        pltpu.SemaphoreType.DMA((5,)),
        pltpu.SemaphoreType.DMA((3,)),
        pltpu.SemaphoreType.DMA((2,)),
        pltpu.SemaphoreType.REGULAR((3,)),
        pltpu.SemaphoreType.REGULAR,
        pltpu.SemaphoreType.REGULAR((5,)),
        pltpu.SemaphoreType.DMA((2, 2)),
        pltpu.SemaphoreType.DMA((2, 2)),
        pltpu.SemaphoreType.DMA((3,)),
        pltpu.SemaphoreType.DMA((3,)),
        pltpu.SemaphoreType.DMA((SWEEPS, 4)),
        pltpu.SemaphoreType.DMA((SWEEPS, 4)),
        pltpu.SemaphoreType.DMA,
        pltpu.SemaphoreType.DMA,
        pltpu.SemaphoreType.DMA,
        pltpu.SemaphoreType.DMA,
        pltpu.SemaphoreType.DMA,
        pltpu.SemaphoreType.DMA,
        pltpu.SemaphoreType.DMA((SWEEPS,)),
        pltpu.SemaphoreType.DMA((SWEEPS,)),
        pltpu.SemaphoreType.DMA,
        pltpu.SemaphoreType.DMA,
        pltpu.SemaphoreType.DMA((2,)),
        pltpu.SemaphoreType.DMA((2,)),
    ]

    def planes(x):
        return jnp.swapaxes(x, -3, -2)

    adjoint, tri_grad = pl.pallas_call(
        kernel,
        out_shape=(
            jax.ShapeDtypeStruct((NC, NZL, NXL, NYL), F32),
            jax.ShapeDtypeStruct((LANES,), F32),
        ),
        in_specs=[pl.BlockSpec(memory_space=pltpu.HBM)] * 7,
        out_specs=(anywhere, pl.BlockSpec(memory_space=pltpu.VMEM)),
        scratch_shapes=scratch,
        compiler_params=pltpu.CompilerParams(
            collective_id=0, has_side_effects=True, vmem_limit_bytes=32 * 1024 * 1024
        ),
    )(
        *(
            pltpu.with_memory_space_constraint(x, pltpu.HBM)
            for x in (
                planes(adjoint_source),
                planes(velocity),
                planes(penalty),
                planes(adjoint_start),
                planes(cell_band),
                tri_band,
                tri_weight,
            )
        )
    )
    return planes(adjoint), tri_grad


def solution(mesh):
    return jax.shard_map(
        shards,
        mesh=mesh,
        in_specs=(
            P(None, "stream", "span", "vert"),
            P(None, "stream", "span", "vert"),
            P("stream", "span", "vert"),
            P(None, "stream", "span", "vert"),
            P("stream", "span", "vert"),
            P(("stream", "vert", "span")),
            P(("stream", "vert", "span")),
        ),
        out_specs=(P(None, "stream", "span", "vert"), P(("stream", "vert", "span"))),
        check_vma=False,
    )
```

```python
import functools

import jax
import jax.numpy as jnp
from jax import lax
from jax.experimental import pallas as pl
from jax.experimental.pallas import tpu as pltpu
from jax.sharding import PartitionSpec as P

SWEEPS = 2
NBANDS = 256

STREAM = 16
CHIPS = 8
VERT = 4
SPAN = 4
NC = 3
NXL = 8
NXC = 16
NZL = 12
NYL = 256
LANES = 128
OWNERS = 6
ROWS = NZL // OWNERS
FIRST = 2
FAR_FIRST = (4, 3, 5, 2, 6, 1, 7)

stream_coef = 1000.0
stream_conv = 200.0
cross_coef = 0.25
cross_conv = 0.25
shift_coef = 0.5

MESH = pl.DeviceIdType.MESH
F32 = jnp.float32


def kernel(
    src_h,
    vel_h,
    pen_h,
    start_h,
    band_h,
    tb_h,
    tw_h,
    out_h,
    tri_ref,
    SRC,
    VEL,
    PEN,
    BAND,
    A1,
    A2,
    A3,
    PP,
    IP,
    M1,
    M2,
    M4,
    MT,
    F1,
    F2,
    F4,
    FT,
    LL,
    RC,
    STG,
    YF,
    YS,
    YR,
    MS,
    MR,
    CB,
    CE,
    OWN,
    QS,
    QR,
    CO,
    OC,
    S1,
    G1,
    D1,
    R1,
    S2,
    R2,
    E2,
    RE,
    AL,
    AR,
    OHH,
    OHL,
    B1S,
    B1R,
    B2S,
    B2R,
    TB,
    TW,
    in_sem,
    side_send,
    side_recv,
    out_sem,
    tri_sem,
    LT,
    LD,
    LP,
    fz_send,
    fz_recv,
    fv_send,
    fv_recv,
    halo_send,
    halo_recv,
    m_send,
    m_recv,
    q_send,
    q_recv,
    d_send,
    d_recv,
    p_send,
    p_recv,
    e_send,
    e_recv,
    b_send,
    b_recv,
):
    me = lax.axis_index("stream")
    mv = lax.axis_index("vert")
    mp = lax.axis_index("span")
    chip = me // 2
    q = lax.rem(me, 2)
    partner = 2 * chip + (1 - q)

    def lanes_of(half):
        return pl.ds(pl.multiple_of(half * LANES, LANES), LANES)

    def pieces(ref, dst):
        rank = len(ref.shape)
        lead = (slice(None),) * (rank - 1)
        return lambda half: ref.at[lead + (lanes_of(half),)], dst

    inner = A1.at[:, pl.ds(1, NZL)]
    inputs = (
        (start_h, inner),
        (vel_h, VEL),
        (pen_h, PEN),
        (src_h, SRC),
        (band_h, BAND),
    )

    def slot(dst, half):
        if len(dst.shape) == 5:
            return dst.at[:, :, half]
        return dst.at[:, half]

    def part(src, half):
        if len(src.shape) == 4:
            return src.at[:, :, :, lanes_of(half)]
        return src.at[:, :, lanes_of(half)]

    own_copies = []
    side_copies = []
    for i, (src, dst) in enumerate(inputs):
        own_copies.append(pltpu.make_async_copy(part(src, q), slot(dst, q), in_sem.at[i]))
        side_copies.append(
            pltpu.make_async_remote_copy(
                src_ref=part(src, 1 - q),
                dst_ref=slot(dst, q),
                send_sem=side_send.at[i],
                recv_sem=side_recv.at[i],
                device_id=(partner, mv, mp),
                device_id_type=MESH,
            )
        )
    stage = pltpu.make_async_copy(start_h, STG, in_sem.at[5])
    stage.start()
    for i in (1, 2, 0, 3, 4):
        own_copies[i].start()
    tb_copy = pltpu.make_async_copy(tb_h, TB, tri_sem.at[0])
    tw_copy = pltpu.make_async_copy(tw_h, TW, tri_sem.at[1])

    barrier = pltpu.get_barrier_semaphore()

    def either(condition):
        return jnp.where(condition, 1, 0)

    has_v = (mv > 0, mv < VERT - 1)
    has_p = (mp > 0, mp < SPAN - 1)
    v_near = either(has_v[0]) + either(has_v[1])
    p_near = either(has_p[0]) + either(has_p[1])

    def call(sem, device):
        pl.semaphore_signal(sem, inc=1, device_id=device, device_id_type=MESH)

    def stream_at(step):
        return (lax.rem(me + 2 * step + STREAM, STREAM), mv, mp)

    def call_line(sem, along_v):
        for i, step in enumerate((-1, 1)):
            if along_v:
                pl.when(has_v[i])(lambda: call(sem, (me, mv + step, mp)))
            else:
                pl.when(has_p[i])(lambda: call(sem, (me, mv, mp + step)))

    outer_v = mv - 1 + 2 * q
    has_outer = jnp.logical_and(outer_v >= 0, outer_v < VERT)
    outer_id = (partner, lax.rem(outer_v + VERT, VERT), mp)

    nothing = jnp.zeros((2, 8, LANES), F32)
    for A in (A1, A2):
        for c in range(NC):
            A[c, 0] = nothing
            A[c, NZL + 1] = nothing
    YR[...] = jnp.zeros(YR.shape, F32)

    upper = chip >= CHIPS // 2
    inside = (lax.rem(chip, 4) > 0, lax.rem(chip, 4) < 3)
    in_near = either(inside[0]) + either(inside[1])
    from_lower = either(upper) * (4 - either(jnp.logical_or(chip == 4, chip == 7)))

    def chip_at(target):
        return (2 * target + q, mv, mp)

    def call_inside(sem):
        for i, step in enumerate((-1, 1)):
            pl.when(inside[i])(lambda: call(sem, chip_at(chip + step)))

    for target in range(4, CHIPS):
        apart = jnp.logical_and(chip != target - 1, lax.rem(target + 1, CHIPS) != chip)
        pl.when(jnp.logical_and(jnp.logical_not(upper), apart))(
            lambda: call(barrier, chip_at(target))
        )
    call(barrier, (partner, mv, mp))
    call(barrier, stream_at(-1))
    call(barrier, stream_at(1))
    for i, step in enumerate((-1, 1)):
        for core in range(2):
            other = 2 * chip + core
            pl.when(has_v[i])(lambda: call(barrier, (other, mv + step, mp)))
            pl.when(has_p[i])(lambda: call(barrier, (other, mv, mp + step)))

    tb_copy.start()
    tw_copy.start()
    row = lax.broadcasted_iota(jnp.int32, (8, LANES), 0)
    lane = lax.broadcasted_iota(jnp.int32, (8, LANES), 1)

    def pack_edges(k, pair, packs):
        low, high = packs
        hit = lane == k
        low = tuple(jnp.where(hit, pltpu.roll(pair[h], k, 1), low[h]) for h in range(2))
        high = tuple(jnp.where(hit, pltpu.roll(pair[h], k + 1, 1), high[h]) for h in range(2))
        return low, high

    blank = jnp.zeros((8, LANES), F32)
    no_packs = ((blank, blank), (blank, blank))

    stage.wait()

    def pack_start(z, packs):
        low, high = packs
        for c in range(NC):
            pair = (STG[c, z, :, 0:LANES], STG[c, z, :, LANES:NYL])
            low, high = pack_edges(c * NZL + z, pair, (low, high))
        return low, high

    low, high = lax.fori_loop(0, NZL, pack_start, no_packs, unroll=4)
    for i, value in enumerate((low[0], high[1], high[0], low[1])):
        YF[i] = value
    pl.semaphore_wait(barrier, 3 + 2 * v_near + 2 * p_near + from_lower)
    for i in range(3):
        side_copies[i].start()
    for target in range(4):
        pl.when(upper)(lambda: call(LD, chip_at(target)))
    call_inside(LT.at[0])
    call_line(LP.at[0], True)

    def send_halo(s, A, packs):
        for side in range(2):
            for h in range(2):
                YS[s, side, h] = packs[side][h]

        def remote(i, src, dst, device):
            return pltpu.make_async_remote_copy(
                src_ref=src,
                dst_ref=dst,
                send_sem=halo_send.at[s, i],
                recv_sem=halo_recv.at[s, i],
                device_id=device,
                device_id_type=MESH,
            )

        copies = (
            (
                remote(0, A.at[:, NZL], A.at[:, 0], (me, mv, lax.rem(mp + 1, SPAN))),
                mp < SPAN - 1,
                mp > 0,
            ),
            (
                remote(1, A.at[:, 1], A.at[:, NZL + 1], (me, mv, lax.rem(mp + SPAN - 1, SPAN))),
                mp > 0,
                mp < SPAN - 1,
            ),
            (remote(2, YS.at[s, q], YR.at[s, 1 - q], outer_id), has_outer, has_outer),
            (remote(3, YS.at[s, 1 - q], YR.at[s, q], (partner, mv, mp)), None, None),
        )
        each(copies, 1, lambda c: c.start())
        return copies

    def each(copies, which, act):
        for item in copies:
            if item[which] is None:
                act(item[0])
            else:
                pl.when(item[which])(functools.partial(act, item[0]))

    first_halo = []
    for i, step in enumerate((-1, 1)):
        for core in range(2):
            first_halo.append(
                (
                    pltpu.make_async_remote_copy(
                        src_ref=start_h.at[:, (0, NZL - 1)[i], :, pl.ds(core * LANES, LANES)],
                        dst_ref=A1.at[:, (NZL + 1, 0)[i], q],
                        send_sem=fz_send.at[i, core],
                        recv_sem=fz_recv.at[i, q],
                        device_id=(2 * chip + core, mv, mp + step),
                        device_id_type=MESH,
                    ),
                    has_p[i],
                )
            )
    for copy, there in first_halo:
        pl.when(there)(copy.start)

    for i, step in enumerate((-1, 1)):
        copy = pltpu.make_async_remote_copy(
            src_ref=YF.at[i],
            dst_ref=YR.at[0, 1 - i, q],
            send_sem=fv_send.at[i],
            recv_sem=fv_recv.at[q],
            device_id=(2 * chip + 1 - i, mv + step, mp),
            device_id_type=MESH,
        )
        first_halo.append((copy, has_v[i]))
        pl.when(has_v[i])(copy.start)
    middle = pltpu.make_async_remote_copy(
        src_ref=YF.at[2 + q],
        dst_ref=YR.at[0, q, q],
        send_sem=fv_send.at[2],
        recv_sem=fv_recv.at[2],
        device_id=(partner, mv, mp),
        device_id_type=MESH,
    )
    middle.start()
    YR[0, 1 - q, q] = YF[3 - q]

    def first_arrivals():
        for i in range(2):
            for sender in range(2):
                slab = A1.at[:, (0, NZL + 1)[i], sender]
                pl.when(has_p[i])(
                    lambda: pltpu.make_async_copy(slab, slab, fz_recv.at[1 - i, sender]).wait()
                )
        for sender in range(2):
            pl.when(has_outer)(
                lambda: pltpu.make_async_copy(YF.at[0], YF.at[0], fv_recv.at[sender]).wait()
            )
        middle.wait_recv()

    for i in range(3, 5):
        side_copies[i].start()

    for i in (1, 2):
        own_copies[i].wait()
        side_copies[i].wait_recv()

    pl.semaphore_wait(LT.at[0], in_near)
    call_inside(LT.at[1])

    def flat(ref):
        count = 1
        for size in ref.shape[:-1]:
            count *= size
        return ref.reshape(count, LANES)

    velocity2, penalty2 = flat(VEL), flat(PEN)
    ip2, m2, f2 = flat(IP), flat(M1), flat(F1)
    l2, r2, p2 = flat(LL), flat(RC), flat(PP)

    def level(ref2, x, c=0):
        return ref2[pl.ds(c * NZL * NXC + x, NZL, stride=NXC), :]

    delta = jnp.ones((NZL, LANES), F32)
    for x in range(NXC):
        u = level(velocity2, x, 0)
        west = stream_coef + stream_conv * jnp.maximum(-u, 0.0)
        east = stream_coef + stream_conv * jnp.maximum(u, 0.0)
        excess = (
            (4.0 * cross_coef + shift_coef)
            + cross_conv * (jnp.abs(level(velocity2, x, 1)) + jnp.abs(level(velocity2, x, 2)))
            + level(penalty2, x)
        )
        sink = excess + west * delta
        ip = 1.0 / (east + sink)
        delta = sink * ip
        place = pl.ds(x, NZL, stride=NXC)
        ip2[place, :] = ip
        m2[place, :] = west * ip
        f2[place, :] = east * ip

    def ahead(v, n, fill):
        return jnp.where(row >= n, pltpu.roll(v, n, 0), fill)

    def behind(v, n, fill):
        return jnp.where(row < 8 - n, pltpu.roll(v, 8 - n, 0), fill)

    def fold_up(values, f1, f2, f4, ft):
        new = []
        for h in range(2):
            v = values[h]
            v = v + f1[h] * pltpu.roll(v, 7, 0)
            v = v + f2[h] * pltpu.roll(v, 6, 0)
            v = v + f4[h] * pltpu.roll(v, 4, 0)
            new.append(v)
        new[0] = new[0] + ft * jnp.broadcast_to(new[1][0:1], (8, LANES))
        return new

    def factor(z, carry):
        chains = []
        tails = []
        f1s, f2s, f4s, fts = [], [], [], []
        for h in range(2):
            m = M1[z, h]
            f = F1[z, h]
            m1 = jnp.where(row >= 1, m, 0.0)
            mm = m1 * ahead(m, 1, 0.0)
            m4 = jnp.where(row >= 4, jnp.where(row >= 2, mm, 0.0) * pltpu.roll(mm, 2, 0), 0.0)
            mm = jnp.where(row >= 2, mm, 0.0)
            M1[z, h] = m1
            M2[z, h] = mm
            M4[z, h] = m4
            t = m * ahead(m, 1, 1.0)
            t = t * ahead(t, 2, 1.0)
            chains.append(t * ahead(t, 4, 1.0))
            f1 = jnp.where(row < 7, f, 0.0)
            ff = jnp.where(row < 6, f1 * behind(f, 1, 0.0), 0.0)
            f4 = jnp.where(row < 4, ff * pltpu.roll(ff, 6, 0), 0.0)
            F1[z, h] = f1
            F2[z, h] = ff
            F4[z, h] = f4
            f1s.append(f1)
            f2s.append(ff)
            f4s.append(f4)
            t = f * behind(f, 1, 1.0)
            t = t * behind(t, 2, 1.0)
            tails.append(t * behind(t, 4, 1.0))
        MT[z] = chains[1]
        FT[z] = tails[0]
        left = [chains[0], chains[1] * jnp.broadcast_to(chains[0][7:8], (8, LANES))]
        left = fold_up(left, f1s, f2s, f4s, tails[0])
        right = [tails[0] * jnp.broadcast_to(tails[1][0:1], (8, LANES)), tails[1]]
        for h in range(2):
            LL[z, h] = left[h]
            RC[z, h] = right[h]
        return carry

    lax.fori_loop(0, NZL, factor, 0)
    for k, ref2 in enumerate((l2, r2)):
        MS[2 * k] = level(ref2, 0)
        MS[2 * k + 1] = level(ref2, NXC - 1)

    def to_chips(src_of, dst, send_sem, recv_sem):
        for j in FAR_FIRST:
            target = lax.rem(chip + j, CHIPS)
            pltpu.make_async_remote_copy(
                src_ref=src_of(target),
                dst_ref=dst.at[chip],
                send_sem=send_sem,
                recv_sem=recv_sem,
                device_id=(2 * target + q, mv, mp),
                device_id_type=MESH,
            ).start()

    def arrive(slots, sem):
        got = slots.at[pl.ds(1, CHIPS - 1)]
        pltpu.make_async_copy(got, got, sem).wait()

    pl.semaphore_wait(LT.at[1], in_near)

    @pl.when(jnp.logical_not(upper))
    def _():
        pl.semaphore_wait(LD, 4)

    call(LT.at[2], (partner, mv, mp))

    my_o = lax.rem(chip + FIRST, CHIPS)
    is_owner = my_o < OWNERS
    owner_sends = jnp.where(is_owner, OWNERS - 1, OWNERS)

    def to_owners(src_of, dst, send_sem, recv_sem):
        for j in FAR_FIRST:
            target = lax.rem(chip + j, CHIPS)
            o = lax.rem(target + FIRST, CHIPS)

            @pl.when(o < OWNERS)
            def _():
                pltpu.make_async_remote_copy(
                    src_ref=src_of(o),
                    dst_ref=dst,
                    send_sem=send_sem,
                    recv_sem=recv_sem,
                    device_id=(2 * target + q, mv, mp),
                    device_id_type=MESH,
                ).start()

        @pl.when(is_owner)
        def _():
            pltpu.make_async_copy(src_of(my_o), dst, recv_sem).start()

    for k in range(4):
        value = MS[k]
        for o in range(OWNERS):
            QS[k, o] = value[ROWS * o : ROWS * o + ROWS]
    to_owners(lambda o: QS.at[:, o], QR.at[chip], q_send, q_recv)

    for i in (3,):
        own_copies[i].wait()
        side_copies[i].wait_recv()

    first = lane == 0
    last = lane == LANES - 1

    def eliminate(s, A, low, count, unroll):
        if s is not None:
            edges = [[YR[s, side, h] for h in range(2)] for side in range(2)]

        def plane(z, carry):
            cross = []
            for h in range(2):
                v = VEL[1, z, h]
                w = VEL[2, z, h]
                cross.append(
                    (
                        cross_coef + cross_conv * jnp.maximum(-v, 0.0),
                        cross_coef + cross_conv * jnp.maximum(v, 0.0),
                        cross_coef + cross_conv * jnp.maximum(-w, 0.0),
                        cross_coef + cross_conv * jnp.maximum(w, 0.0),
                    )
                )
            ip = [IP[z, h] for h in range(2)]
            m1 = [M1[z, h] for h in range(2)]
            m2 = [M2[z, h] for h in range(2)]
            m4 = [M4[z, h] for h in range(2)]
            f1 = [F1[z, h] for h in range(2)]
            f2 = [F2[z, h] for h in range(2)]
            f4 = [F4[z, h] for h in range(2)]
            mt = MT[z]
            ft = FT[z]
            for c in range(NC):
                k = c * NZL + z
                o = []
                for h in range(2):
                    south, north, below, above = cross[h]
                    a = A[c, z + 1, h]
                    lo = hi = blank
                    if s is not None:
                        lo = pltpu.roll(edges[0][h], lax.rem(LANES - k, LANES), 1)
                        hi = pltpu.roll(edges[1][h], LANES - 1 - k, 1)
                    y_lo = jnp.where(first, lo, pltpu.roll(a, 1, 1))
                    y_hi = jnp.where(last, hi, pltpu.roll(a, LANES - 1, 1))
                    rhs = SRC[c, z, h] + shift_coef * a
                    rhs = rhs + south * y_lo + north * y_hi
                    rhs = rhs + below * A[c, z, h] + above * A[c, z + 2, h]
                    v = rhs * ip[h]
                    v = v + m1[h] * pltpu.roll(v, 1, 0)
                    v = v + m2[h] * pltpu.roll(v, 2, 0)
                    v = v + m4[h] * pltpu.roll(v, 4, 0)
                    o.append(v)
                o[1] = o[1] + mt * jnp.broadcast_to(o[0][7:8], (8, LANES))
                p = fold_up(o, f1, f2, f4, ft)
                for h in range(2):
                    PP[c, z, h] = p[h]
            return carry

        lax.fori_loop(low, low + count, plane, 0, unroll=unroll)

    own_copies[0].wait()
    side_copies[0].wait_recv()
    first_arrivals()
    pl.semaphore_wait(LP.at[0], v_near)
    call_line(LP.at[1], True)
    eliminate(0, A1, 0, NZL, 12)
    for c in range(NC):
        for i, x in enumerate((0, NXC - 1)):
            value = level(p2, x, c)
            for o in range(OWNERS):
                S1[i, c, o] = value[ROWS * o : ROWS * o + ROWS]
    to_owners(lambda o: S1.at[:, :, o], G1.at[chip], p_send.at[0], p_recv.at[0])
    pl.semaphore_wait(LP.at[1], v_near)
    call_line(LP.at[2], False)
    to_chips(lambda target: MS, MR, m_send, m_recv)

    own_copies[4].wait()
    side_copies[4].wait_recv()

    def indicator(digit, count):
        return jnp.concatenate(
            [jnp.where(digit == i, 1.0, 0.0) for i in range(count)], axis=0
        ).astype(jnp.bfloat16)

    digit32 = lax.broadcasted_iota(jnp.int32, (32, LANES), 0)

    def onehot(z, carry):
        for h in range(2):
            cut = slice(h * LANES, (h + 1) * LANES)
            low = lax.rem(BAND[z, h], 32)
            OHL[z, :, cut] = jnp.concatenate(
                [
                    jnp.where(jnp.broadcast_to(low[x : x + 1], (32, LANES)) == digit32, 1.0, 0.0)
                    for x in range(8)
                ],
                axis=0,
            ).astype(jnp.bfloat16)
            OHH[z, :, cut] = indicator(BAND[z, h] // 32, 8)
        return carry

    lax.fori_loop(0, NZL, onehot, 0)

    @pl.when(is_owner)
    def _():
        pltpu.make_async_copy(QR, QR, q_recv).wait()
        ahead_f = jnp.zeros((ROWS, LANES), F32)
        for k in range(CHIPS):
            lf, lg, rf, rg = (QR[k, i] for i in range(4))
            inv = 1.0 / (1.0 - lf * ahead_f)
            b = lg * inv
            g = b * ahead_f
            for i, value in enumerate((g, b, inv, lf * inv, rf * inv, ahead_f)):
                CO[k, i] = value
            ahead_f = rg + g * rf

        pltpu.make_async_copy(G1, G1, p_recv.at[0]).wait()
        nil = jnp.zeros((ROWS, LANES), F32)
        O = [nil] * NC
        for k in range(CHIPS):
            for c in range(NC):
                OC[k, c] = O[c]
                O[c] = G1[k, 1, c] + CO[k, 0] * G1[k, 0, c] + CO[k, 1] * O[c]
        after = [nil] * NC
        for k in reversed(range(CHIPS)):
            for c in range(NC):
                D1[k, 1, c] = after[c]
                before = OC[k, c]
                after[c] = CO[k, 2] * G1[k, 0, c] + CO[k, 3] * before + CO[k, 4] * after[c]
                D1[k, 0, c] = CO[k, 5] * after[c] + before

        for j in FAR_FIRST:
            target = lax.rem(chip + j, CHIPS)
            pltpu.make_async_remote_copy(
                src_ref=D1.at[target],
                dst_ref=R1.at[:, :, my_o],
                send_sem=d_send,
                recv_sem=d_recv,
                device_id=(2 * target + q, mv, mp),
                device_id_type=MESH,
            ).start()

        pltpu.make_async_copy(D1.at[chip], R1.at[:, :, my_o], d_recv).start()

    arrive(MR, m_recv)

    row_z = lax.broadcasted_iota(jnp.int32, (NZL, LANES), 0)
    lane_z = lax.broadcasted_iota(jnp.int32, (NZL, LANES), 1)

    def write_edges(ref, values):
        packed = jnp.zeros((NZL, LANES), F32)
        for c in range(NC):
            v = values[c]
            for side in range(2):
                ref[2 * c + side : 2 * c + side + 1, :] = v[
                    side * (NZL - 1) : side * (NZL - 1) + 1
                ]
                column = v[:, side * (LANES - 1) : side * (LANES - 1) + 1]
                packed = jnp.where(
                    lane_z == NZL * (2 * c + side) + row_z,
                    jnp.broadcast_to(column, (NZL, LANES)),
                    packed,
                )
        ref[6:7, :] = jnp.sum(packed, axis=0, keepdims=True)
        ref[7:8, :] = jnp.zeros((1, LANES), F32)

    def upstream(k, F):
        lf, lg, rf, rg = (MR[k, i] for i in range(4))
        b = lg / (1.0 - lf * F)
        g = b * F
        CB[k] = b
        return rg + g * rf

    def downstream(i, H):
        k = CHIPS - 1 - i
        lf, lg, rf, rg = (MR[k, i] for i in range(4))
        b = rf / (1.0 - rg * H)
        g = b * H
        CB[k] = b
        return lf + g * lg

    none = jnp.zeros((NZL, LANES), F32)
    F = lax.fori_loop(0, chip, upstream, none)
    H = lax.fori_loop(0, CHIPS - 1 - chip, downstream, none)
    lf, lg, rf, rg = (MS[i] for i in range(4))
    from_left = 1.0 - lf * F
    from_right = 1.0 - rg * H
    inv = 1.0 / (from_left * from_right - (F * rf) * (H * lg))
    for i, value in enumerate(
        (
            F,
            H,
            from_right * inv,
            F * rf * inv,
            H * lg * inv,
            from_left * inv,
            lg / from_left * F,
            rf / from_right * H,
        )
    ):
        OWN[i] = value

    def close(incoming):
        for c in range(NC):
            first_p = level(p2, 0, c)
            last_p = level(p2, NXC - 1, c)
            x = OWN[0] * first_p + incoming[0][c]
            y = OWN[1] * last_p + incoming[1][c]
            AL[c] = OWN[2] * x + OWN[3] * y
            AR[c] = OWN[4] * x + OWN[5] * y

    def solved(c, z, h):
        return (
            PP[c, z, h]
            + LL[z, h] * jnp.broadcast_to(AL[c, pl.ds(z, 1), :], (8, LANES))
            + RC[z, h] * jnp.broadcast_to(AR[c, pl.ds(z, 1), :], (8, LANES))
        )

    pltpu.make_async_copy(R1, R1, d_recv).wait()
    pl.semaphore_wait(LP.at[2], p_near)
    call_line(LP.at[3], False)
    trio = (none,) * NC
    for c in range(NC):
        for o in range(OWNERS):
            AL[c, ROWS * o : ROWS * o + ROWS, :] = R1[0, c, o]
            AR[c, ROWS * o : ROWS * o + ROWS, :] = R1[1, c, o]

    def line_first(z, packs):
        for c in range(NC):
            pair = tuple(solved(c, z, h) for h in range(2))
            for h in range(2):
                A2[c, z + 1, h] = pair[h]
            packs = pack_edges(c * NZL + z, pair, packs)
        return packs

    halo2 = send_halo(1, A2, lax.fori_loop(0, NZL, line_first, no_packs, unroll=12))

    def ends(write):
        for c in range(NC):
            first_p = level(p2, 0, c)
            last_p = level(p2, NXC - 1, c)
            write(c, last_p + OWN[6] * first_p, first_p + OWN[7] * last_p)

    def write_rows(c, up, down):
        S2[0, c] = up
        S2[1, c] = down

    def side_of(target):
        return jnp.where(target > chip, 0, 1)

    eliminate(None, A2, 1, NZL - 2, 10)
    ends(write_rows)
    to_chips(lambda target: S2.at[side_of(target)], R2, p_send.at[1], p_recv.at[1])

    def edge_coefficients(k, carry):
        write_edges(CE.at[k], (CB[k],) * NC)
        return carry

    lax.fori_loop(0, chip, edge_coefficients, 0)
    lax.fori_loop(chip + 1, CHIPS, edge_coefficients, 0)

    each(halo2, 2, lambda c: c.wait_recv())
    pl.semaphore_wait(LP.at[3], p_near)
    call_line(LP.at[4], False)
    eliminate(1, A2, 0, NZL, 12)
    final = ([], [])

    def keep_ends(c, up, down):
        final[0].append(up)
        final[1].append(down)

    ends(keep_ends)
    for i in range(2):
        write_edges(E2.at[i], final[i])
    to_chips(lambda target: E2.at[side_of(target)], RE, e_send, e_recv)
    ways = ((chip, lambda i: i), (CHIPS - 1 - chip, lambda i: CHIPS - 1 - i))
    arrive(R2, p_recv.at[1])

    def bring(k, O):
        return tuple(R2[k, c] + CB[k] * O[c] for c in range(NC))

    rows_brought = [
        lax.fori_loop(0, steps, lambda i, v: bring(chip_of(i), v), trio) for steps, chip_of in ways
    ]
    arrive(RE, e_recv)

    def brought(O, way):
        steps, chip_of = way
        edge = lax.fori_loop(
            0, steps, lambda i, v: RE[chip_of(i)] + CE[chip_of(i)] * v, blank
        )
        packed = jnp.broadcast_to(edge[6:7], (NZL, LANES))
        whole = []
        for c in range(NC):
            value = O[c]
            for side in range(2):
                at = lane_z == NZL * (2 * c + side) + row_z
                column = jnp.sum(jnp.where(at, packed, 0.0), axis=1, keepdims=True)
                value = jnp.where(
                    lane_z == side * (LANES - 1), jnp.broadcast_to(column, (NZL, LANES)), value
                )
            for side in range(2):
                value = jnp.where(
                    row_z == side * (NZL - 1),
                    jnp.broadcast_to(edge[2 * c + side : 2 * c + side + 1], (NZL, LANES)),
                    value,
                )
            whole.append(value)
        return whole

    close(
        (
            brought(rows_brought[0], ways[0]),
            brought(rows_brought[1], ways[1]),
        )
    )

    pl.semaphore_wait(LT.at[2], 1)
    pl.semaphore_wait(LP.at[4], p_near)

    def line_last(z, acc):
        parts = ([], [])
        for h in range(2):
            total = None
            for c in range(NC):
                a = solved(c, z, h)
                A3[c, z, h] = a
                term = VEL[c, z, h] * a
                total = term if total is None else total + term
            total = total * PEN[z, h]
            coarse = total.astype(jnp.bfloat16).astype(F32)
            for part, value in zip(parts, (coarse, total - coarse)):
                part.append(jnp.concatenate([value, value], axis=0).astype(jnp.bfloat16))
        weights = jnp.concatenate(
            [
                jnp.concatenate([jnp.concatenate(part, axis=1)] * 4, axis=0) * OHH[z]
                for part in parts
            ],
            axis=0,
        )
        return acc + lax.dot_general(
            weights, OHL[z], (((1,), (1,)), ((), ())), preferred_element_type=F32
        )

    acc = lax.fori_loop(0, NZL, line_last, jnp.zeros((LANES, 2 * LANES), F32), unroll=12)
    acc = acc[0:64] + acc[64:128]
    keep = [lane // 32 + 4 * r == row for r in range(2)]
    tall = blank
    for j in range(8):
        tile = acc[8 * j : 8 * j + 8]
        own_x = jnp.where(keep[0], tile[:, 0:LANES], 0.0) + jnp.where(
            keep[1], tile[:, LANES : 2 * LANES], 0.0
        )
        line = jnp.sum(own_x, axis=0, keepdims=True)
        tall = jnp.where(row == j, jnp.broadcast_to(line, (8, LANES)), tall)
    tall = tall + pltpu.roll(tall, 64, 1)
    tall = tall + pltpu.roll(tall, 32, 1)
    for r in range(2):
        B1S[r : r + 1, :] = jnp.sum(jnp.where(keep[r], tall, 0.0), axis=0, keepdims=True)

    def band_round(r, own, slots, order, device_of, beside):
        for j in order:
            pltpu.make_async_remote_copy(
                src_ref=own,
                dst_ref=slots.at[j],
                send_sem=b_send.at[r],
                recv_sem=b_recv.at[r],
                device_id=device_of(j),
                device_id_type=MESH,
            ).start()
        beside()
        got = slots.at[pl.ds(1, STREAM - 1)]
        pltpu.make_async_copy(got, got, b_recv.at[r]).wait()
        terms = [own[...]] + [slots[j] for j in range(1, STREAM)]
        while len(terms) > 1:
            terms = [terms[i] + terms[i + 1] for i in range(0, len(terms), 2)]
        return terms[0]

    def drain(count, ref, sem):
        def one(j, carry):
            pltpu.make_async_copy(ref, ref, sem).wait()
            return carry

        lax.fori_loop(0, count, one, 0)

    def sent(bytes_like, sem):
        pltpu.make_async_copy(bytes_like, bytes_like, sem).wait()

    out_own = pltpu.make_async_copy(A3.at[:, :, q], out_h.at[:, :, :, lanes_of(q)], out_sem.at[0])
    out_side = pltpu.make_async_remote_copy(
        src_ref=A3.at[:, :, 1 - q],
        dst_ref=out_h.at[:, :, :, lanes_of(q)],
        send_sem=out_sem.at[1],
        recv_sem=out_sem.at[2],
        device_id=(partner, mv, mp),
        device_id_type=MESH,
    )

    def beside_first():
        out_own.start()
        out_side.start()
        for copy in side_copies:
            copy.wait_send()
        for copy, there in first_halo:
            pl.when(there)(copy.wait_send)
        middle.wait_send()
        each(halo2, 1, lambda c: c.wait_send())
        others = pl.ds(1, CHIPS - 1)
        sent(MR.at[others], m_send)
        sent(R2.at[others], p_send.at[1])
        sent(RE.at[others], e_send)
        drain(owner_sends, QS.at[:, 0], q_send)
        drain(owner_sends, S1.at[:, :, 0], p_send.at[0])

        @pl.when(is_owner)
        def _():
            sent(D1.at[others], d_send)

        tb_copy.wait()
        tw_copy.wait()

    def beside_second():
        sent(B1R.at[pl.ds(1, STREAM - 1)], b_send.at[0])
        out_own.wait()
        out_side.wait()

    line_order = (8, 7, 9, 6, 10, 5, 11, 4, 12, 3, 13, 2, 14, 1, 15)
    plane_order = (10, 6, 9, 11, 14, 2, 8, 5, 7, 13, 15, 1, 3, 4, 12)
    B2S[...] = band_round(
        0, B1S, B1R, line_order, lambda j: (lax.rem(me + j, STREAM), mv, mp), beside_first
    )
    bands = band_round(
        1,
        B2S,
        B2R,
        plane_order,
        lambda j: (me, lax.rem(mv + j // SPAN, VERT), lax.rem(mp + j % SPAN, SPAN)),
        beside_second,
    )
    cells = STREAM * VERT * SPAN * NXL * NZL * NYL
    bands = bands * ((NBANDS / cells) ** 0.5)
    tb = TB[...].reshape(1, LANES)
    spot = lax.rem(tb, LANES)
    spot = jnp.broadcast_to(spot, (8, LANES))
    low_half = jnp.take_along_axis(jnp.broadcast_to(bands[0:1], (8, LANES)), spot, axis=1)
    high_half = jnp.take_along_axis(jnp.broadcast_to(bands[1:2], (8, LANES)), spot, axis=1)
    picked = jnp.where(tb < LANES, low_half[0:1], high_half[0:1])
    tri_ref[...] = (TW[...].reshape(1, LANES) * picked).reshape(LANES)
    sent(B2R.at[pl.ds(1, STREAM - 1)], b_send.at[1])


def shards(adjoint_source, velocity, penalty, adjoint_start, cell_band, tri_band, tri_weight):
    anywhere = pl.BlockSpec(memory_space=pl.ANY)

    def field():
        return pltpu.VMEM((NZL, 2, 8, LANES), F32)

    scratch = [
        pltpu.VMEM((NC, NZL, 2, 8, LANES), F32),
        pltpu.VMEM((NC, NZL, 2, 8, LANES), F32),
        field(),
        pltpu.VMEM((NZL, 2, 8, LANES), jnp.int32),
        pltpu.VMEM((NC, NZL + 2, 2, 8, LANES), F32),
        pltpu.VMEM((NC, NZL + 2, 2, 8, LANES), F32),
        pltpu.VMEM((NC, NZL, 2, 8, LANES), F32),
        pltpu.VMEM((NC, NZL, 2, 8, LANES), F32),
        field(),
        field(),
        field(),
        field(),
        pltpu.VMEM((NZL, 8, LANES), F32),
        field(),
        field(),
        field(),
        pltpu.VMEM((NZL, 8, LANES), F32),
        field(),
        field(),
        pltpu.VMEM((NC, NZL, NXL, NYL), F32),
        pltpu.VMEM((4, 8, LANES), F32),
        pltpu.VMEM((SWEEPS, 2, 2, 8, LANES), F32),
        pltpu.VMEM((SWEEPS, 2, 2, 8, LANES), F32),
        pltpu.VMEM((4, NZL, LANES), F32),
        pltpu.VMEM((CHIPS, 4, NZL, LANES), F32),
        pltpu.VMEM((CHIPS, NZL, LANES), F32),
        pltpu.VMEM((CHIPS, 8, LANES), F32),
        pltpu.VMEM((8, NZL, LANES), F32),
        pltpu.VMEM((4, OWNERS, ROWS, LANES), F32),
        pltpu.VMEM((CHIPS, 4, ROWS, LANES), F32),
        pltpu.VMEM((CHIPS, 6, ROWS, LANES), F32),
        pltpu.VMEM((CHIPS, NC, ROWS, LANES), F32),
        pltpu.VMEM((2, NC, OWNERS, ROWS, LANES), F32),
        pltpu.VMEM((CHIPS, 2, NC, ROWS, LANES), F32),
        pltpu.VMEM((CHIPS, 2, NC, ROWS, LANES), F32),
        pltpu.VMEM((2, NC, OWNERS, ROWS, LANES), F32),
        pltpu.VMEM((2, NC, NZL, LANES), F32),
        pltpu.VMEM((CHIPS, NC, NZL, LANES), F32),
        pltpu.VMEM((2, 8, LANES), F32),
        pltpu.VMEM((CHIPS, 8, LANES), F32),
        pltpu.VMEM((NC, NZL, LANES), F32),
        pltpu.VMEM((NC, NZL, LANES), F32),
        pltpu.VMEM((NZL, 64, 2 * LANES), jnp.bfloat16),
        pltpu.VMEM((NZL, 2 * LANES, 2 * LANES), jnp.bfloat16),
        pltpu.VMEM((2, LANES), F32),
        pltpu.VMEM((STREAM, 2, LANES), F32),
        pltpu.VMEM((2, LANES), F32),
        pltpu.VMEM((STREAM, 2, LANES), F32),
        pltpu.VMEM((LANES,), jnp.int32),
        pltpu.VMEM((LANES,), F32),
        pltpu.SemaphoreType.DMA((6,)),
        pltpu.SemaphoreType.DMA((5,)),
        pltpu.SemaphoreType.DMA((5,)),
        pltpu.SemaphoreType.DMA((3,)),
        pltpu.SemaphoreType.DMA((2,)),
        pltpu.SemaphoreType.REGULAR((3,)),
        pltpu.SemaphoreType.REGULAR,
        pltpu.SemaphoreType.REGULAR((5,)),
        pltpu.SemaphoreType.DMA((2, 2)),
        pltpu.SemaphoreType.DMA((2, 2)),
        pltpu.SemaphoreType.DMA((3,)),
        pltpu.SemaphoreType.DMA((3,)),
        pltpu.SemaphoreType.DMA((SWEEPS, 4)),
        pltpu.SemaphoreType.DMA((SWEEPS, 4)),
        pltpu.SemaphoreType.DMA,
        pltpu.SemaphoreType.DMA,
        pltpu.SemaphoreType.DMA,
        pltpu.SemaphoreType.DMA,
        pltpu.SemaphoreType.DMA,
        pltpu.SemaphoreType.DMA,
        pltpu.SemaphoreType.DMA((SWEEPS,)),
        pltpu.SemaphoreType.DMA((SWEEPS,)),
        pltpu.SemaphoreType.DMA,
        pltpu.SemaphoreType.DMA,
        pltpu.SemaphoreType.DMA((2,)),
        pltpu.SemaphoreType.DMA((2,)),
    ]

    def planes(x):
        return jnp.swapaxes(x, -3, -2)

    adjoint, tri_grad = pl.pallas_call(
        kernel,
        out_shape=(
            jax.ShapeDtypeStruct((NC, NZL, NXL, NYL), F32),
            jax.ShapeDtypeStruct((LANES,), F32),
        ),
        in_specs=[pl.BlockSpec(memory_space=pltpu.HBM)] * 7,
        out_specs=(anywhere, pl.BlockSpec(memory_space=pltpu.VMEM)),
        scratch_shapes=scratch,
        compiler_params=pltpu.CompilerParams(
            collective_id=0, has_side_effects=True, vmem_limit_bytes=32 * 1024 * 1024
        ),
    )(
        *(
            pltpu.with_memory_space_constraint(x, pltpu.HBM)
            for x in (
                planes(adjoint_source),
                planes(velocity),
                planes(penalty),
                planes(adjoint_start),
                planes(cell_band),
                tri_band,
                tri_weight,
            )
        )
    )
    return planes(adjoint), tri_grad


def solution(mesh):
    return jax.shard_map(
        shards,
        mesh=mesh,
        in_specs=(
            P(None, "stream", "span", "vert"),
            P(None, "stream", "span", "vert"),
            P("stream", "span", "vert"),
            P(None, "stream", "span", "vert"),
            P("stream", "span", "vert"),
            P(("stream", "vert", "span")),
            P(("stream", "vert", "span")),
        ),
        out_specs=(P(None, "stream", "span", "vert"), P(("stream", "vert", "span"))),
        check_vma=False,
    )
```
